32 devices in a mesh: dp: 4 (over y, x), ctx: 8 (over z, core).
Axes of the slice: x: 2, y: 2, z: 4, core: 2. Of those that a mesh axis runs over, the one named last changes fastest.
Arguments:
- hyena_q: bfloat16 [4096, 4096], P(('dp', 'ctx')), parts along dimension 0, may hold values from -6 to 6
- hyena_k: bfloat16 [4096, 4096], P(('dp', 'ctx')), parts along dimension 0, may hold values from -6 to 6
- hyena_v: bfloat16 [4096, 4096], P(('dp', 'ctx')), parts along dimension 0, may hold values from -6 to 6
- short_filter: float32 [3, 3, 4096], replicated, may hold values from -3.5 to 3.5
- residue: float32 [4096, 16], P('ctx'), may hold values from -0.09375 to 0.09375
- decay_rate: float32 [4096, 16], P('ctx'), may hold values from 0.00024414062 to 0.034
- att_query: bfloat16 [4096, 4096], P(('dp', 'ctx')), parts along dimension 0, may hold values from -32 to 32
- att_key: bfloat16 [4096, 4096], P(('dp', 'ctx')), parts along dimension 0, may hold values from -6 to 6
- att_value: bfloat16 [4096, 4096], P(('dp', 'ctx')), parts along dimension 0, may hold values from -6 to 6
Outputs:
- hyena_out: bfloat16 [4096, 4096], P(('dp', 'ctx')), parts along dimension 0
- att_out: bfloat16 [4096, 4096], P(('dp', 'ctx')), parts along dimension 0
The draws below stay inside these ranges and needn't reach their ends.
There are 4 independent parts, one for each index of `dp`. The reference program is written for one: setup_inputs(seed, part) draws one part's arguments, and reference() takes and returns one part's arrays. A program takes and returns all parts, laid end to end along the dimension named above; an argument that names none is the same for every part. Nothing has to cross between parts.
All inputs are finite; a program needn't handle non-finite values.
Results may differ from the reference program's by a relative error of at most 0.0058.
Values may be sent and summed in bfloat16 or wider, within the bound.
No kernel may reach another device: no remote copies, remote signals or barrier semaphores. Data moves between devices by JAX's collectives and lax.ppermute only.
A program may use at most 128 MiB of HBM per device.

```python
import math
import jax
import jax.numpy as jnp
from jax import lax

D = 4096
HEADS = 32
HEAD_DIM = 128
ORDER = 16
TAPS = 3
SEQ = 1024


def draw_att_query(key, part):
    key = jax.random.fold_in(key, 11)
    return jnp.clip(jax.random.normal(key, (SEQ, D), jnp.float32), -6.0, 6.0).astype(jnp.bfloat16)


def draw_att_key(key, part):
    key = jax.random.fold_in(key, 12)
    return jnp.clip(jax.random.normal(key, (SEQ, D), jnp.float32), -6.0, 6.0).astype(jnp.bfloat16)


def draw_decay_rate(key, part):
    key = jax.random.fold_in(key, 13)
    lowest = 0.5 / SEQ
    highest = 1.0 / 30.0
    uniform_draw = jax.random.uniform(key, (D, ORDER), jnp.float32)
    return jnp.exp(math.log(lowest) + (math.log(highest) - math.log(lowest)) * uniform_draw)


def block_scale(stream_key, shape, pieces, least, high):
    def one(dim, parts):
        steps = jax.random.uniform(jax.random.fold_in(jax.random.fold_in(stream_key, 6), dim), (parts,), jnp.float32, least / len(pieces), high / len(pieces))
        return jnp.repeat(jnp.exp(steps), shape[dim] // parts).reshape((-1,) + (1,) * (len(shape) - dim - 1))

    factor_of = one(*pieces[0])
    for cut in pieces[1:]:
        factor_of = factor_of * one(*cut)
    return factor_of


def centred(own_key, dims, spread, reach, split=(), kind=jnp.bfloat16):
    drawn = spread * jax.random.normal(own_key, dims, jnp.float32)
    if split:
        drawn = drawn * block_scale(own_key, dims, split, -0.22, 0.18)
    return jnp.clip(drawn, -reach, reach).astype(kind)


def setup_inputs(seed: int = 0, part: int = 0) -> dict:
    key_of = jax.random.split(jax.random.key(seed), 10)
    part_splits = jax.random.split(jax.random.fold_in(key_of[9], part), 10)
    return {
        "hyena_q": centred(part_splits[0], (SEQ, D), 1.0, 6.0, ((0, 8),)),
        "hyena_k": centred(part_splits[1], (SEQ, D), 1.0, 6.0, ((0, 8),)),
        "hyena_v": centred(part_splits[2], (SEQ, D), 1.0, 6.0, ((0, 8),)),
        "short_filter": centred(key_of[3], (3, TAPS, D), 0.6, 3.5, (), jnp.float32),
        "residue": centred(key_of[4], (D, ORDER), (2.0 / (ORDER * SEQ) ** 0.5), 0.09375, ((0, 8),), jnp.float32),
        "decay_rate": draw_decay_rate(jax.random.fold_in(key_of[9], 71), part),
        "att_query": draw_att_query(jax.random.fold_in(jax.random.fold_in(key_of[9], part), 71), part),
        "att_key": draw_att_key(jax.random.fold_in(jax.random.fold_in(key_of[9], part), 71), part),
        "att_value": centred(part_splits[8], (SEQ, D), 1.0, 6.0, ((0, 8),)),
    }


def short_mix(feature, tap_weights):
    values = feature.astype(jnp.float32)
    padded = jnp.concatenate([jnp.zeros((TAPS - 1, values.shape[1]), jnp.float32), values], 0)
    length = values.shape[0]
    result = tap_weights[0] * padded[TAPS - 1:TAPS - 1 + length]
    for offset in range(1, TAPS):
        result = result + tap_weights[offset] * padded[TAPS - 1 - offset:TAPS - 1 - offset + length]
    return result


def long_kernel(residue, decay_rate, length):
    time_index = jnp.arange(length, dtype=jnp.float32)[:, None]
    kernel = jnp.zeros((length, residue.shape[0]), jnp.float32)
    for mode_index in range(ORDER):
        kernel = kernel + residue[:, mode_index] * jnp.exp(-decay_rate[:, mode_index] * time_index)
    return kernel


def one_head(items):
    query_head, key_head, value_head = items
    scores = jnp.dot(query_head, key_head.T, preferred_element_type=jnp.float32) * (HEAD_DIM ** -0.5)
    row_pos = jnp.arange(SEQ, dtype=jnp.int32)[:, None]
    col_pos = jnp.arange(SEQ, dtype=jnp.int32)[None, :]
    scores = jnp.where(col_pos <= row_pos, scores, -jnp.inf)
    row_top = jnp.max(scores, axis=1, keepdims=True)
    expo = jnp.exp(scores - row_top)
    denominator = jnp.sum(expo, axis=1)
    weights = expo.astype(jnp.bfloat16)
    mixed_out = jnp.dot(weights, value_head, preferred_element_type=jnp.float32) / denominator[:, None]
    return mixed_out.astype(jnp.bfloat16)


def reference(hyena_q, hyena_k, hyena_v, short_filter, residue, decay_rate, att_query, att_key, att_value):
    query_mix = short_mix(hyena_q, short_filter[0])
    key_mix = short_mix(hyena_k, short_filter[1])
    value_mix = short_mix(hyena_v, short_filter[2])
    product = lax.optimization_barrier((key_mix * value_mix).astype(jnp.bfloat16))
    kernel = long_kernel(residue, decay_rate, SEQ)
    spectrum = jnp.fft.rfft(product.astype(jnp.float32), n=2 * SEQ, axis=0) * jnp.fft.rfft(kernel, n=2 * SEQ, axis=0)
    smoothed = jnp.fft.irfft(spectrum, n=2 * SEQ, axis=0)[:SEQ].astype(jnp.bfloat16)
    smoothed = lax.optimization_barrier(smoothed)
    hyena_out = (query_mix * smoothed.astype(jnp.float32)).astype(jnp.bfloat16)

    def by_heads(matrix):
        return matrix.reshape(SEQ, HEADS, HEAD_DIM).transpose(1, 0, 2)

    heads = lax.map(one_head, (by_heads(att_query), by_heads(att_key), by_heads(att_value)))
    att_out = heads.transpose(1, 0, 2).reshape(SEQ, D)
    return (hyena_out, att_out)
```

```python
import functools
import math

import jax
import jax.numpy as jnp
from jax import lax
from jax.experimental import pallas as pl
from jax.experimental.pallas import tpu as pltpu
from jax.sharding import PartitionSpec as P

HEAD_DIM = 128
LANES = 128
SUBLANES = 8
CHUNKS = 4
NEGATIVE = -1e30
EXP_SCALE = HEAD_DIM**-0.5 * math.log2(math.e)
VMEM_LIMIT = 40 * 1024 * 1024


def params(**kwargs):
    return pltpu.CompilerParams(vmem_limit_bytes=VMEM_LIMIT, **kwargs)


def to_positions(source_ref, scratch_ref, first):
    rows, columns = source_ref.shape
    step = 16
    for start in range(0, rows, step):
        for block in range(columns // LANES):
            piece = source_ref[start : start + step, block * LANES : (block + 1) * LANES]
            scratch_ref[pl.ds((first + start) * SUBLANES + block, step, SUBLANES), :] = piece.astype(
                jnp.float32
            )


def rim_to_positions(rim_ref, first_row, scratch_ref):
    taps = 2
    for block in range(rim_ref.shape[1] // LANES):
        piece = rim_ref[first_row : first_row + taps, block * LANES : (block + 1) * LANES]
        scratch_ref[pl.ds(block, taps, SUBLANES), :] = piece


def vector_at(ref, position):
    return ref[pl.ds(pl.multiple_of(position * SUBLANES, SUBLANES), SUBLANES), :]


def state_kernel(modes, k_ref, v_ref, rim_ref, taps_ref, par_ref, p_ref, s_ref, k_scr, v_scr):
    rows = k_ref.shape[0]
    to_positions(k_ref, k_scr, 2)
    to_positions(v_ref, v_scr, 2)
    rim_to_positions(rim_ref, 2, k_scr)
    rim_to_positions(rim_ref, 4, v_scr)
    decay = [
        jnp.exp(-par_ref[pl.ds(mode, SUBLANES, 2 * modes), :]) for mode in range(modes)
    ]
    k_taps = [taps_ref[3 + tap] for tap in range(3)]
    v_taps = [taps_ref[6 + tap] for tap in range(3)]

    def body(position, carry):
        k_two, k_one, v_two, v_one, states = carry
        k_now = vector_at(k_scr, position + 2)
        v_now = vector_at(v_scr, position + 2)
        k_mix = k_taps[0] * k_now + k_taps[1] * k_one + k_taps[2] * k_two
        v_mix = v_taps[0] * v_now + v_taps[1] * v_one + v_taps[2] * v_two
        product = (k_mix * v_mix).astype(jnp.bfloat16).astype(jnp.float32)
        p_ref[pl.ds(pl.multiple_of(position * SUBLANES, SUBLANES), SUBLANES), :] = product
        states = tuple(state * rate + product for state, rate in zip(states, decay))
        return (k_one, k_now, v_one, v_now, states)

    zero = jnp.zeros((SUBLANES, LANES), jnp.float32)
    start = (
        vector_at(k_scr, 0),
        vector_at(k_scr, 1),
        vector_at(v_scr, 0),
        vector_at(v_scr, 1),
        (zero,) * modes,
    )
    states = lax.fori_loop(0, rows, body, start, unroll=4)[4]
    for mode in range(modes):
        s_ref[pl.ds(mode, SUBLANES, modes), :] = states[mode]


def output_kernel(
    modes, q_ref, p_ref, rim_ref, taps_ref, par_ref, carry_ref, out_ref, q_scr, out_scr
):
    rows = q_ref.shape[0]
    to_positions(q_ref, q_scr, 2)
    rim_to_positions(rim_ref, 0, q_scr)
    decay = [
        jnp.exp(-par_ref[pl.ds(mode, SUBLANES, 2 * modes), :]) for mode in range(modes)
    ]
    residue = [par_ref[pl.ds(modes + mode, SUBLANES, 2 * modes), :] for mode in range(modes)]
    q_taps = [taps_ref[tap] for tap in range(3)]

    def body(position, carry):
        q_two, q_one, states = carry
        q_now = vector_at(q_scr, position + 2)
        product = vector_at(p_ref, position)
        q_mix = q_taps[0] * q_now + q_taps[1] * q_one + q_taps[2] * q_two
        states = tuple(state * rate + product for state, rate in zip(states, decay))
        terms = [state * weight for state, weight in zip(states, residue)]
        while len(terms) > 1:
            terms = [left + right for left, right in zip(terms[::2], terms[1::2])]
        smoothed = terms[0].astype(jnp.bfloat16).astype(jnp.float32)
        out_scr[pl.ds(pl.multiple_of(position * SUBLANES, SUBLANES), SUBLANES), :] = q_mix * smoothed
        return (q_one, q_now, states)

    start = (
        vector_at(q_scr, 0),
        vector_at(q_scr, 1),
        tuple(carry_ref[pl.ds(mode, SUBLANES, modes), :] for mode in range(modes)),
    )
    lax.fori_loop(0, rows, body, start, unroll=4)
    step = 16
    for first in range(0, rows, step):
        for block in range(q_ref.shape[1] // LANES):
            piece = out_scr[pl.ds(first * SUBLANES + block, step, SUBLANES), :]
            out_ref[first : first + step, block * LANES : (block + 1) * LANES] = piece.astype(
                out_ref.dtype
            )


def convolve(hyena_q, hyena_k, hyena_v, short_filter, residue, decay_rate):
    rows, channels = hyena_q.shape
    devices = lax.axis_size("ctx")
    modes = residue.shape[1]
    own_blocks = residue.shape[0] // LANES
    blocks = channels // LANES
    groups = blocks // SUBLANES
    width = SUBLANES * LANES
    group_rows = SUBLANES * modes

    def by_blocks(array):
        return array.reshape(own_blocks, LANES, modes).transpose(0, 2, 1)

    rim = jnp.concatenate([hyena_q[rows - 2 :], hyena_k[rows - 2 :], hyena_v[rows - 2 :]], 0)
    rim = lax.ppermute(rim, "ctx", [(index, index + 1) for index in range(devices - 1)])
    rim = jnp.pad(rim.astype(jnp.float32), ((0, 2), (0, 0)))
    own_rate = by_blocks(decay_rate)
    own_par = jnp.concatenate([own_rate, by_blocks(residue)], 1).reshape(
        own_blocks * 2 * modes, LANES
    )
    par = lax.all_gather(own_par, "ctx", axis=0, tiled=True)
    taps = short_filter.reshape(9, blocks, LANES)

    def wide(index):
        return (0, index)

    feature_spec = pl.BlockSpec((rows, width), wide)
    rim_spec = pl.BlockSpec((8, width), wide)
    taps_spec = pl.BlockSpec((9, SUBLANES, LANES), lambda index: (0, index, 0))
    par_spec = pl.BlockSpec((2 * group_rows, LANES), lambda index: (index, 0))
    state_spec = pl.BlockSpec((group_rows, LANES), lambda index: (index, 0))
    product_spec = pl.BlockSpec((rows * SUBLANES, LANES), lambda index: (index, 0))
    padded = pltpu.VMEM(((rows + 2) * SUBLANES, LANES), jnp.float32)
    product, state = pl.pallas_call(
        functools.partial(state_kernel, modes),
        grid=(groups,),
        in_specs=[feature_spec, feature_spec, rim_spec, taps_spec, par_spec],
        out_specs=[product_spec, state_spec],
        out_shape=[
            jax.ShapeDtypeStruct((groups * rows * SUBLANES, LANES), jnp.float32),
            jax.ShapeDtypeStruct((groups * group_rows, LANES), jnp.float32),
        ],
        scratch_shapes=[padded, padded],
        compiler_params=params(),
        cost_estimate=pl.CostEstimate(
            flops=4 * 10**9, bytes_accessed=8 * 2**20, transcendentals=0
        ),
        name="conv_state",
    )(hyena_k, hyena_v, rim, taps, par)
    arrived = lax.all_to_all(state, "ctx", split_axis=0, concat_axis=0, tiled=True).reshape(
        devices, own_blocks, modes, LANES
    )
    chunk_decay = jnp.exp(-own_rate * rows)
    entering = [jnp.zeros((own_blocks, modes, LANES), jnp.float32)]
    for index in range(devices - 1):
        entering.append(entering[-1] * chunk_decay + arrived[index])
    entering = jnp.stack(entering).reshape(devices * own_blocks * modes, LANES)
    carry = lax.all_to_all(entering, "ctx", split_axis=0, concat_axis=0, tiled=True)
    return pl.pallas_call(
        functools.partial(output_kernel, modes),
        grid=(groups,),
        in_specs=[feature_spec, product_spec, rim_spec, taps_spec, par_spec, state_spec],
        out_specs=feature_spec,
        out_shape=jax.ShapeDtypeStruct((rows, channels), jnp.bfloat16),
        scratch_shapes=[padded, pltpu.VMEM((rows * SUBLANES, LANES), jnp.float32)],
        compiler_params=params(),
        cost_estimate=pl.CostEstimate(
            flops=6 * 10**9, bytes_accessed=8 * 2**20, transcendentals=0
        ),
        name="conv_output",
    )(hyena_q, product, rim, taps, par, carry)


def head_slice(head):
    return pl.ds(pl.multiple_of(head * HEAD_DIM, HEAD_DIM), HEAD_DIM)


def lane_index(rows):
    return lax.broadcasted_iota(jnp.int32, (rows, LANES), 1)


def soft(query, keys, values, mask=None):
    scores = lax.dot_general(
        query, keys, (((1,), (1,)), ((), ())), preferred_element_type=jnp.float32
    )
    if mask is not None:
        scores = jnp.where(mask, scores, NEGATIVE)
    top = jnp.max(scores, axis=1, keepdims=True) * EXP_SCALE
    expo = jnp.exp2(scores * EXP_SCALE - top)
    total = jnp.sum(expo, axis=1, keepdims=True)
    mixed = jnp.dot(expo.astype(jnp.bfloat16), values, preferred_element_type=jnp.float32)
    return mixed / total, top + jnp.log2(total)


def partial_kernel(slots, role_ref, q_ref, k_ref, v_ref, kp_ref, vp_ref, g_ref, gp_ref, *rest):
    remote_refs = rest[:slots]
    own_ref, lse_ref = rest[slots : slots + 2]
    back_refs = rest[slots + 2 : 2 * slots + 2]
    rows, width = q_ref.shape
    heads = width // HEAD_DIM
    odd = role_ref[0] == 1
    gathered = role_ref[1] == 1

    def key_value(head, with_quad):
        cut = head_slice(head)
        keys = [kp_ref[:, cut], k_ref[:, cut]]
        values = [vp_ref[:, cut], v_ref[:, cut]]
        if with_quad:
            keys = [g_ref[0, :, cut], gp_ref[0, :, cut]] + keys
            values = [g_ref[1, :, cut], gp_ref[1, :, cut]] + values
        return jnp.concatenate(keys, 0), jnp.concatenate(values, 0)

    def run(with_quad):
        key_count = rows * (4 if with_quad else 2)
        row = lax.broadcasted_iota(jnp.int32, (rows, key_count), 0)
        column = lax.broadcasted_iota(jnp.int32, (rows, key_count), 1) - (key_count - 2 * rows)
        partner_limit = jnp.where(odd, rows, 0)
        mask = (column < partner_limit) | ((column >= rows) & (column - rows <= row))
        lanes = lane_index(rows)

        def own_body(head, sums):
            keys, values = key_value(head, with_quad)
            mixed, lse = soft(q_ref[:, head_slice(head)], keys, values, mask)
            own_ref[:, head_slice(head)] = mixed
            return jnp.where(lanes == head, lse, sums)

        lse_ref[...] = lax.fori_loop(
            0, heads, own_body, jnp.zeros((rows, LANES), jnp.float32)
        )

        for slot in range(slots):

            @pl.when(role_ref[2 + slot] == 1)
            def _():
                def remote_body(head, sums):
                    keys, values = key_value(head, with_quad)
                    mixed, lse = soft(remote_refs[slot][:, head_slice(head)], keys, values)
                    back_refs[slot][:, head_slice(head)] = mixed.astype(jnp.bfloat16)
                    first = lse.astype(jnp.bfloat16).astype(jnp.float32)
                    second = (lse - first).astype(jnp.bfloat16).astype(jnp.float32)
                    third = lse - first - second
                    sums = jnp.where(lanes == head, first, sums)
                    sums = jnp.where(lanes == heads + head, second, sums)
                    return jnp.where(lanes == 2 * heads + head, third, sums)

                sums = lax.fori_loop(
                    0, heads, remote_body, jnp.zeros((rows, LANES), jnp.float32)
                )
                back_refs[slot][:, width:] = sums.astype(jnp.bfloat16)

    @pl.when(gathered)
    def _():
        run(True)

    @pl.when(jnp.logical_not(gathered))
    def _():
        run(False)


def merge_kernel(slots, heads, role_ref, *refs):
    own_ref, lse_ref = refs[:2]
    back_refs = refs[2 : 2 + slots]
    out_ref = refs[-1]
    rows = own_ref.shape[0]
    width = heads * HEAD_DIM
    lanes = lane_index(rows)

    def body(head, nothing):
        cut = head_slice(head)
        mixed = [own_ref[:, cut]]
        sums = [jnp.sum(jnp.where(lanes == head, lse_ref[...], 0.0), axis=1, keepdims=True)]
        mine = (lanes == head) | (lanes == heads + head) | (lanes == 2 * heads + head)
        for slot in range(slots):
            valid = role_ref[2 + slots + slot] == 1
            tail = back_refs[slot][:, width:].astype(jnp.float32)
            lse = jnp.sum(jnp.where(mine, tail, 0.0), axis=1, keepdims=True)
            sums.append(jnp.where(valid, lse, NEGATIVE))
            mixed.append(back_refs[slot][:, cut].astype(jnp.float32))
        top = functools.reduce(jnp.maximum, sums)
        weights = [jnp.exp2(part - top) for part in sums]
        total = functools.reduce(jnp.add, weights)
        result = functools.reduce(
            jnp.add, [part * (weight / total) for part, weight in zip(mixed, weights)]
        )
        out_ref[:, cut] = result.astype(out_ref.dtype)
        return nothing

    lax.fori_loop(0, heads, body, 0)


def query_moves(devices):
    quads = devices // 4
    moves = []
    for distance in range(1, quads):
        for half in range(2):
            moves.append(
                [
                    (4 * quad + 2 * half + core, 4 * (quad - distance) + 2 + core)
                    for quad in range(distance, quads)
                    for core in range(2)
                ]
            )
    if not moves:
        moves.append([])
    moves[0] = moves[0] + [(devices - 2 + core, devices - 4 + core) for core in range(2)]
    return moves


def attend(query, key, value):
    rows, columns = query.shape
    devices = lax.axis_size("ctx")
    quads = devices // 4
    me = lax.axis_index("ctx")
    moves = query_moves(devices)
    slots = len(moves)
    width = columns // CHUNKS
    heads = width // HEAD_DIM

    def flag(members):
        table = [1 if index in members else 0 for index in range(devices)]
        return jnp.asarray(table, jnp.int32)[me]

    gathers = [
        (4 * quad + core, 4 * quad + 2 + core) for quad in range(quads - 1) for core in range(2)
    ]
    gather_swap = [
        (4 * quad + 2 + core, 4 * quad + 3 - core) for quad in range(quads - 1) for core in range(2)
    ]
    swap = [(index, index ^ 1) for index in range(devices)]
    role = jnp.stack(
        [me % 2, flag([target for _, target in gathers])]
        + [flag([target for _, target in pairs]) for pairs in moves]
        + [flag([source for source, _ in pairs]) for pairs in moves]
    ).astype(jnp.int32)
    key_swapped = lax.ppermute(key, "ctx", swap)
    value_swapped = lax.ppermute(value, "ctx", swap)
    smem = pl.BlockSpec(memory_space=pltpu.SMEM)
    result = None
    for chunk in range(CHUNKS):
        cut = slice(chunk * width, (chunk + 1) * width)
        both = jnp.stack([key[:, cut], value[:, cut]])
        from_below = lax.ppermute(both, "ctx", gathers)
        from_below_swapped = lax.ppermute(from_below, "ctx", gather_swap)
        query_cut = query[:, cut]
        remote = [lax.ppermute(query_cut, "ctx", pairs) for pairs in moves]
        here = pl.BlockSpec((rows, width), lambda step, chunk=chunk: (0, chunk))
        alone = pl.BlockSpec((rows, width), lambda step: (0, 0))
        quad_spec = pl.BlockSpec((2, rows, width), lambda step: (0, 0, 0))
        lse_spec = pl.BlockSpec((rows, LANES), lambda step: (0, 0))
        back_spec = pl.BlockSpec((rows, width + LANES), lambda step: (0, 0))
        outs = pl.pallas_call(
            functools.partial(partial_kernel, slots),
            grid=(1,),
            in_specs=[smem] + [here] * 5 + [quad_spec] * 2 + [alone] * slots,
            out_specs=[alone, lse_spec] + [back_spec] * slots,
            out_shape=[
                jax.ShapeDtypeStruct((rows, width), jnp.float32),
                jax.ShapeDtypeStruct((rows, LANES), jnp.float32),
            ]
            + [jax.ShapeDtypeStruct((rows, width + LANES), jnp.bfloat16)] * slots,
            compiler_params=params(),
            cost_estimate=pl.CostEstimate(
                flops=3 * 10**9, bytes_accessed=4 * 2**20, transcendentals=0
            ),
            name="att_partial",
        )(role, query, key, value, key_swapped, value_swapped, from_below, from_below_swapped, *remote)
        back = [
            lax.ppermute(part, "ctx", [(target, source) for source, target in pairs])
            for part, pairs in zip(outs[2:], moves)
        ]
        operands = [role, outs[0], outs[1], *back]
        specs = [smem, alone, lse_spec] + [back_spec] * slots
        aliases = {}
        if result is not None:
            aliases = {len(operands): 0}
            operands.append(result)
            specs.append(pl.BlockSpec(memory_space=pl.ANY))
        result = pl.pallas_call(
            functools.partial(merge_kernel, slots, heads),
            grid=(1,),
            in_specs=specs,
            out_specs=here,
            out_shape=jax.ShapeDtypeStruct((rows, columns), jnp.bfloat16),
            input_output_aliases=aliases,
            compiler_params=params(),
            cost_estimate=pl.CostEstimate(
                flops=10**9, bytes_accessed=2 * 2**20, transcendentals=0
            ),
            name="att_merge",
        )(*operands)
    return result


def local(
    hyena_q, hyena_k, hyena_v, short_filter, residue, decay_rate, att_query, att_key, att_value
):
    att_out = attend(att_query, att_key, att_value)
    hyena_out = convolve(hyena_q, hyena_k, hyena_v, short_filter, residue, decay_rate)
    return (hyena_out, att_out)


def solution(mesh):
    rows = P(("dp", "ctx"), None)
    shared = P("ctx", None)
    return jax.shard_map(
        local,
        mesh=mesh,
        in_specs=(rows, rows, rows, P(), shared, shared, rows, rows, rows),
        out_specs=(rows, rows),
        check_vma=False,
    )
```

```python
import functools
import math

import jax
import jax.numpy as jnp
from jax import lax
from jax.experimental import pallas as pl
from jax.experimental.pallas import tpu as pltpu
from jax.sharding import PartitionSpec as P

HEAD_DIM = 128
LANES = 128
SUBLANES = 8
TAPS = 3
CHUNKS = 4
UNROLL = 2
NEGATIVE = -1e30
EXP_SCALE = HEAD_DIM**-0.5 * math.log2(math.e)
VMEM_LIMIT = 56 * 1024 * 1024


def params(**kwargs):
    return pltpu.CompilerParams(vmem_limit_bytes=VMEM_LIMIT, **kwargs)


def cost(microseconds):
    return pl.CostEstimate(
        flops=microseconds * 10**9, bytes_accessed=2**20, transcendentals=0
    )


def block_lanes(block):
    return slice(block * LANES, (block + 1) * LANES)


def segment_size(modes, own_blocks, blocks):
    return 2 * modes + 2 * TAPS * blocks // own_blocks


def rim_pack_kernel(modes, rate_ref, residue_ref, q_ref, k_ref, v_ref, out_ref):
    own_blocks = rate_ref.shape[0] // LANES
    blocks = q_ref.shape[1] // LANES
    share = 2 * TAPS * blocks // own_blocks
    size = 2 * modes + share
    for block in range(own_blocks):
        rows = slice(block * LANES, (block + 1) * LANES)
        fill = jnp.zeros((LANES, LANES - 2 * modes), jnp.float32)
        both = jnp.concatenate([rate_ref[rows, :], residue_ref[rows, :], fill], 1)
        out_ref[block * size : block * size + 2 * modes, :] = jnp.transpose(both)[: 2 * modes]
    for feature, ref in enumerate((q_ref, k_ref, v_ref)):
        last = ref[...].astype(jnp.float32)[ref.shape[0] - 2 :]
        for row in range(2):
            for block in range(blocks):
                place = (2 * feature + row) * blocks + block
                target = place // share * size + 2 * modes + place % share
                out_ref[target : target + 1, :] = last[row : row + 1, block_lanes(block)]


def rim_rows(shared_ref, modes, own_blocks, blocks, feature, block):
    me = lax.axis_index("ctx")
    share = 2 * TAPS * blocks // own_blocks
    size = 2 * modes + share
    before = jnp.maximum(me - 1, 0) * own_blocks
    rows = []
    for row in range(2):
        place = (2 * feature + row) * blocks + block
        target = (before + place // share) * size + 2 * modes + place % share
        rows.append(jnp.where(me == 0, 0.0, shared_ref[pl.ds(target, 1), :]))
    return rows


def short_mix(feature, rim, taps):
    two_before, one_before = rim
    row = lax.broadcasted_iota(jnp.int32, feature.shape, 0)
    one = jnp.where(row == 0, one_before, pltpu.roll(feature, 1, 0))
    two = jnp.where(row == 0, two_before, jnp.where(row == 1, one_before, pltpu.roll(feature, 2, 0)))
    return taps[0] * feature + taps[1] * one + taps[2] * two


def tap_rows(taps_ref, feature, lanes):
    return [taps_ref[feature, pl.ds(tap, 1), lanes] for tap in range(TAPS)]


def state_kernel(
    modes, own_blocks, blocks, k_ref, v_ref, shared_ref, taps_ref, y_ref, s_ref, p_scr, y_scr
):
    group = pl.program_id(0)
    rows = k_ref.shape[0]
    size = segment_size(modes, own_blocks, blocks)
    for block in range(SUBLANES):
        lanes = block_lanes(block)
        mixes = [
            short_mix(
                ref[:, lanes].astype(jnp.float32),
                rim_rows(
                    shared_ref, modes, own_blocks, blocks, feature, group * SUBLANES + block
                ),
                tap_rows(taps_ref, feature, lanes),
            )
            for feature, ref in ((1, k_ref), (2, v_ref))
        ]
        product = (mixes[0] * mixes[1]).astype(jnp.bfloat16).astype(jnp.float32)
        p_scr[pl.ds(block, rows, SUBLANES), :] = product
    first = group * SUBLANES * size
    decay = [
        jnp.exp(-shared_ref[pl.ds(first + mode, SUBLANES, size), :]) for mode in range(modes)
    ]
    residue = [
        shared_ref[pl.ds(first + modes + mode, SUBLANES, size), :] for mode in range(modes)
    ]

    def body(position, states):
        here = pl.ds(pl.multiple_of(position * SUBLANES, SUBLANES), SUBLANES)
        product = p_scr[here, :]
        states = tuple(state * rate + product for state, rate in zip(states, decay))
        terms = [state * weight for state, weight in zip(states, residue)]
        while len(terms) > 1:
            terms = [left + right for left, right in zip(terms[::2], terms[1::2])]
        y_scr[here, :] = terms[0]
        return states

    zero = jnp.zeros((SUBLANES, LANES), jnp.float32)
    states = lax.fori_loop(0, rows, body, (zero,) * modes, unroll=4)
    for mode in range(modes):
        s_ref[pl.ds(mode, SUBLANES, modes), :] = states[mode]
    for block in range(SUBLANES):
        y_ref[:, block_lanes(block)] = y_scr[pl.ds(block, rows, SUBLANES), :]


def output_kernel(
    modes, own_blocks, blocks, devices, q_ref, y_ref, shared_ref, state_ref, taps_ref, out_ref
):
    group = pl.program_id(0)
    me = lax.axis_index("ctx")
    rows = q_ref.shape[0]
    size = segment_size(modes, own_blocks, blocks)
    step = lax.broadcasted_iota(jnp.int32, (SUBLANES, LANES), 0).astype(jnp.float32) + 1.0

    def body(block, nothing):
        place = group * SUBLANES + block
        lanes = pl.ds(pl.multiple_of(block * LANES, LANES), LANES)
        rate = shared_ref[pl.ds(pl.multiple_of(place * size, SUBLANES), modes), :]
        residue = shared_ref[pl.ds(pl.multiple_of(place * size + modes, SUBLANES), modes), :]
        chunk_decay = jnp.exp(-rate * rows)
        entering = jnp.zeros((modes, LANES), jnp.float32)
        for device in range(devices - 1):
            start = pl.multiple_of((device * blocks + place) * modes, SUBLANES)
            after = entering * chunk_decay + state_ref[pl.ds(start, modes), :]
            entering = jnp.where(device < me, after, entering)
        weighted = residue * entering
        eight = jnp.exp(-rate * SUBLANES)
        terms = [
            weighted[mode : mode + 1] * jnp.exp(-rate[mode : mode + 1] * step)
            for mode in range(modes)
        ]
        eights = [jnp.broadcast_to(eight[mode : mode + 1], terms[0].shape) for mode in range(modes)]
        added = []
        for start in range(0, rows, SUBLANES):
            sums = list(terms)
            while len(sums) > 1:
                sums = [left + right for left, right in zip(sums[::2], sums[1::2])]
            added.append(sums[0])
            if start + SUBLANES < rows:
                terms = [term * decay for term, decay in zip(terms, eights)]
        smoothed = y_ref[:, lanes] + jnp.concatenate(added, 0)
        smoothed = smoothed.astype(jnp.bfloat16).astype(jnp.float32)
        mix = short_mix(
            q_ref[:, lanes].astype(jnp.float32),
            rim_rows(shared_ref, modes, own_blocks, blocks, 0, place),
            tap_rows(taps_ref, 0, lanes),
        )
        out_ref[:, lanes] = (mix * smoothed).astype(out_ref.dtype)
        return nothing

    lax.fori_loop(0, SUBLANES, body, 0)


def convolve(hyena_q, hyena_k, hyena_v, short_filter, residue, decay_rate):
    rows, channels = hyena_q.shape
    devices = lax.axis_size("ctx")
    modes = residue.shape[1]
    own_blocks = residue.shape[0] // LANES
    blocks = channels // LANES
    groups = blocks // SUBLANES
    width = SUBLANES * LANES
    size = segment_size(modes, own_blocks, blocks)
    end = rows // 16 - 1
    last_spec = pl.BlockSpec((16, channels), lambda step: (end, 0))
    own_spec = pl.BlockSpec(residue.shape, lambda step: (0, 0))
    own_shared = pl.pallas_call(
        functools.partial(rim_pack_kernel, modes),
        grid=(1,),
        in_specs=[own_spec] * 2 + [last_spec] * 3,
        out_specs=pl.BlockSpec((own_blocks * size, LANES), lambda step: (0, 0)),
        out_shape=jax.ShapeDtypeStruct((own_blocks * size, LANES), jnp.float32),
        compiler_params=params(),
        cost_estimate=cost(1),
        name="conv_pack",
    )(decay_rate, residue, hyena_q, hyena_k, hyena_v)
    shared = lax.all_gather(own_shared, "ctx", axis=0, tiled=True)
    feature_spec = pl.BlockSpec((rows, width), lambda group: (0, group))
    shared_spec = pl.BlockSpec((blocks * size, LANES), lambda group: (0, 0))
    taps_spec = pl.BlockSpec((TAPS, TAPS, width), lambda group: (0, 0, group))
    positions = pltpu.VMEM((rows * SUBLANES, LANES), jnp.float32)
    local_result, state = pl.pallas_call(
        functools.partial(state_kernel, modes, own_blocks, blocks),
        grid=(groups,),
        in_specs=[feature_spec, feature_spec, shared_spec, taps_spec],
        out_specs=[
            feature_spec,
            pl.BlockSpec((SUBLANES * modes, LANES), lambda group: (group, 0)),
        ],
        out_shape=[
            jax.ShapeDtypeStruct((rows, channels), jnp.float32),
            jax.ShapeDtypeStruct((blocks * modes, LANES), jnp.float32),
        ],
        scratch_shapes=[positions, positions],
        compiler_params=params(),
        cost_estimate=cost(8),
        name="conv_state",
    )(hyena_k, hyena_v, shared, short_filter)
    states = lax.all_gather(state, "ctx", axis=0, tiled=True)
    return pl.pallas_call(
        functools.partial(output_kernel, modes, own_blocks, blocks, devices),
        grid=(groups,),
        in_specs=[
            feature_spec,
            feature_spec,
            shared_spec,
            pl.BlockSpec(states.shape, lambda group: (0, 0)),
            taps_spec,
        ],
        out_specs=feature_spec,
        out_shape=jax.ShapeDtypeStruct((rows, channels), jnp.bfloat16),
        compiler_params=params(),
        cost_estimate=cost(5),
        name="conv_output",
    )(hyena_q, local_result, shared, states, short_filter)


def head_slice(head, rows=HEAD_DIM):
    return pl.ds(pl.multiple_of(head * rows, rows), rows)


def among(me, members):
    return functools.reduce(jnp.logical_or, [me == member for member in members])


def plan_moves(devices):
    quads = devices // 4
    transfers = [[(devices - 1, devices - 3)]]
    for distance in range(1, quads):
        if distance > len(transfers):
            transfers.append([])
        for quad in range(distance, quads):
            target = 4 * (quad - distance) + 2
            transfers[distance - 1] += [(4 * quad, target), (4 * quad + 2, target + 1)]
    return transfers


def soft(query, keys, values, mask=None):
    scores = lax.dot_general(
        query, keys, (((1,), (1,)), ((), ())), preferred_element_type=jnp.float32
    )
    if mask is not None:
        scores = jnp.where(mask, scores, NEGATIVE)
    top = jnp.max(scores, axis=1, keepdims=True) * EXP_SCALE
    expo = jnp.exp2(scores * EXP_SCALE - top).astype(jnp.bfloat16)
    mixed = jnp.dot(expo, values, preferred_element_type=jnp.float32)
    total = mixed[:, HEAD_DIM:]
    return mixed[:, :HEAD_DIM] / total, top + jnp.log2(total)


def key_pack_kernel(k_ref, v_ref, *outs):
    heads = outs[0].shape[0] // 2 // HEAD_DIM
    for index, out in enumerate(outs):
        for which, ref in enumerate((k_ref, v_ref)):
            for head in range(heads):
                row = (which * heads + head) * HEAD_DIM
                out[row : row + HEAD_DIM, :] = ref[:, block_lanes(index * heads + head)]


def query_pack_kernel(q_ref, qs_ref, *outs):
    rows = q_ref.shape[0]
    heads = outs[0].shape[0] // 2 // rows
    odd = lax.axis_index("ctx") % 2
    for index, out in enumerate(outs):
        for head in range(heads):
            for ref, half in ((q_ref, odd), (qs_ref, 1 - odd)):
                place = pl.ds(pl.multiple_of((2 * head + half) * rows, rows), rows)
                out[place, :] = ref[:, block_lanes(index * heads + head)]


def tail_rows(heads):
    return -(-3 * heads // 16) * 16


def partial_kernel(transfers, upper, heads, *refs):
    count = len(transfers)
    q_ref, k_ref, v_ref, kp_ref, vp_ref, g_ref, gp_ref = refs[:7]
    ask_refs = refs[7 : 7 + count]
    own_ref, lse_ref = refs[7 + count : 9 + count]
    answer_refs = refs[9 + count :]
    me = lax.axis_index("ctx")
    rows = q_ref.shape[0]
    tail = tail_rows(heads)

    def key_value(head, with_quad):
        cut = head_slice(head)
        keys = [kp_ref[:, cut], k_ref[:, cut]]
        values = [vp_ref[:, cut], v_ref[:, cut]]
        if with_quad:
            value_cut = head_slice(heads + head)
            keys = [g_ref[cut, :], gp_ref[cut, :]] + keys
            values = [g_ref[value_cut, :], gp_ref[value_cut, :]] + values
        values = jnp.concatenate(values, 0)
        return jnp.concatenate(keys, 0), jnp.concatenate([values, jnp.ones_like(values)], 1)

    def run(with_quad):
        key_count = rows * (4 if with_quad else 2)
        row = lax.broadcasted_iota(jnp.int32, (rows, key_count), 0)
        column = lax.broadcasted_iota(jnp.int32, (rows, key_count), 1)
        column = column - (key_count - 2 * rows)
        partner_limit = jnp.where(me % 2 == 1, rows, 0)
        mask = (column < partner_limit) | ((column >= rows) & (column - rows <= row))
        lanes = lax.broadcasted_iota(jnp.int32, (rows, LANES), 1)

        def own_body(head, sums):
            keys, values = key_value(head, with_quad)
            mixed, lse = soft(q_ref[:, head_slice(head)], keys, values, mask)
            own_ref[:, head_slice(head)] = mixed
            return jnp.where(lanes == head, lse, sums)

        zeros = jnp.zeros((rows, LANES), jnp.float32)
        lse_ref[...] = lax.fori_loop(0, heads, own_body, zeros, unroll=UNROLL)

        def answer(index):
            lanes = lax.broadcasted_iota(jnp.int32, (2 * rows, LANES), 1)

            def body(head, sums):
                keys, values = key_value(head, with_quad)
                place = head_slice(head, 2 * rows)
                mixed, lse = soft(ask_refs[index][place, :], keys, values)
                answer_refs[index][place, :] = mixed.astype(jnp.bfloat16)
                first = lse.astype(jnp.bfloat16).astype(jnp.float32)
                second = (lse - first).astype(jnp.bfloat16).astype(jnp.float32)
                sums = jnp.where(lanes == head, first, sums)
                sums = jnp.where(lanes == heads + head, second, sums)
                return jnp.where(lanes == 2 * heads + head, lse - first - second, sums)

            zeros = jnp.zeros((2 * rows, LANES), jnp.float32)
            sums = lax.fori_loop(0, heads, body, zeros, unroll=UNROLL)
            for half in range(2):
                part = jnp.transpose(sums[half * rows : (half + 1) * rows])[:tail]
                start = 2 * heads * rows + half * tail
                answer_refs[index][start : start + tail, :] = part.astype(jnp.bfloat16)

        for index, pairs in enumerate(transfers):
            asked = [target for _, target in pairs if (target in upper) == with_quad]
            if asked:
                pl.when(among(me, asked))(functools.partial(answer, index))

    if upper:
        pl.when(among(me, upper))(functools.partial(run, True))
        pl.when(jnp.logical_not(among(me, upper)))(functools.partial(run, False))
    else:
        run(False)


def merge_kernel(transfers, heads, chunks, onto, *refs):
    per_chunk = 2 + 2 * len(transfers)
    out_ref = refs[-1]
    me = lax.axis_index("ctx")
    odd = me % 2
    rows = out_ref.shape[0]
    tail = tail_rows(heads)
    returned = [[source for source, _ in pairs] for pairs in transfers]
    with_partner = [members + [member ^ 1 for member in members] for members in returned]
    answered = among(me, sorted(set(sum(with_partner, []))))
    for position in range(chunks):
        own_ref, lse_ref, *others = refs[position * per_chunk : (position + 1) * per_chunk]
        base = position * heads * HEAD_DIM

        @pl.when(answered)
        def _():
            valid, sums = [], []
            for index, ref in enumerate(others):
                members = returned[index // 2]
                if index % 2:
                    members = [member ^ 1 for member in members]
                valid.append(among(me, members))
                start = pl.multiple_of(2 * heads * rows + odd * tail, 16)
                part = ref[pl.ds(start, tail), :].astype(jnp.float32)
                part = part[:heads] + part[heads : 2 * heads] + part[2 * heads : 3 * heads]
                fill = jnp.zeros((LANES - heads, rows), jnp.float32)
                sums.append(jnp.transpose(jnp.concatenate([part, fill], 0)))
            for head in range(heads):
                cut = block_lanes(head)
                logs = [lse_ref[:, head : head + 1]]
                mixed = [own_ref[:, cut]]
                for index, ref in enumerate(others):
                    logs.append(jnp.where(valid[index], sums[index][:, head : head + 1], NEGATIVE))
                    place = pl.ds(pl.multiple_of((2 * head + odd) * rows, rows), rows)
                    part = ref[place, :].astype(jnp.float32)
                    mixed.append(jnp.where(valid[index], part, 0.0))
                top = functools.reduce(jnp.maximum, logs)
                weights = [jnp.exp2(part - top) for part in logs]
                total = functools.reduce(jnp.add, weights)
                terms = [part * (weight / total) for part, weight in zip(mixed, weights)]
                out_ref[:, base + head * HEAD_DIM : base + (head + 1) * HEAD_DIM] = (
                    functools.reduce(jnp.add, terms).astype(out_ref.dtype)
                )

        @pl.when(jnp.logical_not(answered))
        def _():
            out_ref[:, base : base + heads * HEAD_DIM] = own_ref[...].astype(out_ref.dtype)


def attend(query, key, value):
    rows, columns = query.shape
    devices = lax.axis_size("ctx")
    quads = devices // 4
    transfers = plan_moves(devices)
    width = columns // CHUNKS
    heads = width // HEAD_DIM
    upper = [4 * quad + 2 + core for quad in range(quads - 1) for core in range(2)]
    gathers = [(who - 2, who) for who in upper]
    swap = [(index, index ^ 1) for index in range(devices)]

    def whole(shape):
        return pl.BlockSpec(shape, lambda step: (0,) * len(shape))

    def chunk_spec(chunk):
        return pl.BlockSpec((rows, width), lambda step: (0, chunk))

    query_swapped = lax.ppermute(query, "ctx", swap)
    key_swapped = lax.ppermute(key, "ctx", swap)
    value_swapped = lax.ppermute(value, "ctx", swap)
    kv_shape = (2 * width, HEAD_DIM)
    key_packs = pl.pallas_call(
        key_pack_kernel,
        grid=(1,),
        in_specs=[whole((rows, columns))] * 2,
        out_specs=[whole(kv_shape)] * CHUNKS,
        out_shape=[jax.ShapeDtypeStruct(kv_shape, jnp.bfloat16)] * CHUNKS,
        compiler_params=params(),
        cost_estimate=cost(3),
        name="key_pack",
    )(key, value)
    ask_shape = (2 * heads * rows, HEAD_DIM)
    query_packs = pl.pallas_call(
        query_pack_kernel,
        grid=(1,),
        in_specs=[whole((rows, columns))] * 2,
        out_specs=[whole(ask_shape)] * CHUNKS,
        out_shape=[jax.ShapeDtypeStruct(ask_shape, jnp.bfloat16)] * CHUNKS,
        compiler_params=params(),
        cost_estimate=cost(3),
        name="query_pack",
    )(query, query_swapped)
    asks, quad_kv = [], []
    for chunk in range(CHUNKS):
        arrived = lax.ppermute(key_packs[chunk], "ctx", gathers)
        asks.append([lax.ppermute(query_packs[chunk], "ctx", pairs) for pairs in transfers])
        quad_kv.append([arrived, lax.ppermute(arrived, "ctx", swap)])

    answer_shape = (2 * heads * rows + 2 * tail_rows(heads), HEAD_DIM)
    parts = []
    for chunk in range(CHUNKS):
        own, lse, *answers = pl.pallas_call(
            functools.partial(partial_kernel, transfers, upper, heads),
            grid=(1,),
            in_specs=[chunk_spec(chunk)] * 5
            + [whole(kv_shape)] * 2
            + [whole(ask_shape)] * len(transfers),
            out_specs=[whole((rows, width)), whole((rows, LANES))]
            + [whole(answer_shape)] * len(transfers),
            out_shape=[
                jax.ShapeDtypeStruct((rows, width), jnp.float32),
                jax.ShapeDtypeStruct((rows, LANES), jnp.float32),
            ]
            + [jax.ShapeDtypeStruct(answer_shape, jnp.bfloat16)] * len(transfers),
            compiler_params=params(),
            cost_estimate=cost(4),
            name="att_partial",
        )(query, key, value, key_swapped, value_swapped, *quad_kv[chunk], *asks[chunk])
        parts.append([own, lse])
        for answer, pairs in zip(answers, transfers):
            back = lax.ppermute(answer, "ctx", [(target, source) for source, target in pairs])
            parts[-1] += [back, lax.ppermute(back, "ctx", swap)]

    def merge(result, first, count):
        operands = sum(parts[first : first + count], [])
        specs = [whole(operand.shape) for operand in operands]
        aliases = {}
        if result is not None:
            aliases = {len(operands): 0}
            operands.append(result)
            specs.append(pl.BlockSpec(memory_space=pl.ANY))
        return pl.pallas_call(
            functools.partial(merge_kernel, transfers, heads, count, result is not None),
            grid=(1,),
            in_specs=specs,
            out_specs=pl.BlockSpec((rows, count * width), lambda step: (0, first // count)),
            out_shape=jax.ShapeDtypeStruct((rows, columns), jnp.bfloat16),
            input_output_aliases=aliases,
            compiler_params=params(),
            cost_estimate=cost(2),
            name="att_merge",
        )(*operands)

    if CHUNKS == 1:
        return merge(None, 0, 1)
    result = merge(None, 0, CHUNKS - 1)
    return merge(result, CHUNKS - 1, 1)


def local(
    hyena_q, hyena_k, hyena_v, short_filter, residue, decay_rate, att_query, att_key, att_value
):
    att_out = attend(att_query, att_key, att_value)
    hyena_out = convolve(hyena_q, hyena_k, hyena_v, short_filter, residue, decay_rate)
    return (hyena_out, att_out)


def solution(mesh):
    rows = P(("dp", "ctx"), None)
    shared = P("ctx", None)
    return jax.shard_map(
        local,
        mesh=mesh,
        in_specs=(rows, rows, rows, P(), shared, shared, rows, rows, rows),
        out_specs=(rows, rows),
        check_vma=False,
    )
```

```python
import functools
import math

import jax
import jax.numpy as jnp
from jax import lax
from jax.experimental import pallas as pl
from jax.experimental.pallas import tpu as pltpu
from jax.sharding import PartitionSpec as P

HEAD_DIM = 128
LANES = 128
SUBLANES = 8
TAPS = 3
HEADS_PER_STEP = 4
CHUNK_STEPS = (2, 2, 2, 2)
TAIL = 16
NEGATIVE = -1e30
EXP_SCALE = HEAD_DIM**-0.5 * math.log2(math.e)
VMEM_LIMIT = 60 * 1024 * 1024


def params(**kwargs):
    return pltpu.CompilerParams(vmem_limit_bytes=VMEM_LIMIT, **kwargs)


def cost(microseconds):
    return pl.CostEstimate(
        flops=microseconds * 10**8, bytes_accessed=2**16, transcendentals=0
    )


def block_lanes(block):
    return slice(block * LANES, (block + 1) * LANES)


def conv_pack_kernel(rate_ref, residue_ref, q_ref, k_ref, v_ref, par_ref, rim_ref):
    modes = rate_ref.shape[0]
    for block in range(rate_ref.shape[1] // LANES):
        for which, ref in enumerate((rate_ref, residue_ref)):
            start = (2 * block + which) * modes
            for device in range(par_ref.shape[0]):
                par_ref[device, start : start + modes, :] = ref[:, block_lanes(block)]
    for feature, ref in enumerate((q_ref, k_ref, v_ref)):
        last = ref[...].astype(jnp.float32)[ref.shape[0] - 2 :]
        rim_ref[2 * feature : 2 * feature + 2, :] = last
    rim_ref[2 * TAPS :, :] = jnp.zeros((2, rim_ref.shape[1]), jnp.float32)


def rim_rows(rim_ref, feature, lanes):
    return [rim_ref[pl.ds(2 * feature + row, 1), lanes] for row in range(2)]


def short_mix(feature, rim, taps):
    two_before, one_before = rim
    row = lax.broadcasted_iota(jnp.int32, feature.shape, 0)
    one = jnp.where(row == 0, one_before, pltpu.roll(feature, 1, 0))
    two = jnp.where(row == 0, two_before, jnp.where(row == 1, one_before, pltpu.roll(feature, 2, 0)))
    return taps[0] * feature + taps[1] * one + taps[2] * two


def tap_rows(taps_ref, feature, lanes):
    return [taps_ref[feature, pl.ds(tap, 1), lanes] for tap in range(TAPS)]


def state_kernel(modes, k_ref, v_ref, rim_ref, par_ref, taps_ref, y_ref, s_ref, p_scr, y_scr):
    rows = k_ref.shape[0]
    for block in range(SUBLANES):
        lanes = block_lanes(block)
        mixes = [
            short_mix(
                ref[:, lanes].astype(jnp.float32),
                rim_rows(rim_ref, feature, lanes),
                tap_rows(taps_ref, feature, lanes),
            )
            for feature, ref in ((1, k_ref), (2, v_ref))
        ]
        product = (mixes[0] * mixes[1]).astype(jnp.bfloat16).astype(jnp.float32)
        p_scr[pl.ds(block, rows, SUBLANES), :] = product
    decay = [jnp.exp(-par_ref[pl.ds(mode, SUBLANES, 2 * modes), :]) for mode in range(modes)]
    residue = [par_ref[pl.ds(modes + mode, SUBLANES, 2 * modes), :] for mode in range(modes)]

    def body(position, states):
        here = pl.ds(pl.multiple_of(position * SUBLANES, SUBLANES), SUBLANES)
        product = p_scr[here, :]
        states = tuple(state * rate + product for state, rate in zip(states, decay))
        terms = [state * weight for state, weight in zip(states, residue)]
        while len(terms) > 1:
            terms = [left + right for left, right in zip(terms[::2], terms[1::2])]
        y_scr[here, :] = terms[0]
        return states

    zero = jnp.zeros((SUBLANES, LANES), jnp.float32)
    states = lax.fori_loop(0, rows, body, (zero,) * modes, unroll=4)
    for mode in range(modes):
        s_ref[pl.ds(mode, SUBLANES, modes), :] = states[mode]
    for block in range(SUBLANES):
        y_ref[:, block_lanes(block)] = y_scr[pl.ds(block, rows, SUBLANES), :]


def output_kernel(modes, q_ref, y_ref, rim_ref, par_ref, state_ref, taps_ref, out_ref):
    me = lax.axis_index("ctx")
    rows = q_ref.shape[0]
    step = lax.broadcasted_iota(jnp.int32, (SUBLANES, LANES), 0).astype(jnp.float32) + 1.0

    def body(block, nothing):
        lanes = pl.ds(pl.multiple_of(block * LANES, LANES), LANES)
        rate = par_ref[pl.ds(pl.multiple_of(2 * block * modes, SUBLANES), modes), :]
        residue = par_ref[pl.ds(pl.multiple_of((2 * block + 1) * modes, SUBLANES), modes), :]
        chunk_decay = jnp.exp(-rate * rows)
        entering = jnp.zeros((modes, LANES), jnp.float32)
        for device in range(state_ref.shape[0] - 1):
            start = pl.multiple_of(block * modes, SUBLANES)
            after = entering * chunk_decay + state_ref[device, pl.ds(start, modes), :]
            entering = jnp.where(device < me, after, entering)
        weighted = residue * entering
        eight = jnp.exp(-rate * SUBLANES)
        terms = [
            weighted[mode : mode + 1] * jnp.exp(-rate[mode : mode + 1] * step)
            for mode in range(modes)
        ]
        eights = [jnp.broadcast_to(eight[mode : mode + 1], terms[0].shape) for mode in range(modes)]
        added = []
        for start in range(0, rows, SUBLANES):
            sums = list(terms)
            while len(sums) > 1:
                sums = [left + right for left, right in zip(sums[::2], sums[1::2])]
            added.append(sums[0])
            if start + SUBLANES < rows:
                terms = [term * decay for term, decay in zip(terms, eights)]
        smoothed = y_ref[:, lanes] + jnp.concatenate(added, 0)
        smoothed = smoothed.astype(jnp.bfloat16).astype(jnp.float32)
        mix = short_mix(
            q_ref[:, lanes].astype(jnp.float32),
            rim_rows(rim_ref, 0, lanes),
            tap_rows(taps_ref, 0, lanes),
        )
        out_ref[:, lanes] = (mix * smoothed).astype(out_ref.dtype)
        return nothing

    lax.fori_loop(0, SUBLANES, body, 0)


def convolve(hyena_q, hyena_k, hyena_v, short_filter, residue, decay_rate):
    rows, channels = hyena_q.shape
    devices = lax.axis_size("ctx")
    modes = residue.shape[1]
    own_blocks = residue.shape[0] // LANES
    blocks = channels // LANES
    groups = blocks // SUBLANES
    width = SUBLANES * LANES
    end = rows // 16 - 1
    par_rows = 2 * own_blocks * modes
    own_par, rim = pl.pallas_call(
        conv_pack_kernel,
        grid=(1,),
        in_specs=[pl.BlockSpec((modes, residue.shape[0]), lambda step: (0, 0))] * 2
        + [pl.BlockSpec((16, channels), lambda step: (end, 0))] * 3,
        out_specs=[
            pl.BlockSpec((devices, par_rows, LANES), lambda step: (0, 0, 0)),
            pl.BlockSpec((8, channels), lambda step: (0, 0)),
        ],
        out_shape=[
            jax.ShapeDtypeStruct((devices, par_rows, LANES), jnp.float32),
            jax.ShapeDtypeStruct((8, channels), jnp.float32),
        ],
        compiler_params=params(),
        cost_estimate=cost(1),
        name="conv_pack",
    )(decay_rate.T, residue.T, hyena_q, hyena_k, hyena_v)
    par = lax.all_to_all(own_par, "ctx", split_axis=0, concat_axis=0, tiled=True)
    par = par.reshape(devices * par_rows, LANES)
    rim = lax.ppermute(rim, "ctx", [(index, index + 1) for index in range(devices - 1)])
    feature_spec = pl.BlockSpec((rows, width), lambda group: (0, group))
    rim_spec = pl.BlockSpec((8, width), lambda group: (0, group))
    par_spec = pl.BlockSpec((2 * SUBLANES * modes, LANES), lambda group: (group, 0))
    taps_spec = pl.BlockSpec((TAPS, TAPS, width), lambda group: (0, 0, group))
    positions = pltpu.VMEM((rows * SUBLANES, LANES), jnp.float32)
    local_result, state = pl.pallas_call(
        functools.partial(state_kernel, modes),
        grid=(groups,),
        in_specs=[feature_spec, feature_spec, rim_spec, par_spec, taps_spec],
        out_specs=[
            feature_spec,
            pl.BlockSpec((SUBLANES * modes, LANES), lambda group: (group, 0)),
        ],
        out_shape=[
            jax.ShapeDtypeStruct((rows, channels), jnp.float32),
            jax.ShapeDtypeStruct((blocks * modes, LANES), jnp.float32),
        ],
        scratch_shapes=[positions, positions],
        compiler_params=params(),
        cost_estimate=cost(8),
        name="conv_state",
    )(hyena_k, hyena_v, rim, par, short_filter)
    states = lax.all_gather(state, "ctx", axis=0, tiled=True)
    states = states.reshape(devices, blocks * modes, LANES)
    return pl.pallas_call(
        functools.partial(output_kernel, modes),
        grid=(groups,),
        in_specs=[
            feature_spec,
            feature_spec,
            rim_spec,
            par_spec,
            pl.BlockSpec((devices, SUBLANES * modes, LANES), lambda group: (0, group, 0)),
            taps_spec,
        ],
        out_specs=feature_spec,
        out_shape=jax.ShapeDtypeStruct((rows, channels), jnp.bfloat16),
        compiler_params=params(),
        cost_estimate=cost(5),
        name="conv_output",
    )(hyena_q, local_result, rim, par, states, short_filter)


def among(me, members):
    return functools.reduce(jnp.logical_or, [me == member for member in members])


def plan_moves(devices):
    quads = devices // 4
    transfers = [[(devices - 1, devices - 3)]]
    for distance in range(1, quads):
        if distance > len(transfers):
            transfers.append([])
        for quad in range(distance, quads):
            target = 4 * (quad - distance) + 2
            transfers[distance - 1] += [(4 * quad, target), (4 * quad + 2, target + 1)]
    return transfers


def soft(query, keys, values, mask=None):
    scores = lax.dot_general(
        query, keys, (((1,), (1,)), ((), ())), preferred_element_type=jnp.float32
    )
    if mask is not None:
        scores = jnp.where(mask, scores, NEGATIVE)
    top = jnp.max(scores, axis=1, keepdims=True) * EXP_SCALE
    expo = jnp.exp2(scores * EXP_SCALE - top).astype(jnp.bfloat16)
    mixed = jnp.dot(expo, values, preferred_element_type=jnp.float32)
    total = mixed[:, HEAD_DIM:]
    return mixed[:, :HEAD_DIM] / total, top + jnp.log2(total)


def pack_kernel(gathers, askers, widths, starts, q_ref, qs_ref, k_ref, v_ref, *rest):
    count = len(widths)
    key_outs, query_outs, sems = rest[:count], rest[count : 2 * count], rest[-1]
    me = lax.axis_index("ctx")
    odd = me % 2
    rows = q_ref.shape[0]

    def run(pairs):
        copies = [
            pltpu.make_async_copy(source, target, sems.at[index])
            for index, (source, target) in enumerate(pairs)
        ]
        for copy in copies:
            copy.start()
        for copy in copies:
            copy.wait()

    def cut(ref, chunk):
        return ref.at[:, pl.ds(starts[chunk], widths[chunk])]

    if gathers:

        @pl.when(among(me, gathers))
        def _():
            run(
                [
                    (cut(ref, chunk), key_outs[chunk].at[which])
                    for chunk in range(count)
                    for which, ref in enumerate((k_ref, v_ref))
                ]
            )

    @pl.when(among(me, askers))
    def _():
        run(
            [
                (cut(ref, chunk), query_outs[chunk].at[half])
                for chunk in range(count)
                for ref, half in ((q_ref, odd), (qs_ref, 1 - odd))
            ]
        )


def spread(rows_of_heads, count):
    lanes = lax.broadcasted_iota(jnp.int32, rows_of_heads[0].shape, 1)
    sums = jnp.zeros_like(rows_of_heads[0])
    for index, column in enumerate(rows_of_heads):
        sums = jnp.where(lanes == index, column, sums)
    return jnp.transpose(sums)[:count]


def partial_kernel(transfers, upper, *refs):
    count = len(transfers)
    q_ref, k_ref, v_ref, kp_ref, vp_ref, g_ref, gp_ref = refs[:7]
    ask_refs = refs[7 : 7 + count]
    own_ref, lse_ref = refs[7 + count : 9 + count]
    answer_refs = refs[9 + count :]
    me = lax.axis_index("ctx")
    rows = q_ref.shape[0]
    heads = q_ref.shape[1] // HEAD_DIM
    half_rows = heads * rows + TAIL

    def key_value(head, with_quad):
        cut = block_lanes(head)
        keys = [kp_ref[:, cut], k_ref[:, cut]]
        values = [vp_ref[:, cut], v_ref[:, cut]]
        if with_quad:
            keys = [g_ref[0, :, cut], gp_ref[0, :, cut]] + keys
            values = [g_ref[1, :, cut], gp_ref[1, :, cut]] + values
        values = jnp.concatenate(values, 0)
        return jnp.concatenate(keys, 0), jnp.concatenate([values, jnp.ones_like(values)], 1)

    def run(with_quad):
        key_count = rows * (4 if with_quad else 2)
        row = lax.broadcasted_iota(jnp.int32, (rows, key_count), 0)
        column = lax.broadcasted_iota(jnp.int32, (rows, key_count), 1)
        column = column - (key_count - 2 * rows)
        partner_limit = jnp.where(me % 2 == 1, rows, 0)
        mask = (column < partner_limit) | ((column >= rows) & (column - rows <= row))
        sums = []
        for head in range(heads):
            keys, values = key_value(head, with_quad)
            mixed, lse = soft(q_ref[:, block_lanes(head)], keys, values, mask)
            own_ref[:, block_lanes(head)] = mixed
            sums.append(lse)
        lse_ref[...] = spread(sums, SUBLANES)

        def answer(index):
            sums = [[], []]
            for head in range(heads):
                keys, values = key_value(head, with_quad)
                query = ask_refs[index][:, :, block_lanes(head)].reshape(2 * rows, HEAD_DIM)
                mixed, lse = soft(query, keys, values)
                first = lse.astype(jnp.bfloat16).astype(jnp.float32)
                second = (lse - first).astype(jnp.bfloat16).astype(jnp.float32)
                for half in range(2):
                    cut = slice(half * rows, (half + 1) * rows)
                    start = half * half_rows + head * rows
                    answer_refs[index][start : start + rows, :] = mixed[cut].astype(jnp.bfloat16)
                    sums[half] += [first[cut], second[cut], (lse - first - second)[cut]]
            for half in range(2):
                start = half * half_rows + heads * rows
                tail = spread(sums[half], TAIL).astype(jnp.bfloat16)
                answer_refs[index][start : start + TAIL, :] = tail

        for index, pairs in enumerate(transfers):
            asked = [target for _, target in pairs if (target in upper) == with_quad]
            if asked:
                pl.when(among(me, asked))(functools.partial(answer, index))

    if upper:
        pl.when(among(me, upper))(functools.partial(run, True))
        pl.when(jnp.logical_not(among(me, upper)))(functools.partial(run, False))
    else:
        run(False)


def merge_kernel(transfers, me_ref, own_ref, lse_ref, *refs):
    others = refs[: 2 * len(transfers)]
    out_ref = refs[-1]
    me = me_ref[0]
    rows, width = out_ref.shape
    heads = width // HEAD_DIM
    returned = []
    for pairs in transfers:
        members = [source for source, _ in pairs]
        returned += [members, [member ^ 1 for member in members]]
    answered = among(me, sorted(set(sum(returned, []))))

    def columns(part):
        fill = jnp.zeros((LANES - part.shape[0], rows), jnp.float32)
        return jnp.transpose(jnp.concatenate([part, fill], 0))

    @pl.when(answered)
    def _():
        own_sums = columns(lse_ref[...])
        valid = [among(me, members) for members in returned]
        sums = [columns(ref[heads * rows :, :].astype(jnp.float32)) for ref in others]
        for head in range(heads):
            cut = block_lanes(head)
            logs = [own_sums[:, head : head + 1]]
            mixed = [own_ref[:, cut]]
            for index, ref in enumerate(others):
                parts = [sums[index][:, 3 * head + part : 3 * head + part + 1] for part in range(3)]
                logs.append(jnp.where(valid[index], parts[0] + parts[1] + parts[2], NEGATIVE))
                part = ref[head * rows : (head + 1) * rows, :].astype(jnp.float32)
                mixed.append(jnp.where(valid[index], part, 0.0))
            top = functools.reduce(jnp.maximum, logs)
            weights = [jnp.exp2(part - top) for part in logs]
            total = functools.reduce(jnp.add, weights)
            terms = [part * (weight / total) for part, weight in zip(mixed, weights)]
            out_ref[:, cut] = functools.reduce(jnp.add, terms).astype(out_ref.dtype)

    @pl.when(jnp.logical_not(answered))
    def _():
        out_ref[...] = own_ref[...].astype(out_ref.dtype)


def after(array, *others):
    return lax.optimization_barrier((array, *others))[0]


def attend(query, key, value):
    rows, columns = query.shape
    devices = lax.axis_size("ctx")
    quads = devices // 4
    transfers = plan_moves(devices)
    step_width = HEADS_PER_STEP * HEAD_DIM
    chunks = len(CHUNK_STEPS)
    first_steps = [sum(CHUNK_STEPS[:chunk]) for chunk in range(chunks)]
    widths = [steps * step_width for steps in CHUNK_STEPS]
    starts = [step * step_width for step in first_steps]
    upper = [4 * quad + 2 + core for quad in range(quads - 1) for core in range(2)]
    gathers = [(who - 2, who) for who in upper]
    askers = sorted({source for pairs in transfers for source, _ in pairs})
    swap = [(index, index ^ 1) for index in range(devices)]
    me = lax.axis_index("ctx").astype(jnp.int32).reshape(1)

    query_swapped = lax.ppermute(query, "ctx", swap)
    key_swapped = lax.ppermute(key, "ctx", swap)
    value_swapped = lax.ppermute(value, "ctx", swap)

    def pack(members):
        hbm = pl.BlockSpec(memory_space=pl.ANY)
        shapes = [
            jax.ShapeDtypeStruct((2, rows, widths[chunk]), jnp.bfloat16) for chunk in members
        ]
        outs = pl.pallas_call(
            functools.partial(
                pack_kernel,
                [source for source, _ in gathers],
                askers,
                [widths[chunk] for chunk in members],
                [starts[chunk] for chunk in members],
            ),
            in_specs=[hbm] * 4,
            out_specs=[hbm] * (2 * len(members)),
            out_shape=shapes * 2,
            scratch_shapes=[pltpu.SemaphoreType.DMA((2 * len(members),))],
            compiler_params=params(),
            cost_estimate=cost(1),
            name="att_pack",
        )(query, query_swapped, key, value)
        return list(zip(outs[: len(members)], outs[len(members) :]))

    packs = pack([0]) + (pack(list(range(1, chunks))) if chunks > 1 else [])
    asks, quad_kv = [], []
    for chunk in range(chunks):
        key_pack, query_pack = packs[chunk]
        if chunk:
            key_pack = after(key_pack, quad_kv[-1][0])
            query_pack = after(query_pack, *asks[-1])
        arrived = lax.ppermute(key_pack, "ctx", gathers)
        asks.append([lax.ppermute(query_pack, "ctx", pairs) for pairs in transfers])
        quad_kv.append([arrived, lax.ppermute(arrived, "ctx", swap)])

    half_rows = HEADS_PER_STEP * rows + TAIL
    result = None
    for chunk in range(chunks):
        steps, first = CHUNK_STEPS[chunk], first_steps[chunk]
        whole_spec = pl.BlockSpec((rows, step_width), lambda step, first=first: (0, first + step))
        chunk_spec = pl.BlockSpec((rows, step_width), lambda step: (0, step))
        pair_spec = pl.BlockSpec((2, rows, step_width), lambda step: (0, 0, step))
        lse_spec = pl.BlockSpec((SUBLANES, LANES), lambda step: (step, 0))
        answer_spec = pl.BlockSpec((2 * half_rows, LANES), lambda step: (step, 0))
        answer_shape = jax.ShapeDtypeStruct((2 * half_rows * steps, LANES), jnp.bfloat16)
        own, lse, *answers = pl.pallas_call(
            functools.partial(partial_kernel, transfers, upper),
            grid=(steps,),
            in_specs=[whole_spec] * 5 + [pair_spec] * (2 + len(transfers)),
            out_specs=[chunk_spec, lse_spec] + [answer_spec] * len(transfers),
            out_shape=[
                jax.ShapeDtypeStruct((rows, widths[chunk]), jnp.float32),
                jax.ShapeDtypeStruct((SUBLANES * steps, LANES), jnp.float32),
            ]
            + [answer_shape] * len(transfers),
            compiler_params=params(),
            cost_estimate=cost(4),
            name="att_partial",
        )(query, key, value, key_swapped, value_swapped, *quad_kv[chunk], *asks[chunk])
        operands = [me, own, lse]
        for answer, pairs in zip(answers, transfers):
            back = lax.ppermute(answer, "ctx", [(target, source) for source, target in pairs])
            operands += [back, lax.ppermute(back, "ctx", swap)]

        def shifted(step, me_ref, first=first):
            return (0, first + step)

        half_spec = pl.BlockSpec(
            (half_rows, LANES), lambda step, me_ref: (2 * step + me_ref[0] % 2, 0)
        )
        specs = [
            pl.BlockSpec((rows, step_width), lambda step, me_ref: (0, step)),
            pl.BlockSpec((SUBLANES, LANES), lambda step, me_ref: (step, 0)),
        ] + [half_spec] * (2 * len(transfers))
        aliases = {}
        if result is not None:
            aliases = {len(operands): 0}
            operands.append(result)
            specs.append(pl.BlockSpec(memory_space=pl.ANY))
        result = pl.pallas_call(
            functools.partial(merge_kernel, transfers),
            grid_spec=pltpu.PrefetchScalarGridSpec(
                num_scalar_prefetch=1,
                grid=(steps,),
                in_specs=specs,
                out_specs=pl.BlockSpec((rows, step_width), shifted),
            ),
            out_shape=jax.ShapeDtypeStruct((rows, columns), jnp.bfloat16),
            input_output_aliases=aliases,
            compiler_params=params(),
            cost_estimate=cost(2),
            name="att_merge",
        )(*operands)
    return result


def local(
    hyena_q, hyena_k, hyena_v, short_filter, residue, decay_rate, att_query, att_key, att_value
):
    att_out = attend(att_query, att_key, att_value)
    hyena_out = convolve(hyena_q, hyena_k, hyena_v, short_filter, residue, decay_rate)
    return (hyena_out, att_out)


def solution(mesh):
    rows = P(("dp", "ctx"), None)
    shared = P("ctx", None)
    return jax.shard_map(
        local,
        mesh=mesh,
        in_specs=(rows, rows, rows, P(), shared, shared, rows, rows, rows),
        out_specs=(rows, rows),
        check_vma=False,
    )
```

```python
import functools
import math

import jax
import jax.numpy as jnp
from jax import lax
from jax.experimental import pallas as pl
from jax.experimental.pallas import tpu as pltpu
from jax.sharding import PartitionSpec as P

HEAD_DIM = 128
LANES = 128
SUBLANES = 8
TAIL = 4 * SUBLANES
TAPS = 3
HEADS_PER_STEP = 4
CHUNK_STEPS = (2, 2, 2, 2)
NEGATIVE = -1e30
EXP_SCALE = HEAD_DIM**-0.5 * math.log2(math.e)
VMEM_LIMIT = 255 * 1024 * 256


def params(**kwargs):
    return pltpu.CompilerParams(vmem_limit_bytes=VMEM_LIMIT, **kwargs)


def cost(microseconds):
    return pl.CostEstimate(
        flops=microseconds * 10**9, bytes_accessed=2**20, transcendentals=0
    )


def block_lanes(block):
    return slice(block * LANES, (block + 1) * LANES)


def conv_pack_kernel(rate_ref, residue_ref, q_ref, k_ref, v_ref, par_ref, rim_ref):
    modes = rate_ref.shape[0]
    for block in range(rate_ref.shape[1] // LANES):
        for which, ref in enumerate((rate_ref, residue_ref)):
            start = (2 * block + which) * modes
            for device in range(par_ref.shape[0]):
                par_ref[device, start : start + modes, :] = ref[:, block_lanes(block)]
    for feature, ref in enumerate((q_ref, k_ref, v_ref)):
        last = ref[...].astype(jnp.float32)[ref.shape[0] - 2 :]
        rim_ref[2 * feature : 2 * feature + 2, :] = last
    rim_ref[2 * TAPS :, :] = jnp.zeros((2, rim_ref.shape[1]), jnp.float32)


def rim_rows(rim_ref, feature, lanes):
    return [rim_ref[pl.ds(2 * feature + row, 1), lanes] for row in range(2)]


def short_mix(feature, rim, taps):
    two_before, one_before = rim
    row = lax.broadcasted_iota(jnp.int32, feature.shape, 0)
    one = jnp.where(row == 0, one_before, pltpu.roll(feature, 1, 0))
    two = jnp.where(row == 0, two_before, jnp.where(row == 1, one_before, pltpu.roll(feature, 2, 0)))
    return taps[0] * feature + taps[1] * one + taps[2] * two


def tap_rows(taps_ref, feature, lanes):
    return [taps_ref[feature, pl.ds(tap, 1), lanes] for tap in range(TAPS)]


def state_kernel(modes, k_ref, v_ref, rim_ref, par_ref, taps_ref, y_ref, s_ref, p_scr, y_scr):
    rows = k_ref.shape[0]
    for block in range(SUBLANES):
        lanes = block_lanes(block)
        mixes = [
            short_mix(
                ref[:, lanes].astype(jnp.float32),
                rim_rows(rim_ref, feature, lanes),
                tap_rows(taps_ref, feature, lanes),
            )
            for feature, ref in ((1, k_ref), (2, v_ref))
        ]
        product = (mixes[0] * mixes[1]).astype(jnp.bfloat16).astype(jnp.float32)
        p_scr[pl.ds(block, rows, SUBLANES), :] = product
    decay = [jnp.exp(-par_ref[pl.ds(mode, SUBLANES, 2 * modes), :]) for mode in range(modes)]
    residue = [par_ref[pl.ds(modes + mode, SUBLANES, 2 * modes), :] for mode in range(modes)]

    def body(position, states):
        here = pl.ds(pl.multiple_of(position * SUBLANES, SUBLANES), SUBLANES)
        product = p_scr[here, :]
        states = tuple(state * rate + product for state, rate in zip(states, decay))
        terms = [state * weight for state, weight in zip(states, residue)]
        while len(terms) > 1:
            terms = [left + right for left, right in zip(terms[::2], terms[1::2])]
        y_scr[here, :] = terms[0]
        return states

    zero = jnp.zeros((SUBLANES, LANES), jnp.float32)
    states = lax.fori_loop(0, rows, body, (zero,) * modes, unroll=4)
    for mode in range(modes):
        s_ref[pl.ds(mode, SUBLANES, modes), :] = states[mode]
    for block in range(SUBLANES):
        y_ref[:, block_lanes(block)] = y_scr[pl.ds(block, rows, SUBLANES), :]


def output_kernel(modes, q_ref, y_ref, rim_ref, par_ref, state_ref, taps_ref, out_ref):
    me = lax.axis_index("ctx")
    rows = q_ref.shape[0]
    step = lax.broadcasted_iota(jnp.int32, (SUBLANES, LANES), 0).astype(jnp.float32) + 1.0

    def body(block, nothing):
        lanes = pl.ds(pl.multiple_of(block * LANES, LANES), LANES)
        rate = par_ref[pl.ds(pl.multiple_of(2 * block * modes, SUBLANES), modes), :]
        residue = par_ref[pl.ds(pl.multiple_of((2 * block + 1) * modes, SUBLANES), modes), :]
        chunk_decay = jnp.exp(-rate * rows)
        entering = jnp.zeros((modes, LANES), jnp.float32)
        for device in range(state_ref.shape[0] - 1):
            start = pl.multiple_of(block * modes, SUBLANES)
            after = entering * chunk_decay + state_ref[device, pl.ds(start, modes), :]
            entering = jnp.where(device < me, after, entering)
        weighted = residue * entering
        eight = jnp.exp(-rate * SUBLANES)
        terms = [
            weighted[mode : mode + 1] * jnp.exp(-rate[mode : mode + 1] * step)
            for mode in range(modes)
        ]
        eights = [jnp.broadcast_to(eight[mode : mode + 1], terms[0].shape) for mode in range(modes)]
        added = []
        for start in range(0, rows, SUBLANES):
            sums = list(terms)
            while len(sums) > 1:
                sums = [left + right for left, right in zip(sums[::2], sums[1::2])]
            added.append(sums[0])
            if start + SUBLANES < rows:
                terms = [term * decay for term, decay in zip(terms, eights)]
        smoothed = y_ref[:, lanes] + jnp.concatenate(added, 0)
        smoothed = smoothed.astype(jnp.bfloat16).astype(jnp.float32)
        mix = short_mix(
            q_ref[:, lanes].astype(jnp.float32),
            rim_rows(rim_ref, 0, lanes),
            tap_rows(taps_ref, 0, lanes),
        )
        out_ref[:, lanes] = (mix * smoothed).astype(out_ref.dtype)
        return nothing

    lax.fori_loop(0, SUBLANES, body, 0)


def convolution(hyena_q, hyena_k, hyena_v, short_filter, residue, decay_rate):
    rows, channels = hyena_q.shape
    devices = lax.axis_size("ctx")
    modes = residue.shape[1]
    own_blocks = residue.shape[0] // LANES
    blocks = channels // LANES
    groups = blocks // SUBLANES
    width = SUBLANES * LANES
    end = rows // 16 - 1
    par_rows = 2 * own_blocks * modes
    feature_spec = pl.BlockSpec((rows, width), lambda group: (0, group))
    rim_spec = pl.BlockSpec((8, width), lambda group: (0, group))
    par_spec = pl.BlockSpec((2 * SUBLANES * modes, LANES), lambda group: (group, 0))
    taps_spec = pl.BlockSpec((TAPS, TAPS, width), lambda group: (0, 0, group))
    positions = pltpu.VMEM((rows * SUBLANES, LANES), jnp.float32)

    def first_part(token):
        own_par, rim = pl.pallas_call(
            conv_pack_kernel,
            grid=(1,),
            in_specs=[pl.BlockSpec((modes, residue.shape[0]), lambda step: (0, 0))] * 2
            + [pl.BlockSpec((16, channels), lambda step: (end, 0))] * 3,
            out_specs=[
                pl.BlockSpec((devices, par_rows, LANES), lambda step: (0, 0, 0)),
                pl.BlockSpec((8, channels), lambda step: (0, 0)),
            ],
            out_shape=[
                jax.ShapeDtypeStruct((devices, par_rows, LANES), jnp.float32),
                jax.ShapeDtypeStruct((8, channels), jnp.float32),
            ],
            compiler_params=params(),
            cost_estimate=cost(1),
            name="conv_pack",
        )(after(decay_rate.T, token), residue.T, hyena_q, hyena_k, hyena_v)
        par = lax.all_to_all(own_par, "ctx", split_axis=0, concat_axis=0, tiled=True)
        par = par.reshape(devices * par_rows, LANES)
        rim = lax.ppermute(rim, "ctx", [(index, index + 1) for index in range(devices - 1)])
        local_result, state = pl.pallas_call(
            functools.partial(state_kernel, modes),
            grid=(groups,),
            in_specs=[feature_spec, feature_spec, rim_spec, par_spec, taps_spec],
            out_specs=[
                feature_spec,
                pl.BlockSpec((SUBLANES * modes, LANES), lambda group: (group, 0)),
            ],
            out_shape=[
                jax.ShapeDtypeStruct((rows, channels), jnp.float32),
                jax.ShapeDtypeStruct((blocks * modes, LANES), jnp.float32),
            ],
            scratch_shapes=[positions, positions],
            compiler_params=params(),
            cost_estimate=cost(9),
            name="conv_state",
        )(hyena_k, hyena_v, rim, par, short_filter)
        return local_result, state, rim, par

    def last_part(local_result, state, rim, par):
        states = lax.all_gather(state, "ctx", axis=0, tiled=True)
        states = states.reshape(devices, blocks * modes, LANES)
        return pl.pallas_call(
            functools.partial(output_kernel, modes),
            grid=(groups,),
            in_specs=[
                feature_spec,
                feature_spec,
                rim_spec,
                par_spec,
                pl.BlockSpec((devices, SUBLANES * modes, LANES), lambda group: (0, group, 0)),
                taps_spec,
            ],
            out_specs=feature_spec,
            out_shape=jax.ShapeDtypeStruct((rows, channels), jnp.bfloat16),
            compiler_params=params(),
            cost_estimate=cost(6),
            name="conv_output",
        )(hyena_q, local_result, rim, par, states, short_filter)

    return first_part, last_part


def among(me, members):
    return functools.reduce(jnp.logical_or, [me == member for member in members])


def plan_moves(devices):
    quads = devices // 4
    transfers = [[(devices - 1, devices - 3)]]
    for distance in range(1, quads):
        if distance > len(transfers):
            transfers.append([])
        for quad in range(distance, quads):
            target = 4 * (quad - distance) + 2
            transfers[distance - 1] += [(4 * quad, target), (4 * quad + 2, target + 1)]
    return transfers


def soft(query, keys, values, mask=None):
    scores = lax.dot_general(
        query, keys, (((1,), (1,)), ((), ())), preferred_element_type=jnp.float32
    )
    if mask is not None:
        scores = jnp.where(mask, scores, NEGATIVE)
    top = jnp.max(scores, axis=1, keepdims=True) * EXP_SCALE
    expo = jnp.exp2(scores * EXP_SCALE - top).astype(jnp.bfloat16)
    mixed = jnp.dot(expo, values, preferred_element_type=jnp.float32)
    total = mixed[:, HEAD_DIM:]
    return mixed[:, :HEAD_DIM] / total, top + jnp.log2(total)


def pack_kernel(gathers, askers, widths, starts, q_ref, qs_ref, k_ref, v_ref, *rest):
    count = len(widths)
    key_outs, query_outs = rest[:count], rest[count : 2 * count]
    stages, in_sems, out_sems = rest[2 * count : 4 * count], rest[-2], rest[-1]
    me = lax.axis_index("ctx")
    odd = me % 2

    def run(pairs):
        loads = [
            pltpu.make_async_copy(source, stage, in_sems.at[index])
            for index, ((source, _), stage) in enumerate(zip(pairs, stages))
        ]
        stores = [
            pltpu.make_async_copy(stage, target, out_sems.at[index])
            for index, ((_, target), stage) in enumerate(zip(pairs, stages))
        ]
        for load in loads:
            load.start()
        for load, store in zip(loads, stores):
            load.wait()
            store.start()
        for store in stores:
            store.wait()

    def cut(ref, chunk):
        return ref.at[:, pl.ds(starts[chunk], widths[chunk])]

    if gathers:

        @pl.when(among(me, gathers))
        def _():
            run(
                [
                    (cut(ref, chunk), key_outs[chunk].at[which])
                    for chunk in range(count)
                    for which, ref in enumerate((k_ref, v_ref))
                ]
            )

    @pl.when(among(me, askers))
    def _():
        run(
            [
                (cut(ref, chunk), query_outs[chunk].at[half])
                for chunk in range(count)
                for ref, half in ((q_ref, odd), (qs_ref, 1 - odd))
            ]
        )


def as_rows(columns):
    lanes = lax.broadcasted_iota(jnp.int32, columns[0].shape, 1)
    sums = jnp.zeros_like(columns[0])
    for index, column in enumerate(columns):
        sums = jnp.where(lanes == index, column, sums)
    return jnp.transpose(sums)[:SUBLANES]


def as_columns(part):
    fill = jnp.zeros((LANES - part.shape[0], part.shape[1]), jnp.float32)
    return jnp.transpose(jnp.concatenate([part, fill], 0))


def partial_kernel(transfers, upper, *refs):
    count = len(transfers)
    q_ref, k_ref, v_ref, kp_ref, vp_ref, g_ref, gp_ref = refs[:7]
    ask_refs = refs[7 : 7 + count]
    own_ref, lse_ref = refs[7 + count : 9 + count]
    answer_refs = refs[9 + count :]
    me = lax.axis_index("ctx")
    rows = q_ref.shape[0]
    heads = q_ref.shape[1] // HEAD_DIM
    half_rows = heads * rows + TAIL

    def key_value(head, with_quad):
        cut = block_lanes(head)
        keys = [kp_ref[:, cut], k_ref[:, cut]]
        values = [vp_ref[:, cut], v_ref[:, cut]]
        if with_quad:
            keys = [g_ref[0, :, cut], gp_ref[0, :, cut]] + keys
            values = [g_ref[1, :, cut], gp_ref[1, :, cut]] + values
        values = jnp.concatenate(values, 0)
        return jnp.concatenate(keys, 0), jnp.concatenate([values, jnp.ones_like(values)], 1)

    def run(with_quad):
        key_count = rows * (4 if with_quad else 2)
        row = lax.broadcasted_iota(jnp.int32, (rows, key_count), 0)
        column = lax.broadcasted_iota(jnp.int32, (rows, key_count), 1)
        column = column - (key_count - 2 * rows)
        partner_limit = jnp.where(me % 2 == 1, rows, 0)
        mask = (column < partner_limit) | ((column >= rows) & (column - rows <= row))
        sums = []
        for head in range(heads):
            keys, values = key_value(head, with_quad)
            mixed, lse = soft(q_ref[:, block_lanes(head)], keys, values, mask)
            own_ref[:, block_lanes(head)] = mixed
            sums.append(lse)
        lse_ref[...] = as_rows(sums)

        def answer(index):
            sums = [[], []]
            for head in range(heads):
                keys, values = key_value(head, with_quad)
                query = ask_refs[index][:, :, block_lanes(head)].reshape(2 * rows, HEAD_DIM)
                mixed, lse = soft(query, keys, values)
                for half in range(2):
                    cut = slice(half * rows, (half + 1) * rows)
                    start = half * half_rows + head * rows
                    answer_refs[index][start : start + rows, :] = mixed[cut].astype(jnp.bfloat16)
                    sums[half].append(lse[cut])
            for half in range(2):
                start = half * half_rows + heads * rows
                lse = as_rows(sums[half])
                first = lse.astype(jnp.bfloat16).astype(jnp.float32)
                second = (lse - first).astype(jnp.bfloat16).astype(jnp.float32)
                third = lse - first - second
                tail = jnp.concatenate([first, second, third, jnp.zeros_like(lse)], 0)
                answer_refs[index][start : start + TAIL, :] = tail.astype(jnp.bfloat16)

        for index, pairs in enumerate(transfers):
            asked = [target for _, target in pairs if (target in upper) == with_quad]
            if asked:
                pl.when(among(me, asked))(functools.partial(answer, index))

    if upper:
        pl.when(among(me, upper))(functools.partial(run, True))
        pl.when(jnp.logical_not(among(me, upper)))(functools.partial(run, False))
    else:
        run(False)


def merge_kernel(transfers, me_ref, own_ref, lse_ref, *refs):
    others = refs[: 2 * len(transfers)]
    out_ref = refs[-1]
    me = me_ref[0]
    rows, width = out_ref.shape
    heads = width // HEAD_DIM
    returned = []
    for pairs in transfers:
        members = [source for source, _ in pairs]
        returned += [members, [member ^ 1 for member in members]]
    answered = among(me, sorted(set(sum(returned, []))))

    @pl.when(answered)
    def _():
        valid = [among(me, members) for members in returned]
        logs = [lse_ref[...]]
        for index, ref in enumerate(others):
            tail = ref[heads * rows :, :].astype(jnp.float32)
            tail = tail[:SUBLANES] + tail[SUBLANES : 2 * SUBLANES] + tail[2 * SUBLANES : 3 * SUBLANES]
            logs.append(jnp.where(valid[index], tail, NEGATIVE))
        top = functools.reduce(jnp.maximum, logs)
        weights = [jnp.exp2(part - top) for part in logs]
        total = functools.reduce(jnp.add, weights)
        shares = [as_columns(weight / total) for weight in weights]
        for head in range(heads):
            cut = block_lanes(head)
            mixed = [own_ref[:, cut]]
            for index, ref in enumerate(others):
                part = ref[head * rows : (head + 1) * rows, :].astype(jnp.float32)
                mixed.append(jnp.where(valid[index], part, 0.0))
            terms = [part * share[:, head : head + 1] for part, share in zip(mixed, shares)]
            out_ref[:, cut] = functools.reduce(jnp.add, terms).astype(out_ref.dtype)

    @pl.when(jnp.logical_not(answered))
    def _():
        out_ref[...] = own_ref[...].astype(out_ref.dtype)


def after(array, *others):
    return lax.optimization_barrier((array, *others))[0]


def attend(query, key, value, conv):
    rows, columns = query.shape
    devices = lax.axis_size("ctx")
    quads = devices // 4
    transfers = plan_moves(devices)
    step_width = HEADS_PER_STEP * HEAD_DIM
    chunks = len(CHUNK_STEPS)
    first_steps = [sum(CHUNK_STEPS[:chunk]) for chunk in range(chunks)]
    widths = [steps * step_width for steps in CHUNK_STEPS]
    starts = [step * step_width for step in first_steps]
    upper = [4 * quad + 2 + core for quad in range(quads - 1) for core in range(2)]
    gathers = [(who - 2, who) for who in upper]
    askers = sorted({source for pairs in transfers for source, _ in pairs})
    swap = [(index, index ^ 1) for index in range(devices)]
    me = lax.axis_index("ctx").astype(jnp.int32).reshape(1)

    query_swapped = lax.ppermute(query, "ctx", swap)
    key_swapped = lax.ppermute(key, "ctx", swap)
    value_swapped = lax.ppermute(value, "ctx", swap)

    def pack(members):
        hbm = pl.BlockSpec(memory_space=pl.ANY)
        shapes = [
            jax.ShapeDtypeStruct((2, rows, widths[chunk]), jnp.bfloat16) for chunk in members
        ]
        outs = pl.pallas_call(
            functools.partial(
                pack_kernel,
                [source for source, _ in gathers],
                askers,
                [widths[chunk] for chunk in members],
                [starts[chunk] for chunk in members],
            ),
            in_specs=[hbm] * 4,
            out_specs=[hbm] * (2 * len(members)),
            out_shape=shapes * 2,
            scratch_shapes=[
                pltpu.VMEM((rows, widths[chunk]), jnp.bfloat16)
                for chunk in members
                for _ in range(2)
            ]
            + [pltpu.SemaphoreType.DMA((2 * len(members),))] * 2,
            compiler_params=params(),
            cost_estimate=cost(1),
            name="att_pack",
        )(query, query_swapped, key, value)
        return list(zip(outs[: len(members)], outs[len(members) :]))

    packs = pack([0])
    conv_state, conv_output = conv
    local_result, state, *conv_shared = conv_state(packs[0][1])
    packs += pack(list(range(1, chunks))) if chunks > 1 else []
    asks, quad_kv, all_answers = [], [], []

    def send(chunk):
        key_pack, query_pack = packs[chunk]
        if chunk:
            key_pack = after(key_pack, quad_kv[-1][0])
            query_pack = after(query_pack, *asks[-1])
        if chunk > 1:
            key_pack = after(key_pack, all_answers[chunk - 2][0])
            query_pack = after(query_pack, all_answers[chunk - 2][0])
        arrived = lax.ppermute(key_pack, "ctx", gathers)
        asks.append([lax.ppermute(query_pack, "ctx", pairs) for pairs in transfers])
        quad_kv.append([arrived, lax.ppermute(arrived, "ctx", swap)])

    send(0)
    half_rows = HEADS_PER_STEP * rows + TAIL
    result = None
    for chunk in range(chunks):
        if chunk + 1 < chunks:
            send(chunk + 1)
        if chunk == 0:
            asks[0] = [after(asked, state) for asked in asks[0]]
        steps, first = CHUNK_STEPS[chunk], first_steps[chunk]
        whole_spec = pl.BlockSpec((rows, step_width), lambda step, first=first: (0, first + step))
        chunk_spec = pl.BlockSpec((rows, step_width), lambda step: (0, step))
        pair_spec = pl.BlockSpec((2, rows, step_width), lambda step: (0, 0, step))
        lse_spec = pl.BlockSpec((SUBLANES, LANES), lambda step: (step, 0))
        answer_spec = pl.BlockSpec((2 * half_rows, LANES), lambda step: (step, 0))
        answer_shape = jax.ShapeDtypeStruct((2 * half_rows * steps, LANES), jnp.bfloat16)
        own, lse, *answers = pl.pallas_call(
            functools.partial(partial_kernel, transfers, upper),
            grid=(steps,),
            in_specs=[whole_spec] * 5 + [pair_spec] * (2 + len(transfers)),
            out_specs=[chunk_spec, lse_spec] + [answer_spec] * len(transfers),
            out_shape=[
                jax.ShapeDtypeStruct((rows, widths[chunk]), jnp.float32),
                jax.ShapeDtypeStruct((SUBLANES * steps, LANES), jnp.float32),
            ]
            + [answer_shape] * len(transfers),
            compiler_params=params(),
            cost_estimate=cost(4),
            name="att_partial",
        )(query, key, value, key_swapped, value_swapped, *quad_kv[chunk], *asks[chunk])
        all_answers.append(answers)
        operands = [me, own, lse]
        for answer, pairs in zip(answers, transfers):
            back = lax.ppermute(answer, "ctx", [(target, source) for source, target in pairs])
            operands += [back, lax.ppermute(back, "ctx", swap)]

        def shifted(step, me_ref, first=first):
            return (0, first + step)

        half_spec = pl.BlockSpec(
            (half_rows, LANES), lambda step, me_ref: (2 * step + me_ref[0] % 2, 0)
        )
        specs = [
            pl.BlockSpec((rows, step_width), lambda step, me_ref: (0, step)),
            pl.BlockSpec((SUBLANES, LANES), lambda step, me_ref: (step, 0)),
        ] + [half_spec] * (2 * len(transfers))
        aliases = {}
        if result is not None:
            aliases = {len(operands): 0}
            operands.append(result)
            specs.append(pl.BlockSpec(memory_space=pl.ANY))
        result = pl.pallas_call(
            functools.partial(merge_kernel, transfers),
            grid_spec=pltpu.PrefetchScalarGridSpec(
                num_scalar_prefetch=1,
                grid=(steps,),
                in_specs=specs,
                out_specs=pl.BlockSpec((rows, step_width), shifted),
            ),
            out_shape=jax.ShapeDtypeStruct((rows, columns), jnp.bfloat16),
            input_output_aliases=aliases,
            compiler_params=params(),
            cost_estimate=cost(2),
            name="att_merge",
        )(*operands)
    shared = [after(part, all_answers[-1][0]) for part in conv_shared]
    return conv_output(local_result, state, *shared), result


def local(
    hyena_q, hyena_k, hyena_v, short_filter, residue, decay_rate, att_query, att_key, att_value
):
    conv = convolution(hyena_q, hyena_k, hyena_v, short_filter, residue, decay_rate)
    return attend(att_query, att_key, att_value, conv)


def solution(mesh):
    rows = P(("dp", "ctx"), None)
    shared = P("ctx", None)
    return jax.shard_map(
        local,
        mesh=mesh,
        in_specs=(rows, rows, rows, P(), shared, shared, rows, rows, rows),
        out_specs=(rows, rows),
        check_vma=False,
    )
```

```python
import functools
import math

import jax
import jax.numpy as jnp
from jax import lax
from jax.experimental import pallas as pl
from jax.experimental.pallas import tpu as pltpu
from jax.sharding import PartitionSpec as P

HEAD_DIM = 128
LANES = 128
SUBLANES = 8
TAIL = 4 * SUBLANES
TAPS = 3
HEADS_PER_STEP = 4
CHUNK_STEPS = (2, 2, 2, 2)
NEGATIVE = -1e30
EXP_SCALE = HEAD_DIM**-0.5 * math.log2(math.e)
VMEM_LIMIT = 255 * 1024 * 256


def params(**kwargs):
    return pltpu.CompilerParams(vmem_limit_bytes=VMEM_LIMIT, **kwargs)


def cost(microseconds):
    return pl.CostEstimate(
        flops=microseconds * 10**8, bytes_accessed=2**16, transcendentals=0
    )


def block_lanes(block):
    return slice(block * LANES, (block + 1) * LANES)


def conv_pack_kernel(rate_ref, residue_ref, q_ref, k_ref, v_ref, par_ref, rim_ref):
    modes = rate_ref.shape[0]
    for block in range(rate_ref.shape[1] // LANES):
        for which, ref in enumerate((rate_ref, residue_ref)):
            start = (2 * block + which) * modes
            for device in range(par_ref.shape[0]):
                par_ref[device, start : start + modes, :] = ref[:, block_lanes(block)]
    for feature, ref in enumerate((q_ref, k_ref, v_ref)):
        last = ref[...].astype(jnp.float32)[ref.shape[0] - 2 :]
        rim_ref[2 * feature : 2 * feature + 2, :] = last
    rim_ref[2 * TAPS :, :] = jnp.zeros((2, rim_ref.shape[1]), jnp.float32)


def rim_rows(rim_ref, feature, lanes):
    return [rim_ref[pl.ds(2 * feature + row, 1), lanes] for row in range(2)]


def short_mix(feature, rim, taps):
    two_before, one_before = rim
    row = lax.broadcasted_iota(jnp.int32, feature.shape, 0)
    one = jnp.where(row == 0, one_before, pltpu.roll(feature, 1, 0))
    two = jnp.where(row == 0, two_before, jnp.where(row == 1, one_before, pltpu.roll(feature, 2, 0)))
    return taps[0] * feature + taps[1] * one + taps[2] * two


def tap_rows(taps_ref, feature, lanes):
    return [taps_ref[feature, pl.ds(tap, 1), lanes] for tap in range(TAPS)]


def state_kernel(modes, k_ref, v_ref, rim_ref, par_ref, taps_ref, y_ref, s_ref, p_scr, y_scr):
    rows = k_ref.shape[0]
    for block in range(SUBLANES):
        lanes = block_lanes(block)
        mixes = [
            short_mix(
                ref[:, lanes].astype(jnp.float32),
                rim_rows(rim_ref, feature, lanes),
                tap_rows(taps_ref, feature, lanes),
            )
            for feature, ref in ((1, k_ref), (2, v_ref))
        ]
        product = (mixes[0] * mixes[1]).astype(jnp.bfloat16).astype(jnp.float32)
        p_scr[pl.ds(block, rows, SUBLANES), :] = product
    decay = [jnp.exp(-par_ref[pl.ds(mode, SUBLANES, 2 * modes), :]) for mode in range(modes)]
    residue = [par_ref[pl.ds(modes + mode, SUBLANES, 2 * modes), :] for mode in range(modes)]

    def body(position, states):
        here = pl.ds(pl.multiple_of(position * SUBLANES, SUBLANES), SUBLANES)
        product = p_scr[here, :]
        states = tuple(state * rate + product for state, rate in zip(states, decay))
        terms = [state * weight for state, weight in zip(states, residue)]
        while len(terms) > 1:
            terms = [left + right for left, right in zip(terms[::2], terms[1::2])]
        y_scr[here, :] = terms[0]
        return states

    zero = jnp.zeros((SUBLANES, LANES), jnp.float32)
    states = lax.fori_loop(0, rows, body, (zero,) * modes, unroll=4)
    for mode in range(modes):
        s_ref[pl.ds(mode, SUBLANES, modes), :] = states[mode]
    for block in range(SUBLANES):
        y_ref[:, block_lanes(block)] = y_scr[pl.ds(block, rows, SUBLANES), :]


def output_kernel(modes, q_ref, y_ref, rim_ref, par_ref, enter_ref, taps_ref, out_ref):
    rows = q_ref.shape[0]
    step = lax.broadcasted_iota(jnp.int32, (SUBLANES, LANES), 0).astype(jnp.float32) + 1.0

    def body(block, nothing):
        lanes = pl.ds(pl.multiple_of(block * LANES, LANES), LANES)
        rate = par_ref[pl.ds(pl.multiple_of(2 * block * modes, SUBLANES), modes), :]
        residue = par_ref[pl.ds(pl.multiple_of((2 * block + 1) * modes, SUBLANES), modes), :]
        entering = enter_ref[pl.ds(pl.multiple_of(block * modes, SUBLANES), modes), :]
        weighted = residue * entering
        eight = jnp.exp(-rate * SUBLANES)
        terms = [
            weighted[mode : mode + 1] * jnp.exp(-rate[mode : mode + 1] * step)
            for mode in range(modes)
        ]
        eights = [jnp.broadcast_to(eight[mode : mode + 1], terms[0].shape) for mode in range(modes)]
        added = []
        for start in range(0, rows, SUBLANES):
            sums = list(terms)
            while len(sums) > 1:
                sums = [left + right for left, right in zip(sums[::2], sums[1::2])]
            added.append(sums[0])
            if start + SUBLANES < rows:
                terms = [term * decay for term, decay in zip(terms, eights)]
        smoothed = y_ref[:, lanes] + jnp.concatenate(added, 0)
        smoothed = smoothed.astype(jnp.bfloat16).astype(jnp.float32)
        mix = short_mix(
            q_ref[:, lanes].astype(jnp.float32),
            rim_rows(rim_ref, 0, lanes),
            tap_rows(taps_ref, 0, lanes),
        )
        out_ref[:, lanes] = (mix * smoothed).astype(out_ref.dtype)
        return nothing

    lax.fori_loop(0, SUBLANES, body, 0)


def convolution(hyena_q, hyena_k, hyena_v, short_filter, residue, decay_rate):
    rows, channels = hyena_q.shape
    devices = lax.axis_size("ctx")
    modes = residue.shape[1]
    own_blocks = residue.shape[0] // LANES
    blocks = channels // LANES
    groups = blocks // SUBLANES
    width = SUBLANES * LANES
    end = rows // 16 - 1
    par_rows = 2 * own_blocks * modes
    feature_spec = pl.BlockSpec((rows, width), lambda group: (0, group))
    rim_spec = pl.BlockSpec((8, width), lambda group: (0, group))
    par_spec = pl.BlockSpec((2 * SUBLANES * modes, LANES), lambda group: (group, 0))
    taps_spec = pl.BlockSpec((TAPS, TAPS, width), lambda group: (0, 0, group))
    positions = pltpu.VMEM((rows * SUBLANES, LANES), jnp.float32)

    def first_part(token):
        own_par, rim = pl.pallas_call(
            conv_pack_kernel,
            grid=(1,),
            in_specs=[pl.BlockSpec((modes, residue.shape[0]), lambda step: (0, 0))] * 2
            + [pl.BlockSpec((16, channels), lambda step: (end, 0))] * 3,
            out_specs=[
                pl.BlockSpec((devices, par_rows, LANES), lambda step: (0, 0, 0)),
                pl.BlockSpec((8, channels), lambda step: (0, 0)),
            ],
            out_shape=[
                jax.ShapeDtypeStruct((devices, par_rows, LANES), jnp.float32),
                jax.ShapeDtypeStruct((8, channels), jnp.float32),
            ],
            compiler_params=params(),
            cost_estimate=cost(1),
            name="conv_pack",
        )(decay_rate.T, residue.T, hyena_q, hyena_k, hyena_v)
        par = lax.all_to_all(after(own_par, token), "ctx", split_axis=0, concat_axis=0, tiled=True)
        par = par.reshape(devices * par_rows, LANES)
        rim = lax.ppermute(after(rim, token), "ctx", [(index, index + 1) for index in range(devices - 1)])
        local_result, state = pl.pallas_call(
            functools.partial(state_kernel, modes),
            grid=(groups,),
            in_specs=[feature_spec, feature_spec, rim_spec, par_spec, taps_spec],
            out_specs=[
                feature_spec,
                pl.BlockSpec((SUBLANES * modes, LANES), lambda group: (group, 0)),
            ],
            out_shape=[
                jax.ShapeDtypeStruct((rows, channels), jnp.float32),
                jax.ShapeDtypeStruct((blocks * modes, LANES), jnp.float32),
            ],
            scratch_shapes=[positions, positions],
            compiler_params=params(),
            cost_estimate=cost(9),
            name="conv_state",
        )(hyena_k, hyena_v, rim, par, short_filter)
        return local_result, entering_state(state, par), rim, par

    def entering_state(state, par):
        me = lax.axis_index("ctx")
        swap = [(index, index ^ 1) for index in range(devices)]
        rate = par.reshape(blocks, 2 * modes, LANES)[:, :modes].reshape(blocks * modes, LANES)
        other = lax.ppermute(state, "ctx", swap)
        total = state + jnp.exp(-rows * rate) * other
        entering = jnp.zeros_like(state)
        reach = 1
        while 2 * reach < devices:
            moves = [(index, index + 2 * reach) for index in range(1, devices - 2 * reach, 2)]
            arrived = lax.ppermute(total, "ctx", moves)
            entering = entering + jnp.exp(-2.0 * rows * (reach - 1) * rate) * arrived
            total = total + jnp.exp(-2.0 * rows * reach * rate) * arrived
            reach *= 2
        from_second = lax.ppermute(entering, "ctx", swap)
        return jnp.where(me % 2 == 1, jnp.exp(-rows * rate) * entering + other, from_second)

    def last_part(local_result, entering, rim, par):
        return pl.pallas_call(
            functools.partial(output_kernel, modes),
            grid=(groups,),
            in_specs=[
                feature_spec,
                feature_spec,
                rim_spec,
                par_spec,
                pl.BlockSpec((SUBLANES * modes, LANES), lambda group: (group, 0)),
                taps_spec,
            ],
            out_specs=feature_spec,
            out_shape=jax.ShapeDtypeStruct((rows, channels), jnp.bfloat16),
            compiler_params=params(),
            cost_estimate=cost(6),
            name="conv_output",
        )(hyena_q, local_result, rim, par, entering, short_filter)

    return first_part, last_part


def among(me, members):
    return functools.reduce(jnp.logical_or, [me == member for member in members])


def plan_moves(devices):
    quads = devices // 4
    transfers = [[(devices - 1, devices - 3)]]
    for distance in range(1, quads):
        if distance > len(transfers):
            transfers.append([])
        for quad in range(distance, quads):
            target = 4 * (quad - distance) + 2
            transfers[distance - 1] += [(4 * quad, target), (4 * quad + 2, target + 1)]
    return transfers


def soft(query, keys, values, mask=None):
    scores = lax.dot_general(
        query, keys, (((1,), (1,)), ((), ())), preferred_element_type=jnp.float32
    )
    if mask is not None:
        scores = jnp.where(mask, scores, NEGATIVE)
    top = jnp.max(scores, axis=1, keepdims=True) * EXP_SCALE
    expo = jnp.exp2(scores * EXP_SCALE - top).astype(jnp.bfloat16)
    mixed = jnp.dot(expo, values, preferred_element_type=jnp.float32)
    total = mixed[:, HEAD_DIM:]
    return mixed[:, :HEAD_DIM] / total, top + jnp.log2(total)


def pack_kernel(gathers, askers, widths, starts, q_ref, qs_ref, k_ref, v_ref, *rest):
    count = len(widths)
    key_outs, query_outs = rest[:count], rest[count : 2 * count]
    stages, in_sems, out_sems = rest[2 * count : 4 * count], rest[-2], rest[-1]
    me = lax.axis_index("ctx")
    odd = me % 2

    def run(pairs):
        loads = [
            pltpu.make_async_copy(source, stage, in_sems.at[index])
            for index, ((source, _), stage) in enumerate(zip(pairs, stages))
        ]
        stores = [
            pltpu.make_async_copy(stage, target, out_sems.at[index])
            for index, ((_, target), stage) in enumerate(zip(pairs, stages))
        ]
        for load in loads:
            load.start()
        for load, store in zip(loads, stores):
            load.wait()
            store.start()
        for store in stores:
            store.wait()

    def cut(ref, chunk):
        return ref.at[:, pl.ds(starts[chunk], widths[chunk])]

    if gathers:

        @pl.when(among(me, gathers))
        def _():
            run(
                [
                    (cut(ref, chunk), key_outs[chunk].at[which])
                    for chunk in range(count)
                    for which, ref in enumerate((k_ref, v_ref))
                ]
            )

    @pl.when(among(me, askers))
    def _():
        run(
            [
                (cut(ref, chunk), query_outs[chunk].at[half])
                for chunk in range(count)
                for ref, half in ((q_ref, odd), (qs_ref, 1 - odd))
            ]
        )


def as_rows(columns):
    lanes = lax.broadcasted_iota(jnp.int32, columns[0].shape, 1)
    sums = jnp.zeros_like(columns[0])
    for index, column in enumerate(columns):
        sums = jnp.where(lanes == index, column, sums)
    return jnp.transpose(sums)[:SUBLANES]


def as_columns(part):
    fill = jnp.zeros((LANES - part.shape[0], part.shape[1]), jnp.float32)
    return jnp.transpose(jnp.concatenate([part, fill], 0))


def partial_kernel(transfers, upper, onto, *refs):
    count = len(transfers)
    out_ref = refs[-1]
    q_ref, k_ref, v_ref, kp_ref, vp_ref, g_ref, gp_ref = refs[:7]
    ask_refs = refs[7 : 7 + count]
    own_ref, lse_ref = refs[7 + count + onto : 9 + count + onto]
    answer_refs = refs[9 + count + onto : -1]
    me = lax.axis_index("ctx")
    rows = q_ref.shape[0]
    heads = q_ref.shape[1] // HEAD_DIM
    half_rows = heads * rows + TAIL

    def key_value(head, with_quad):
        cut = block_lanes(head)
        keys = [kp_ref[:, cut], k_ref[:, cut]]
        values = [vp_ref[:, cut], v_ref[:, cut]]
        if with_quad:
            keys = [g_ref[0, :, cut], gp_ref[0, :, cut]] + keys
            values = [g_ref[1, :, cut], gp_ref[1, :, cut]] + values
        values = jnp.concatenate(values, 0)
        return jnp.concatenate(keys, 0), jnp.concatenate([values, jnp.ones_like(values)], 1)

    def run(with_quad):
        key_count = rows * (4 if with_quad else 2)
        row = lax.broadcasted_iota(jnp.int32, (rows, key_count), 0)
        column = lax.broadcasted_iota(jnp.int32, (rows, key_count), 1)
        column = column - (key_count - 2 * rows)
        partner_limit = jnp.where(me % 2 == 1, rows, 0)
        mask = (column < partner_limit) | ((column >= rows) & (column - rows <= row))
        sums = []
        for head in range(heads):
            keys, values = key_value(head, with_quad)
            mixed, lse = soft(q_ref[:, block_lanes(head)], keys, values, mask)
            own_ref[:, block_lanes(head)] = mixed
            out_ref[:, block_lanes(head)] = mixed.astype(out_ref.dtype)
            sums.append(lse)
        lse_ref[...] = as_rows(sums)

        def answer(index):
            sums = [[], []]
            for head in range(heads):
                keys, values = key_value(head, with_quad)
                query = ask_refs[index][:, :, block_lanes(head)].reshape(2 * rows, HEAD_DIM)
                mixed, lse = soft(query, keys, values)
                for half in range(2):
                    cut = slice(half * rows, (half + 1) * rows)
                    start = half * half_rows + head * rows
                    answer_refs[index][start : start + rows, :] = mixed[cut].astype(jnp.bfloat16)
                    sums[half].append(lse[cut])
            for half in range(2):
                start = half * half_rows + heads * rows
                lse = as_rows(sums[half])
                first = lse.astype(jnp.bfloat16).astype(jnp.float32)
                second = (lse - first).astype(jnp.bfloat16).astype(jnp.float32)
                third = lse - first - second
                tail = jnp.concatenate([first, second, third, jnp.zeros_like(lse)], 0)
                answer_refs[index][start : start + TAIL, :] = tail.astype(jnp.bfloat16)

        for index, pairs in enumerate(transfers):
            asked = [target for _, target in pairs if (target in upper) == with_quad]
            if asked:
                pl.when(among(me, asked))(functools.partial(answer, index))

    if upper:
        pl.when(among(me, upper))(functools.partial(run, True))
        pl.when(jnp.logical_not(among(me, upper)))(functools.partial(run, False))
    else:
        run(False)


def merge_kernel(transfers, steps, start, own_hbm, lse_hbm, *refs):
    count = 2 * len(transfers)
    others_hbm, out_hbm = refs[:count], refs[count + 1]
    own_ref, lse_ref, *other_refs = refs[count + 2 : 2 * count + 4]
    out_ref, sems = refs[-2:]
    me = lax.axis_index("ctx")
    odd = me % 2
    rows, width = own_ref.shape
    heads = HEADS_PER_STEP
    half_rows = heads * rows + TAIL
    returned = []
    for pairs in transfers:
        members = [source for source, _ in pairs]
        returned += [members, [member ^ 1 for member in members]]

    @pl.when(among(me, sorted(set(sum(returned, [])))))
    def _():
        loads = [(own_hbm, own_ref), (lse_hbm, lse_ref)]
        for hbm, ref in zip(others_hbm, other_refs):
            for step in range(steps):
                half = pl.ds(pl.multiple_of((2 * step + odd) * half_rows, TAIL), half_rows)
                loads.append((hbm.at[half, :], ref.at[step]))
        copies = [
            pltpu.make_async_copy(source, target, sems.at[index])
            for index, (source, target) in enumerate(loads)
        ]
        for copy in copies:
            copy.start()
        for copy in copies:
            copy.wait()
        valid = [among(me, members) for members in returned]
        for step in range(steps):
            logs = [lse_ref[step * SUBLANES : (step + 1) * SUBLANES, :]]
            for index, ref in enumerate(other_refs):
                tail = ref[step, heads * rows :, :].astype(jnp.float32)
                parts = [tail[part * SUBLANES : (part + 1) * SUBLANES] for part in range(3)]
                logs.append(jnp.where(valid[index], parts[0] + parts[1] + parts[2], NEGATIVE))
            top = functools.reduce(jnp.maximum, logs)
            weights = [jnp.exp2(part - top) for part in logs]
            total = functools.reduce(jnp.add, weights)
            shares = [as_columns(weight / total) for weight in weights]
            for head in range(heads):
                cut = block_lanes(step * heads + head)
                mixed = [own_ref[:, cut]]
                for index, ref in enumerate(other_refs):
                    part = ref[step, head * rows : (head + 1) * rows, :].astype(jnp.float32)
                    mixed.append(jnp.where(valid[index], part, 0.0))
                terms = [part * share[:, head : head + 1] for part, share in zip(mixed, shares)]
                out_ref[:, cut] = functools.reduce(jnp.add, terms).astype(out_ref.dtype)
        store = pltpu.make_async_copy(
            out_ref, out_hbm.at[:, pl.ds(start, width)], sems.at[len(copies)]
        )
        store.start()
        store.wait()


def after(array, *others):
    return lax.optimization_barrier((array, *others))[0]


def attend(query, key, value, conv):
    rows, columns = query.shape
    devices = lax.axis_size("ctx")
    quads = devices // 4
    transfers = plan_moves(devices)
    step_width = HEADS_PER_STEP * HEAD_DIM
    chunks = len(CHUNK_STEPS)
    first_steps = [sum(CHUNK_STEPS[:chunk]) for chunk in range(chunks)]
    widths = [steps * step_width for steps in CHUNK_STEPS]
    starts = [step * step_width for step in first_steps]
    upper = [4 * quad + 2 + core for quad in range(quads - 1) for core in range(2)]
    gathers = [(who - 2, who) for who in upper]
    askers = sorted({source for pairs in transfers for source, _ in pairs})
    swap = [(index, index ^ 1) for index in range(devices)]

    query_swapped = lax.ppermute(query, "ctx", swap)
    key_swapped = lax.ppermute(key, "ctx", swap)
    value_swapped = lax.ppermute(value, "ctx", swap)

    def pack(members):
        hbm = pl.BlockSpec(memory_space=pl.ANY)
        shapes = [
            jax.ShapeDtypeStruct((2, rows, widths[chunk]), jnp.bfloat16) for chunk in members
        ]
        outs = pl.pallas_call(
            functools.partial(
                pack_kernel,
                [source for source, _ in gathers],
                askers,
                [widths[chunk] for chunk in members],
                [starts[chunk] for chunk in members],
            ),
            in_specs=[hbm] * 4,
            out_specs=[hbm] * (2 * len(members)),
            out_shape=shapes * 2,
            scratch_shapes=[
                pltpu.VMEM((rows, widths[chunk]), jnp.bfloat16)
                for chunk in members
                for _ in range(2)
            ]
            + [pltpu.SemaphoreType.DMA((2 * len(members),))] * 2,
            compiler_params=params(),
            cost_estimate=cost(1),
            name="att_pack",
        )(query, query_swapped, key, value)
        return list(zip(outs[: len(members)], outs[len(members) :]))

    packs = pack(list(range(chunks)))
    conv_first, conv_last = conv
    local_result, *conv_shared = conv_first(packs[0][1])
    asks, quad_kv, all_answers = [], [], []

    def send(chunk):
        key_pack, query_pack = packs[chunk]
        if chunk > 1:
            key_pack = after(key_pack, quad_kv[chunk - 2][0], all_answers[chunk - 2][0])
            query_pack = after(query_pack, *asks[chunk - 2], all_answers[chunk - 2][0])
        arrived = lax.ppermute(key_pack, "ctx", gathers)
        asks.append([lax.ppermute(query_pack, "ctx", pairs) for pairs in transfers])
        quad_kv.append([arrived])

    half_rows = HEADS_PER_STEP * rows + TAIL
    hbm = pl.BlockSpec(memory_space=pl.ANY)
    send(0)
    result = None
    returned = []
    for chunk in range(chunks):
        if chunk + 1 < chunks:
            send(chunk + 1)
        if chunk == 0:
            quad_kv[0] = [after(quad_kv[0][0], local_result)]
            asks[0] = [after(asked, local_result) for asked in asks[0]]
        quad_kv[chunk].append(lax.ppermute(quad_kv[chunk][0], "ctx", swap))
        steps, first = CHUNK_STEPS[chunk], first_steps[chunk]
        whole_spec = pl.BlockSpec((rows, step_width), lambda step, first=first: (0, first + step))
        chunk_spec = pl.BlockSpec((rows, step_width), lambda step: (0, step))
        pair_spec = pl.BlockSpec((2, rows, step_width), lambda step: (0, 0, step))
        lse_spec = pl.BlockSpec((SUBLANES, LANES), lambda step: (step, 0))
        answer_spec = pl.BlockSpec((2 * half_rows, LANES), lambda step: (step, 0))
        answer_shape = jax.ShapeDtypeStruct((2 * half_rows * steps, LANES), jnp.bfloat16)
        operands = [query, key, value, key_swapped, value_swapped, *quad_kv[chunk], *asks[chunk]]
        specs = [whole_spec] * 5 + [pair_spec] * (2 + len(transfers))
        aliases = {}
        if result is not None:
            aliases = {len(operands): 2 + len(transfers)}
            operands.append(result)
            specs.append(hbm)
        own, lse, *answers, result = pl.pallas_call(
            functools.partial(partial_kernel, transfers, upper, len(aliases)),
            grid=(steps,),
            in_specs=specs,
            out_specs=[chunk_spec, lse_spec] + [answer_spec] * len(transfers) + [whole_spec],
            out_shape=[
                jax.ShapeDtypeStruct((rows, widths[chunk]), jnp.float32),
                jax.ShapeDtypeStruct((SUBLANES * steps, LANES), jnp.float32),
            ]
            + [answer_shape] * len(transfers)
            + [jax.ShapeDtypeStruct((rows, columns), jnp.bfloat16)],
            input_output_aliases=aliases,
            compiler_params=params(),
            cost_estimate=cost(4),
            name="att_partial",
        )(*operands)
        all_answers.append(answers)
        parts = [own, lse]
        for answer, pairs in zip(answers, transfers):
            back = lax.ppermute(answer, "ctx", [(target, source) for source, target in pairs])
            parts += [back, lax.ppermute(back, "ctx", swap)]
        returned.append(parts)
    conv_shared = [after(part, all_answers[-1][0]) for part in conv_shared]
    for chunk, parts in enumerate(returned):
        steps = CHUNK_STEPS[chunk]
        count = 2 * len(transfers)
        result = pl.pallas_call(
            functools.partial(merge_kernel, transfers, steps, starts[chunk]),
            in_specs=[hbm] * (len(parts) + 1),
            out_specs=hbm,
            out_shape=jax.ShapeDtypeStruct((rows, columns), jnp.bfloat16),
            input_output_aliases={len(parts): 0},
            scratch_shapes=[
                pltpu.VMEM((rows, widths[chunk]), jnp.float32),
                pltpu.VMEM((SUBLANES * steps, LANES), jnp.float32),
            ]
            + [pltpu.VMEM((steps, half_rows, LANES), jnp.bfloat16)] * count
            + [
                pltpu.VMEM((rows, widths[chunk]), jnp.bfloat16),
                pltpu.SemaphoreType.DMA((3 + count * steps,)),
            ],
            compiler_params=params(),
            cost_estimate=cost(2),
            name="att_merge",
        )(*parts, result)
    return conv_last(local_result, *conv_shared), result


def local(
    hyena_q, hyena_k, hyena_v, short_filter, residue, decay_rate, att_query, att_key, att_value
):
    conv = convolution(hyena_q, hyena_k, hyena_v, short_filter, residue, decay_rate)
    return attend(att_query, att_key, att_value, conv)


def solution(mesh):
    rows = P(("dp", "ctx"), None)
    shared = P("ctx", None)
    return jax.shard_map(
        local,
        mesh=mesh,
        in_specs=(rows, rows, rows, P(), shared, shared, rows, rows, rows),
        out_specs=(rows, rows),
        check_vma=False,
    )
```

```python
import functools
import math

import jax
import jax.numpy as jnp
from jax import lax
from jax.experimental import pallas as pl
from jax.experimental.pallas import tpu as pltpu
from jax.sharding import PartitionSpec as P

HEAD_DIM = 128
LANES = 128
SUBLANES = 8
TAIL = 4 * SUBLANES
TAPS = 3
HEADS_PER_STEP = 4
CHUNK_STEPS = (2, 2, 2, 2)
LAG = 2
NEGATIVE = -1e30
EXP_SCALE = HEAD_DIM**-0.5 * math.log2(math.e)
VMEM_LIMIT = 255 * 1024 * 256


def params(**kwargs):
    return pltpu.CompilerParams(vmem_limit_bytes=VMEM_LIMIT, **kwargs)


def cost(microseconds):
    return pl.CostEstimate(
        flops=microseconds * 10**8, bytes_accessed=2**16, transcendentals=0
    )


def block_lanes(block):
    return slice(block * LANES, (block + 1) * LANES)


def conv_pack_kernel(rate_ref, residue_ref, q_ref, k_ref, v_ref, par_ref, rim_ref):
    modes = rate_ref.shape[0]
    for block in range(rate_ref.shape[1] // LANES):
        for which, ref in enumerate((rate_ref, residue_ref)):
            start = (2 * block + which) * modes
            for device in range(par_ref.shape[0]):
                par_ref[device, start : start + modes, :] = ref[:, block_lanes(block)]
    for feature, ref in enumerate((q_ref, k_ref, v_ref)):
        last = ref[...].astype(jnp.float32)[ref.shape[0] - 2 :]
        rim_ref[2 * feature : 2 * feature + 2, :] = last
    rim_ref[2 * TAPS :, :] = jnp.zeros((2, rim_ref.shape[1]), jnp.float32)


def rim_rows(rim_ref, feature, lanes):
    return [rim_ref[pl.ds(2 * feature + row, 1), lanes] for row in range(2)]


def short_mix(feature, rim, taps):
    two_before, one_before = rim
    row = lax.broadcasted_iota(jnp.int32, feature.shape, 0)
    one = jnp.where(row == 0, one_before, pltpu.roll(feature, 1, 0))
    two = jnp.where(row == 0, two_before, jnp.where(row == 1, one_before, pltpu.roll(feature, 2, 0)))
    return taps[0] * feature + taps[1] * one + taps[2] * two


def tap_rows(taps_ref, feature, lanes):
    return [taps_ref[feature, pl.ds(tap, 1), lanes] for tap in range(TAPS)]


def state_kernel(
    modes, k_ref, v_ref, rim_ref, par_ref, taps_ref, y_ref, s_ref, d_ref, p_scr, y_scr
):
    rows = k_ref.shape[0]
    for block in range(SUBLANES):
        lanes = block_lanes(block)
        mixes = [
            short_mix(
                ref[:, lanes].astype(jnp.float32),
                rim_rows(rim_ref, feature, lanes),
                tap_rows(taps_ref, feature, lanes),
            )
            for feature, ref in ((1, k_ref), (2, v_ref))
        ]
        product = (mixes[0] * mixes[1]).astype(jnp.bfloat16).astype(jnp.float32)
        p_scr[pl.ds(block, rows, SUBLANES), :] = product
    decay = [jnp.exp(-par_ref[pl.ds(mode, SUBLANES, 2 * modes), :]) for mode in range(modes)]
    residue = [par_ref[pl.ds(modes + mode, SUBLANES, 2 * modes), :] for mode in range(modes)]

    def body(position, states):
        here = pl.ds(pl.multiple_of(position * SUBLANES, SUBLANES), SUBLANES)
        product = p_scr[here, :]
        states = tuple(state * rate + product for state, rate in zip(states, decay))
        terms = [state * weight for state, weight in zip(states, residue)]
        while len(terms) > 1:
            terms = [left + right for left, right in zip(terms[::2], terms[1::2])]
        y_scr[here, :] = terms[0]
        return states

    zero = jnp.zeros((SUBLANES, LANES), jnp.float32)
    states = lax.fori_loop(0, rows, body, (zero,) * modes, unroll=4)
    for mode in range(modes):
        s_ref[pl.ds(mode, SUBLANES, modes), :] = states[mode]
    for block in range(SUBLANES):
        rate = par_ref[2 * block * modes : (2 * block + 1) * modes, :]
        d_ref[block * modes : (block + 1) * modes, :] = jnp.exp(-rate * rows)
    for block in range(SUBLANES):
        y_ref[:, block_lanes(block)] = y_scr[pl.ds(block, rows, SUBLANES), :]


def output_kernel(
    modes,
    q_ref,
    y_ref,
    rim_ref,
    par_ref,
    decay_ref,
    enter_ref,
    enter_first_ref,
    other_ref,
    taps_ref,
    out_ref,
):
    second = lax.axis_index("ctx") % 2 == 1
    rows = q_ref.shape[0]
    step = lax.broadcasted_iota(jnp.int32, (SUBLANES, LANES), 0).astype(jnp.float32) + 1.0

    def body(block, nothing):
        lanes = pl.ds(pl.multiple_of(block * LANES, LANES), LANES)
        rate = par_ref[pl.ds(pl.multiple_of(2 * block * modes, SUBLANES), modes), :]
        residue = par_ref[pl.ds(pl.multiple_of((2 * block + 1) * modes, SUBLANES), modes), :]
        here = pl.ds(pl.multiple_of(block * modes, SUBLANES), modes)
        after_first = decay_ref[here, :] * enter_ref[here, :] + other_ref[here, :]
        entering = jnp.where(second, after_first, enter_first_ref[here, :])
        weighted = residue * entering
        eight = jnp.exp(-rate * SUBLANES)
        terms = [
            weighted[mode : mode + 1] * jnp.exp(-rate[mode : mode + 1] * step)
            for mode in range(modes)
        ]
        eights = [jnp.broadcast_to(eight[mode : mode + 1], terms[0].shape) for mode in range(modes)]
        added = []
        for start in range(0, rows, SUBLANES):
            sums = list(terms)
            while len(sums) > 1:
                sums = [left + right for left, right in zip(sums[::2], sums[1::2])]
            added.append(sums[0])
            if start + SUBLANES < rows:
                terms = [term * decay for term, decay in zip(terms, eights)]
        smoothed = y_ref[:, lanes] + jnp.concatenate(added, 0)
        smoothed = smoothed.astype(jnp.bfloat16).astype(jnp.float32)
        mix = short_mix(
            q_ref[:, lanes].astype(jnp.float32),
            rim_rows(rim_ref, 0, lanes),
            tap_rows(taps_ref, 0, lanes),
        )
        out_ref[:, lanes] = (mix * smoothed).astype(out_ref.dtype)
        return nothing

    lax.fori_loop(0, SUBLANES, body, 0)


def convolution(hyena_q, hyena_k, hyena_v, short_filter, residue, decay_rate):
    rows, channels = hyena_q.shape
    devices = lax.axis_size("ctx")
    modes = residue.shape[1]
    own_blocks = residue.shape[0] // LANES
    blocks = channels // LANES
    groups = blocks // SUBLANES
    width = SUBLANES * LANES
    end = rows // 16 - 1
    par_rows = 2 * own_blocks * modes
    feature_spec = pl.BlockSpec((rows, width), lambda group: (0, group))
    rim_spec = pl.BlockSpec((8, width), lambda group: (0, group))
    par_spec = pl.BlockSpec((2 * SUBLANES * modes, LANES), lambda group: (group, 0))
    taps_spec = pl.BlockSpec((TAPS, TAPS, width), lambda group: (0, 0, group))
    positions = pltpu.VMEM((rows * SUBLANES, LANES), jnp.float32)

    def first_part(token):
        own_par, rim = pl.pallas_call(
            conv_pack_kernel,
            grid=(1,),
            in_specs=[pl.BlockSpec((modes, residue.shape[0]), lambda step: (0, 0))] * 2
            + [pl.BlockSpec((16, channels), lambda step: (end, 0))] * 3,
            out_specs=[
                pl.BlockSpec((devices, par_rows, LANES), lambda step: (0, 0, 0)),
                pl.BlockSpec((8, channels), lambda step: (0, 0)),
            ],
            out_shape=[
                jax.ShapeDtypeStruct((devices, par_rows, LANES), jnp.float32),
                jax.ShapeDtypeStruct((8, channels), jnp.float32),
            ],
            compiler_params=params(),
            cost_estimate=cost(1),
            name="conv_pack",
        )(decay_rate.T, residue.T, hyena_q, hyena_k, hyena_v)
        rim = lax.ppermute(rim, "ctx", [(index, index + 1) for index in range(devices - 1)])
        own_par = after(own_par, rim, token)
        par = lax.all_to_all(own_par, "ctx", split_axis=0, concat_axis=0, tiled=True)
        par = par.reshape(devices * par_rows, LANES)
        state_spec = pl.BlockSpec((SUBLANES * modes, LANES), lambda group: (group, 0))
        local_result, state, decay = pl.pallas_call(
            functools.partial(state_kernel, modes),
            grid=(groups,),
            in_specs=[feature_spec, feature_spec, rim_spec, par_spec, taps_spec],
            out_specs=[feature_spec, state_spec, state_spec],
            out_shape=[
                jax.ShapeDtypeStruct((rows, channels), jnp.float32),
                jax.ShapeDtypeStruct((blocks * modes, LANES), jnp.float32),
                jax.ShapeDtypeStruct((blocks * modes, LANES), jnp.float32),
            ],
            scratch_shapes=[positions, positions],
            compiler_params=params(),
            cost_estimate=cost(9),
            name="conv_state",
        )(hyena_k, hyena_v, rim, par, short_filter)
        return local_result, rim, par, decay, *entering_state(state, decay)

    def entering_state(state, decay):
        swap = [(index, index ^ 1) for index in range(devices)]
        other = lax.ppermute(state, "ctx", swap)
        total = state + decay * other
        entering = None
        reach = 1
        while 2 * reach < devices:
            moves = [(index, index + 2 * reach) for index in range(1, devices - 2 * reach, 2)]
            arrived = lax.ppermute(total, "ctx", moves)
            if reach == 1:
                entering = arrived
            else:
                entering = entering + decay ** (2 * (reach - 1)) * arrived
            if 4 * reach < devices:
                total = total + decay ** (2 * reach) * arrived
            reach *= 2
        return entering, lax.ppermute(entering, "ctx", swap), other

    def last_part(local_result, rim, par, decay, entering, entering_first, other):
        state_spec = pl.BlockSpec((SUBLANES * modes, LANES), lambda group: (group, 0))
        return pl.pallas_call(
            functools.partial(output_kernel, modes),
            grid=(groups,),
            in_specs=[feature_spec, feature_spec, rim_spec, par_spec]
            + [state_spec] * 4
            + [taps_spec],
            out_specs=feature_spec,
            out_shape=jax.ShapeDtypeStruct((rows, channels), jnp.bfloat16),
            compiler_params=params(),
            cost_estimate=cost(6),
            name="conv_output",
        )(
            hyena_q,
            local_result,
            rim,
            par,
            decay,
            entering,
            entering_first,
            other,
            short_filter,
        )

    return first_part, last_part


def among(me, members):
    return functools.reduce(jnp.logical_or, [me == member for member in members])


def plan_moves(devices):
    quads = devices // 4
    transfers = [[(devices - 1, devices - 3)]]
    for distance in range(1, quads):
        if distance > len(transfers):
            transfers.append([])
        for quad in range(distance, quads):
            target = 4 * (quad - distance) + 2
            transfers[distance - 1] += [(4 * quad, target), (4 * quad + 2, target + 1)]
    return transfers


def soft(query, keys, values, mask=None):
    scores = lax.dot_general(
        query, keys, (((1,), (1,)), ((), ())), preferred_element_type=jnp.float32
    )
    if mask is not None:
        scores = jnp.where(mask, scores, NEGATIVE)
    top = jnp.max(scores, axis=1, keepdims=True) * EXP_SCALE
    expo = jnp.exp2(scores * EXP_SCALE - top).astype(jnp.bfloat16)
    mixed = jnp.dot(expo, values, preferred_element_type=jnp.float32)
    total = mixed[:, HEAD_DIM:]
    return mixed[:, :HEAD_DIM] / total, top + jnp.log2(total)


def pack_kernel(gathers, askers, asked, widths, starts, q_ref, qs_ref, k_ref, v_ref, *rest):
    count = len(widths)
    key_outs, query_outs = rest[:count], rest[count : count + asked]
    stages, in_sems, out_sems = rest[count + asked : -2], rest[-2], rest[-1]
    me = lax.axis_index("ctx")
    odd = me % 2

    def run(pairs):
        loads = [
            pltpu.make_async_copy(source, stage, in_sems.at[index])
            for index, ((source, _), stage) in enumerate(zip(pairs, stages))
        ]
        stores = [
            pltpu.make_async_copy(stage, target, out_sems.at[index])
            for index, ((_, target), stage) in enumerate(zip(pairs, stages))
        ]
        for load in loads:
            load.start()
        for load, store in zip(loads, stores):
            load.wait()
            store.start()
        for store in stores:
            store.wait()

    def cut(ref, chunk):
        return ref.at[:, pl.ds(starts[chunk], widths[chunk])]

    if gathers:

        @pl.when(among(me, gathers))
        def _():
            run(
                [
                    (cut(ref, chunk), key_outs[chunk].at[which])
                    for chunk in range(count)
                    for which, ref in enumerate((k_ref, v_ref))
                ]
            )

    @pl.when(among(me, askers))
    def _():
        run(
            [
                (cut(ref, chunk), query_outs[chunk].at[half])
                for chunk in range(asked)
                for ref, half in ((q_ref, odd), (qs_ref, 1 - odd))
            ]
        )


def as_rows(columns):
    lanes = lax.broadcasted_iota(jnp.int32, columns[0].shape, 1)
    sums = jnp.zeros_like(columns[0])
    for index, column in enumerate(columns):
        sums = jnp.where(lanes == index, column, sums)
    return jnp.transpose(sums)[:SUBLANES]


def as_columns(part):
    fill = jnp.zeros((LANES - part.shape[0], part.shape[1]), jnp.float32)
    return jnp.transpose(jnp.concatenate([part, fill], 0))


def partial_kernel(transfers, upper, natural, asking, onto, *refs):
    count = len(transfers)
    out_ref = refs[-1]
    if asking:
        next_refs = refs[7 + count : 9 + count]
        refs = refs[: 7 + count] + refs[9 + count :]
    q_ref, k_ref, v_ref, kp_ref, vp_ref, g_ref, gp_ref = refs[:7]
    ask_refs = refs[7 : 7 + count]
    own_ref, lse_ref = refs[7 + count + onto : 9 + count + onto]
    answer_refs = refs[9 + count + onto : -1]
    me = lax.axis_index("ctx")
    rows = q_ref.shape[0]
    heads = q_ref.shape[1] // HEAD_DIM
    half_rows = heads * rows + TAIL

    def key_value(head, with_quad):
        cut = block_lanes(head)
        keys = [kp_ref[:, cut], k_ref[:, cut]]
        values = [vp_ref[:, cut], v_ref[:, cut]]
        if with_quad:
            keys = [g_ref[0, :, cut], gp_ref[0, :, cut]] + keys
            values = [g_ref[1, :, cut], gp_ref[1, :, cut]] + values
        values = jnp.concatenate(values, 0)
        return jnp.concatenate(keys, 0), jnp.concatenate([values, jnp.ones_like(values)], 1)

    def run(with_quad):
        key_count = rows * (4 if with_quad else 2)
        row = lax.broadcasted_iota(jnp.int32, (rows, key_count), 0)
        column = lax.broadcasted_iota(jnp.int32, (rows, key_count), 1)
        column = column - (key_count - 2 * rows)
        partner_limit = jnp.where(me % 2 == 1, rows, 0)
        mask = (column < partner_limit) | ((column >= rows) & (column - rows <= row))
        sums = []
        for head in range(heads):
            keys, values = key_value(head, with_quad)
            mixed, lse = soft(q_ref[:, block_lanes(head)], keys, values, mask)
            own_ref[:, block_lanes(head)] = mixed
            out_ref[:, block_lanes(head)] = mixed.astype(out_ref.dtype)
            sums.append(lse)
        lse_ref[...] = as_rows(sums)

        def answer(index):
            sums = [[], []]
            for head in range(heads):
                keys, values = key_value(head, with_quad)
                if natural:
                    query = ask_refs[index][:, :, block_lanes(head)].reshape(2 * rows, HEAD_DIM)
                else:
                    halves = [half * half_rows + head * rows for half in range(2)]
                    query = jnp.concatenate(
                        [ask_refs[index][start : start + rows, :] for start in halves], 0
                    )
                mixed, lse = soft(query, keys, values)
                for half in range(2):
                    cut = slice(half * rows, (half + 1) * rows)
                    start = half * half_rows + head * rows
                    answer_refs[index][start : start + rows, :] = mixed[cut].astype(jnp.bfloat16)
                    sums[half].append(lse[cut])
            for half in range(2):
                start = half * half_rows + heads * rows
                lse = as_rows(sums[half])
                first = lse.astype(jnp.bfloat16).astype(jnp.float32)
                second = (lse - first).astype(jnp.bfloat16).astype(jnp.float32)
                third = lse - first - second
                tail = jnp.concatenate([first, second, third, jnp.zeros_like(lse)], 0)
                answer_refs[index][start : start + TAIL, :] = tail.astype(jnp.bfloat16)

        for index, pairs in enumerate(transfers):
            asked = [target for _, target in pairs if (target in upper) == with_quad]
            if asked:
                pl.when(among(me, asked))(functools.partial(answer, index))

    if upper:
        pl.when(among(me, upper))(functools.partial(run, True))
        pl.when(jnp.logical_not(among(me, upper)))(functools.partial(run, False))
    else:
        run(False)

    if asking:
        for index, pairs in enumerate(transfers):

            @pl.when(among(me, [source for source, _ in pairs]))
            def _():
                for ref, half in zip(next_refs, (me % 2, 1 - me % 2)):
                    for head in range(heads):
                        start = pl.multiple_of(half * half_rows + head * rows, TAIL)
                        answer_refs[index][pl.ds(start, rows), :] = ref[:, block_lanes(head)]


def merge_kernel(transfers, steps, start, own_hbm, lse_hbm, *refs):
    count = 2 * len(transfers)
    others_hbm, out_hbm = refs[:count], refs[count + 1]
    own_ref, lse_ref, *other_refs = refs[count + 2 : 2 * count + 4]
    out_ref, sems = refs[-2:]
    me = lax.axis_index("ctx")
    odd = me % 2
    rows, width = own_ref.shape
    heads = HEADS_PER_STEP
    half_rows = heads * rows + TAIL
    returned = []
    for pairs in transfers:
        members = [source for source, _ in pairs]
        returned += [members, [member ^ 1 for member in members]]

    @pl.when(among(me, sorted(set(sum(returned, [])))))
    def _():
        loads = [(own_hbm, own_ref), (lse_hbm, lse_ref)]
        for hbm, ref in zip(others_hbm, other_refs):
            for step in range(steps):
                half = pl.ds(pl.multiple_of((2 * step + odd) * half_rows, TAIL), half_rows)
                loads.append((hbm.at[half, :], ref.at[step]))
        copies = [
            pltpu.make_async_copy(source, target, sems.at[index])
            for index, (source, target) in enumerate(loads)
        ]
        for copy in copies:
            copy.start()
        for copy in copies:
            copy.wait()
        valid = [among(me, members) for members in returned]
        for step in range(steps):
            logs = [lse_ref[step * SUBLANES : (step + 1) * SUBLANES, :]]
            for index, ref in enumerate(other_refs):
                tail = ref[step, heads * rows :, :].astype(jnp.float32)
                parts = [tail[part * SUBLANES : (part + 1) * SUBLANES] for part in range(3)]
                logs.append(jnp.where(valid[index], parts[0] + parts[1] + parts[2], NEGATIVE))
            top = functools.reduce(jnp.maximum, logs)
            weights = [jnp.exp2(part - top) for part in logs]
            total = functools.reduce(jnp.add, weights)
            shares = [as_columns(weight / total) for weight in weights]
            for head in range(heads):
                cut = block_lanes(step * heads + head)
                mixed = [own_ref[:, cut]]
                for index, ref in enumerate(other_refs):
                    part = ref[step, head * rows : (head + 1) * rows, :].astype(jnp.float32)
                    mixed.append(jnp.where(valid[index], part, 0.0))
                terms = [part * share[:, head : head + 1] for part, share in zip(mixed, shares)]
                out_ref[:, cut] = functools.reduce(jnp.add, terms).astype(out_ref.dtype)
        store = pltpu.make_async_copy(
            out_ref, out_hbm.at[:, pl.ds(start, width)], sems.at[len(copies)]
        )
        store.start()
        store.wait()


def after(array, *others):
    return lax.optimization_barrier((array, *others))[0]


def attend(query, key, value, conv):
    rows, columns = query.shape
    devices = lax.axis_size("ctx")
    quads = devices // 4
    transfers = plan_moves(devices)
    step_width = HEADS_PER_STEP * HEAD_DIM
    chunks = len(CHUNK_STEPS)
    first_steps = [sum(CHUNK_STEPS[:chunk]) for chunk in range(chunks)]
    widths = [steps * step_width for steps in CHUNK_STEPS]
    starts = [step * step_width for step in first_steps]
    upper = [4 * quad + 2 + core for quad in range(quads - 1) for core in range(2)]
    gathers = [(who - 2, who) for who in upper]
    askers = sorted({source for pairs in transfers for source, _ in pairs})
    swap = [(index, index ^ 1) for index in range(devices)]

    query_swapped = lax.ppermute(query, "ctx", swap)
    key_swapped = lax.ppermute(key, "ctx", swap)
    value_swapped = lax.ppermute(value, "ctx", swap)

    both_ways = chunks > LAG and all(
        not {source for source, _ in pairs} & {target for _, target in pairs}
        for pairs in transfers
    )
    asked = LAG if both_ways else chunks

    def pack():
        hbm = pl.BlockSpec(memory_space=pl.ANY)
        shapes = [jax.ShapeDtypeStruct((2, rows, width), jnp.bfloat16) for width in widths]
        outs = pl.pallas_call(
            functools.partial(
                pack_kernel,
                [source for source, _ in gathers],
                askers,
                asked,
                widths,
                starts,
            ),
            in_specs=[hbm] * 4,
            out_specs=[hbm] * (chunks + asked),
            out_shape=shapes + shapes[:asked],
            scratch_shapes=[
                pltpu.VMEM((rows, width), jnp.bfloat16) for width in widths for _ in range(2)
            ]
            + [pltpu.SemaphoreType.DMA((2 * chunks,))] * 2,
            compiler_params=params(),
            cost_estimate=cost(1),
            name="att_pack",
        )(query, query_swapped, key, value)
        return outs[:chunks], outs[chunks:]

    key_packs, query_packs = pack()
    conv_first, conv_last = conv
    local_result, *conv_shared = conv_first(query_packs[0])
    asks, quad_kv, all_answers = {}, [], []

    def send(chunk):
        key_pack = key_packs[chunk]
        if chunk >= LAG:
            key_pack = after(key_pack, quad_kv[chunk - LAG][0], all_answers[chunk - LAG][0])
        quad_kv.append([lax.ppermute(key_pack, "ctx", gathers)])
        if chunk < asked:
            query_pack = query_packs[chunk]
            if chunk >= LAG:
                query_pack = after(query_pack, *asks[chunk - LAG], all_answers[chunk - LAG][0])
            asks[chunk] = [lax.ppermute(query_pack, "ctx", pairs) for pairs in transfers]

    half_rows = HEADS_PER_STEP * rows + TAIL
    hbm = pl.BlockSpec(memory_space=pl.ANY)
    for chunk in range(min(LAG, chunks)):
        send(chunk)
    result = None
    returned = []
    for chunk in range(chunks):
        if chunk == 0:
            quad_kv[0] = [after(quad_kv[0][0], local_result)]
            asks[0] = [after(asked, local_result) for asked in asks[0]]
        quad_kv[chunk].append(lax.ppermute(quad_kv[chunk][0], "ctx", swap))
        steps, first = CHUNK_STEPS[chunk], first_steps[chunk]
        whole_spec = pl.BlockSpec((rows, step_width), lambda step, first=first: (0, first + step))
        chunk_spec = pl.BlockSpec((rows, step_width), lambda step: (0, step))
        pair_spec = pl.BlockSpec((2, rows, step_width), lambda step: (0, 0, step))
        lse_spec = pl.BlockSpec((SUBLANES, LANES), lambda step: (step, 0))
        answer_spec = pl.BlockSpec((2 * half_rows, LANES), lambda step: (step, 0))
        answer_shape = jax.ShapeDtypeStruct((2 * half_rows * steps, LANES), jnp.bfloat16)
        asking = both_ways and chunk + LAG < chunks
        natural = chunk < asked
        operands = [query, key, value, key_swapped, value_swapped, *quad_kv[chunk], *asks[chunk]]
        specs = [whole_spec] * 5 + [pair_spec] * 2
        specs += [pair_spec if natural else answer_spec] * len(transfers)
        if asking:
            later = first_steps[chunk + LAG]
            operands += [query, query_swapped]
            specs += [
                pl.BlockSpec((rows, step_width), lambda step, later=later: (0, later + step))
            ] * 2
        aliases = {}
        if result is not None:
            aliases = {len(operands): 2 + len(transfers)}
            operands.append(result)
            specs.append(hbm)
        own, lse, *answers, result = pl.pallas_call(
            functools.partial(partial_kernel, transfers, upper, natural, asking, len(aliases)),
            grid=(steps,),
            in_specs=specs,
            out_specs=[chunk_spec, lse_spec] + [answer_spec] * len(transfers) + [whole_spec],
            out_shape=[
                jax.ShapeDtypeStruct((rows, widths[chunk]), jnp.float32),
                jax.ShapeDtypeStruct((SUBLANES * steps, LANES), jnp.float32),
            ]
            + [answer_shape] * len(transfers)
            + [jax.ShapeDtypeStruct((rows, columns), jnp.bfloat16)],
            input_output_aliases=aliases,
            compiler_params=params(),
            cost_estimate=cost(4),
            name="att_partial",
        )(*operands)
        all_answers.append(answers)
        parts = [own, lse]
        arrivals = []
        for answer, pairs in zip(answers, transfers):
            moves = [(target, source) for source, target in pairs]
            if asking:
                moves += pairs
            arrivals.append(lax.ppermute(answer, "ctx", moves))
        if asking:
            asks[chunk + LAG] = arrivals
        returned.append([own, lse, arrivals])
        if chunk + LAG < chunks:
            send(chunk + LAG)
    conv_shared = [after(part, all_answers[-1][0]) for part in conv_shared]
    hyena_out = conv_last(local_result, *conv_shared)
    for chunk, (own, lse, arrivals) in enumerate(returned):
        parts = [own, lse]
        for arrival in arrivals:
            if chunk == chunks - 1:
                arrival = after(arrival, hyena_out, result)
            parts += [arrival, lax.ppermute(arrival, "ctx", swap)]
        steps = CHUNK_STEPS[chunk]
        count = 2 * len(transfers)
        result = pl.pallas_call(
            functools.partial(merge_kernel, transfers, steps, starts[chunk]),
            in_specs=[hbm] * (len(parts) + 1),
            out_specs=hbm,
            out_shape=jax.ShapeDtypeStruct((rows, columns), jnp.bfloat16),
            input_output_aliases={len(parts): 0},
            scratch_shapes=[
                pltpu.VMEM((rows, widths[chunk]), jnp.float32),
                pltpu.VMEM((SUBLANES * steps, LANES), jnp.float32),
            ]
            + [pltpu.VMEM((steps, half_rows, LANES), jnp.bfloat16)] * count
            + [
                pltpu.VMEM((rows, widths[chunk]), jnp.bfloat16),
                pltpu.SemaphoreType.DMA((3 + count * steps,)),
            ],
            compiler_params=params(),
            cost_estimate=cost(2),
            name="att_merge",
        )(*parts, result)
    return hyena_out, result


def local(
    hyena_q, hyena_k, hyena_v, short_filter, residue, decay_rate, att_query, att_key, att_value
):
    conv = convolution(hyena_q, hyena_k, hyena_v, short_filter, residue, decay_rate)
    return attend(att_query, att_key, att_value, conv)


def solution(mesh):
    rows = P(("dp", "ctx"), None)
    shared = P("ctx", None)
    return jax.shard_map(
        local,
        mesh=mesh,
        in_specs=(rows, rows, rows, P(), shared, shared, rows, rows, rows),
        out_specs=(rows, rows),
        check_vma=False,
    )
```

```python
import functools
import math

import jax
import jax.numpy as jnp
from jax import lax
from jax.experimental import pallas as pl
from jax.experimental.pallas import tpu as pltpu
from jax.sharding import PartitionSpec as P

HEAD_DIM = 128
LANES = 128
SUBLANES = 8
TAIL = 4 * SUBLANES
TAPS = 3
HEADS_PER_STEP = 4
CHUNK_STEPS = (2, 2, 2, 2)
LAG = 2
NEGATIVE = -1e30
EXP_SCALE = HEAD_DIM**-0.5 * math.log2(math.e)
VMEM_LIMIT = 255 * 1024 * 256


def params(**kwargs):
    return pltpu.CompilerParams(vmem_limit_bytes=VMEM_LIMIT, **kwargs)


def cost(microseconds):
    return pl.CostEstimate(
        flops=microseconds * 10**9, bytes_accessed=2**20, transcendentals=0
    )


def block_lanes(block):
    return slice(block * LANES, (block + 1) * LANES)


def conv_pack_kernel(rate_ref, residue_ref, q_ref, k_ref, v_ref, par_ref, rim_ref):
    modes = rate_ref.shape[0]
    for block in range(rate_ref.shape[1] // LANES):
        for which, ref in enumerate((rate_ref, residue_ref)):
            start = (2 * block + which) * modes
            for device in range(par_ref.shape[0]):
                par_ref[device, start : start + modes, :] = ref[:, block_lanes(block)]
    for feature, ref in enumerate((q_ref, k_ref, v_ref)):
        last = ref[...].astype(jnp.float32)[ref.shape[0] - 2 :]
        rim_ref[2 * feature : 2 * feature + 2, :] = last
    rim_ref[2 * TAPS :, :] = jnp.zeros((2, rim_ref.shape[1]), jnp.float32)


def rim_rows(rim_ref, feature, lanes):
    return [rim_ref[pl.ds(2 * feature + row, 1), lanes] for row in range(2)]


def short_mix(feature, rim, taps):
    two_before, one_before = rim
    row = lax.broadcasted_iota(jnp.int32, feature.shape, 0)
    one = jnp.where(row == 0, one_before, pltpu.roll(feature, 1, 0))
    two = jnp.where(row == 0, two_before, jnp.where(row == 1, one_before, pltpu.roll(feature, 2, 0)))
    return taps[0] * feature + taps[1] * one + taps[2] * two


def tap_rows(taps_ref, feature, lanes):
    return [taps_ref[feature, pl.ds(tap, 1), lanes] for tap in range(TAPS)]


def state_kernel(
    modes, k_ref, v_ref, rim_ref, par_ref, taps_ref, y_ref, s_ref, d_ref, p_scr, y_scr
):
    rows = k_ref.shape[0]
    for block in range(SUBLANES):
        lanes = block_lanes(block)
        mixes = [
            short_mix(
                ref[:, lanes].astype(jnp.float32),
                rim_rows(rim_ref, feature, lanes),
                tap_rows(taps_ref, feature, lanes),
            )
            for feature, ref in ((1, k_ref), (2, v_ref))
        ]
        product = (mixes[0] * mixes[1]).astype(jnp.bfloat16).astype(jnp.float32)
        p_scr[pl.ds(block, rows, SUBLANES), :] = product
    decay = [jnp.exp(-par_ref[pl.ds(mode, SUBLANES, 2 * modes), :]) for mode in range(modes)]
    residue = [par_ref[pl.ds(modes + mode, SUBLANES, 2 * modes), :] for mode in range(modes)]

    def body(position, states):
        here = pl.ds(pl.multiple_of(position * SUBLANES, SUBLANES), SUBLANES)
        product = p_scr[here, :]
        states = tuple(state * rate + product for state, rate in zip(states, decay))
        terms = [state * weight for state, weight in zip(states, residue)]
        while len(terms) > 1:
            terms = [left + right for left, right in zip(terms[::2], terms[1::2])]
        y_scr[here, :] = terms[0]
        return states

    zero = jnp.zeros((SUBLANES, LANES), jnp.float32)
    states = lax.fori_loop(0, rows, body, (zero,) * modes, unroll=4)
    for mode in range(modes):
        s_ref[pl.ds(mode, SUBLANES, modes), :] = states[mode]
    for block in range(SUBLANES):
        rate = par_ref[2 * block * modes : (2 * block + 1) * modes, :]
        d_ref[block * modes : (block + 1) * modes, :] = jnp.exp(-rate * rows)
    for block in range(SUBLANES):
        y_ref[:, block_lanes(block)] = y_scr[pl.ds(block, rows, SUBLANES), :]


def output_kernel(
    modes,
    q_ref,
    y_ref,
    rim_ref,
    par_ref,
    decay_ref,
    enter_ref,
    enter_first_ref,
    other_ref,
    taps_ref,
    out_ref,
):
    second = lax.axis_index("ctx") % 2 == 1
    rows = q_ref.shape[0]
    step = lax.broadcasted_iota(jnp.int32, (SUBLANES, LANES), 0).astype(jnp.float32) + 1.0

    def body(block, nothing):
        lanes = pl.ds(pl.multiple_of(block * LANES, LANES), LANES)
        rate = par_ref[pl.ds(pl.multiple_of(2 * block * modes, SUBLANES), modes), :]
        residue = par_ref[pl.ds(pl.multiple_of((2 * block + 1) * modes, SUBLANES), modes), :]
        here = pl.ds(pl.multiple_of(block * modes, SUBLANES), modes)
        after_first = decay_ref[here, :] * enter_ref[here, :] + other_ref[here, :]
        entering = jnp.where(second, after_first, enter_first_ref[here, :])
        weighted = residue * entering
        eight = jnp.exp(-rate * SUBLANES)
        terms = [
            weighted[mode : mode + 1] * jnp.exp(-rate[mode : mode + 1] * step)
            for mode in range(modes)
        ]
        eights = [jnp.broadcast_to(eight[mode : mode + 1], terms[0].shape) for mode in range(modes)]
        added = []
        for start in range(0, rows, SUBLANES):
            sums = list(terms)
            while len(sums) > 1:
                sums = [left + right for left, right in zip(sums[::2], sums[1::2])]
            added.append(sums[0])
            if start + SUBLANES < rows:
                terms = [term * decay for term, decay in zip(terms, eights)]
        smoothed = y_ref[:, lanes] + jnp.concatenate(added, 0)
        smoothed = smoothed.astype(jnp.bfloat16).astype(jnp.float32)
        mix = short_mix(
            q_ref[:, lanes].astype(jnp.float32),
            rim_rows(rim_ref, 0, lanes),
            tap_rows(taps_ref, 0, lanes),
        )
        out_ref[:, lanes] = (mix * smoothed).astype(out_ref.dtype)
        return nothing

    lax.fori_loop(0, SUBLANES, body, 0)


def convolution(hyena_q, hyena_k, hyena_v, short_filter, residue, decay_rate):
    rows, channels = hyena_q.shape
    devices = lax.axis_size("ctx")
    modes = residue.shape[1]
    own_blocks = residue.shape[0] // LANES
    blocks = channels // LANES
    groups = blocks // SUBLANES
    width = SUBLANES * LANES
    end = rows // 16 - 1
    par_rows = 2 * own_blocks * modes
    feature_spec = pl.BlockSpec((rows, width), lambda group: (0, group))
    rim_spec = pl.BlockSpec((8, width), lambda group: (0, group))
    par_spec = pl.BlockSpec((2 * SUBLANES * modes, LANES), lambda group: (group, 0))
    taps_spec = pl.BlockSpec((TAPS, TAPS, width), lambda group: (0, 0, group))
    positions = pltpu.VMEM((rows * SUBLANES, LANES), jnp.float32)

    def first_part(token, state_token):
        own_par, rim = pl.pallas_call(
            conv_pack_kernel,
            grid=(1,),
            in_specs=[pl.BlockSpec((modes, residue.shape[0]), lambda step: (0, 0))] * 2
            + [pl.BlockSpec((16, channels), lambda step: (end, 0))] * 3,
            out_specs=[
                pl.BlockSpec((devices, par_rows, LANES), lambda step: (0, 0, 0)),
                pl.BlockSpec((8, channels), lambda step: (0, 0)),
            ],
            out_shape=[
                jax.ShapeDtypeStruct((devices, par_rows, LANES), jnp.float32),
                jax.ShapeDtypeStruct((8, channels), jnp.float32),
            ],
            compiler_params=params(),
            cost_estimate=cost(1),
            name="conv_pack",
        )(decay_rate.T, residue.T, hyena_q, hyena_k, hyena_v)
        rim = after(rim, token)
        rim = lax.ppermute(rim, "ctx", [(index, index + 1) for index in range(devices - 1)])
        own_par = after(own_par, rim)
        par = lax.all_to_all(own_par, "ctx", split_axis=0, concat_axis=0, tiled=True)
        par = par.reshape(devices * par_rows, LANES)
        state_spec = pl.BlockSpec((SUBLANES * modes, LANES), lambda group: (group, 0))
        local_result, state, decay = pl.pallas_call(
            functools.partial(state_kernel, modes),
            grid=(groups,),
            in_specs=[feature_spec, feature_spec, rim_spec, par_spec, taps_spec],
            out_specs=[feature_spec, state_spec, state_spec],
            out_shape=[
                jax.ShapeDtypeStruct((rows, channels), jnp.float32),
                jax.ShapeDtypeStruct((blocks * modes, LANES), jnp.float32),
                jax.ShapeDtypeStruct((blocks * modes, LANES), jnp.float32),
            ],
            scratch_shapes=[positions, positions],
            compiler_params=params(),
            cost_estimate=cost(9),
            name="conv_state",
        )(hyena_k, hyena_v, after(rim, state_token), par, short_filter)
        return local_result, rim, par, decay, *entering_state(state, decay)

    def entering_state(state, decay):
        swap = [(index, index ^ 1) for index in range(devices)]
        other = lax.ppermute(state, "ctx", swap)
        total = state + decay * other
        entering = None
        reach = 1
        while 2 * reach < devices:
            moves = [(index, index + 2 * reach) for index in range(1, devices - 2 * reach, 2)]
            arrived = lax.ppermute(total, "ctx", moves)
            if reach == 1:
                entering = arrived
            else:
                entering = entering + decay ** (2 * (reach - 1)) * arrived
            if 4 * reach < devices:
                total = total + decay ** (2 * reach) * arrived
            reach *= 2
        return entering, lax.ppermute(entering, "ctx", swap), other

    def last_part(local_result, rim, par, decay, entering, entering_first, other):
        state_spec = pl.BlockSpec((SUBLANES * modes, LANES), lambda group: (group, 0))
        return pl.pallas_call(
            functools.partial(output_kernel, modes),
            grid=(groups,),
            in_specs=[feature_spec, feature_spec, rim_spec, par_spec]
            + [state_spec] * 4
            + [taps_spec],
            out_specs=feature_spec,
            out_shape=jax.ShapeDtypeStruct((rows, channels), jnp.bfloat16),
            compiler_params=params(),
            cost_estimate=cost(6),
            name="conv_output",
        )(
            hyena_q,
            local_result,
            rim,
            par,
            decay,
            entering,
            entering_first,
            other,
            short_filter,
        )

    return first_part, last_part


def among(me, members):
    return functools.reduce(jnp.logical_or, [me == member for member in members])


def plan_moves(devices):
    quads = devices // 4
    transfers = [[(devices - 1, devices - 3)]]
    for distance in range(1, quads):
        if distance > len(transfers):
            transfers.append([])
        for quad in range(distance, quads):
            target = 4 * (quad - distance) + 2
            transfers[distance - 1] += [(4 * quad, target), (4 * quad + 2, target + 1)]
    return transfers


def soft(query, keys, values, mask=None):
    scores = lax.dot_general(
        query, keys, (((1,), (1,)), ((), ())), preferred_element_type=jnp.float32
    )
    if mask is not None:
        scores = jnp.where(mask, scores, NEGATIVE)
    top = jnp.max(scores, axis=1, keepdims=True) * EXP_SCALE
    expo = jnp.exp2(scores * EXP_SCALE - top).astype(jnp.bfloat16)
    mixed = jnp.dot(expo, values, preferred_element_type=jnp.float32)
    total = mixed[:, HEAD_DIM:]
    return mixed[:, :HEAD_DIM] / total, top + jnp.log2(total)


def pack_kernel(gathers, askers, key_cuts, query_cuts, q_ref, qs_ref, k_ref, v_ref, *rest):
    count = len(key_cuts)
    total = count + len(query_cuts)
    key_outs, query_outs = rest[:count], rest[count:total]
    key_stages, query_stages = rest[total : total + 2 * count], rest[total + 2 * count : -2]
    in_sems, out_sems = rest[-2:]
    me = lax.axis_index("ctx")
    odd = me % 2

    def run(pairs, stages):
        loads = [
            pltpu.make_async_copy(source, stage, in_sems.at[index])
            for index, ((source, _), stage) in enumerate(zip(pairs, stages))
        ]
        stores = [
            pltpu.make_async_copy(stage, target, out_sems.at[index])
            for index, ((_, target), stage) in enumerate(zip(pairs, stages))
        ]
        for load in loads:
            load.start()
        for load, store in zip(loads, stores):
            load.wait()
            store.start()
        for store in stores:
            store.wait()

    def cut(ref, columns):
        return ref.at[:, pl.ds(*columns)]

    if gathers:

        @pl.when(among(me, gathers))
        def _():
            pairs = [
                (cut(ref, columns), out.at[which])
                for columns, out in zip(key_cuts, key_outs)
                for which, ref in enumerate((k_ref, v_ref))
            ]
            run(pairs, key_stages)

    @pl.when(among(me, askers))
    def _():
        pairs = [
            (cut(ref, columns), out.at[half])
            for columns, out in zip(query_cuts, query_outs)
            for ref, half in ((q_ref, odd), (qs_ref, 1 - odd))
        ]
        run(pairs, query_stages)


def as_rows(columns):
    lanes = lax.broadcasted_iota(jnp.int32, columns[0].shape, 1)
    sums = jnp.zeros_like(columns[0])
    for index, column in enumerate(columns):
        sums = jnp.where(lanes == index, column, sums)
    return jnp.transpose(sums)[:SUBLANES]


def as_columns(part):
    fill = jnp.zeros((LANES - part.shape[0], part.shape[1]), jnp.float32)
    return jnp.transpose(jnp.concatenate([part, fill], 0))


def partial_kernel(transfers, upper, natural, asking, onto, *refs):
    count = len(transfers)
    out_ref = refs[-1]
    if asking:
        next_refs = refs[7 + count : 9 + count]
        refs = refs[: 7 + count] + refs[9 + count :]
    q_ref, k_ref, v_ref, kp_ref, vp_ref, g_ref, gp_ref = refs[:7]
    ask_refs = refs[7 : 7 + count]
    own_ref, lse_ref = refs[7 + count + onto : 9 + count + onto]
    answer_refs = refs[9 + count + onto : -1]
    me = lax.axis_index("ctx")
    rows = q_ref.shape[0]
    heads = q_ref.shape[1] // HEAD_DIM
    half_rows = heads * rows + TAIL

    def key_value(head, with_quad):
        cut = block_lanes(head)
        keys = [kp_ref[:, cut], k_ref[:, cut]]
        values = [vp_ref[:, cut], v_ref[:, cut]]
        if with_quad:
            keys = [g_ref[0, :, cut], gp_ref[0, :, cut]] + keys
            values = [g_ref[1, :, cut], gp_ref[1, :, cut]] + values
        values = jnp.concatenate(values, 0)
        return jnp.concatenate(keys, 0), jnp.concatenate([values, jnp.ones_like(values)], 1)

    def run(with_quad):
        key_count = rows * (4 if with_quad else 2)
        row = lax.broadcasted_iota(jnp.int32, (rows, key_count), 0)
        column = lax.broadcasted_iota(jnp.int32, (rows, key_count), 1)
        column = column - (key_count - 2 * rows)
        partner_limit = jnp.where(me % 2 == 1, rows, 0)
        mask = (column < partner_limit) | ((column >= rows) & (column - rows <= row))
        sums = []
        for head in range(heads):
            keys, values = key_value(head, with_quad)
            mixed, lse = soft(q_ref[:, block_lanes(head)], keys, values, mask)
            own_ref[:, block_lanes(head)] = mixed
            out_ref[:, block_lanes(head)] = mixed.astype(out_ref.dtype)
            sums.append(lse)
        lse_ref[...] = as_rows(sums)

        def answer(index):
            sums = [[], []]
            for head in range(heads):
                keys, values = key_value(head, with_quad)
                if natural:
                    query = ask_refs[index][:, :, block_lanes(head)].reshape(2 * rows, HEAD_DIM)
                else:
                    halves = [half * half_rows + head * rows for half in range(2)]
                    query = jnp.concatenate(
                        [ask_refs[index][start : start + rows, :] for start in halves], 0
                    )
                mixed, lse = soft(query, keys, values)
                for half in range(2):
                    cut = slice(half * rows, (half + 1) * rows)
                    start = half * half_rows + head * rows
                    answer_refs[index][start : start + rows, :] = mixed[cut].astype(jnp.bfloat16)
                    sums[half].append(lse[cut])
            for half in range(2):
                start = half * half_rows + heads * rows
                lse = as_rows(sums[half])
                first = lse.astype(jnp.bfloat16).astype(jnp.float32)
                second = (lse - first).astype(jnp.bfloat16).astype(jnp.float32)
                third = lse - first - second
                tail = jnp.concatenate([first, second, third, jnp.zeros_like(lse)], 0)
                answer_refs[index][start : start + TAIL, :] = tail.astype(jnp.bfloat16)

        for index, pairs in enumerate(transfers):
            asked = [target for _, target in pairs if (target in upper) == with_quad]
            if asked:
                pl.when(among(me, asked))(functools.partial(answer, index))

    if upper:
        pl.when(among(me, upper))(functools.partial(run, True))
        pl.when(jnp.logical_not(among(me, upper)))(functools.partial(run, False))
    else:
        run(False)

    if asking:
        for index, pairs in enumerate(transfers):

            @pl.when(among(me, [source for source, _ in pairs]))
            def _():
                for ref, half in zip(next_refs, (me % 2, 1 - me % 2)):
                    for head in range(heads):
                        start = pl.multiple_of(half * half_rows + head * rows, TAIL)
                        answer_refs[index][pl.ds(start, rows), :] = ref[:, block_lanes(head)]


def merge_kernel(transfers, steps, start, own_hbm, lse_hbm, *refs):
    count = 2 * len(transfers)
    others_hbm, out_hbm = refs[:count], refs[count + 1]
    own_ref, lse_ref, *other_refs = refs[count + 2 : 2 * count + 4]
    out_ref, sems = refs[-2:]
    me = lax.axis_index("ctx")
    odd = me % 2
    rows, width = own_ref.shape
    heads = HEADS_PER_STEP
    half_rows = heads * rows + TAIL
    returned = []
    for pairs in transfers:
        members = [source for source, _ in pairs]
        returned += [members, [member ^ 1 for member in members]]

    @pl.when(among(me, sorted(set(sum(returned, [])))))
    def _():
        loads = [(own_hbm, own_ref), (lse_hbm, lse_ref)]
        for hbm, ref in zip(others_hbm, other_refs):
            for step in range(steps):
                half = pl.ds(pl.multiple_of((2 * step + odd) * half_rows, TAIL), half_rows)
                loads.append((hbm.at[half, :], ref.at[step]))
        copies = [
            pltpu.make_async_copy(source, target, sems.at[index])
            for index, (source, target) in enumerate(loads)
        ]
        for copy in copies:
            copy.start()
        for copy in copies:
            copy.wait()
        valid = [among(me, members) for members in returned]
        for step in range(steps):
            logs = [lse_ref[step * SUBLANES : (step + 1) * SUBLANES, :]]
            for index, ref in enumerate(other_refs):
                tail = ref[step, heads * rows :, :].astype(jnp.float32)
                parts = [tail[part * SUBLANES : (part + 1) * SUBLANES] for part in range(3)]
                logs.append(jnp.where(valid[index], parts[0] + parts[1] + parts[2], NEGATIVE))
            top = functools.reduce(jnp.maximum, logs)
            weights = [jnp.exp2(part - top) for part in logs]
            total = functools.reduce(jnp.add, weights)
            shares = [as_columns(weight / total) for weight in weights]
            for head in range(heads):
                cut = block_lanes(step * heads + head)
                mixed = [own_ref[:, cut]]
                for index, ref in enumerate(other_refs):
                    part = ref[step, head * rows : (head + 1) * rows, :].astype(jnp.float32)
                    mixed.append(jnp.where(valid[index], part, 0.0))
                terms = [part * share[:, head : head + 1] for part, share in zip(mixed, shares)]
                out_ref[:, cut] = functools.reduce(jnp.add, terms).astype(out_ref.dtype)
        store = pltpu.make_async_copy(
            out_ref, out_hbm.at[:, pl.ds(start, width)], sems.at[len(copies)]
        )
        store.start()
        store.wait()


def after(array, *others):
    return lax.optimization_barrier((array, *others))[0]


def attend(query, key, value, conv):
    rows, columns = query.shape
    devices = lax.axis_size("ctx")
    quads = devices // 4
    transfers = plan_moves(devices)
    step_width = HEADS_PER_STEP * HEAD_DIM
    chunks = len(CHUNK_STEPS)
    first_steps = [sum(CHUNK_STEPS[:chunk]) for chunk in range(chunks)]
    widths = [steps * step_width for steps in CHUNK_STEPS]
    starts = [step * step_width for step in first_steps]
    upper = [4 * quad + 2 + core for quad in range(quads - 1) for core in range(2)]
    gathers = [(who - 2, who) for who in upper]
    askers = sorted({source for pairs in transfers for source, _ in pairs})
    swap = [(index, index ^ 1) for index in range(devices)]

    query_swapped = lax.ppermute(query, "ctx", swap)
    key_swapped = lax.ppermute(key, "ctx", swap)
    value_swapped = lax.ppermute(value, "ctx", swap)

    both_ways = chunks > LAG and all(
        not {source for source, _ in pairs} & {target for _, target in pairs}
        for pairs in transfers
    )
    asked = LAG if both_ways else chunks

    def pack():
        hbm = pl.BlockSpec(memory_space=pl.ANY)
        key_cuts = list(zip(starts, widths))
        query_cuts = key_cuts[:asked]
        outs = pl.pallas_call(
            functools.partial(
                pack_kernel,
                [source for source, _ in gathers],
                askers,
                key_cuts,
                query_cuts,
            ),
            in_specs=[hbm] * 4,
            out_specs=[hbm] * (chunks + asked),
            out_shape=[
                jax.ShapeDtypeStruct((2, rows, width), jnp.bfloat16)
                for _, width in key_cuts + query_cuts
            ],
            scratch_shapes=[
                pltpu.VMEM((rows, width), jnp.bfloat16)
                for _, width in key_cuts + query_cuts
                for _ in range(2)
            ]
            + [pltpu.SemaphoreType.DMA((2 * chunks,))] * 2,
            compiler_params=params(),
            cost_estimate=cost(1),
            name="att_pack",
        )(query, query_swapped, key, value)
        return outs[:chunks], outs[chunks:]

    key_packs, query_packs = pack()
    conv_first, conv_last = conv
    asks, quad_kv, all_answers = {}, [], []
    for chunk in range(chunks):
        key_pack = key_packs[chunk]
        if chunk:
            key_pack = after(key_pack, quad_kv[-1][0])
        quad_kv.append([lax.ppermute(key_pack, "ctx", gathers)])
    for chunk in range(asked):
        query_pack = query_packs[chunk]
        if chunk:
            query_pack = after(query_pack, *asks[chunk - 1])
        asks[chunk] = [lax.ppermute(query_pack, "ctx", pairs) for pairs in transfers]

    half_rows = HEADS_PER_STEP * rows + TAIL
    hbm = pl.BlockSpec(memory_space=pl.ANY)
    result = None
    returned = []

    def merged(result, chunk, *earlier):
        own, lse, arrivals = returned[chunk]
        parts = [own, lse]
        for arrival in arrivals:
            if earlier:
                arrival = after(arrival, *earlier)
            parts += [arrival, lax.ppermute(arrival, "ctx", swap)]
        steps = CHUNK_STEPS[chunk]
        count = 2 * len(transfers)
        return pl.pallas_call(
            functools.partial(merge_kernel, transfers, steps, starts[chunk]),
            in_specs=[hbm] * (len(parts) + 1),
            out_specs=hbm,
            out_shape=jax.ShapeDtypeStruct((rows, columns), jnp.bfloat16),
            input_output_aliases={len(parts): 0},
            scratch_shapes=[
                pltpu.VMEM((rows, widths[chunk]), jnp.float32),
                pltpu.VMEM((SUBLANES * steps, LANES), jnp.float32),
            ]
            + [pltpu.VMEM((steps, half_rows, LANES), jnp.bfloat16)] * count
            + [
                pltpu.VMEM((rows, widths[chunk]), jnp.bfloat16),
                pltpu.SemaphoreType.DMA((3 + count * steps,)),
            ],
            compiler_params=params(),
            cost_estimate=cost(2),
            name="att_merge",
        )(*parts, result)

    merged_count = 0
    for chunk in range(chunks):
        arrived = quad_kv[chunk][0]
        if chunk:
            arrived = after(arrived, all_answers[-1][0])
        quad_kv[chunk] = [arrived, lax.ppermute(arrived, "ctx", swap)]
        if chunk > LAG:
            result = merged(result, merged_count)
            merged_count += 1
        steps, first = CHUNK_STEPS[chunk], first_steps[chunk]
        whole_spec = pl.BlockSpec((rows, step_width), lambda step, first=first: (0, first + step))
        chunk_spec = pl.BlockSpec((rows, step_width), lambda step: (0, step))
        pair_spec = pl.BlockSpec((2, rows, step_width), lambda step: (0, 0, step))
        lse_spec = pl.BlockSpec((SUBLANES, LANES), lambda step: (step, 0))
        answer_spec = pl.BlockSpec((2 * half_rows, LANES), lambda step: (step, 0))
        answer_shape = jax.ShapeDtypeStruct((2 * half_rows * steps, LANES), jnp.bfloat16)
        asking = both_ways and chunk + LAG < chunks
        natural = chunk < asked
        operands = [query, key, value, key_swapped, value_swapped, *quad_kv[chunk], *asks[chunk]]
        specs = [whole_spec] * 5 + [pair_spec] * 2
        specs += [pair_spec if natural else answer_spec] * len(transfers)
        if asking:
            later = first_steps[chunk + LAG]
            operands += [query, query_swapped]
            specs += [
                pl.BlockSpec((rows, step_width), lambda step, later=later: (0, later + step))
            ] * 2
        aliases = {}
        if result is not None:
            aliases = {len(operands): 2 + len(transfers)}
            operands.append(result)
            specs.append(hbm)
        own, lse, *answers, result = pl.pallas_call(
            functools.partial(partial_kernel, transfers, upper, natural, asking, len(aliases)),
            grid=(steps,),
            in_specs=specs,
            out_specs=[chunk_spec, lse_spec] + [answer_spec] * len(transfers) + [whole_spec],
            out_shape=[
                jax.ShapeDtypeStruct((rows, widths[chunk]), jnp.float32),
                jax.ShapeDtypeStruct((SUBLANES * steps, LANES), jnp.float32),
            ]
            + [answer_shape] * len(transfers)
            + [jax.ShapeDtypeStruct((rows, columns), jnp.bfloat16)],
            input_output_aliases=aliases,
            compiler_params=params(),
            cost_estimate=cost(4),
            name="att_partial",
        )(*operands)
        all_answers.append(answers)
        arrivals = []
        for answer, pairs in zip(answers, transfers):
            moves = [(target, source) for source, target in pairs]
            if asking:
                moves += pairs
            arrivals.append(lax.ppermute(answer, "ctx", moves))
        if asking:
            asks[chunk + LAG] = arrivals
        returned.append([own, lse, arrivals])
        if chunk == 0:
            local_result, *conv_shared = conv_first(query_packs[0], answers[0])
    conv_shared = [after(part, all_answers[-1][0]) for part in conv_shared]
    hyena_out = conv_last(local_result, *conv_shared)
    for chunk in range(merged_count, chunks):
        last = chunk == chunks - 1
        result = merged(result, chunk, *((hyena_out, result) if last else ()))
    return hyena_out, result


def local(
    hyena_q, hyena_k, hyena_v, short_filter, residue, decay_rate, att_query, att_key, att_value
):
    conv = convolution(hyena_q, hyena_k, hyena_v, short_filter, residue, decay_rate)
    return attend(att_query, att_key, att_value, conv)


def solution(mesh):
    rows = P(("dp", "ctx"), None)
    shared = P("ctx", None)
    return jax.shard_map(
        local,
        mesh=mesh,
        in_specs=(rows, rows, rows, P(), shared, shared, rows, rows, rows),
        out_specs=(rows, rows),
        check_vma=False,
    )
```

```python
import functools
import math

import jax
import jax.numpy as jnp
from jax import lax
from jax.experimental import pallas as pl
from jax.experimental.pallas import tpu as pltpu
from jax.sharding import PartitionSpec as P

HEAD_DIM = 128
LANES = 128
SUBLANES = 8
TAIL = 4 * SUBLANES
TAPS = 3
HEADS_PER_STEP = 4
CHUNK_STEPS = (2, 2, 2, 2)
LAG = 2
PARTS = 2
NEGATIVE = -1e30
EXP_SCALE = HEAD_DIM**-0.5 * math.log2(math.e)
VMEM_LIMIT = 255 * 1024 * 256


def params(**kwargs):
    return pltpu.CompilerParams(vmem_limit_bytes=VMEM_LIMIT, **kwargs)


def cost(microseconds):
    return pl.CostEstimate(
        flops=microseconds * 10**8, bytes_accessed=2**16, transcendentals=0
    )


def block_lanes(block):
    return slice(block * LANES, (block + 1) * LANES)


def conv_pack_kernel(rate_ref, residue_ref, q_ref, k_ref, v_ref, par_ref, rim_ref):
    modes = rate_ref.shape[0]
    for block in range(rate_ref.shape[1] // LANES):
        for which, ref in enumerate((rate_ref, residue_ref)):
            start = (2 * block + which) * modes
            for device in range(par_ref.shape[0]):
                par_ref[device, start : start + modes, :] = ref[:, block_lanes(block)]
    for feature, ref in enumerate((q_ref, k_ref, v_ref)):
        last = ref[...].astype(jnp.float32)[ref.shape[0] - 2 :]
        rim_ref[2 * feature : 2 * feature + 2, :] = last
    rim_ref[2 * TAPS :, :] = jnp.zeros((2, rim_ref.shape[1]), jnp.float32)


def rim_rows(rim_ref, feature, lanes):
    return [rim_ref[pl.ds(2 * feature + row, 1), lanes] for row in range(2)]


def short_mix(feature, rim, taps):
    two_before, one_before = rim
    row = lax.broadcasted_iota(jnp.int32, feature.shape, 0)
    one = jnp.where(row == 0, one_before, pltpu.roll(feature, 1, 0))
    two = jnp.where(row == 0, two_before, jnp.where(row == 1, one_before, pltpu.roll(feature, 2, 0)))
    return taps[0] * feature + taps[1] * one + taps[2] * two


def tap_rows(taps_ref, feature, lanes):
    return [taps_ref[feature, pl.ds(tap, 1), lanes] for tap in range(TAPS)]


def state_kernel(modes, k_ref, v_ref, rim_ref, par_ref, taps_ref, *rest):
    y_ref, s_ref, d_ref, p_scr, y_scr = rest[-5:]
    rows = k_ref.shape[0]
    for block in range(SUBLANES):
        lanes = block_lanes(block)
        mixes = [
            short_mix(
                ref[:, lanes].astype(jnp.float32),
                rim_rows(rim_ref, feature, lanes),
                tap_rows(taps_ref, feature, lanes),
            )
            for feature, ref in ((1, k_ref), (2, v_ref))
        ]
        product = (mixes[0] * mixes[1]).astype(jnp.bfloat16).astype(jnp.float32)
        p_scr[pl.ds(block, rows, SUBLANES), :] = product
    decay = [jnp.exp(-par_ref[pl.ds(mode, SUBLANES, 2 * modes), :]) for mode in range(modes)]
    residue = [par_ref[pl.ds(modes + mode, SUBLANES, 2 * modes), :] for mode in range(modes)]

    def body(position, states):
        here = pl.ds(pl.multiple_of(position * SUBLANES, SUBLANES), SUBLANES)
        product = p_scr[here, :]
        states = tuple(state * rate + product for state, rate in zip(states, decay))
        terms = [state * weight for state, weight in zip(states, residue)]
        while len(terms) > 1:
            terms = [left + right for left, right in zip(terms[::2], terms[1::2])]
        y_scr[here, :] = terms[0]
        return states

    zero = jnp.zeros((SUBLANES, LANES), jnp.float32)
    states = lax.fori_loop(0, rows, body, (zero,) * modes, unroll=4)
    for mode in range(modes):
        s_ref[pl.ds(mode, SUBLANES, modes), :] = states[mode]
    for block in range(SUBLANES):
        rate = par_ref[2 * block * modes : (2 * block + 1) * modes, :]
        d_ref[block * modes : (block + 1) * modes, :] = jnp.exp(-rate * rows)
    for block in range(SUBLANES):
        y_ref[:, block_lanes(block)] = y_scr[pl.ds(block, rows, SUBLANES), :]


def output_kernel(
    modes,
    q_ref,
    y_ref,
    rim_ref,
    par_ref,
    decay_ref,
    enter_ref,
    enter_first_ref,
    other_ref,
    taps_ref,
    out_ref,
):
    second = lax.axis_index("ctx") % 2 == 1
    rows = q_ref.shape[0]
    step = lax.broadcasted_iota(jnp.int32, (SUBLANES, LANES), 0).astype(jnp.float32) + 1.0

    def body(block, nothing):
        lanes = pl.ds(pl.multiple_of(block * LANES, LANES), LANES)
        rate = par_ref[pl.ds(pl.multiple_of(2 * block * modes, SUBLANES), modes), :]
        residue = par_ref[pl.ds(pl.multiple_of((2 * block + 1) * modes, SUBLANES), modes), :]
        here = pl.ds(pl.multiple_of(block * modes, SUBLANES), modes)
        after_first = decay_ref[here, :] * enter_ref[here, :] + other_ref[here, :]
        entering = jnp.where(second, after_first, enter_first_ref[here, :])
        weighted = residue * entering
        eight = jnp.exp(-rate * SUBLANES)
        terms = [
            weighted[mode : mode + 1] * jnp.exp(-rate[mode : mode + 1] * step)
            for mode in range(modes)
        ]
        eights = [jnp.broadcast_to(eight[mode : mode + 1], terms[0].shape) for mode in range(modes)]
        added = []
        for start in range(0, rows, SUBLANES):
            sums = list(terms)
            while len(sums) > 1:
                sums = [left + right for left, right in zip(sums[::2], sums[1::2])]
            added.append(sums[0])
            if start + SUBLANES < rows:
                terms = [term * decay for term, decay in zip(terms, eights)]
        smoothed = y_ref[:, lanes] + jnp.concatenate(added, 0)
        smoothed = smoothed.astype(jnp.bfloat16).astype(jnp.float32)
        mix = short_mix(
            q_ref[:, lanes].astype(jnp.float32),
            rim_rows(rim_ref, 0, lanes),
            tap_rows(taps_ref, 0, lanes),
        )
        out_ref[:, lanes] = (mix * smoothed).astype(out_ref.dtype)
        return nothing

    lax.fori_loop(0, SUBLANES, body, 0)


def convolution(hyena_q, hyena_k, hyena_v, short_filter, residue, decay_rate):
    rows, channels = hyena_q.shape
    devices = lax.axis_size("ctx")
    modes = residue.shape[1]
    own_blocks = residue.shape[0] // LANES
    blocks = channels // LANES
    groups = blocks // SUBLANES
    width = SUBLANES * LANES
    end = rows // 16 - 1
    par_rows = 2 * own_blocks * modes
    feature_spec = pl.BlockSpec((rows, width), lambda group: (0, group))
    rim_spec = pl.BlockSpec((8, width), lambda group: (0, group))
    par_spec = pl.BlockSpec((2 * SUBLANES * modes, LANES), lambda group: (group, 0))
    taps_spec = pl.BlockSpec((TAPS, TAPS, width), lambda group: (0, 0, group))
    positions = pltpu.VMEM((rows * SUBLANES, LANES), jnp.float32)

    def first_part(token):
        own_par, rim = pl.pallas_call(
            conv_pack_kernel,
            grid=(1,),
            in_specs=[pl.BlockSpec((modes, residue.shape[0]), lambda step: (0, 0))] * 2
            + [pl.BlockSpec((16, channels), lambda step: (end, 0))] * 3,
            out_specs=[
                pl.BlockSpec((devices, par_rows, LANES), lambda step: (0, 0, 0)),
                pl.BlockSpec((8, channels), lambda step: (0, 0)),
            ],
            out_shape=[
                jax.ShapeDtypeStruct((devices, par_rows, LANES), jnp.float32),
                jax.ShapeDtypeStruct((8, channels), jnp.float32),
            ],
            compiler_params=params(),
            cost_estimate=cost(1),
            name="conv_pack",
        )(decay_rate.T, residue.T, hyena_q, hyena_k, hyena_v)
        rim = after(rim, token)
        rim = lax.ppermute(rim, "ctx", [(index, index + 1) for index in range(devices - 1)])
        par = lax.all_to_all(own_par, "ctx", split_axis=0, concat_axis=0, tiled=True)
        par = par.reshape(devices * par_rows, LANES)
        return rim, par

    def state_part(rim, par, part, earlier, *tokens):
        count = groups // PARTS
        first = part * count
        blocked = [
            pl.BlockSpec((rows, width), lambda group: (0, first + group)),
            pl.BlockSpec((SUBLANES * modes, LANES), lambda group: (first + group, 0)),
            pl.BlockSpec((SUBLANES * modes, LANES), lambda group: (first + group, 0)),
        ]
        return pl.pallas_call(
            functools.partial(state_kernel, modes),
            grid=(count,),
            in_specs=[
                blocked[0],
                blocked[0],
                pl.BlockSpec((8, width), lambda group: (0, first + group)),
                pl.BlockSpec((2 * SUBLANES * modes, LANES), lambda group: (first + group, 0)),
                pl.BlockSpec((TAPS, TAPS, width), lambda group: (0, 0, first + group)),
            ]
            + [pl.BlockSpec(memory_space=pl.ANY)] * len(earlier),
            out_specs=blocked,
            out_shape=[
                jax.ShapeDtypeStruct((rows, channels), jnp.float32),
                jax.ShapeDtypeStruct((blocks * modes, LANES), jnp.float32),
                jax.ShapeDtypeStruct((blocks * modes, LANES), jnp.float32),
            ],
            scratch_shapes=[positions, positions],
            input_output_aliases={5 + index: index for index in range(len(earlier))},
            compiler_params=params(),
            cost_estimate=cost(5),
            name="conv_state",
        )(hyena_k, hyena_v, after(rim, *tokens) if tokens else rim, par, short_filter, *earlier)

    def entering_state(state, decay, token):
        swap = [(index, index ^ 1) for index in range(devices)]
        other = lax.ppermute(state, "ctx", swap)
        total = after(state, token) + decay * other
        entering = None
        for distance in range(1, devices // 2):
            reach = 2 * distance
            moves = [(index, index + reach) for index in range(1, devices - reach, 2)]
            arrived = lax.ppermute(total, "ctx", moves)
            if distance == 1:
                entering = arrived
            else:
                entering = entering + decay ** (2 * (distance - 1)) * arrived
        return entering, lax.ppermute(entering, "ctx", swap), other

    def last_part(parts, rim, par, token, last_token):
        local_result, state, decay = parts
        entering, entering_first, other = entering_state(state, decay, token)
        entering = after(entering, last_token)
        state_spec = pl.BlockSpec((SUBLANES * modes, LANES), lambda group: (group, 0))
        return pl.pallas_call(
            functools.partial(output_kernel, modes),
            grid=(groups,),
            in_specs=[feature_spec, feature_spec, rim_spec, par_spec]
            + [state_spec] * 4
            + [taps_spec],
            out_specs=feature_spec,
            out_shape=jax.ShapeDtypeStruct((rows, channels), jnp.bfloat16),
            compiler_params=params(),
            cost_estimate=cost(6),
            name="conv_output",
        )(
            hyena_q,
            local_result,
            rim,
            par,
            decay,
            entering,
            entering_first,
            other,
            short_filter,
        )

    return first_part, state_part, last_part


def among(me, members):
    return functools.reduce(jnp.logical_or, [me == member for member in members])


def plan_moves(devices):
    quads = devices // 4
    transfers = [[(devices - 1, devices - 3)]]
    for distance in range(1, quads):
        if distance > len(transfers):
            transfers.append([])
        for quad in range(distance, quads):
            target = 4 * (quad - distance) + 2
            transfers[distance - 1] += [(4 * quad, target), (4 * quad + 2, target + 1)]
    return transfers


def soft(query, keys, values, mask=None):
    scores = lax.dot_general(
        query, keys, (((1,), (1,)), ((), ())), preferred_element_type=jnp.float32
    )
    if mask is not None:
        scores = jnp.where(mask, scores, NEGATIVE)
    top = jnp.max(scores, axis=1, keepdims=True) * EXP_SCALE
    expo = jnp.exp2(scores * EXP_SCALE - top).astype(jnp.bfloat16)
    mixed = jnp.dot(expo, values, preferred_element_type=jnp.float32)
    total = mixed[:, HEAD_DIM:]
    return mixed[:, :HEAD_DIM] / total, top + jnp.log2(total)


def pack_kernel(gathers, askers, key_cuts, query_cuts, q_ref, qs_ref, k_ref, v_ref, *rest):
    count = len(key_cuts)
    total = count + len(query_cuts)
    key_outs, query_outs = rest[:count], rest[count:total]
    key_stages, query_stages = rest[total : total + 2 * count], rest[total + 2 * count : -2]
    in_sems, out_sems = rest[-2:]
    me = lax.axis_index("ctx")
    odd = me % 2

    def run(pairs, stages):
        loads = [
            pltpu.make_async_copy(source, stage, in_sems.at[index])
            for index, ((source, _), stage) in enumerate(zip(pairs, stages))
        ]
        stores = [
            pltpu.make_async_copy(stage, target, out_sems.at[index])
            for index, ((_, target), stage) in enumerate(zip(pairs, stages))
        ]
        for load in loads:
            load.start()
        for load, store in zip(loads, stores):
            load.wait()
            store.start()
        for store in stores:
            store.wait()

    def cut(ref, columns):
        return ref.at[:, pl.ds(*columns)]

    if gathers:

        @pl.when(among(me, gathers))
        def _():
            pairs = [
                (cut(ref, columns), out.at[which])
                for columns, out in zip(key_cuts, key_outs)
                for which, ref in enumerate((k_ref, v_ref))
            ]
            run(pairs, key_stages)

    @pl.when(among(me, askers))
    def _():
        pairs = [
            (cut(ref, columns), out.at[half])
            for columns, out in zip(query_cuts, query_outs)
            for ref, half in ((q_ref, odd), (qs_ref, 1 - odd))
        ]
        run(pairs, query_stages)


def as_rows(columns):
    lanes = lax.broadcasted_iota(jnp.int32, columns[0].shape, 1)
    sums = jnp.zeros_like(columns[0])
    for index, column in enumerate(columns):
        sums = jnp.where(lanes == index, column, sums)
    return jnp.transpose(sums)[:SUBLANES]


def as_columns(part):
    fill = jnp.zeros((LANES - part.shape[0], part.shape[1]), jnp.float32)
    return jnp.transpose(jnp.concatenate([part, fill], 0))


def partial_kernel(transfers, upper, natural, asking, onto, *refs):
    count = len(transfers)
    out_ref = refs[-1]
    if asking:
        next_refs = refs[7 + count : 9 + count]
        refs = refs[: 7 + count] + refs[9 + count :]
    q_ref, k_ref, v_ref, kp_ref, vp_ref, g_ref, gp_ref = refs[:7]
    ask_refs = refs[7 : 7 + count]
    own_ref, lse_ref = refs[7 + count + onto : 9 + count + onto]
    answer_refs = refs[9 + count + onto : -1]
    me = lax.axis_index("ctx")
    rows = q_ref.shape[0]
    heads = q_ref.shape[1] // HEAD_DIM
    half_rows = heads * rows + TAIL

    def key_value(head, with_quad):
        cut = block_lanes(head)
        keys = [kp_ref[:, cut], k_ref[:, cut]]
        values = [vp_ref[:, cut], v_ref[:, cut]]
        if with_quad:
            keys = [g_ref[0, :, cut], gp_ref[0, :, cut]] + keys
            values = [g_ref[1, :, cut], gp_ref[1, :, cut]] + values
        values = jnp.concatenate(values, 0)
        return jnp.concatenate(keys, 0), jnp.concatenate([values, jnp.ones_like(values)], 1)

    def run(with_quad):
        key_count = rows * (4 if with_quad else 2)
        row = lax.broadcasted_iota(jnp.int32, (rows, key_count), 0)
        column = lax.broadcasted_iota(jnp.int32, (rows, key_count), 1)
        column = column - (key_count - 2 * rows)
        partner_limit = jnp.where(me % 2 == 1, rows, 0)
        mask = (column < partner_limit) | ((column >= rows) & (column - rows <= row))
        sums = []
        for head in range(heads):
            keys, values = key_value(head, with_quad)
            mixed, lse = soft(q_ref[:, block_lanes(head)], keys, values, mask)
            own_ref[:, block_lanes(head)] = mixed
            out_ref[:, block_lanes(head)] = mixed.astype(out_ref.dtype)
            sums.append(lse)
        lse_ref[...] = as_rows(sums)

        def answer(index):
            sums = [[], []]
            for head in range(heads):
                keys, values = key_value(head, with_quad)
                if natural:
                    query = ask_refs[index][:, :, block_lanes(head)].reshape(2 * rows, HEAD_DIM)
                else:
                    halves = [half * half_rows + head * rows for half in range(2)]
                    query = jnp.concatenate(
                        [ask_refs[index][start : start + rows, :] for start in halves], 0
                    )
                mixed, lse = soft(query, keys, values)
                for half in range(2):
                    cut = slice(half * rows, (half + 1) * rows)
                    start = half * half_rows + head * rows
                    answer_refs[index][start : start + rows, :] = mixed[cut].astype(jnp.bfloat16)
                    sums[half].append(lse[cut])
            for half in range(2):
                start = half * half_rows + heads * rows
                lse = as_rows(sums[half])
                first = lse.astype(jnp.bfloat16).astype(jnp.float32)
                second = (lse - first).astype(jnp.bfloat16).astype(jnp.float32)
                third = lse - first - second
                tail = jnp.concatenate([first, second, third, jnp.zeros_like(lse)], 0)
                answer_refs[index][start : start + TAIL, :] = tail.astype(jnp.bfloat16)

        for index, pairs in enumerate(transfers):
            asked = [target for _, target in pairs if (target in upper) == with_quad]
            if asked:
                pl.when(among(me, asked))(functools.partial(answer, index))

    if upper:
        pl.when(among(me, upper))(functools.partial(run, True))
        pl.when(jnp.logical_not(among(me, upper)))(functools.partial(run, False))
    else:
        run(False)

    if asking:
        for index, pairs in enumerate(transfers):

            @pl.when(among(me, [source for source, _ in pairs]))
            def _():
                for ref, half in zip(next_refs, (me % 2, 1 - me % 2)):
                    for head in range(heads):
                        start = pl.multiple_of(half * half_rows + head * rows, TAIL)
                        answer_refs[index][pl.ds(start, rows), :] = ref[:, block_lanes(head)]


def merge_kernel(transfers, steps, start, own_hbm, lse_hbm, *refs):
    count = 2 * len(transfers)
    others_hbm, out_hbm = refs[:count], refs[count + 1]
    own_ref, lse_ref, *other_refs = refs[count + 2 : 2 * count + 4]
    out_ref, sems = refs[-2:]
    me = lax.axis_index("ctx")
    odd = me % 2
    rows, width = own_ref.shape
    heads = HEADS_PER_STEP
    half_rows = heads * rows + TAIL
    returned = []
    for pairs in transfers:
        members = [source for source, _ in pairs]
        returned += [members, [member ^ 1 for member in members]]

    @pl.when(among(me, sorted(set(sum(returned, [])))))
    def _():
        loads = [(own_hbm, own_ref), (lse_hbm, lse_ref)]
        for hbm, ref in zip(others_hbm, other_refs):
            for step in range(steps):
                half = pl.ds(pl.multiple_of((2 * step + odd) * half_rows, TAIL), half_rows)
                loads.append((hbm.at[half, :], ref.at[step]))
        copies = [
            pltpu.make_async_copy(source, target, sems.at[index])
            for index, (source, target) in enumerate(loads)
        ]
        for copy in copies:
            copy.start()
        for copy in copies:
            copy.wait()
        valid = [among(me, members) for members in returned]
        for step in range(steps):
            logs = [lse_ref[step * SUBLANES : (step + 1) * SUBLANES, :]]
            for index, ref in enumerate(other_refs):
                tail = ref[step, heads * rows :, :].astype(jnp.float32)
                parts = [tail[part * SUBLANES : (part + 1) * SUBLANES] for part in range(3)]
                logs.append(jnp.where(valid[index], parts[0] + parts[1] + parts[2], NEGATIVE))
            top = functools.reduce(jnp.maximum, logs)
            weights = [jnp.exp2(part - top) for part in logs]
            total = functools.reduce(jnp.add, weights)
            shares = [as_columns(weight / total) for weight in weights]
            for head in range(heads):
                cut = block_lanes(step * heads + head)
                mixed = [own_ref[:, cut]]
                for index, ref in enumerate(other_refs):
                    part = ref[step, head * rows : (head + 1) * rows, :].astype(jnp.float32)
                    mixed.append(jnp.where(valid[index], part, 0.0))
                terms = [part * share[:, head : head + 1] for part, share in zip(mixed, shares)]
                out_ref[:, cut] = functools.reduce(jnp.add, terms).astype(out_ref.dtype)
        store = pltpu.make_async_copy(
            out_ref, out_hbm.at[:, pl.ds(start, width)], sems.at[len(copies)]
        )
        store.start()
        store.wait()


def after(array, *others):
    return lax.optimization_barrier((array, *others))[0]


def attend(query, key, value, conv):
    rows, columns = query.shape
    devices = lax.axis_size("ctx")
    quads = devices // 4
    transfers = plan_moves(devices)
    step_width = HEADS_PER_STEP * HEAD_DIM
    chunks = len(CHUNK_STEPS)
    first_steps = [sum(CHUNK_STEPS[:chunk]) for chunk in range(chunks)]
    widths = [steps * step_width for steps in CHUNK_STEPS]
    starts = [step * step_width for step in first_steps]
    upper = [4 * quad + 2 + core for quad in range(quads - 1) for core in range(2)]
    gathers = [(who - 2, who) for who in upper]
    askers = sorted({source for pairs in transfers for source, _ in pairs})
    swap = [(index, index ^ 1) for index in range(devices)]

    query_swapped = lax.ppermute(query, "ctx", swap)
    key_swapped = lax.ppermute(key, "ctx", swap)
    value_swapped = lax.ppermute(value, "ctx", swap)

    both_ways = chunks > LAG and all(
        not {source for source, _ in pairs} & {target for _, target in pairs}
        for pairs in transfers
    )
    asked = LAG if both_ways else chunks

    def pack():
        hbm = pl.BlockSpec(memory_space=pl.ANY)
        key_cuts = list(zip(starts, widths))
        query_cuts = key_cuts[:asked]
        outs = pl.pallas_call(
            functools.partial(
                pack_kernel,
                [source for source, _ in gathers],
                askers,
                key_cuts,
                query_cuts,
            ),
            in_specs=[hbm] * 4,
            out_specs=[hbm] * (chunks + asked),
            out_shape=[
                jax.ShapeDtypeStruct((2, rows, width), jnp.bfloat16)
                for _, width in key_cuts + query_cuts
            ],
            scratch_shapes=[
                pltpu.VMEM((rows, width), jnp.bfloat16)
                for _, width in key_cuts + query_cuts
                for _ in range(2)
            ]
            + [pltpu.SemaphoreType.DMA((2 * chunks,))] * 2,
            compiler_params=params(),
            cost_estimate=cost(1),
            name="att_pack",
        )(query, query_swapped, key, value)
        return outs[:chunks], outs[chunks:]

    key_packs, query_packs = pack()
    conv_first, conv_state, conv_last = conv
    asks, quad_kv, all_answers = {}, [], []
    for chunk in range(chunks):
        key_pack = key_packs[chunk]
        if chunk:
            key_pack = after(key_pack, quad_kv[-1][0])
        quad_kv.append([lax.ppermute(key_pack, "ctx", gathers)])
    for chunk in range(asked):
        query_pack = query_packs[chunk]
        if chunk:
            query_pack = after(query_pack, *asks[chunk - 1])
        asks[chunk] = [lax.ppermute(query_pack, "ctx", pairs) for pairs in transfers]
    rim, par = conv_first(query_packs[0])
    conv_parts = conv_state(rim, par, 0, ())

    half_rows = HEADS_PER_STEP * rows + TAIL
    hbm = pl.BlockSpec(memory_space=pl.ANY)
    result = None
    returned = []

    def merged(result, chunk, *earlier):
        own, lse, arrivals = returned[chunk]
        parts = [own, lse]
        for arrival in arrivals:
            arrival = after(arrival, *earlier)
            parts += [arrival, lax.ppermute(arrival, "ctx", swap)]
        steps = CHUNK_STEPS[chunk]
        count = 2 * len(transfers)
        return pl.pallas_call(
            functools.partial(merge_kernel, transfers, steps, starts[chunk]),
            in_specs=[hbm] * (len(parts) + 1),
            out_specs=hbm,
            out_shape=jax.ShapeDtypeStruct((rows, columns), jnp.bfloat16),
            input_output_aliases={len(parts): 0},
            scratch_shapes=[
                pltpu.VMEM((rows, widths[chunk]), jnp.float32),
                pltpu.VMEM((SUBLANES * steps, LANES), jnp.float32),
            ]
            + [pltpu.VMEM((steps, half_rows, LANES), jnp.bfloat16)] * count
            + [
                pltpu.VMEM((rows, widths[chunk]), jnp.bfloat16),
                pltpu.SemaphoreType.DMA((3 + count * steps,)),
            ],
            compiler_params=params(),
            cost_estimate=cost(2),
            name="att_merge",
        )(*parts, result)

    merged_count = 0
    for chunk in range(chunks):
        arrived = after(quad_kv[chunk][0], all_answers[-1][0] if chunk else conv_parts[1])
        quad_kv[chunk] = [arrived, lax.ppermute(arrived, "ctx", swap)]
        if chunk > LAG:
            result = merged(result, merged_count, all_answers[-1][0])
            merged_count += 1
        steps, first = CHUNK_STEPS[chunk], first_steps[chunk]
        whole_spec = pl.BlockSpec((rows, step_width), lambda step, first=first: (0, first + step))
        chunk_spec = pl.BlockSpec((rows, step_width), lambda step: (0, step))
        pair_spec = pl.BlockSpec((2, rows, step_width), lambda step: (0, 0, step))
        lse_spec = pl.BlockSpec((SUBLANES, LANES), lambda step: (step, 0))
        answer_spec = pl.BlockSpec((2 * half_rows, LANES), lambda step: (step, 0))
        answer_shape = jax.ShapeDtypeStruct((2 * half_rows * steps, LANES), jnp.bfloat16)
        asking = both_ways and chunk + LAG < chunks
        natural = chunk < asked
        operands = [query, key, value, key_swapped, value_swapped, *quad_kv[chunk], *asks[chunk]]
        specs = [whole_spec] * 5 + [pair_spec] * 2
        specs += [pair_spec if natural else answer_spec] * len(transfers)
        if asking:
            later = first_steps[chunk + LAG]
            operands += [query, query_swapped]
            specs += [
                pl.BlockSpec((rows, step_width), lambda step, later=later: (0, later + step))
            ] * 2
        aliases = {}
        if result is not None:
            aliases = {len(operands): 2 + len(transfers)}
            operands.append(result)
            specs.append(hbm)
        own, lse, *answers, result = pl.pallas_call(
            functools.partial(partial_kernel, transfers, upper, natural, asking, len(aliases)),
            grid=(steps,),
            in_specs=specs,
            out_specs=[chunk_spec, lse_spec] + [answer_spec] * len(transfers) + [whole_spec],
            out_shape=[
                jax.ShapeDtypeStruct((rows, widths[chunk]), jnp.float32),
                jax.ShapeDtypeStruct((SUBLANES * steps, LANES), jnp.float32),
            ]
            + [answer_shape] * len(transfers)
            + [jax.ShapeDtypeStruct((rows, columns), jnp.bfloat16)],
            input_output_aliases=aliases,
            compiler_params=params(),
            cost_estimate=cost(4),
            name="att_partial",
        )(*operands)
        all_answers.append(answers)
        arrivals = []
        for answer, pairs in zip(answers, transfers):
            moves = [(target, source) for source, target in pairs]
            if asking:
                moves += pairs
            arrivals.append(lax.ppermute(answer, "ctx", moves))
        if asking:
            asks[chunk + LAG] = arrivals
        returned.append([own, lse, arrivals])
        if chunk < PARTS - 1:
            conv_parts = conv_state(rim, par, chunk + 1, conv_parts, answers[0])
            asks[chunk + 1] = [after(ask, conv_parts[1]) for ask in asks[chunk + 1]]
    tokens = [all_answers[min(LAG, chunks - 1)][0], all_answers[-1][0]]
    hyena_out = conv_last(conv_parts, rim, par, *tokens)
    for chunk in range(merged_count, chunks):
        last = chunk == chunks - 1
        result = merged(result, chunk, *((hyena_out, result) if last else all_answers[-1][:1]))
    return hyena_out, result


def local(
    hyena_q, hyena_k, hyena_v, short_filter, residue, decay_rate, att_query, att_key, att_value
):
    conv = convolution(hyena_q, hyena_k, hyena_v, short_filter, residue, decay_rate)
    return attend(att_query, att_key, att_value, conv)


def solution(mesh):
    rows = P(("dp", "ctx"), None)
    shared = P("ctx", None)
    return jax.shard_map(
        local,
        mesh=mesh,
        in_specs=(rows, rows, rows, P(), shared, shared, rows, rows, rows),
        out_specs=(rows, rows),
        check_vma=False,
    )
```

```python
import functools
import math

import jax
import jax.numpy as jnp
from jax import lax
from jax.experimental import pallas as pl
from jax.experimental.pallas import tpu as pltpu
from jax.sharding import PartitionSpec as P

HEAD_DIM = 128
LANES = 128
SUBLANES = 8
TAIL = 4 * SUBLANES
TAPS = 3
HEADS_PER_STEP = 4
CHUNK_STEPS = (2, 2, 2, 2)
LAG = 2
NEGATIVE = -1e30
EXP_SCALE = HEAD_DIM**-0.5 * math.log2(math.e)
VMEM_LIMIT = 255 * 1024 * 256


def params(**kwargs):
    return pltpu.CompilerParams(vmem_limit_bytes=VMEM_LIMIT, **kwargs)


def cost(microseconds):
    return pl.CostEstimate(
        flops=microseconds * 10**9, bytes_accessed=2**20, transcendentals=0
    )


def block_lanes(block):
    return slice(block * LANES, (block + 1) * LANES)


def conv_pack_kernel(rate_ref, residue_ref, q_ref, k_ref, v_ref, par_ref, rim_ref):
    modes = rate_ref.shape[0]
    for block in range(rate_ref.shape[1] // LANES):
        for which, ref in enumerate((rate_ref, residue_ref)):
            start = (2 * block + which) * modes
            for device in range(par_ref.shape[0]):
                par_ref[device, start : start + modes, :] = ref[:, block_lanes(block)]
    for feature, ref in enumerate((q_ref, k_ref, v_ref)):
        last = ref[...].astype(jnp.float32)[ref.shape[0] - 2 :]
        rim_ref[2 * feature : 2 * feature + 2, :] = last
    rim_ref[2 * TAPS :, :] = jnp.zeros((2, rim_ref.shape[1]), jnp.float32)


def rim_rows(rim_ref, feature, lanes):
    return [rim_ref[pl.ds(2 * feature + row, 1), lanes] for row in range(2)]


def short_mix(feature, rim, taps):
    two_before, one_before = rim
    row = lax.broadcasted_iota(jnp.int32, feature.shape, 0)
    one = jnp.where(row == 0, one_before, pltpu.roll(feature, 1, 0))
    two = jnp.where(row == 0, two_before, jnp.where(row == 1, one_before, pltpu.roll(feature, 2, 0)))
    return taps[0] * feature + taps[1] * one + taps[2] * two


def tap_rows(taps_ref, feature, lanes):
    return [taps_ref[feature, pl.ds(tap, 1), lanes] for tap in range(TAPS)]


def state_kernel(
    modes, k_ref, v_ref, rim_ref, par_ref, taps_ref, y_ref, s_ref, d_ref, p_scr, y_scr
):
    rows = k_ref.shape[0]
    for block in range(SUBLANES):
        lanes = block_lanes(block)
        mixes = [
            short_mix(
                ref[:, lanes].astype(jnp.float32),
                rim_rows(rim_ref, feature, lanes),
                tap_rows(taps_ref, feature, lanes),
            )
            for feature, ref in ((1, k_ref), (2, v_ref))
        ]
        product = (mixes[0] * mixes[1]).astype(jnp.bfloat16).astype(jnp.float32)
        p_scr[pl.ds(block, rows, SUBLANES), :] = product
    decay = [jnp.exp(-par_ref[pl.ds(mode, SUBLANES, 2 * modes), :]) for mode in range(modes)]
    residue = [par_ref[pl.ds(modes + mode, SUBLANES, 2 * modes), :] for mode in range(modes)]

    def body(position, states):
        here = pl.ds(pl.multiple_of(position * SUBLANES, SUBLANES), SUBLANES)
        product = p_scr[here, :]
        states = tuple(state * rate + product for state, rate in zip(states, decay))
        terms = [state * weight for state, weight in zip(states, residue)]
        while len(terms) > 1:
            terms = [left + right for left, right in zip(terms[::2], terms[1::2])]
        y_scr[here, :] = terms[0]
        return states

    zero = jnp.zeros((SUBLANES, LANES), jnp.float32)
    states = lax.fori_loop(0, rows, body, (zero,) * modes, unroll=4)
    for mode in range(modes):
        s_ref[pl.ds(mode, SUBLANES, modes), :] = states[mode]
    for block in range(SUBLANES):
        rate = par_ref[2 * block * modes : (2 * block + 1) * modes, :]
        d_ref[block * modes : (block + 1) * modes, :] = jnp.exp(-rate * rows)
    for block in range(SUBLANES):
        y_ref[:, block_lanes(block)] = y_scr[pl.ds(block, rows, SUBLANES), :]


def output_kernel(
    modes,
    q_ref,
    y_ref,
    rim_ref,
    par_ref,
    decay_ref,
    enter_ref,
    enter_first_ref,
    other_ref,
    taps_ref,
    out_ref,
):
    second = lax.axis_index("ctx") % 2 == 1
    rows = q_ref.shape[0]
    step = lax.broadcasted_iota(jnp.int32, (SUBLANES, LANES), 0).astype(jnp.float32) + 1.0

    def body(block, nothing):
        lanes = pl.ds(pl.multiple_of(block * LANES, LANES), LANES)
        rate = par_ref[pl.ds(pl.multiple_of(2 * block * modes, SUBLANES), modes), :]
        residue = par_ref[pl.ds(pl.multiple_of((2 * block + 1) * modes, SUBLANES), modes), :]
        here = pl.ds(pl.multiple_of(block * modes, SUBLANES), modes)
        after_first = decay_ref[here, :] * enter_ref[here, :] + other_ref[here, :]
        entering = jnp.where(second, after_first, enter_first_ref[here, :])
        weighted = residue * entering
        eight = jnp.exp(-rate * SUBLANES)
        terms = [
            weighted[mode : mode + 1] * jnp.exp(-rate[mode : mode + 1] * step)
            for mode in range(modes)
        ]
        eights = [jnp.broadcast_to(eight[mode : mode + 1], terms[0].shape) for mode in range(modes)]
        added = []
        for start in range(0, rows, SUBLANES):
            sums = list(terms)
            while len(sums) > 1:
                sums = [left + right for left, right in zip(sums[::2], sums[1::2])]
            added.append(sums[0])
            if start + SUBLANES < rows:
                terms = [term * decay for term, decay in zip(terms, eights)]
        smoothed = y_ref[:, lanes] + jnp.concatenate(added, 0)
        smoothed = smoothed.astype(jnp.bfloat16).astype(jnp.float32)
        mix = short_mix(
            q_ref[:, lanes].astype(jnp.float32),
            rim_rows(rim_ref, 0, lanes),
            tap_rows(taps_ref, 0, lanes),
        )
        out_ref[:, lanes] = (mix * smoothed).astype(out_ref.dtype)
        return nothing

    lax.fori_loop(0, SUBLANES, body, 0)


def convolution(hyena_q, hyena_k, hyena_v, short_filter, residue, decay_rate):
    rows, channels = hyena_q.shape
    devices = lax.axis_size("ctx")
    modes = residue.shape[1]
    own_blocks = residue.shape[0] // LANES
    blocks = channels // LANES
    groups = blocks // SUBLANES
    width = SUBLANES * LANES
    end = rows // 16 - 1
    par_rows = 2 * own_blocks * modes
    feature_spec = pl.BlockSpec((rows, width), lambda group: (0, group))
    rim_spec = pl.BlockSpec((8, width), lambda group: (0, group))
    par_spec = pl.BlockSpec((2 * SUBLANES * modes, LANES), lambda group: (group, 0))
    taps_spec = pl.BlockSpec((TAPS, TAPS, width), lambda group: (0, 0, group))
    positions = pltpu.VMEM((rows * SUBLANES, LANES), jnp.float32)

    def first_part(token):
        own_par, rim = pl.pallas_call(
            conv_pack_kernel,
            grid=(1,),
            in_specs=[pl.BlockSpec((modes, residue.shape[0]), lambda step: (0, 0))] * 2
            + [pl.BlockSpec((16, channels), lambda step: (end, 0))] * 3,
            out_specs=[
                pl.BlockSpec((devices, par_rows, LANES), lambda step: (0, 0, 0)),
                pl.BlockSpec((8, channels), lambda step: (0, 0)),
            ],
            out_shape=[
                jax.ShapeDtypeStruct((devices, par_rows, LANES), jnp.float32),
                jax.ShapeDtypeStruct((8, channels), jnp.float32),
            ],
            compiler_params=params(),
            cost_estimate=cost(1),
            name="conv_pack",
        )(decay_rate.T, residue.T, hyena_q, hyena_k, hyena_v)
        rim = lax.ppermute(rim, "ctx", [(index, index + 1) for index in range(devices - 1)])
        own_par = after(own_par, rim)
        par = lax.all_to_all(own_par, "ctx", split_axis=0, concat_axis=0, tiled=True)
        par = par.reshape(devices * par_rows, LANES)
        state_spec = pl.BlockSpec((SUBLANES * modes, LANES), lambda group: (group, 0))
        local_result, state, decay = pl.pallas_call(
            functools.partial(state_kernel, modes),
            grid=(groups,),
            in_specs=[feature_spec, feature_spec, rim_spec, par_spec, taps_spec],
            out_specs=[feature_spec, state_spec, state_spec],
            out_shape=[
                jax.ShapeDtypeStruct((rows, channels), jnp.float32),
                jax.ShapeDtypeStruct((blocks * modes, LANES), jnp.float32),
                jax.ShapeDtypeStruct((blocks * modes, LANES), jnp.float32),
            ],
            scratch_shapes=[positions, positions],
            compiler_params=params(),
            cost_estimate=cost(9),
            name="conv_state",
        )(hyena_k, hyena_v, rim, par, short_filter)
        return local_result, rim, par, decay, state

    def entering_state(state, decay):
        swap = [(index, index ^ 1) for index in range(devices)]
        other = lax.ppermute(state, "ctx", swap)
        total = state + decay * other
        entering = None
        reach = 1
        while 2 * reach < devices:
            moves = [(index, index + 2 * reach) for index in range(1, devices - 2 * reach, 2)]
            arrived = lax.ppermute(total, "ctx", moves)
            if reach == 1:
                entering = arrived
            else:
                entering = entering + decay ** (2 * (reach - 1)) * arrived
            if 4 * reach < devices:
                total = total + decay ** (2 * reach) * arrived
            reach *= 2
        return entering, lax.ppermute(entering, "ctx", swap), other

    def last_part(local_result, rim, par, decay, state, last_token):
        entering, entering_first, other = entering_state(state, decay)
        entering = after(entering, last_token)
        state_spec = pl.BlockSpec((SUBLANES * modes, LANES), lambda group: (group, 0))
        return pl.pallas_call(
            functools.partial(output_kernel, modes),
            grid=(groups,),
            in_specs=[feature_spec, feature_spec, rim_spec, par_spec]
            + [state_spec] * 4
            + [taps_spec],
            out_specs=feature_spec,
            out_shape=jax.ShapeDtypeStruct((rows, channels), jnp.bfloat16),
            compiler_params=params(),
            cost_estimate=cost(6),
            name="conv_output",
        )(
            hyena_q,
            local_result,
            rim,
            par,
            decay,
            entering,
            entering_first,
            other,
            short_filter,
        )

    return first_part, last_part


def among(me, members):
    return functools.reduce(jnp.logical_or, [me == member for member in members])


def plan_moves(devices):
    quads = devices // 4
    transfers = [[(devices - 1, devices - 3)]]
    for distance in range(1, quads):
        if distance > len(transfers):
            transfers.append([])
        for quad in range(distance, quads):
            target = 4 * (quad - distance) + 2
            transfers[distance - 1] += [(4 * quad, target), (4 * quad + 2, target + 1)]
    return transfers


def soft(query, keys, values, mask=None):
    scores = lax.dot_general(
        query, keys, (((1,), (1,)), ((), ())), preferred_element_type=jnp.float32
    )
    if mask is not None:
        scores = jnp.where(mask, scores, NEGATIVE)
    top = jnp.max(scores, axis=1, keepdims=True) * EXP_SCALE
    expo = jnp.exp2(scores * EXP_SCALE - top).astype(jnp.bfloat16)
    mixed = jnp.dot(expo, values, preferred_element_type=jnp.float32)
    total = mixed[:, HEAD_DIM:]
    return mixed[:, :HEAD_DIM] / total, top + jnp.log2(total)


def pack_kernel(gathers, askers, asked, widths, starts, q_ref, qs_ref, k_ref, v_ref, *rest):
    count = len(widths)
    key_outs, query_outs = rest[:count], rest[count : count + asked]
    stages, in_sems, out_sems = rest[count + asked : -2], rest[-2], rest[-1]
    me = lax.axis_index("ctx")
    odd = me % 2

    def run(pairs):
        loads = [
            pltpu.make_async_copy(source, stage, in_sems.at[index])
            for index, ((source, _), stage) in enumerate(zip(pairs, stages))
        ]
        stores = [
            pltpu.make_async_copy(stage, target, out_sems.at[index])
            for index, ((_, target), stage) in enumerate(zip(pairs, stages))
        ]
        for load in loads:
            load.start()
        for load, store in zip(loads, stores):
            load.wait()
            store.start()
        for store in stores:
            store.wait()

    def cut(ref, chunk):
        return ref.at[:, pl.ds(starts[chunk], widths[chunk])]

    if gathers:

        @pl.when(among(me, gathers))
        def _():
            run(
                [
                    (cut(ref, chunk), key_outs[chunk].at[which])
                    for chunk in range(count)
                    for which, ref in enumerate((k_ref, v_ref))
                ]
            )

    @pl.when(among(me, askers))
    def _():
        run(
            [
                (cut(ref, chunk), query_outs[chunk].at[half])
                for chunk in range(asked)
                for ref, half in ((q_ref, odd), (qs_ref, 1 - odd))
            ]
        )


def as_rows(columns):
    lanes = lax.broadcasted_iota(jnp.int32, columns[0].shape, 1)
    sums = jnp.zeros_like(columns[0])
    for index, column in enumerate(columns):
        sums = jnp.where(lanes == index, column, sums)
    return jnp.transpose(sums)[:SUBLANES]


def as_columns(part):
    fill = jnp.zeros((LANES - part.shape[0], part.shape[1]), jnp.float32)
    return jnp.transpose(jnp.concatenate([part, fill], 0))


def partial_kernel(transfers, upper, natural, asking, onto, *refs):
    count = len(transfers)
    out_ref = refs[-1]
    if asking:
        next_refs = refs[7 + count : 9 + count]
        refs = refs[: 7 + count] + refs[9 + count :]
    q_ref, k_ref, v_ref, kp_ref, vp_ref, g_ref, gp_ref = refs[:7]
    ask_refs = refs[7 : 7 + count]
    own_ref, lse_ref = refs[7 + count + onto : 9 + count + onto]
    answer_refs = refs[9 + count + onto : -1]
    me = lax.axis_index("ctx")
    rows = q_ref.shape[0]
    heads = q_ref.shape[1] // HEAD_DIM
    half_rows = heads * rows + TAIL

    def key_value(head, with_quad):
        cut = block_lanes(head)
        keys = [kp_ref[:, cut], k_ref[:, cut]]
        values = [vp_ref[:, cut], v_ref[:, cut]]
        if with_quad:
            keys = [g_ref[0, :, cut], gp_ref[0, :, cut]] + keys
            values = [g_ref[1, :, cut], gp_ref[1, :, cut]] + values
        values = jnp.concatenate(values, 0)
        return jnp.concatenate(keys, 0), jnp.concatenate([values, jnp.ones_like(values)], 1)

    def run(with_quad):
        key_count = rows * (4 if with_quad else 2)
        row = lax.broadcasted_iota(jnp.int32, (rows, key_count), 0)
        column = lax.broadcasted_iota(jnp.int32, (rows, key_count), 1)
        column = column - (key_count - 2 * rows)
        partner_limit = jnp.where(me % 2 == 1, rows, 0)
        mask = (column < partner_limit) | ((column >= rows) & (column - rows <= row))
        sums = []
        for head in range(heads):
            keys, values = key_value(head, with_quad)
            mixed, lse = soft(q_ref[:, block_lanes(head)], keys, values, mask)
            own_ref[:, block_lanes(head)] = mixed
            out_ref[:, block_lanes(head)] = mixed.astype(out_ref.dtype)
            sums.append(lse)
        lse_ref[...] = as_rows(sums)

        def answer(index):
            sums = [[], []]
            for head in range(heads):
                keys, values = key_value(head, with_quad)
                if natural:
                    query = ask_refs[index][:, :, block_lanes(head)].reshape(2 * rows, HEAD_DIM)
                else:
                    halves = [half * half_rows + head * rows for half in range(2)]
                    query = jnp.concatenate(
                        [ask_refs[index][start : start + rows, :] for start in halves], 0
                    )
                mixed, lse = soft(query, keys, values)
                for half in range(2):
                    cut = slice(half * rows, (half + 1) * rows)
                    start = half * half_rows + head * rows
                    answer_refs[index][start : start + rows, :] = mixed[cut].astype(jnp.bfloat16)
                    sums[half].append(lse[cut])
            for half in range(2):
                start = half * half_rows + heads * rows
                lse = as_rows(sums[half])
                first = lse.astype(jnp.bfloat16).astype(jnp.float32)
                second = (lse - first).astype(jnp.bfloat16).astype(jnp.float32)
                third = lse - first - second
                tail = jnp.concatenate([first, second, third, jnp.zeros_like(lse)], 0)
                answer_refs[index][start : start + TAIL, :] = tail.astype(jnp.bfloat16)

        for index, pairs in enumerate(transfers):
            asked = [target for _, target in pairs if (target in upper) == with_quad]
            if asked:
                pl.when(among(me, asked))(functools.partial(answer, index))

    if upper:
        pl.when(among(me, upper))(functools.partial(run, True))
        pl.when(jnp.logical_not(among(me, upper)))(functools.partial(run, False))
    else:
        run(False)

    if asking:
        for index, pairs in enumerate(transfers):

            @pl.when(among(me, [source for source, _ in pairs]))
            def _():
                for ref, half in zip(next_refs, (me % 2, 1 - me % 2)):
                    for head in range(heads):
                        start = pl.multiple_of(half * half_rows + head * rows, TAIL)
                        answer_refs[index][pl.ds(start, rows), :] = ref[:, block_lanes(head)]


def merge_kernel(transfers, steps, start, own_hbm, lse_hbm, *refs):
    count = 2 * len(transfers)
    others_hbm, out_hbm = refs[:count], refs[count + 1]
    own_ref, lse_ref, *other_refs = refs[count + 2 : 2 * count + 4]
    out_ref, sems = refs[-2:]
    me = lax.axis_index("ctx")
    odd = me % 2
    rows, width = own_ref.shape
    heads = HEADS_PER_STEP
    half_rows = heads * rows + TAIL
    returned = []
    for pairs in transfers:
        members = [source for source, _ in pairs]
        returned += [members, [member ^ 1 for member in members]]

    @pl.when(among(me, sorted(set(sum(returned, [])))))
    def _():
        loads = [(own_hbm, own_ref), (lse_hbm, lse_ref)]
        for hbm, ref in zip(others_hbm, other_refs):
            for step in range(steps):
                half = pl.ds(pl.multiple_of((2 * step + odd) * half_rows, TAIL), half_rows)
                loads.append((hbm.at[half, :], ref.at[step]))
        copies = [
            pltpu.make_async_copy(source, target, sems.at[index])
            for index, (source, target) in enumerate(loads)
        ]
        for copy in copies:
            copy.start()
        for copy in copies:
            copy.wait()
        valid = [among(me, members) for members in returned]
        for step in range(steps):
            logs = [lse_ref[step * SUBLANES : (step + 1) * SUBLANES, :]]
            for index, ref in enumerate(other_refs):
                tail = ref[step, heads * rows :, :].astype(jnp.float32)
                parts = [tail[part * SUBLANES : (part + 1) * SUBLANES] for part in range(3)]
                logs.append(jnp.where(valid[index], parts[0] + parts[1] + parts[2], NEGATIVE))
            top = functools.reduce(jnp.maximum, logs)
            weights = [jnp.exp2(part - top) for part in logs]
            total = functools.reduce(jnp.add, weights)
            shares = [as_columns(weight / total) for weight in weights]
            for head in range(heads):
                cut = block_lanes(step * heads + head)
                mixed = [own_ref[:, cut]]
                for index, ref in enumerate(other_refs):
                    part = ref[step, head * rows : (head + 1) * rows, :].astype(jnp.float32)
                    mixed.append(jnp.where(valid[index], part, 0.0))
                terms = [part * share[:, head : head + 1] for part, share in zip(mixed, shares)]
                out_ref[:, cut] = functools.reduce(jnp.add, terms).astype(out_ref.dtype)
        store = pltpu.make_async_copy(
            out_ref, out_hbm.at[:, pl.ds(start, width)], sems.at[len(copies)]
        )
        store.start()
        store.wait()


def after(array, *others):
    return lax.optimization_barrier((array, *others))[0]


def attend(query, key, value, conv):
    rows, columns = query.shape
    devices = lax.axis_size("ctx")
    quads = devices // 4
    transfers = plan_moves(devices)
    step_width = HEADS_PER_STEP * HEAD_DIM
    chunks = len(CHUNK_STEPS)
    first_steps = [sum(CHUNK_STEPS[:chunk]) for chunk in range(chunks)]
    widths = [steps * step_width for steps in CHUNK_STEPS]
    starts = [step * step_width for step in first_steps]
    upper = [4 * quad + 2 + core for quad in range(quads - 1) for core in range(2)]
    gathers = [(who - 2, who) for who in upper]
    askers = sorted({source for pairs in transfers for source, _ in pairs})
    swap = [(index, index ^ 1) for index in range(devices)]

    query_swapped = lax.ppermute(query, "ctx", swap)
    key_swapped = lax.ppermute(key, "ctx", swap)
    value_swapped = lax.ppermute(value, "ctx", swap)

    both_ways = chunks > LAG and all(
        not {source for source, _ in pairs} & {target for _, target in pairs}
        for pairs in transfers
    )
    asked = LAG if both_ways else chunks

    def pack():
        hbm = pl.BlockSpec(memory_space=pl.ANY)
        shapes = [jax.ShapeDtypeStruct((2, rows, width), jnp.bfloat16) for width in widths]
        outs = pl.pallas_call(
            functools.partial(
                pack_kernel,
                [source for source, _ in gathers],
                askers,
                asked,
                widths,
                starts,
            ),
            in_specs=[hbm] * 4,
            out_specs=[hbm] * (chunks + asked),
            out_shape=shapes + shapes[:asked],
            scratch_shapes=[
                pltpu.VMEM((rows, width), jnp.bfloat16) for width in widths for _ in range(2)
            ]
            + [pltpu.SemaphoreType.DMA((2 * chunks,))] * 2,
            compiler_params=params(),
            cost_estimate=cost(1),
            name="att_pack",
        )(query, query_swapped, key, value)
        return outs[:chunks], outs[chunks:]

    key_packs, query_packs = pack()
    conv_first, conv_last = conv
    local_result, *conv_shared = conv_first(query_packs[0])
    asks, quad_kv, all_answers = {}, [], []

    def send(chunk):
        key_pack = key_packs[chunk]
        if chunk >= LAG:
            key_pack = after(key_pack, quad_kv[chunk - LAG][0], *all_answers[chunk - LAG][:1])
        quad_kv.append([lax.ppermute(key_pack, "ctx", gathers)])
        if chunk < asked:
            query_pack = query_packs[chunk]
            if chunk >= LAG:
                query_pack = after(query_pack, *asks[chunk - LAG], all_answers[chunk - LAG][0])
            asks[chunk] = [lax.ppermute(query_pack, "ctx", pairs) for pairs in transfers]

    half_rows = HEADS_PER_STEP * rows + TAIL
    hbm = pl.BlockSpec(memory_space=pl.ANY)
    for chunk in range(min(LAG, chunks)):
        send(chunk)
    result = None
    returned = []
    for chunk in range(chunks):
        if chunk == 0:
            quad_kv[0] = [after(quad_kv[0][0], local_result)]
            asks[0] = [after(asked, local_result) for asked in asks[0]]
        else:
            quad_kv[chunk] = [after(quad_kv[chunk][0], all_answers[-1][0])]
        quad_kv[chunk].append(lax.ppermute(quad_kv[chunk][0], "ctx", swap))
        steps, first = CHUNK_STEPS[chunk], first_steps[chunk]
        whole_spec = pl.BlockSpec((rows, step_width), lambda step, first=first: (0, first + step))
        chunk_spec = pl.BlockSpec((rows, step_width), lambda step: (0, step))
        pair_spec = pl.BlockSpec((2, rows, step_width), lambda step: (0, 0, step))
        lse_spec = pl.BlockSpec((SUBLANES, LANES), lambda step: (step, 0))
        answer_spec = pl.BlockSpec((2 * half_rows, LANES), lambda step: (step, 0))
        answer_shape = jax.ShapeDtypeStruct((2 * half_rows * steps, LANES), jnp.bfloat16)
        asking = both_ways and chunk + LAG < chunks
        natural = chunk < asked
        operands = [query, key, value, key_swapped, value_swapped, *quad_kv[chunk], *asks[chunk]]
        specs = [whole_spec] * 5 + [pair_spec] * 2
        specs += [pair_spec if natural else answer_spec] * len(transfers)
        if asking:
            later = first_steps[chunk + LAG]
            operands += [query, query_swapped]
            specs += [
                pl.BlockSpec((rows, step_width), lambda step, later=later: (0, later + step))
            ] * 2
        aliases = {}
        if result is not None:
            aliases = {len(operands): 2 + len(transfers)}
            operands.append(result)
            specs.append(hbm)
        own, lse, *answers, result = pl.pallas_call(
            functools.partial(partial_kernel, transfers, upper, natural, asking, len(aliases)),
            grid=(steps,),
            in_specs=specs,
            out_specs=[chunk_spec, lse_spec] + [answer_spec] * len(transfers) + [whole_spec],
            out_shape=[
                jax.ShapeDtypeStruct((rows, widths[chunk]), jnp.float32),
                jax.ShapeDtypeStruct((SUBLANES * steps, LANES), jnp.float32),
            ]
            + [answer_shape] * len(transfers)
            + [jax.ShapeDtypeStruct((rows, columns), jnp.bfloat16)],
            input_output_aliases=aliases,
            compiler_params=params(),
            cost_estimate=cost(4),
            name="att_partial",
        )(*operands)
        all_answers.append(answers)
        parts = [own, lse]
        arrivals = []
        for answer, pairs in zip(answers, transfers):
            moves = [(target, source) for source, target in pairs]
            if asking:
                moves += pairs
            arrivals.append(lax.ppermute(answer, "ctx", moves))
        if asking:
            asks[chunk + LAG] = arrivals
        returned.append([own, lse, arrivals])
        if chunk + LAG < chunks:
            send(chunk + LAG)
    tokens = [all_answers[-1][0]]
    hyena_out = conv_last(local_result, *conv_shared, *tokens)
    for chunk, (own, lse, arrivals) in enumerate(returned):
        parts = [own, lse]
        for arrival in arrivals:
            if chunk == chunks - 1:
                arrival = after(arrival, hyena_out, result)
            elif chunk == chunks - 2:
                arrival = after(arrival, hyena_out)
            parts += [arrival, lax.ppermute(arrival, "ctx", swap)]
        steps = CHUNK_STEPS[chunk]
        count = 2 * len(transfers)
        result = pl.pallas_call(
            functools.partial(merge_kernel, transfers, steps, starts[chunk]),
            in_specs=[hbm] * (len(parts) + 1),
            out_specs=hbm,
            out_shape=jax.ShapeDtypeStruct((rows, columns), jnp.bfloat16),
            input_output_aliases={len(parts): 0},
            scratch_shapes=[
                pltpu.VMEM((rows, widths[chunk]), jnp.float32),
                pltpu.VMEM((SUBLANES * steps, LANES), jnp.float32),
            ]
            + [pltpu.VMEM((steps, half_rows, LANES), jnp.bfloat16)] * count
            + [
                pltpu.VMEM((rows, widths[chunk]), jnp.bfloat16),
                pltpu.SemaphoreType.DMA((3 + count * steps,)),
            ],
            compiler_params=params(),
            cost_estimate=cost(2),
            name="att_merge",
        )(*parts, result)
    return hyena_out, result


def local(
    hyena_q, hyena_k, hyena_v, short_filter, residue, decay_rate, att_query, att_key, att_value
):
    conv = convolution(hyena_q, hyena_k, hyena_v, short_filter, residue, decay_rate)
    return attend(att_query, att_key, att_value, conv)


def solution(mesh):
    rows = P(("dp", "ctx"), None)
    shared = P("ctx", None)
    return jax.shard_map(
        local,
        mesh=mesh,
        in_specs=(rows, rows, rows, P(), shared, shared, rows, rows, rows),
        out_specs=(rows, rows),
        check_vma=False,
    )
```

```python
import functools
import math

import jax
import jax.numpy as jnp
from jax import lax
from jax.experimental import pallas as pl
from jax.experimental.pallas import tpu as pltpu
from jax.sharding import PartitionSpec as P

HEAD_DIM = 128
LANES = 128
SUBLANES = 8
TAIL = 4 * SUBLANES
TAPS = 3
HEADS_PER_STEP = 4
CHUNK_STEPS = (2, 2, 2, 2)
LAG = 2
NEGATIVE = -1e30
EXP_SCALE = HEAD_DIM**-0.5 * math.log2(math.e)
VMEM_LIMIT = 255 * 1024 * 256


def params(**kwargs):
    return pltpu.CompilerParams(vmem_limit_bytes=VMEM_LIMIT, **kwargs)


def cost(microseconds):
    return pl.CostEstimate(
        flops=microseconds * 10**9, bytes_accessed=2**20, transcendentals=0
    )


def block_lanes(block):
    return slice(block * LANES, (block + 1) * LANES)


def conv_pack_kernel(rate_ref, residue_ref, q_ref, k_ref, v_ref, par_ref, rim_ref):
    modes = rate_ref.shape[0]
    for block in range(rate_ref.shape[1] // LANES):
        for which, ref in enumerate((rate_ref, residue_ref)):
            start = (2 * block + which) * modes
            for device in range(par_ref.shape[0]):
                par_ref[device, start : start + modes, :] = ref[:, block_lanes(block)]
    for feature, ref in enumerate((q_ref, k_ref, v_ref)):
        last = ref[...].astype(jnp.float32)[ref.shape[0] - 2 :]
        rim_ref[2 * feature : 2 * feature + 2, :] = last
    rim_ref[2 * TAPS :, :] = jnp.zeros((2, rim_ref.shape[1]), jnp.float32)


def rim_rows(rim_ref, feature, lanes):
    return [rim_ref[pl.ds(2 * feature + row, 1), lanes] for row in range(2)]


def short_mix(feature, rim, taps):
    two_before, one_before = rim
    row = lax.broadcasted_iota(jnp.int32, feature.shape, 0)
    one = jnp.where(row == 0, one_before, pltpu.roll(feature, 1, 0))
    two = jnp.where(row == 0, two_before, jnp.where(row == 1, one_before, pltpu.roll(feature, 2, 0)))
    return taps[0] * feature + taps[1] * one + taps[2] * two


def tap_rows(taps_ref, feature, lanes):
    return [taps_ref[feature, pl.ds(tap, 1), lanes] for tap in range(TAPS)]


def state_kernel(
    modes, k_ref, v_ref, rim_ref, par_ref, taps_ref, y_ref, s_ref, d_ref, p_scr, y_scr
):
    rows = k_ref.shape[0]
    for block in range(SUBLANES):
        lanes = block_lanes(block)
        mixes = [
            short_mix(
                ref[:, lanes].astype(jnp.float32),
                rim_rows(rim_ref, feature, lanes),
                tap_rows(taps_ref, feature, lanes),
            )
            for feature, ref in ((1, k_ref), (2, v_ref))
        ]
        product = (mixes[0] * mixes[1]).astype(jnp.bfloat16).astype(jnp.float32)
        p_scr[pl.ds(block, rows, SUBLANES), :] = product
    decay = [jnp.exp(-par_ref[pl.ds(mode, SUBLANES, 2 * modes), :]) for mode in range(modes)]
    residue = [par_ref[pl.ds(modes + mode, SUBLANES, 2 * modes), :] for mode in range(modes)]

    def body(position, states):
        here = pl.ds(pl.multiple_of(position * SUBLANES, SUBLANES), SUBLANES)
        product = p_scr[here, :]
        states = tuple(state * rate + product for state, rate in zip(states, decay))
        terms = [state * weight for state, weight in zip(states, residue)]
        while len(terms) > 1:
            terms = [left + right for left, right in zip(terms[::2], terms[1::2])]
        y_scr[here, :] = terms[0]
        return states

    zero = jnp.zeros((SUBLANES, LANES), jnp.float32)
    states = lax.fori_loop(0, rows, body, (zero,) * modes, unroll=4)
    for mode in range(modes):
        s_ref[pl.ds(mode, SUBLANES, modes), :] = states[mode]
    for block in range(SUBLANES):
        rate = par_ref[2 * block * modes : (2 * block + 1) * modes, :]
        d_ref[block * modes : (block + 1) * modes, :] = jnp.exp(-rate * rows)
    for block in range(SUBLANES):
        y_ref[:, block_lanes(block)] = y_scr[pl.ds(block, rows, SUBLANES), :]


def output_kernel(
    modes,
    q_ref,
    y_ref,
    rim_ref,
    par_ref,
    decay_ref,
    enter_ref,
    enter_first_ref,
    other_ref,
    taps_ref,
    out_ref,
):
    second = lax.axis_index("ctx") % 2 == 1
    rows = q_ref.shape[0]
    step = lax.broadcasted_iota(jnp.int32, (SUBLANES, LANES), 0).astype(jnp.float32) + 1.0

    def body(block, nothing):
        lanes = pl.ds(pl.multiple_of(block * LANES, LANES), LANES)
        rate = par_ref[pl.ds(pl.multiple_of(2 * block * modes, SUBLANES), modes), :]
        residue = par_ref[pl.ds(pl.multiple_of((2 * block + 1) * modes, SUBLANES), modes), :]
        here = pl.ds(pl.multiple_of(block * modes, SUBLANES), modes)
        after_first = decay_ref[here, :] * enter_ref[here, :] + other_ref[here, :]
        entering = jnp.where(second, after_first, enter_first_ref[here, :])
        weighted = residue * entering
        eight = jnp.exp(-rate * SUBLANES)
        terms = [
            weighted[mode : mode + 1] * jnp.exp(-rate[mode : mode + 1] * step)
            for mode in range(modes)
        ]
        eights = [jnp.broadcast_to(eight[mode : mode + 1], terms[0].shape) for mode in range(modes)]
        added = []
        for start in range(0, rows, SUBLANES):
            sums = list(terms)
            while len(sums) > 1:
                sums = [left + right for left, right in zip(sums[::2], sums[1::2])]
            added.append(sums[0])
            if start + SUBLANES < rows:
                terms = [term * decay for term, decay in zip(terms, eights)]
        smoothed = y_ref[:, lanes] + jnp.concatenate(added, 0)
        smoothed = smoothed.astype(jnp.bfloat16).astype(jnp.float32)
        mix = short_mix(
            q_ref[:, lanes].astype(jnp.float32),
            rim_rows(rim_ref, 0, lanes),
            tap_rows(taps_ref, 0, lanes),
        )
        out_ref[:, lanes] = (mix * smoothed).astype(out_ref.dtype)
        return nothing

    lax.fori_loop(0, SUBLANES, body, 0)


def convolution(hyena_q, hyena_k, hyena_v, short_filter, residue, decay_rate):
    rows, channels = hyena_q.shape
    devices = lax.axis_size("ctx")
    modes = residue.shape[1]
    own_blocks = residue.shape[0] // LANES
    blocks = channels // LANES
    groups = blocks // SUBLANES
    width = SUBLANES * LANES
    end = rows // 16 - 1
    par_rows = 2 * own_blocks * modes
    feature_spec = pl.BlockSpec((rows, width), lambda group: (0, group))
    rim_spec = pl.BlockSpec((8, width), lambda group: (0, group))
    par_spec = pl.BlockSpec((2 * SUBLANES * modes, LANES), lambda group: (group, 0))
    taps_spec = pl.BlockSpec((TAPS, TAPS, width), lambda group: (0, 0, group))
    positions = pltpu.VMEM((rows * SUBLANES, LANES), jnp.float32)

    def first_part():
        own_par, rim = pl.pallas_call(
            conv_pack_kernel,
            grid=(1,),
            in_specs=[pl.BlockSpec((modes, residue.shape[0]), lambda step: (0, 0))] * 2
            + [pl.BlockSpec((16, channels), lambda step: (end, 0))] * 3,
            out_specs=[
                pl.BlockSpec((devices, par_rows, LANES), lambda step: (0, 0, 0)),
                pl.BlockSpec((8, channels), lambda step: (0, 0)),
            ],
            out_shape=[
                jax.ShapeDtypeStruct((devices, par_rows, LANES), jnp.float32),
                jax.ShapeDtypeStruct((8, channels), jnp.float32),
            ],
            compiler_params=params(),
            cost_estimate=cost(1),
            name="conv_pack",
        )(decay_rate.T, residue.T, hyena_q, hyena_k, hyena_v)
        rim = lax.ppermute(rim, "ctx", [(index, index + 1) for index in range(devices - 1)])
        own_par = after(own_par, rim)
        par = lax.all_to_all(own_par, "ctx", split_axis=0, concat_axis=0, tiled=True)
        return rim, par.reshape(devices * par_rows, LANES)

    def state_part(rim, par):
        state_spec = pl.BlockSpec((SUBLANES * modes, LANES), lambda group: (group, 0))
        return pl.pallas_call(
            functools.partial(state_kernel, modes),
            grid=(groups,),
            in_specs=[feature_spec, feature_spec, rim_spec, par_spec, taps_spec],
            out_specs=[feature_spec, state_spec, state_spec],
            out_shape=[
                jax.ShapeDtypeStruct((rows, channels), jnp.float32),
                jax.ShapeDtypeStruct((blocks * modes, LANES), jnp.float32),
                jax.ShapeDtypeStruct((blocks * modes, LANES), jnp.float32),
            ],
            scratch_shapes=[positions, positions],
            compiler_params=params(),
            cost_estimate=cost(9),
            name="conv_state",
        )(hyena_k, hyena_v, rim, par, short_filter)
    def last_part(local_result, rim, par, decay, entering, entering_first, other):
        state_spec = pl.BlockSpec((SUBLANES * modes, LANES), lambda group: (group, 0))
        return pl.pallas_call(
            functools.partial(output_kernel, modes),
            grid=(groups,),
            in_specs=[feature_spec, feature_spec, rim_spec, par_spec]
            + [state_spec] * 4
            + [taps_spec],
            out_specs=feature_spec,
            out_shape=jax.ShapeDtypeStruct((rows, channels), jnp.bfloat16),
            compiler_params=params(),
            cost_estimate=cost(6),
            name="conv_output",
        )(
            hyena_q,
            local_result,
            rim,
            par,
            decay,
            entering,
            entering_first,
            other,
            short_filter,
        )

    return first_part, state_part, last_part


def among(me, members):
    return functools.reduce(jnp.logical_or, [me == member for member in members])


def plan_moves(devices):
    quads = devices // 4
    transfers = [[(devices - 1, devices - 3)]]
    for distance in range(1, quads):
        if distance > len(transfers):
            transfers.append([])
        for quad in range(distance, quads):
            target = 4 * (quad - distance) + 2
            transfers[distance - 1] += [(4 * quad, target), (4 * quad + 2, target + 1)]
    return transfers


def soft(query, keys, values, mask=None):
    scores = lax.dot_general(
        query, keys, (((1,), (1,)), ((), ())), preferred_element_type=jnp.float32
    )
    if mask is not None:
        scores = jnp.where(mask, scores, NEGATIVE)
    top = jnp.max(scores, axis=1, keepdims=True) * EXP_SCALE
    expo = jnp.exp2(scores * EXP_SCALE - top).astype(jnp.bfloat16)
    mixed = jnp.dot(expo, values, preferred_element_type=jnp.float32)
    total = mixed[:, HEAD_DIM:]
    return mixed[:, :HEAD_DIM] / total, top + jnp.log2(total)


def pack_kernel(gathers, askers, asked, widths, starts, q_ref, qs_ref, k_ref, v_ref, *rest):
    count = len(widths)
    key_outs, query_outs = rest[:count], rest[count : count + asked]
    stages, in_sems, out_sems = rest[count + asked : -2], rest[-2], rest[-1]
    me = lax.axis_index("ctx")
    odd = me % 2

    def run(pairs):
        loads = [
            pltpu.make_async_copy(source, stage, in_sems.at[index])
            for index, ((source, _), stage) in enumerate(zip(pairs, stages))
        ]
        stores = [
            pltpu.make_async_copy(stage, target, out_sems.at[index])
            for index, ((_, target), stage) in enumerate(zip(pairs, stages))
        ]
        for load in loads:
            load.start()
        for load, store in zip(loads, stores):
            load.wait()
            store.start()
        for store in stores:
            store.wait()

    def cut(ref, chunk):
        return ref.at[:, pl.ds(starts[chunk], widths[chunk])]

    if gathers:

        @pl.when(among(me, gathers))
        def _():
            run(
                [
                    (cut(ref, chunk), key_outs[chunk].at[which])
                    for chunk in range(count)
                    for which, ref in enumerate((k_ref, v_ref))
                ]
            )

    @pl.when(among(me, askers))
    def _():
        run(
            [
                (cut(ref, chunk), query_outs[chunk].at[half])
                for chunk in range(asked)
                for ref, half in ((q_ref, odd), (qs_ref, 1 - odd))
            ]
        )


def as_rows(columns):
    lanes = lax.broadcasted_iota(jnp.int32, columns[0].shape, 1)
    sums = jnp.zeros_like(columns[0])
    for index, column in enumerate(columns):
        sums = jnp.where(lanes == index, column, sums)
    return jnp.transpose(sums)[:SUBLANES]


def as_columns(part):
    fill = jnp.zeros((LANES - part.shape[0], part.shape[1]), jnp.float32)
    return jnp.transpose(jnp.concatenate([part, fill], 0))


def partial_kernel(transfers, upper, natural, asking, onto, *refs):
    count = len(transfers)
    out_ref = refs[-1]
    if asking:
        next_refs = refs[7 + count : 9 + count]
        refs = refs[: 7 + count] + refs[9 + count :]
    q_ref, k_ref, v_ref, kp_ref, vp_ref, g_ref, gp_ref = refs[:7]
    ask_refs = refs[7 : 7 + count]
    own_ref, lse_ref = refs[7 + count + onto : 9 + count + onto]
    answer_refs = refs[9 + count + onto : -1]
    me = lax.axis_index("ctx")
    rows = q_ref.shape[0]
    heads = q_ref.shape[1] // HEAD_DIM
    half_rows = heads * rows + TAIL

    def key_value(head, with_quad):
        cut = block_lanes(head)
        keys = [kp_ref[:, cut], k_ref[:, cut]]
        values = [vp_ref[:, cut], v_ref[:, cut]]
        if with_quad:
            keys = [g_ref[0, :, cut], gp_ref[0, :, cut]] + keys
            values = [g_ref[1, :, cut], gp_ref[1, :, cut]] + values
        values = jnp.concatenate(values, 0)
        return jnp.concatenate(keys, 0), jnp.concatenate([values, jnp.ones_like(values)], 1)

    def run(with_quad):
        key_count = rows * (4 if with_quad else 2)
        row = lax.broadcasted_iota(jnp.int32, (rows, key_count), 0)
        column = lax.broadcasted_iota(jnp.int32, (rows, key_count), 1)
        column = column - (key_count - 2 * rows)
        partner_limit = jnp.where(me % 2 == 1, rows, 0)
        mask = (column < partner_limit) | ((column >= rows) & (column - rows <= row))
        sums = []
        for head in range(heads):
            keys, values = key_value(head, with_quad)
            mixed, lse = soft(q_ref[:, block_lanes(head)], keys, values, mask)
            own_ref[:, block_lanes(head)] = mixed
            out_ref[:, block_lanes(head)] = mixed.astype(out_ref.dtype)
            sums.append(lse)
        lse_ref[...] = as_rows(sums)

        def answer(index):
            sums = [[], []]
            for head in range(heads):
                keys, values = key_value(head, with_quad)
                if natural:
                    query = ask_refs[index][:, :, block_lanes(head)].reshape(2 * rows, HEAD_DIM)
                else:
                    halves = [half * half_rows + head * rows for half in range(2)]
                    query = jnp.concatenate(
                        [ask_refs[index][start : start + rows, :] for start in halves], 0
                    )
                mixed, lse = soft(query, keys, values)
                for half in range(2):
                    cut = slice(half * rows, (half + 1) * rows)
                    start = half * half_rows + head * rows
                    answer_refs[index][start : start + rows, :] = mixed[cut].astype(jnp.bfloat16)
                    sums[half].append(lse[cut])
            for half in range(2):
                start = half * half_rows + heads * rows
                lse = as_rows(sums[half])
                first = lse.astype(jnp.bfloat16).astype(jnp.float32)
                second = (lse - first).astype(jnp.bfloat16).astype(jnp.float32)
                third = lse - first - second
                tail = jnp.concatenate([first, second, third, jnp.zeros_like(lse)], 0)
                answer_refs[index][start : start + TAIL, :] = tail.astype(jnp.bfloat16)

        for index, pairs in enumerate(transfers):
            asked = [target for _, target in pairs if (target in upper) == with_quad]
            if asked:
                pl.when(among(me, asked))(functools.partial(answer, index))

    if upper:
        pl.when(among(me, upper))(functools.partial(run, True))
        pl.when(jnp.logical_not(among(me, upper)))(functools.partial(run, False))
    else:
        run(False)

    if asking:
        for index, pairs in enumerate(transfers):

            @pl.when(among(me, [source for source, _ in pairs]))
            def _():
                for ref, half in zip(next_refs, (me % 2, 1 - me % 2)):
                    for head in range(heads):
                        start = pl.multiple_of(half * half_rows + head * rows, TAIL)
                        answer_refs[index][pl.ds(start, rows), :] = ref[:, block_lanes(head)]


def merge_kernel(transfers, steps, start, own_hbm, lse_hbm, *refs):
    count = 2 * len(transfers)
    others_hbm, out_hbm = refs[:count], refs[count + 1]
    own_ref, lse_ref, *other_refs = refs[count + 2 : 2 * count + 4]
    out_ref, sems = refs[-2:]
    me = lax.axis_index("ctx")
    odd = me % 2
    rows, width = own_ref.shape
    heads = HEADS_PER_STEP
    half_rows = heads * rows + TAIL
    returned = []
    for pairs in transfers:
        members = [source for source, _ in pairs]
        returned += [members, [member ^ 1 for member in members]]

    @pl.when(among(me, sorted(set(sum(returned, [])))))
    def _():
        loads = [(own_hbm, own_ref), (lse_hbm, lse_ref)]
        for hbm, ref in zip(others_hbm, other_refs):
            for step in range(steps):
                half = pl.ds(pl.multiple_of((2 * step + odd) * half_rows, TAIL), half_rows)
                loads.append((hbm.at[half, :], ref.at[step]))
        copies = [
            pltpu.make_async_copy(source, target, sems.at[index])
            for index, (source, target) in enumerate(loads)
        ]
        for copy in copies:
            copy.start()
        for copy in copies:
            copy.wait()
        valid = [among(me, members) for members in returned]
        for step in range(steps):
            logs = [lse_ref[step * SUBLANES : (step + 1) * SUBLANES, :]]
            for index, ref in enumerate(other_refs):
                tail = ref[step, heads * rows :, :].astype(jnp.float32)
                parts = [tail[part * SUBLANES : (part + 1) * SUBLANES] for part in range(3)]
                logs.append(jnp.where(valid[index], parts[0] + parts[1] + parts[2], NEGATIVE))
            top = functools.reduce(jnp.maximum, logs)
            weights = [jnp.exp2(part - top) for part in logs]
            total = functools.reduce(jnp.add, weights)
            shares = [as_columns(weight / total) for weight in weights]
            for head in range(heads):
                cut = block_lanes(step * heads + head)
                mixed = [own_ref[:, cut]]
                for index, ref in enumerate(other_refs):
                    part = ref[step, head * rows : (head + 1) * rows, :].astype(jnp.float32)
                    mixed.append(jnp.where(valid[index], part, 0.0))
                terms = [part * share[:, head : head + 1] for part, share in zip(mixed, shares)]
                out_ref[:, cut] = functools.reduce(jnp.add, terms).astype(out_ref.dtype)
        store = pltpu.make_async_copy(
            out_ref, out_hbm.at[:, pl.ds(start, width)], sems.at[len(copies)]
        )
        store.start()
        store.wait()


def after(array, *others):
    return lax.optimization_barrier((array, *others))[0]


def attend(query, key, value, conv):
    rows, columns = query.shape
    devices = lax.axis_size("ctx")
    quads = devices // 4
    transfers = plan_moves(devices)
    step_width = HEADS_PER_STEP * HEAD_DIM
    chunks = len(CHUNK_STEPS)
    first_steps = [sum(CHUNK_STEPS[:chunk]) for chunk in range(chunks)]
    widths = [steps * step_width for steps in CHUNK_STEPS]
    starts = [step * step_width for step in first_steps]
    upper = [4 * quad + 2 + core for quad in range(quads - 1) for core in range(2)]
    gathers = [(who - 2, who) for who in upper]
    askers = sorted({source for pairs in transfers for source, _ in pairs})
    swap = [(index, index ^ 1) for index in range(devices)]

    query_swapped = lax.ppermute(query, "ctx", swap)
    key_swapped = lax.ppermute(key, "ctx", swap)
    value_swapped = lax.ppermute(value, "ctx", swap)

    both_ways = chunks > LAG and all(
        not {source for source, _ in pairs} & {target for _, target in pairs}
        for pairs in transfers
    )
    asked = LAG if both_ways else chunks

    def pack():
        hbm = pl.BlockSpec(memory_space=pl.ANY)
        shapes = [jax.ShapeDtypeStruct((2, rows, width), jnp.bfloat16) for width in widths]
        outs = pl.pallas_call(
            functools.partial(
                pack_kernel,
                [source for source, _ in gathers],
                askers,
                asked,
                widths,
                starts,
            ),
            in_specs=[hbm] * 4,
            out_specs=[hbm] * (chunks + asked),
            out_shape=shapes + shapes[:asked],
            scratch_shapes=[
                pltpu.VMEM((rows, width), jnp.bfloat16) for width in widths for _ in range(2)
            ]
            + [pltpu.SemaphoreType.DMA((2 * chunks,))] * 2,
            compiler_params=params(),
            cost_estimate=cost(1),
            name="att_pack",
        )(query, query_swapped, key, value)
        return outs[:chunks], outs[chunks:]

    half_rows = HEADS_PER_STEP * rows + TAIL
    hbm = pl.BlockSpec(memory_space=pl.ANY)
    def partial(chunk, ask, quad, result):
        steps, first = CHUNK_STEPS[chunk], first_steps[chunk]
        whole_spec = pl.BlockSpec((rows, step_width), lambda step, first=first: (0, first + step))
        chunk_spec = pl.BlockSpec((rows, step_width), lambda step: (0, step))
        pair_spec = pl.BlockSpec((2, rows, step_width), lambda step: (0, 0, step))
        lse_spec = pl.BlockSpec((SUBLANES, LANES), lambda step: (step, 0))
        answer_spec = pl.BlockSpec((2 * half_rows, LANES), lambda step: (step, 0))
        answer_shape = jax.ShapeDtypeStruct((2 * half_rows * steps, LANES), jnp.bfloat16)
        asking = both_ways and chunk + LAG < chunks
        natural = chunk < asked
        operands = [query, key, value, key_swapped, value_swapped, *quad, *ask]
        specs = [whole_spec] * 5 + [pair_spec] * 2
        specs += [pair_spec if natural else answer_spec] * len(transfers)
        if asking:
            later = first_steps[chunk + LAG]
            operands += [query, query_swapped]
            specs += [
                pl.BlockSpec((rows, step_width), lambda step, later=later: (0, later + step))
            ] * 2
        aliases = {}
        if result is not None:
            aliases = {len(operands): 2 + len(transfers)}
            operands.append(result)
            specs.append(hbm)
        return pl.pallas_call(
            functools.partial(partial_kernel, transfers, upper, natural, asking, len(aliases)),
            grid=(steps,),
            in_specs=specs,
            out_specs=[chunk_spec, lse_spec] + [answer_spec] * len(transfers) + [whole_spec],
            out_shape=[
                jax.ShapeDtypeStruct((rows, widths[chunk]), jnp.float32),
                jax.ShapeDtypeStruct((SUBLANES * steps, LANES), jnp.float32),
            ]
            + [answer_shape] * len(transfers)
            + [jax.ShapeDtypeStruct((rows, columns), jnp.bfloat16)],
            input_output_aliases=aliases,
            compiler_params=params(),
            cost_estimate=cost(4),
            name="att_partial",
        )(*operands)

    def merge(chunk, parts, result):
        steps = CHUNK_STEPS[chunk]
        count = 2 * len(transfers)
        return pl.pallas_call(
            functools.partial(merge_kernel, transfers, steps, starts[chunk]),
            in_specs=[hbm] * (len(parts) + 1),
            out_specs=hbm,
            out_shape=jax.ShapeDtypeStruct((rows, columns), jnp.bfloat16),
            input_output_aliases={len(parts): 0},
            scratch_shapes=[
                pltpu.VMEM((rows, widths[chunk]), jnp.float32),
                pltpu.VMEM((SUBLANES * steps, LANES), jnp.float32),
            ]
            + [pltpu.VMEM((steps, half_rows, LANES), jnp.bfloat16)] * count
            + [
                pltpu.VMEM((rows, widths[chunk]), jnp.bfloat16),
                pltpu.SemaphoreType.DMA((3 + count * steps,)),
            ],
            compiler_params=params(),
            cost_estimate=cost(2),
            name="att_merge",
        )(*parts, result)
    def exchange(operands, ways):
        moved = []
        for operand, pairs in zip(operands, transfers):
            back = [(target, source) for source, target in pairs]
            moves = pairs if ways == 1 else back if ways == -1 else pairs + back
            moved.append(lax.ppermute(operand, "ctx", moves))
        return moved

    def swapped(array):
        return lax.ppermute(array, "ctx", swap)

    def with_swapped(arrays):
        return [item for array in arrays for item in (array, swapped(array))]

    conv_first, conv_state, conv_last = conv
    rim, par = conv_first()
    key_packs, query_packs = pack()
    rim, key_packs, query_packs = lax.optimization_barrier((rim, key_packs, query_packs))

    asks = [exchange([query_packs[0]] * len(transfers), 1)]
    quad = lax.ppermute(key_packs[0], "ctx", gathers)
    local_result, state, decay = conv_state(rim, par)
    live = (asks[0], quad, local_result, state, decay, key_packs[1:], query_packs[1:])
    asks[0], quad, local_result, state, decay, key_packs, query_packs = (
        lax.optimization_barrier(live)
    )

    other = total = entering = answers = result = None
    hops = devices // 2 - 1
    hop_pairs = [(index, index + 2) for index in range(1, devices - 2, 2)]

    def hop(entering):
        leaving = total if entering is None else total + decay * decay * entering
        return lax.ppermute(leaving, "ctx", hop_pairs)

    owns, waiting = [], []
    for chunk in range(chunks):
        last = chunk == chunks - 1
        next_ask = next_quad = back = None
        if not last:
            next_quad = lax.ppermute(key_packs[chunk], "ctx", gathers)
        if not last and chunk + 1 < asked:
            next_ask = exchange([query_packs[chunk]] * len(transfers), 1)
        if chunk:
            both = next_ask is None and not last
            back = exchange(answers, 0 if both else -1)
            if both:
                next_ask = back
        if chunk == 0:
            other = swapped(state)
            total = state + decay * other
        if hops:
            entering = hop(entering)
            hops -= 1
        parts = with_swapped(waiting[0]) if waiting else None
        quad_swapped = swapped(quad)
        own, lse, *answers, result = partial(chunk, asks[chunk], (quad, quad_swapped), result)
        owns.append([own, lse])
        if parts:
            result = merge(chunk - 2, owns[chunk - 2] + parts, result)
            waiting = waiting[1:]
        if back:
            waiting.append(back)
        live = (next_ask, next_quad, waiting, answers, result, total, entering, owns[chunk])
        next_ask, quad, waiting, answers, result, total, entering, owns[chunk] = (
            lax.optimization_barrier(live)
        )
        asks.append(next_ask)

    back = exchange(answers, -1)
    for _ in range(hops):
        entering = hop(entering)
    hyena_out = conv_last(
        local_result, rim, par, decay, entering, swapped(entering), other
    )
    for chunk, arrivals in zip(range(chunks - 1 - len(waiting), chunks - 1), waiting):
        result = merge(chunk, owns[chunk] + with_swapped(arrivals), result)
    back, hyena_out, result = lax.optimization_barrier((back, hyena_out, result))
    result = merge(chunks - 1, owns[-1] + with_swapped(back), result)
    return hyena_out, result


def local(
    hyena_q, hyena_k, hyena_v, short_filter, residue, decay_rate, att_query, att_key, att_value
):
    conv = convolution(hyena_q, hyena_k, hyena_v, short_filter, residue, decay_rate)
    return attend(att_query, att_key, att_value, conv)


def solution(mesh):
    rows = P(("dp", "ctx"), None)
    shared = P("ctx", None)
    return jax.shard_map(
        local,
        mesh=mesh,
        in_specs=(rows, rows, rows, P(), shared, shared, rows, rows, rows),
        out_specs=(rows, rows),
        check_vma=False,
    )
```

```python
import functools
import math

import jax
import jax.numpy as jnp
from jax import lax
from jax.experimental import pallas as pl
from jax.experimental.pallas import tpu as pltpu
from jax.sharding import PartitionSpec as P

HEAD_DIM = 128
LANES = 128
SUBLANES = 8
TAIL = 4 * SUBLANES
TAPS = 3
HEADS_PER_STEP = 4
CHUNK_STEPS = (2, 2, 2, 2)
LAG = 2
NEGATIVE = -1e30
EXP_SCALE = HEAD_DIM**-0.5 * math.log2(math.e)
VMEM_LIMIT = 255 * 1024 * 256


def params(**kwargs):
    return pltpu.CompilerParams(vmem_limit_bytes=VMEM_LIMIT, **kwargs)


def cost(microseconds):
    return pl.CostEstimate(
        flops=microseconds * 10**9, bytes_accessed=2**20, transcendentals=0
    )


def block_lanes(block):
    return slice(block * LANES, (block + 1) * LANES)


def conv_pack_kernel(rate_ref, residue_ref, q_ref, k_ref, v_ref, par_ref, rim_ref):
    modes = rate_ref.shape[0]
    for block in range(rate_ref.shape[1] // LANES):
        for which, ref in enumerate((rate_ref, residue_ref)):
            start = (2 * block + which) * modes
            for device in range(par_ref.shape[0]):
                par_ref[device, start : start + modes, :] = ref[:, block_lanes(block)]
    for feature, ref in enumerate((q_ref, k_ref, v_ref)):
        last = ref[...].astype(jnp.float32)[ref.shape[0] - 2 :]
        rim_ref[2 * feature : 2 * feature + 2, :] = last
    rim_ref[2 * TAPS :, :] = jnp.zeros((2, rim_ref.shape[1]), jnp.float32)


def rim_rows(rim_ref, feature, lanes):
    return [rim_ref[pl.ds(2 * feature + row, 1), lanes] for row in range(2)]


def short_mix(feature, rim, taps):
    two_before, one_before = rim
    row = lax.broadcasted_iota(jnp.int32, feature.shape, 0)
    one = jnp.where(row == 0, one_before, pltpu.roll(feature, 1, 0))
    two = jnp.where(row == 0, two_before, jnp.where(row == 1, one_before, pltpu.roll(feature, 2, 0)))
    return taps[0] * feature + taps[1] * one + taps[2] * two


def tap_rows(taps_ref, feature, lanes):
    return [taps_ref[feature, pl.ds(tap, 1), lanes] for tap in range(TAPS)]


def state_kernel(
    modes, k_ref, v_ref, rim_ref, par_ref, taps_ref, y_ref, s_ref, d_ref, p_scr, y_scr
):
    rows = k_ref.shape[0]
    for block in range(SUBLANES):
        lanes = block_lanes(block)
        mixes = [
            short_mix(
                ref[:, lanes].astype(jnp.float32),
                rim_rows(rim_ref, feature, lanes),
                tap_rows(taps_ref, feature, lanes),
            )
            for feature, ref in ((1, k_ref), (2, v_ref))
        ]
        product = (mixes[0] * mixes[1]).astype(jnp.bfloat16).astype(jnp.float32)
        p_scr[pl.ds(block, rows, SUBLANES), :] = product
    decay = [jnp.exp(-par_ref[pl.ds(mode, SUBLANES, 2 * modes), :]) for mode in range(modes)]
    residue = [par_ref[pl.ds(modes + mode, SUBLANES, 2 * modes), :] for mode in range(modes)]

    def body(position, states):
        here = pl.ds(pl.multiple_of(position * SUBLANES, SUBLANES), SUBLANES)
        product = p_scr[here, :]
        states = tuple(state * rate + product for state, rate in zip(states, decay))
        terms = [state * weight for state, weight in zip(states, residue)]
        while len(terms) > 1:
            terms = [left + right for left, right in zip(terms[::2], terms[1::2])]
        y_scr[here, :] = terms[0]
        return states

    zero = jnp.zeros((SUBLANES, LANES), jnp.float32)
    states = lax.fori_loop(0, rows, body, (zero,) * modes, unroll=4)
    for mode in range(modes):
        s_ref[pl.ds(mode, SUBLANES, modes), :] = states[mode]
    for block in range(SUBLANES):
        rate = par_ref[2 * block * modes : (2 * block + 1) * modes, :]
        d_ref[block * modes : (block + 1) * modes, :] = jnp.exp(-rate * rows)
    for block in range(SUBLANES):
        y_ref[:, block_lanes(block)] = y_scr[pl.ds(block, rows, SUBLANES), :]


def output_kernel(
    modes,
    q_ref,
    y_ref,
    rim_ref,
    par_ref,
    decay_ref,
    enter_ref,
    enter_first_ref,
    other_ref,
    taps_ref,
    out_ref,
):
    second = lax.axis_index("ctx") % 2 == 1
    rows = q_ref.shape[0]
    step = lax.broadcasted_iota(jnp.int32, (SUBLANES, LANES), 0).astype(jnp.float32) + 1.0

    def body(block, nothing):
        lanes = pl.ds(pl.multiple_of(block * LANES, LANES), LANES)
        rate = par_ref[pl.ds(pl.multiple_of(2 * block * modes, SUBLANES), modes), :]
        residue = par_ref[pl.ds(pl.multiple_of((2 * block + 1) * modes, SUBLANES), modes), :]
        here = pl.ds(pl.multiple_of(block * modes, SUBLANES), modes)
        after_first = decay_ref[here, :] * enter_ref[here, :] + other_ref[here, :]
        entering = jnp.where(second, after_first, enter_first_ref[here, :])
        weighted = residue * entering
        eight = jnp.exp(-rate * SUBLANES)
        terms = [
            weighted[mode : mode + 1] * jnp.exp(-rate[mode : mode + 1] * step)
            for mode in range(modes)
        ]
        eights = [jnp.broadcast_to(eight[mode : mode + 1], terms[0].shape) for mode in range(modes)]
        added = []
        for start in range(0, rows, SUBLANES):
            sums = list(terms)
            while len(sums) > 1:
                sums = [left + right for left, right in zip(sums[::2], sums[1::2])]
            added.append(sums[0])
            if start + SUBLANES < rows:
                terms = [term * decay for term, decay in zip(terms, eights)]
        smoothed = y_ref[:, lanes] + jnp.concatenate(added, 0)
        smoothed = smoothed.astype(jnp.bfloat16).astype(jnp.float32)
        mix = short_mix(
            q_ref[:, lanes].astype(jnp.float32),
            rim_rows(rim_ref, 0, lanes),
            tap_rows(taps_ref, 0, lanes),
        )
        out_ref[:, lanes] = (mix * smoothed).astype(out_ref.dtype)
        return nothing

    lax.fori_loop(0, SUBLANES, body, 0)


def convolution(hyena_q, hyena_k, hyena_v, short_filter, residue, decay_rate):
    rows, channels = hyena_q.shape
    devices = lax.axis_size("ctx")
    modes = residue.shape[1]
    own_blocks = residue.shape[0] // LANES
    blocks = channels // LANES
    groups = blocks // SUBLANES
    width = SUBLANES * LANES
    end = rows // 16 - 1
    par_rows = 2 * own_blocks * modes
    feature_spec = pl.BlockSpec((rows, width), lambda group: (0, group))
    rim_spec = pl.BlockSpec((8, width), lambda group: (0, group))
    par_spec = pl.BlockSpec((2 * SUBLANES * modes, LANES), lambda group: (group, 0))
    taps_spec = pl.BlockSpec((TAPS, TAPS, width), lambda group: (0, 0, group))
    positions = pltpu.VMEM((rows * SUBLANES, LANES), jnp.float32)

    def first_part():
        own_par, rim = pl.pallas_call(
            conv_pack_kernel,
            grid=(1,),
            in_specs=[pl.BlockSpec((modes, residue.shape[0]), lambda step: (0, 0))] * 2
            + [pl.BlockSpec((16, channels), lambda step: (end, 0))] * 3,
            out_specs=[
                pl.BlockSpec((devices, par_rows, LANES), lambda step: (0, 0, 0)),
                pl.BlockSpec((8, channels), lambda step: (0, 0)),
            ],
            out_shape=[
                jax.ShapeDtypeStruct((devices, par_rows, LANES), jnp.float32),
                jax.ShapeDtypeStruct((8, channels), jnp.float32),
            ],
            compiler_params=params(),
            cost_estimate=cost(1),
            name="conv_pack",
        )(decay_rate.T, residue.T, hyena_q, hyena_k, hyena_v)
        rim = lax.ppermute(rim, "ctx", [(index, index + 1) for index in range(devices - 1)])
        return rim, own_par

    def shared_part(own_par):
        par = lax.all_to_all(own_par, "ctx", split_axis=0, concat_axis=0, tiled=True)
        return par.reshape(devices * par_rows, LANES)

    def state_part(rim, par):
        state_spec = pl.BlockSpec((SUBLANES * modes, LANES), lambda group: (group, 0))
        return pl.pallas_call(
            functools.partial(state_kernel, modes),
            grid=(groups,),
            in_specs=[feature_spec, feature_spec, rim_spec, par_spec, taps_spec],
            out_specs=[feature_spec, state_spec, state_spec],
            out_shape=[
                jax.ShapeDtypeStruct((rows, channels), jnp.float32),
                jax.ShapeDtypeStruct((blocks * modes, LANES), jnp.float32),
                jax.ShapeDtypeStruct((blocks * modes, LANES), jnp.float32),
            ],
            scratch_shapes=[positions, positions],
            compiler_params=params(),
            cost_estimate=cost(9),
            name="conv_state",
        )(hyena_k, hyena_v, rim, par, short_filter)
    def last_part(local_result, rim, par, decay, entering, entering_first, other):
        state_spec = pl.BlockSpec((SUBLANES * modes, LANES), lambda group: (group, 0))
        return pl.pallas_call(
            functools.partial(output_kernel, modes),
            grid=(groups,),
            in_specs=[feature_spec, feature_spec, rim_spec, par_spec]
            + [state_spec] * 4
            + [taps_spec],
            out_specs=feature_spec,
            out_shape=jax.ShapeDtypeStruct((rows, channels), jnp.bfloat16),
            compiler_params=params(),
            cost_estimate=cost(6),
            name="conv_output",
        )(
            hyena_q,
            local_result,
            rim,
            par,
            decay,
            entering,
            entering_first,
            other,
            short_filter,
        )

    return first_part, shared_part, state_part, last_part


def among(me, members):
    return functools.reduce(jnp.logical_or, [me == member for member in members])


def plan_moves(devices):
    quads = devices // 4
    transfers = [[(devices - 1, devices - 3)]]
    for distance in range(1, quads):
        if distance > len(transfers):
            transfers.append([])
        for quad in range(distance, quads):
            target = 4 * (quad - distance) + 2
            transfers[distance - 1] += [(4 * quad, target), (4 * quad + 2, target + 1)]
    return transfers


def soft(query, keys, values, mask=None):
    scores = lax.dot_general(
        query, keys, (((1,), (1,)), ((), ())), preferred_element_type=jnp.float32
    )
    if mask is not None:
        scores = jnp.where(mask, scores, NEGATIVE)
    top = jnp.max(scores, axis=1, keepdims=True) * EXP_SCALE
    expo = jnp.exp2(scores * EXP_SCALE - top).astype(jnp.bfloat16)
    mixed = jnp.dot(expo, values, preferred_element_type=jnp.float32)
    total = mixed[:, HEAD_DIM:]
    return mixed[:, :HEAD_DIM] / total, top + jnp.log2(total)


def pack_kernel(gathers, askers, asked, widths, starts, q_ref, qs_ref, k_ref, v_ref, *rest):
    count = len(widths)
    key_outs, query_outs = rest[:count], rest[count : count + asked]
    stages, in_sems, out_sems = rest[count + asked : -2], rest[-2], rest[-1]
    me = lax.axis_index("ctx")
    odd = me % 2

    def run(pairs):
        loads = [
            pltpu.make_async_copy(source, stage, in_sems.at[index])
            for index, ((source, _), stage) in enumerate(zip(pairs, stages))
        ]
        stores = [
            pltpu.make_async_copy(stage, target, out_sems.at[index])
            for index, ((_, target), stage) in enumerate(zip(pairs, stages))
        ]
        for load in loads:
            load.start()
        for load, store in zip(loads, stores):
            load.wait()
            store.start()
        for store in stores:
            store.wait()

    def cut(ref, chunk):
        return ref.at[:, pl.ds(starts[chunk], widths[chunk])]

    if gathers:

        @pl.when(among(me, gathers))
        def _():
            run(
                [
                    (cut(ref, chunk), key_outs[chunk].at[which])
                    for chunk in range(count)
                    for which, ref in enumerate((k_ref, v_ref))
                ]
            )

    @pl.when(among(me, askers))
    def _():
        run(
            [
                (cut(ref, chunk), query_outs[chunk].at[half])
                for chunk in range(asked)
                for ref, half in ((q_ref, odd), (qs_ref, 1 - odd))
            ]
        )


def as_rows(columns):
    lanes = lax.broadcasted_iota(jnp.int32, columns[0].shape, 1)
    sums = jnp.zeros_like(columns[0])
    for index, column in enumerate(columns):
        sums = jnp.where(lanes == index, column, sums)
    return jnp.transpose(sums)[:SUBLANES]


def as_columns(part):
    fill = jnp.zeros((LANES - part.shape[0], part.shape[1]), jnp.float32)
    return jnp.transpose(jnp.concatenate([part, fill], 0))


def partial_kernel(transfers, upper, natural, asking, onto, *refs):
    count = len(transfers)
    out_ref = refs[-1]
    if asking:
        next_refs = refs[7 + count : 9 + count]
        refs = refs[: 7 + count] + refs[9 + count :]
    q_ref, k_ref, v_ref, kp_ref, vp_ref, g_ref, gp_ref = refs[:7]
    ask_refs = refs[7 : 7 + count]
    own_ref, lse_ref = refs[7 + count + onto : 9 + count + onto]
    answer_refs = refs[9 + count + onto : -1]
    me = lax.axis_index("ctx")
    rows = q_ref.shape[0]
    heads = q_ref.shape[1] // HEAD_DIM
    half_rows = heads * rows + TAIL

    def key_value(head, with_quad):
        cut = block_lanes(head)
        keys = [kp_ref[:, cut], k_ref[:, cut]]
        values = [vp_ref[:, cut], v_ref[:, cut]]
        if with_quad:
            keys = [g_ref[0, :, cut], gp_ref[0, :, cut]] + keys
            values = [g_ref[1, :, cut], gp_ref[1, :, cut]] + values
        values = jnp.concatenate(values, 0)
        return jnp.concatenate(keys, 0), jnp.concatenate([values, jnp.ones_like(values)], 1)

    def run(with_quad):
        key_count = rows * (4 if with_quad else 2)
        row = lax.broadcasted_iota(jnp.int32, (rows, key_count), 0)
        column = lax.broadcasted_iota(jnp.int32, (rows, key_count), 1)
        column = column - (key_count - 2 * rows)
        partner_limit = jnp.where(me % 2 == 1, rows, 0)
        mask = (column < partner_limit) | ((column >= rows) & (column - rows <= row))
        sums = []
        for head in range(heads):
            keys, values = key_value(head, with_quad)
            mixed, lse = soft(q_ref[:, block_lanes(head)], keys, values, mask)
            own_ref[:, block_lanes(head)] = mixed
            out_ref[:, block_lanes(head)] = mixed.astype(out_ref.dtype)
            sums.append(lse)
        lse_ref[...] = as_rows(sums)

        def answer(index):
            sums = [[], []]
            for head in range(heads):
                keys, values = key_value(head, with_quad)
                if natural:
                    query = ask_refs[index][:, :, block_lanes(head)].reshape(2 * rows, HEAD_DIM)
                else:
                    halves = [half * half_rows + head * rows for half in range(2)]
                    query = jnp.concatenate(
                        [ask_refs[index][start : start + rows, :] for start in halves], 0
                    )
                mixed, lse = soft(query, keys, values)
                for half in range(2):
                    cut = slice(half * rows, (half + 1) * rows)
                    start = half * half_rows + head * rows
                    answer_refs[index][start : start + rows, :] = mixed[cut].astype(jnp.bfloat16)
                    sums[half].append(lse[cut])
            for half in range(2):
                start = half * half_rows + heads * rows
                lse = as_rows(sums[half])
                first = lse.astype(jnp.bfloat16).astype(jnp.float32)
                second = (lse - first).astype(jnp.bfloat16).astype(jnp.float32)
                third = lse - first - second
                tail = jnp.concatenate([first, second, third, jnp.zeros_like(lse)], 0)
                answer_refs[index][start : start + TAIL, :] = tail.astype(jnp.bfloat16)

        for index, pairs in enumerate(transfers):
            asked = [target for _, target in pairs if (target in upper) == with_quad]
            if asked:
                pl.when(among(me, asked))(functools.partial(answer, index))

    if upper:
        pl.when(among(me, upper))(functools.partial(run, True))
        pl.when(jnp.logical_not(among(me, upper)))(functools.partial(run, False))
    else:
        run(False)

    if asking:
        for index, pairs in enumerate(transfers):

            @pl.when(among(me, [source for source, _ in pairs]))
            def _():
                for ref, half in zip(next_refs, (me % 2, 1 - me % 2)):
                    for head in range(heads):
                        start = pl.multiple_of(half * half_rows + head * rows, TAIL)
                        answer_refs[index][pl.ds(start, rows), :] = ref[:, block_lanes(head)]


def merge_kernel(transfers, steps, start, own_hbm, lse_hbm, *refs):
    count = 2 * len(transfers)
    others_hbm, out_hbm = refs[:count], refs[count + 1]
    own_ref, lse_ref, *other_refs = refs[count + 2 : 2 * count + 4]
    out_ref, sems = refs[-2:]
    me = lax.axis_index("ctx")
    odd = me % 2
    rows, width = own_ref.shape
    heads = HEADS_PER_STEP
    half_rows = heads * rows + TAIL
    returned = []
    for pairs in transfers:
        members = [source for source, _ in pairs]
        returned += [members, [member ^ 1 for member in members]]

    @pl.when(among(me, sorted(set(sum(returned, [])))))
    def _():
        loads = [(own_hbm, own_ref), (lse_hbm, lse_ref)]
        for hbm, ref in zip(others_hbm, other_refs):
            for step in range(steps):
                half = pl.ds(pl.multiple_of((2 * step + odd) * half_rows, TAIL), half_rows)
                loads.append((hbm.at[half, :], ref.at[step]))
        copies = [
            pltpu.make_async_copy(source, target, sems.at[index])
            for index, (source, target) in enumerate(loads)
        ]
        for copy in copies:
            copy.start()
        for copy in copies:
            copy.wait()
        valid = [among(me, members) for members in returned]
        for step in range(steps):
            logs = [lse_ref[step * SUBLANES : (step + 1) * SUBLANES, :]]
            for index, ref in enumerate(other_refs):
                tail = ref[step, heads * rows :, :].astype(jnp.float32)
                parts = [tail[part * SUBLANES : (part + 1) * SUBLANES] for part in range(3)]
                logs.append(jnp.where(valid[index], parts[0] + parts[1] + parts[2], NEGATIVE))
            top = functools.reduce(jnp.maximum, logs)
            weights = [jnp.exp2(part - top) for part in logs]
            total = functools.reduce(jnp.add, weights)
            shares = [as_columns(weight / total) for weight in weights]
            for head in range(heads):
                cut = block_lanes(step * heads + head)
                mixed = [own_ref[:, cut]]
                for index, ref in enumerate(other_refs):
                    part = ref[step, head * rows : (head + 1) * rows, :].astype(jnp.float32)
                    mixed.append(jnp.where(valid[index], part, 0.0))
                terms = [part * share[:, head : head + 1] for part, share in zip(mixed, shares)]
                out_ref[:, cut] = functools.reduce(jnp.add, terms).astype(out_ref.dtype)
        store = pltpu.make_async_copy(
            out_ref, out_hbm.at[:, pl.ds(start, width)], sems.at[len(copies)]
        )
        store.start()
        store.wait()


def after(array, *others):
    return lax.optimization_barrier((array, *others))[0]


def attend(query, key, value, conv):
    rows, columns = query.shape
    devices = lax.axis_size("ctx")
    quads = devices // 4
    transfers = plan_moves(devices)
    step_width = HEADS_PER_STEP * HEAD_DIM
    chunks = len(CHUNK_STEPS)
    first_steps = [sum(CHUNK_STEPS[:chunk]) for chunk in range(chunks)]
    widths = [steps * step_width for steps in CHUNK_STEPS]
    starts = [step * step_width for step in first_steps]
    upper = [4 * quad + 2 + core for quad in range(quads - 1) for core in range(2)]
    gathers = [(who - 2, who) for who in upper]
    askers = sorted({source for pairs in transfers for source, _ in pairs})
    swap = [(index, index ^ 1) for index in range(devices)]

    query_swapped = lax.ppermute(query, "ctx", swap)
    key_swapped = lax.ppermute(key, "ctx", swap)
    value_swapped = lax.ppermute(value, "ctx", swap)

    both_ways = chunks > LAG and all(
        not {source for source, _ in pairs} & {target for _, target in pairs}
        for pairs in transfers
    )
    asked = LAG if both_ways else chunks

    def pack():
        hbm = pl.BlockSpec(memory_space=pl.ANY)
        shapes = [jax.ShapeDtypeStruct((2, rows, width), jnp.bfloat16) for width in widths]
        outs = pl.pallas_call(
            functools.partial(
                pack_kernel,
                [source for source, _ in gathers],
                askers,
                asked,
                widths,
                starts,
            ),
            in_specs=[hbm] * 4,
            out_specs=[hbm] * (chunks + asked),
            out_shape=shapes + shapes[:asked],
            scratch_shapes=[
                pltpu.VMEM((rows, width), jnp.bfloat16) for width in widths for _ in range(2)
            ]
            + [pltpu.SemaphoreType.DMA((2 * chunks,))] * 2,
            compiler_params=params(),
            cost_estimate=cost(1),
            name="att_pack",
        )(query, query_swapped, key, value)
        return outs[:chunks], outs[chunks:]

    half_rows = HEADS_PER_STEP * rows + TAIL
    hbm = pl.BlockSpec(memory_space=pl.ANY)
    def partial(chunk, ask, quad, result):
        steps, first = CHUNK_STEPS[chunk], first_steps[chunk]
        whole_spec = pl.BlockSpec((rows, step_width), lambda step, first=first: (0, first + step))
        chunk_spec = pl.BlockSpec((rows, step_width), lambda step: (0, step))
        pair_spec = pl.BlockSpec((2, rows, step_width), lambda step: (0, 0, step))
        lse_spec = pl.BlockSpec((SUBLANES, LANES), lambda step: (step, 0))
        answer_spec = pl.BlockSpec((2 * half_rows, LANES), lambda step: (step, 0))
        answer_shape = jax.ShapeDtypeStruct((2 * half_rows * steps, LANES), jnp.bfloat16)
        asking = both_ways and chunk + LAG < chunks
        natural = chunk < asked
        operands = [query, key, value, key_swapped, value_swapped, *quad, *ask]
        specs = [whole_spec] * 5 + [pair_spec] * 2
        specs += [pair_spec if natural else answer_spec] * len(transfers)
        if asking:
            later = first_steps[chunk + LAG]
            operands += [query, query_swapped]
            specs += [
                pl.BlockSpec((rows, step_width), lambda step, later=later: (0, later + step))
            ] * 2
        aliases = {}
        if result is not None:
            aliases = {len(operands): 2 + len(transfers)}
            operands.append(result)
            specs.append(hbm)
        return pl.pallas_call(
            functools.partial(partial_kernel, transfers, upper, natural, asking, len(aliases)),
            grid=(steps,),
            in_specs=specs,
            out_specs=[chunk_spec, lse_spec] + [answer_spec] * len(transfers) + [whole_spec],
            out_shape=[
                jax.ShapeDtypeStruct((rows, widths[chunk]), jnp.float32),
                jax.ShapeDtypeStruct((SUBLANES * steps, LANES), jnp.float32),
            ]
            + [answer_shape] * len(transfers)
            + [jax.ShapeDtypeStruct((rows, columns), jnp.bfloat16)],
            input_output_aliases=aliases,
            compiler_params=params(),
            cost_estimate=cost(4),
            name="att_partial",
        )(*operands)

    def merge(chunk, parts, result):
        steps = CHUNK_STEPS[chunk]
        count = 2 * len(transfers)
        return pl.pallas_call(
            functools.partial(merge_kernel, transfers, steps, starts[chunk]),
            in_specs=[hbm] * (len(parts) + 1),
            out_specs=hbm,
            out_shape=jax.ShapeDtypeStruct((rows, columns), jnp.bfloat16),
            input_output_aliases={len(parts): 0},
            scratch_shapes=[
                pltpu.VMEM((rows, widths[chunk]), jnp.float32),
                pltpu.VMEM((SUBLANES * steps, LANES), jnp.float32),
            ]
            + [pltpu.VMEM((steps, half_rows, LANES), jnp.bfloat16)] * count
            + [
                pltpu.VMEM((rows, widths[chunk]), jnp.bfloat16),
                pltpu.SemaphoreType.DMA((3 + count * steps,)),
            ],
            compiler_params=params(),
            cost_estimate=cost(2),
            name="att_merge",
        )(*parts, result)
    def exchange(operands, ways):
        moved = []
        for operand, pairs in zip(operands, transfers):
            back = [(target, source) for source, target in pairs]
            moves = pairs if ways == 1 else back if ways == -1 else pairs + back
            moved.append(lax.ppermute(operand, "ctx", moves))
        return moved

    def swapped(array):
        return lax.ppermute(array, "ctx", swap)

    def with_swapped(arrays):
        return [item for array in arrays for item in (array, swapped(array))]

    conv_first, conv_shared, conv_state, conv_last = conv
    rim, own_par = conv_first()
    key_packs, query_packs = pack()
    live = (rim, own_par, key_packs, query_packs)
    rim, own_par, key_packs, query_packs = lax.optimization_barrier(live)

    asks = [exchange([query_packs[0]] * len(transfers), 1)]
    quad = lax.ppermute(key_packs[0], "ctx", gathers)
    par = conv_shared(own_par)
    live = (asks[0], quad, rim, par, key_packs[1:], query_packs[1:])
    asks[0], quad, rim, par, key_packs, query_packs = lax.optimization_barrier(live)

    local_result = state = decay = None
    other = total = entering = answers = result = None
    hops = devices // 2 - 1
    hop_pairs = [(index, index + 2) for index in range(1, devices - 2, 2)]

    def hop(entering):
        leaving = total if entering is None else total + decay * decay * entering
        return lax.ppermute(leaving, "ctx", hop_pairs)

    owns, waiting = [], []
    for chunk in range(chunks):
        last = chunk == chunks - 1
        next_ask = next_quad = back = None
        if not last:
            next_quad = lax.ppermute(key_packs[chunk], "ctx", gathers)
        if not last and chunk + 1 < asked:
            next_ask = exchange([query_packs[chunk]] * len(transfers), 1)
        if chunk:
            both = next_ask is None and not last
            back = exchange(answers, 0 if both else -1)
            if both:
                next_ask = back
        if chunk == 0:
            local_result, state, decay = conv_state(rim, par)
        if chunk == 1:
            other = swapped(state)
            total = state + decay * other
        if chunk and hops:
            entering = hop(entering)
            hops -= 1
        parts = with_swapped(waiting[0]) if waiting else None
        quad_swapped = swapped(quad)
        own, lse, *answers, result = partial(chunk, asks[chunk], (quad, quad_swapped), result)
        owns.append([own, lse])
        if parts:
            result = merge(chunk - 2, owns[chunk - 2] + parts, result)
            waiting = waiting[1:]
        if back:
            waiting.append(back)
        convolved = (local_result, state, decay, total, entering)
        live = (next_ask, next_quad, waiting, answers, result, convolved, owns[chunk])
        next_ask, quad, waiting, answers, result, convolved, owns[chunk] = (
            lax.optimization_barrier(live)
        )
        local_result, state, decay, total, entering = convolved
        asks.append(next_ask)

    back = exchange(answers, -1)
    for _ in range(hops):
        entering = hop(entering)
    hyena_out = conv_last(
        local_result, rim, par, decay, entering, swapped(entering), other
    )
    for chunk, arrivals in zip(range(chunks - 1 - len(waiting), chunks - 1), waiting):
        result = merge(chunk, owns[chunk] + with_swapped(arrivals), result)
    back, hyena_out, result = lax.optimization_barrier((back, hyena_out, result))
    result = merge(chunks - 1, owns[-1] + with_swapped(back), result)
    return hyena_out, result


def local(
    hyena_q, hyena_k, hyena_v, short_filter, residue, decay_rate, att_query, att_key, att_value
):
    conv = convolution(hyena_q, hyena_k, hyena_v, short_filter, residue, decay_rate)
    return attend(att_query, att_key, att_value, conv)


def solution(mesh):
    rows = P(("dp", "ctx"), None)
    shared = P("ctx", None)
    return jax.shard_map(
        local,
        mesh=mesh,
        in_specs=(rows, rows, rows, P(), shared, shared, rows, rows, rows),
        out_specs=(rows, rows),
        check_vma=False,
    )
```

```python
import functools
import math

import jax
import jax.numpy as jnp
from jax import lax
from jax.experimental import pallas as pl
from jax.experimental.pallas import tpu as pltpu
from jax.sharding import PartitionSpec as P

HEAD_DIM = 128
LANES = 128
SUBLANES = 8
TAIL = 4 * SUBLANES
TAPS = 3
HEADS_PER_STEP = 4
CHUNK_STEPS = (2, 2, 2, 2)
LAG = 2
NEGATIVE = -1e30
EXP_SCALE = HEAD_DIM**-0.5 * math.log2(math.e)
VMEM_LIMIT = 255 * 1024 * 256


def params(**kwargs):
    return pltpu.CompilerParams(vmem_limit_bytes=VMEM_LIMIT, **kwargs)


def cost(microseconds):
    return pl.CostEstimate(
        flops=microseconds * 10**8, bytes_accessed=2**16, transcendentals=0
    )


def block_lanes(block):
    return slice(block * LANES, (block + 1) * LANES)


def conv_pack_kernel(rate_ref, residue_ref, q_ref, k_ref, v_ref, par_ref, rim_ref):
    modes = rate_ref.shape[0]
    for block in range(rate_ref.shape[1] // LANES):
        for which, ref in enumerate((rate_ref, residue_ref)):
            start = (2 * block + which) * modes
            for device in range(par_ref.shape[0]):
                par_ref[device, start : start + modes, :] = ref[:, block_lanes(block)]
    for feature, ref in enumerate((q_ref, k_ref, v_ref)):
        last = ref[...].astype(jnp.float32)[ref.shape[0] - 2 :]
        rim_ref[2 * feature : 2 * feature + 2, :] = last
    rim_ref[2 * TAPS :, :] = jnp.zeros((2, rim_ref.shape[1]), jnp.float32)


def rim_rows(rim_ref, feature, lanes):
    return [rim_ref[pl.ds(2 * feature + row, 1), lanes] for row in range(2)]


def short_mix(feature, rim, taps):
    two_before, one_before = rim
    row = lax.broadcasted_iota(jnp.int32, feature.shape, 0)
    one = jnp.where(row == 0, one_before, pltpu.roll(feature, 1, 0))
    two = jnp.where(row == 0, two_before, jnp.where(row == 1, one_before, pltpu.roll(feature, 2, 0)))
    return taps[0] * feature + taps[1] * one + taps[2] * two


def tap_rows(taps_ref, feature, lanes):
    return [taps_ref[feature, pl.ds(tap, 1), lanes] for tap in range(TAPS)]


def join_parameters(same_ref, other_ref, par_ref):
    odd = lax.axis_index("ctx") % 2
    chips, rows, _ = same_ref.shape
    for chip in range(chips):
        for ref, core in ((same_ref, odd), (other_ref, 1 - odd)):
            start = pl.multiple_of((2 * chip + core) * rows, SUBLANES)
            par_ref[pl.ds(start, rows), :] = ref[chip]


def state_kernel(
    modes,
    k_ref,
    v_ref,
    rim_ref,
    same_ref,
    other_ref,
    taps_ref,
    y_ref,
    s_ref,
    d_ref,
    par_ref,
    p_scr,
    y_scr,
):
    join_parameters(same_ref, other_ref, par_ref)
    rows = k_ref.shape[0]
    for block in range(SUBLANES):
        lanes = block_lanes(block)
        mixes = [
            short_mix(
                ref[:, lanes].astype(jnp.float32),
                rim_rows(rim_ref, feature, lanes),
                tap_rows(taps_ref, feature, lanes),
            )
            for feature, ref in ((1, k_ref), (2, v_ref))
        ]
        product = (mixes[0] * mixes[1]).astype(jnp.bfloat16).astype(jnp.float32)
        p_scr[pl.ds(block, rows, SUBLANES), :] = product
    decay = [jnp.exp(-par_ref[pl.ds(mode, SUBLANES, 2 * modes), :]) for mode in range(modes)]
    residue = [par_ref[pl.ds(modes + mode, SUBLANES, 2 * modes), :] for mode in range(modes)]

    def body(position, states):
        here = pl.ds(pl.multiple_of(position * SUBLANES, SUBLANES), SUBLANES)
        product = p_scr[here, :]
        states = tuple(state * rate + product for state, rate in zip(states, decay))
        terms = [state * weight for state, weight in zip(states, residue)]
        while len(terms) > 1:
            terms = [left + right for left, right in zip(terms[::2], terms[1::2])]
        y_scr[here, :] = terms[0]
        return states

    zero = jnp.zeros((SUBLANES, LANES), jnp.float32)
    states = lax.fori_loop(0, rows, body, (zero,) * modes, unroll=4)
    for mode in range(modes):
        s_ref[pl.ds(mode, SUBLANES, modes), :] = states[mode]
    for block in range(SUBLANES):
        rate = par_ref[2 * block * modes : (2 * block + 1) * modes, :]
        d_ref[block * modes : (block + 1) * modes, :] = jnp.exp(-rate * rows)
    for block in range(SUBLANES):
        y_ref[:, block_lanes(block)] = y_scr[pl.ds(block, rows, SUBLANES), :]


def output_kernel(
    modes,
    q_ref,
    y_ref,
    rim_ref,
    same_ref,
    other_par_ref,
    decay_ref,
    enter_ref,
    enter_first_ref,
    other_ref,
    taps_ref,
    out_ref,
    par_ref,
):
    join_parameters(same_ref, other_par_ref, par_ref)
    second = lax.axis_index("ctx") % 2 == 1
    rows = q_ref.shape[0]
    step = lax.broadcasted_iota(jnp.int32, (SUBLANES, LANES), 0).astype(jnp.float32) + 1.0

    def body(block, nothing):
        lanes = pl.ds(pl.multiple_of(block * LANES, LANES), LANES)
        rate = par_ref[pl.ds(pl.multiple_of(2 * block * modes, SUBLANES), modes), :]
        residue = par_ref[pl.ds(pl.multiple_of((2 * block + 1) * modes, SUBLANES), modes), :]
        here = pl.ds(pl.multiple_of(block * modes, SUBLANES), modes)
        after_first = decay_ref[here, :] * enter_ref[here, :] + other_ref[here, :]
        entering = jnp.where(second, after_first, enter_first_ref[here, :])
        weighted = residue * entering
        eight = jnp.exp(-rate * SUBLANES)
        terms = [
            weighted[mode : mode + 1] * jnp.exp(-rate[mode : mode + 1] * step)
            for mode in range(modes)
        ]
        eights = [jnp.broadcast_to(eight[mode : mode + 1], terms[0].shape) for mode in range(modes)]
        added = []
        for start in range(0, rows, SUBLANES):
            sums = list(terms)
            while len(sums) > 1:
                sums = [left + right for left, right in zip(sums[::2], sums[1::2])]
            added.append(sums[0])
            if start + SUBLANES < rows:
                terms = [term * decay for term, decay in zip(terms, eights)]
        smoothed = y_ref[:, lanes] + jnp.concatenate(added, 0)
        smoothed = smoothed.astype(jnp.bfloat16).astype(jnp.float32)
        mix = short_mix(
            q_ref[:, lanes].astype(jnp.float32),
            rim_rows(rim_ref, 0, lanes),
            tap_rows(taps_ref, 0, lanes),
        )
        out_ref[:, lanes] = (mix * smoothed).astype(out_ref.dtype)
        return nothing

    lax.fori_loop(0, SUBLANES, body, 0)


def convolution(hyena_q, hyena_k, hyena_v, short_filter, residue, decay_rate):
    rows, channels = hyena_q.shape
    devices = lax.axis_size("ctx")
    modes = residue.shape[1]
    own_blocks = residue.shape[0] // LANES
    blocks = channels // LANES
    groups = blocks // SUBLANES
    width = SUBLANES * LANES
    end = rows // 16 - 1
    par_rows = 2 * own_blocks * modes
    feature_spec = pl.BlockSpec((rows, width), lambda group: (0, group))
    rim_spec = pl.BlockSpec((8, width), lambda group: (0, group))
    chips = SUBLANES // (2 * own_blocks)
    par_spec = pl.BlockSpec((chips, par_rows, LANES), lambda group: (group, 0, 0))
    par_scratch = pltpu.VMEM((2 * SUBLANES * modes, LANES), jnp.float32)
    taps_spec = pl.BlockSpec((TAPS, TAPS, width), lambda group: (0, 0, group))
    positions = pltpu.VMEM((rows * SUBLANES, LANES), jnp.float32)

    def first_part(token):
        own_par, rim = pl.pallas_call(
            conv_pack_kernel,
            grid=(1,),
            in_specs=[pl.BlockSpec((modes, residue.shape[0]), lambda step: (0, 0))] * 2
            + [pl.BlockSpec((16, channels), lambda step: (end, 0))] * 3,
            out_specs=[
                pl.BlockSpec((devices // 2, par_rows, LANES), lambda step: (0, 0, 0)),
                pl.BlockSpec((8, channels), lambda step: (0, 0)),
            ],
            out_shape=[
                jax.ShapeDtypeStruct((devices // 2, par_rows, LANES), jnp.float32),
                jax.ShapeDtypeStruct((8, channels), jnp.float32),
            ],
            compiler_params=params(),
            cost_estimate=cost(1),
            name="conv_pack",
        )(decay_rate.T, residue.T, hyena_q, hyena_k, hyena_v)
        rim = lax.ppermute(rim, "ctx", [(index, index + 1) for index in range(devices - 1)])
        own_par = after(own_par, rim, token)
        same = lax.all_to_all(
            own_par,
            "ctx",
            split_axis=0,
            concat_axis=0,
            axis_index_groups=[list(range(core, devices, 2)) for core in range(2)],
            tiled=True,
        )
        par = (same, lax.ppermute(same, "ctx", [(index, index ^ 1) for index in range(devices)]))
        state_spec = pl.BlockSpec((SUBLANES * modes, LANES), lambda group: (group, 0))
        local_result, state, decay = pl.pallas_call(
            functools.partial(state_kernel, modes),
            grid=(groups,),
            in_specs=[feature_spec, feature_spec, rim_spec, par_spec, par_spec, taps_spec],
            out_specs=[feature_spec, state_spec, state_spec],
            out_shape=[
                jax.ShapeDtypeStruct((rows, channels), jnp.float32),
                jax.ShapeDtypeStruct((blocks * modes, LANES), jnp.float32),
                jax.ShapeDtypeStruct((blocks * modes, LANES), jnp.float32),
            ],
            scratch_shapes=[par_scratch, positions, positions],
            compiler_params=params(),
            cost_estimate=cost(9),
            name="conv_state",
        )(hyena_k, hyena_v, rim, *par, short_filter)
        return local_result, rim, par, decay, *entering_state(state, decay)

    def entering_state(state, decay):
        swap = [(index, index ^ 1) for index in range(devices)]
        other = lax.ppermute(state, "ctx", swap)
        total = state + decay * other
        entering = None
        reach = 1
        while 2 * reach < devices:
            moves = [(index, index + 2 * reach) for index in range(1, devices - 2 * reach, 2)]
            arrived = lax.ppermute(total, "ctx", moves)
            if reach == 1:
                entering = arrived
            else:
                entering = entering + decay ** (2 * (reach - 1)) * arrived
            if 4 * reach < devices:
                total = total + decay ** (2 * reach) * arrived
            reach *= 2
        return entering, lax.ppermute(entering, "ctx", swap), other

    def last_part(local_result, rim, par, decay, entering, entering_first, other):
        state_spec = pl.BlockSpec((SUBLANES * modes, LANES), lambda group: (group, 0))
        return pl.pallas_call(
            functools.partial(output_kernel, modes),
            grid=(groups,),
            in_specs=[feature_spec, feature_spec, rim_spec, par_spec, par_spec]
            + [state_spec] * 4
            + [taps_spec],
            out_specs=feature_spec,
            out_shape=jax.ShapeDtypeStruct((rows, channels), jnp.bfloat16),
            scratch_shapes=[par_scratch],
            compiler_params=params(),
            cost_estimate=cost(6),
            name="conv_output",
        )(
            hyena_q,
            local_result,
            rim,
            *par,
            decay,
            entering,
            entering_first,
            other,
            short_filter,
        )

    return first_part, last_part


def among(me, members):
    return functools.reduce(jnp.logical_or, [me == member for member in members])


def plan_moves(devices):
    quads = devices // 4
    transfers = [[(devices - 1, devices - 3)]]
    for distance in range(1, quads):
        if distance > len(transfers):
            transfers.append([])
        for quad in range(distance, quads):
            target = 4 * (quad - distance) + 2
            transfers[distance - 1] += [(4 * quad, target), (4 * quad + 2, target + 1)]
    return transfers


def soft(query, keys, values, mask=None):
    scores = lax.dot_general(
        query, keys, (((1,), (1,)), ((), ())), preferred_element_type=jnp.float32
    )
    if mask is not None:
        scores = jnp.where(mask, scores, NEGATIVE)
    top = jnp.max(scores, axis=1, keepdims=True) * EXP_SCALE
    expo = jnp.exp2(scores * EXP_SCALE - top).astype(jnp.bfloat16)
    mixed = jnp.dot(expo, values, preferred_element_type=jnp.float32)
    total = mixed[:, HEAD_DIM:]
    return mixed[:, :HEAD_DIM] / total, top + jnp.log2(total)


def pack_kernel(gathers, askers, asked, widths, starts, q_ref, qs_ref, k_ref, v_ref, *rest):
    count = len(widths)
    key_outs, query_outs = rest[:count], rest[count : count + asked]
    stages, in_sems, out_sems = rest[count + asked : -2], rest[-2], rest[-1]
    me = lax.axis_index("ctx")
    odd = me % 2

    def run(pairs):
        loads = [
            pltpu.make_async_copy(source, stage, in_sems.at[index])
            for index, ((source, _), stage) in enumerate(zip(pairs, stages))
        ]
        stores = [
            pltpu.make_async_copy(stage, target, out_sems.at[index])
            for index, ((_, target), stage) in enumerate(zip(pairs, stages))
        ]
        for load in loads:
            load.start()
        for load, store in zip(loads, stores):
            load.wait()
            store.start()
        for store in stores:
            store.wait()

    def cut(ref, chunk):
        return ref.at[:, pl.ds(starts[chunk], widths[chunk])]

    if gathers:

        @pl.when(among(me, gathers))
        def _():
            run(
                [
                    (cut(ref, chunk), key_outs[chunk].at[which])
                    for chunk in range(count)
                    for which, ref in enumerate((k_ref, v_ref))
                ]
            )

    @pl.when(among(me, askers))
    def _():
        run(
            [
                (cut(ref, chunk), query_outs[chunk].at[half])
                for chunk in range(asked)
                for ref, half in ((q_ref, odd), (qs_ref, 1 - odd))
            ]
        )


def as_rows(columns):
    lanes = lax.broadcasted_iota(jnp.int32, columns[0].shape, 1)
    sums = jnp.zeros_like(columns[0])
    for index, column in enumerate(columns):
        sums = jnp.where(lanes == index, column, sums)
    return jnp.transpose(sums)[:SUBLANES]


def as_columns(part):
    fill = jnp.zeros((LANES - part.shape[0], part.shape[1]), jnp.float32)
    return jnp.transpose(jnp.concatenate([part, fill], 0))


def partial_kernel(transfers, upper, natural, asking, onto, *refs):
    count = len(transfers)
    out_ref = refs[-1]
    if asking:
        next_refs = refs[7 + count : 9 + count]
        refs = refs[: 7 + count] + refs[9 + count :]
    q_ref, k_ref, v_ref, kp_ref, vp_ref, g_ref, gp_ref = refs[:7]
    ask_refs = refs[7 : 7 + count]
    own_ref, lse_ref = refs[7 + count + onto : 9 + count + onto]
    answer_refs = refs[9 + count + onto : -1]
    me = lax.axis_index("ctx")
    rows = q_ref.shape[0]
    heads = q_ref.shape[1] // HEAD_DIM
    half_rows = heads * rows + TAIL

    def key_value(head, with_quad):
        cut = block_lanes(head)
        keys = [kp_ref[:, cut], k_ref[:, cut]]
        values = [vp_ref[:, cut], v_ref[:, cut]]
        if with_quad:
            keys = [g_ref[0, :, cut], gp_ref[0, :, cut]] + keys
            values = [g_ref[1, :, cut], gp_ref[1, :, cut]] + values
        values = jnp.concatenate(values, 0)
        return jnp.concatenate(keys, 0), jnp.concatenate([values, jnp.ones_like(values)], 1)

    def run(with_quad):
        key_count = rows * (4 if with_quad else 2)
        row = lax.broadcasted_iota(jnp.int32, (rows, key_count), 0)
        column = lax.broadcasted_iota(jnp.int32, (rows, key_count), 1)
        column = column - (key_count - 2 * rows)
        partner_limit = jnp.where(me % 2 == 1, rows, 0)
        mask = (column < partner_limit) | ((column >= rows) & (column - rows <= row))
        sums = []
        for head in range(heads):
            keys, values = key_value(head, with_quad)
            mixed, lse = soft(q_ref[:, block_lanes(head)], keys, values, mask)
            own_ref[:, block_lanes(head)] = mixed
            out_ref[:, block_lanes(head)] = mixed.astype(out_ref.dtype)
            sums.append(lse)
        lse_ref[...] = as_rows(sums)

        def answer(index):
            sums = [[], []]
            for head in range(heads):
                keys, values = key_value(head, with_quad)
                if natural:
                    query = ask_refs[index][:, :, block_lanes(head)].reshape(2 * rows, HEAD_DIM)
                else:
                    halves = [half * half_rows + head * rows for half in range(2)]
                    query = jnp.concatenate(
                        [ask_refs[index][start : start + rows, :] for start in halves], 0
                    )
                mixed, lse = soft(query, keys, values)
                for half in range(2):
                    cut = slice(half * rows, (half + 1) * rows)
                    start = half * half_rows + head * rows
                    answer_refs[index][start : start + rows, :] = mixed[cut].astype(jnp.bfloat16)
                    sums[half].append(lse[cut])
            for half in range(2):
                start = half * half_rows + heads * rows
                lse = as_rows(sums[half])
                first = lse.astype(jnp.bfloat16).astype(jnp.float32)
                second = (lse - first).astype(jnp.bfloat16).astype(jnp.float32)
                third = lse - first - second
                tail = jnp.concatenate([first, second, third, jnp.zeros_like(lse)], 0)
                answer_refs[index][start : start + TAIL, :] = tail.astype(jnp.bfloat16)

        for index, pairs in enumerate(transfers):
            asked = [target for _, target in pairs if (target in upper) == with_quad]
            if asked:
                pl.when(among(me, asked))(functools.partial(answer, index))

    if upper:
        pl.when(among(me, upper))(functools.partial(run, True))
        pl.when(jnp.logical_not(among(me, upper)))(functools.partial(run, False))
    else:
        run(False)

    if asking:
        for index, pairs in enumerate(transfers):

            @pl.when(among(me, [source for source, _ in pairs]))
            def _():
                for ref, half in zip(next_refs, (me % 2, 1 - me % 2)):
                    for head in range(heads):
                        start = pl.multiple_of(half * half_rows + head * rows, TAIL)
                        answer_refs[index][pl.ds(start, rows), :] = ref[:, block_lanes(head)]


def merge_kernel(transfers, steps, start, own_hbm, lse_hbm, *refs):
    count = 2 * len(transfers)
    others_hbm, out_hbm = refs[:count], refs[count + 1]
    own_ref, lse_ref, *other_refs = refs[count + 2 : 2 * count + 4]
    out_ref, sems = refs[-2:]
    me = lax.axis_index("ctx")
    odd = me % 2
    rows, width = own_ref.shape
    heads = HEADS_PER_STEP
    half_rows = heads * rows + TAIL
    returned = []
    for pairs in transfers:
        members = [source for source, _ in pairs]
        returned += [members, [member ^ 1 for member in members]]

    @pl.when(among(me, sorted(set(sum(returned, [])))))
    def _():
        loads = [(own_hbm, own_ref), (lse_hbm, lse_ref)]
        for hbm, ref in zip(others_hbm, other_refs):
            for step in range(steps):
                half = pl.ds(pl.multiple_of((2 * step + odd) * half_rows, TAIL), half_rows)
                loads.append((hbm.at[half, :], ref.at[step]))
        copies = [
            pltpu.make_async_copy(source, target, sems.at[index])
            for index, (source, target) in enumerate(loads)
        ]
        for copy in copies:
            copy.start()
        for copy in copies:
            copy.wait()
        valid = [among(me, members) for members in returned]
        for step in range(steps):
            logs = [lse_ref[step * SUBLANES : (step + 1) * SUBLANES, :]]
            for index, ref in enumerate(other_refs):
                tail = ref[step, heads * rows :, :].astype(jnp.float32)
                parts = [tail[part * SUBLANES : (part + 1) * SUBLANES] for part in range(3)]
                logs.append(jnp.where(valid[index], parts[0] + parts[1] + parts[2], NEGATIVE))
            top = functools.reduce(jnp.maximum, logs)
            weights = [jnp.exp2(part - top) for part in logs]
            total = functools.reduce(jnp.add, weights)
            shares = [as_columns(weight / total) for weight in weights]
            for head in range(heads):
                cut = block_lanes(step * heads + head)
                mixed = [own_ref[:, cut]]
                for index, ref in enumerate(other_refs):
                    part = ref[step, head * rows : (head + 1) * rows, :].astype(jnp.float32)
                    mixed.append(jnp.where(valid[index], part, 0.0))
                terms = [part * share[:, head : head + 1] for part, share in zip(mixed, shares)]
                out_ref[:, cut] = functools.reduce(jnp.add, terms).astype(out_ref.dtype)
        store = pltpu.make_async_copy(
            out_ref, out_hbm.at[:, pl.ds(start, width)], sems.at[len(copies)]
        )
        store.start()
        store.wait()


def after(array, *others):
    return lax.optimization_barrier((array, *others))[0]


def attend(query, key, value, conv):
    rows, columns = query.shape
    devices = lax.axis_size("ctx")
    quads = devices // 4
    transfers = plan_moves(devices)
    step_width = HEADS_PER_STEP * HEAD_DIM
    chunks = len(CHUNK_STEPS)
    first_steps = [sum(CHUNK_STEPS[:chunk]) for chunk in range(chunks)]
    widths = [steps * step_width for steps in CHUNK_STEPS]
    starts = [step * step_width for step in first_steps]
    upper = [4 * quad + 2 + core for quad in range(quads - 1) for core in range(2)]
    gathers = [(who - 2, who) for who in upper]
    askers = sorted({source for pairs in transfers for source, _ in pairs})
    swap = [(index, index ^ 1) for index in range(devices)]

    query_swapped = lax.ppermute(query, "ctx", swap)
    key_swapped = lax.ppermute(key, "ctx", swap)
    value_swapped = lax.ppermute(value, "ctx", swap)

    both_ways = chunks > LAG and all(
        not {source for source, _ in pairs} & {target for _, target in pairs}
        for pairs in transfers
    )
    asked = LAG if both_ways else chunks

    def pack():
        hbm = pl.BlockSpec(memory_space=pl.ANY)
        shapes = [jax.ShapeDtypeStruct((2, rows, width), jnp.bfloat16) for width in widths]
        outs = pl.pallas_call(
            functools.partial(
                pack_kernel,
                [source for source, _ in gathers],
                askers,
                asked,
                widths,
                starts,
            ),
            in_specs=[hbm] * 4,
            out_specs=[hbm] * (chunks + asked),
            out_shape=shapes + shapes[:asked],
            scratch_shapes=[
                pltpu.VMEM((rows, width), jnp.bfloat16) for width in widths for _ in range(2)
            ]
            + [pltpu.SemaphoreType.DMA((2 * chunks,))] * 2,
            compiler_params=params(),
            cost_estimate=cost(1),
            name="att_pack",
        )(query, query_swapped, key, value)
        return outs[:chunks], outs[chunks:]

    key_packs, query_packs = pack()
    conv_first, conv_last = conv
    local_result, *conv_shared = conv_first(query_packs[0])
    asks, quad_kv, all_answers = {}, [], []

    def send(chunk):
        key_pack = key_packs[chunk]
        if chunk >= LAG:
            key_pack = after(key_pack, quad_kv[chunk - LAG][0], *all_answers[chunk - LAG][:1])
        quad_kv.append([lax.ppermute(key_pack, "ctx", gathers)])
        if chunk < asked:
            query_pack = query_packs[chunk]
            if chunk >= LAG:
                query_pack = after(query_pack, *asks[chunk - LAG], all_answers[chunk - LAG][0])
            asks[chunk] = [lax.ppermute(query_pack, "ctx", pairs) for pairs in transfers]

    half_rows = HEADS_PER_STEP * rows + TAIL
    hbm = pl.BlockSpec(memory_space=pl.ANY)
    for chunk in range(min(LAG, chunks)):
        send(chunk)
    result = None
    returned = []
    for chunk in range(chunks):
        if chunk == 0:
            quad_kv[0] = [after(quad_kv[0][0], local_result)]
            asks[0] = [after(asked, local_result) for asked in asks[0]]
        quad_kv[chunk].append(lax.ppermute(quad_kv[chunk][0], "ctx", swap))
        steps, first = CHUNK_STEPS[chunk], first_steps[chunk]
        whole_spec = pl.BlockSpec((rows, step_width), lambda step, first=first: (0, first + step))
        chunk_spec = pl.BlockSpec((rows, step_width), lambda step: (0, step))
        pair_spec = pl.BlockSpec((2, rows, step_width), lambda step: (0, 0, step))
        lse_spec = pl.BlockSpec((SUBLANES, LANES), lambda step: (step, 0))
        answer_spec = pl.BlockSpec((2 * half_rows, LANES), lambda step: (step, 0))
        answer_shape = jax.ShapeDtypeStruct((2 * half_rows * steps, LANES), jnp.bfloat16)
        asking = both_ways and chunk + LAG < chunks
        natural = chunk < asked
        operands = [query, key, value, key_swapped, value_swapped, *quad_kv[chunk], *asks[chunk]]
        specs = [whole_spec] * 5 + [pair_spec] * 2
        specs += [pair_spec if natural else answer_spec] * len(transfers)
        if asking:
            later = first_steps[chunk + LAG]
            operands += [query, query_swapped]
            specs += [
                pl.BlockSpec((rows, step_width), lambda step, later=later: (0, later + step))
            ] * 2
        aliases = {}
        if result is not None:
            aliases = {len(operands): 2 + len(transfers)}
            operands.append(result)
            specs.append(hbm)
        own, lse, *answers, result = pl.pallas_call(
            functools.partial(partial_kernel, transfers, upper, natural, asking, len(aliases)),
            grid=(steps,),
            in_specs=specs,
            out_specs=[chunk_spec, lse_spec] + [answer_spec] * len(transfers) + [whole_spec],
            out_shape=[
                jax.ShapeDtypeStruct((rows, widths[chunk]), jnp.float32),
                jax.ShapeDtypeStruct((SUBLANES * steps, LANES), jnp.float32),
            ]
            + [answer_shape] * len(transfers)
            + [jax.ShapeDtypeStruct((rows, columns), jnp.bfloat16)],
            input_output_aliases=aliases,
            compiler_params=params(),
            cost_estimate=cost(4),
            name="att_partial",
        )(*operands)
        all_answers.append(answers)
        parts = [own, lse]
        arrivals = []
        for answer, pairs in zip(answers, transfers):
            moves = [(target, source) for source, target in pairs]
            if asking:
                moves += pairs
            if chunk == chunks - 1:
                live = (answer, conv_shared, [part[2] for part in returned], result)
                answer, conv_shared, early, result = lax.optimization_barrier(live)
                returned = [part[:2] + [back] for part, back in zip(returned, early)]
            arrivals.append(lax.ppermute(answer, "ctx", moves))
        if asking:
            asks[chunk + LAG] = arrivals
        returned.append([own, lse, arrivals])
        if chunk + LAG < chunks:
            send(chunk + LAG)
    hyena_out = conv_last(local_result, *conv_shared)
    for chunk, (own, lse, arrivals) in enumerate(returned):
        if chunk == chunks - 1:
            live = (arrivals, hyena_out, result)
            arrivals, hyena_out, result = lax.optimization_barrier(live)
        parts = [own, lse]
        for arrival in arrivals:
            parts += [arrival, lax.ppermute(arrival, "ctx", swap)]
        steps = CHUNK_STEPS[chunk]
        count = 2 * len(transfers)
        result = pl.pallas_call(
            functools.partial(merge_kernel, transfers, steps, starts[chunk]),
            in_specs=[hbm] * (len(parts) + 1),
            out_specs=hbm,
            out_shape=jax.ShapeDtypeStruct((rows, columns), jnp.bfloat16),
            input_output_aliases={len(parts): 0},
            scratch_shapes=[
                pltpu.VMEM((rows, widths[chunk]), jnp.float32),
                pltpu.VMEM((SUBLANES * steps, LANES), jnp.float32),
            ]
            + [pltpu.VMEM((steps, half_rows, LANES), jnp.bfloat16)] * count
            + [
                pltpu.VMEM((rows, widths[chunk]), jnp.bfloat16),
                pltpu.SemaphoreType.DMA((3 + count * steps,)),
            ],
            compiler_params=params(),
            cost_estimate=cost(2),
            name="att_merge",
        )(*parts, result)
    return hyena_out, result


def local(
    hyena_q, hyena_k, hyena_v, short_filter, residue, decay_rate, att_query, att_key, att_value
):
    conv = convolution(hyena_q, hyena_k, hyena_v, short_filter, residue, decay_rate)
    return attend(att_query, att_key, att_value, conv)


def solution(mesh):
    rows = P(("dp", "ctx"), None)
    shared = P("ctx", None)
    return jax.shard_map(
        local,
        mesh=mesh,
        in_specs=(rows, rows, rows, P(), shared, shared, rows, rows, rows),
        out_specs=(rows, rows),
        check_vma=False,
    )
```

```python
import functools
import math

import jax
import jax.numpy as jnp
from jax import lax
from jax.experimental import pallas as pl
from jax.experimental.pallas import tpu as pltpu
from jax.sharding import PartitionSpec as P

HEAD_DIM = 128
LANES = 128
SUBLANES = 8
TAIL = 4 * SUBLANES
TAPS = 3
HEADS_PER_STEP = 4
CHUNK_STEPS = (2, 2, 2, 2)
LAG = 2
NEGATIVE = -1e30
EXP_SCALE = HEAD_DIM**-0.5 * math.log2(math.e)
VMEM_LIMIT = 255 * 1024 * 256


def params(**kwargs):
    return pltpu.CompilerParams(vmem_limit_bytes=VMEM_LIMIT, **kwargs)


def cost(microseconds):
    return pl.CostEstimate(
        flops=microseconds * 10**8, bytes_accessed=2**16, transcendentals=0
    )


def block_lanes(block):
    return slice(block * LANES, (block + 1) * LANES)


def conv_pack_kernel(rate_ref, residue_ref, q_ref, k_ref, v_ref, par_ref, rim_ref):
    modes = rate_ref.shape[0]
    for block in range(rate_ref.shape[1] // LANES):
        for which, ref in enumerate((rate_ref, residue_ref)):
            start = (2 * block + which) * modes
            for device in range(par_ref.shape[0]):
                par_ref[device, start : start + modes, :] = ref[:, block_lanes(block)]
    for feature, ref in enumerate((q_ref, k_ref, v_ref)):
        last = ref[...].astype(jnp.float32)[ref.shape[0] - 2 :]
        rim_ref[2 * feature : 2 * feature + 2, :] = last
    rim_ref[2 * TAPS :, :] = jnp.zeros((2, rim_ref.shape[1]), jnp.float32)


def rim_rows(rim_ref, feature, lanes):
    return [rim_ref[pl.ds(2 * feature + row, 1), lanes] for row in range(2)]


def short_mix(feature, rim, taps):
    two_before, one_before = rim
    row = lax.broadcasted_iota(jnp.int32, feature.shape, 0)
    one = jnp.where(row == 0, one_before, pltpu.roll(feature, 1, 0))
    two = jnp.where(row == 0, two_before, jnp.where(row == 1, one_before, pltpu.roll(feature, 2, 0)))
    return taps[0] * feature + taps[1] * one + taps[2] * two


def tap_rows(taps_ref, feature, lanes):
    return [taps_ref[feature, pl.ds(tap, 1), lanes] for tap in range(TAPS)]


def join_parameters(same_ref, other_ref, par_ref):
    odd = lax.axis_index("ctx") % 2
    chips, rows, _ = same_ref.shape
    for chip in range(chips):
        for ref, core in ((same_ref, odd), (other_ref, 1 - odd)):
            start = pl.multiple_of((2 * chip + core) * rows, SUBLANES)
            par_ref[pl.ds(start, rows), :] = ref[chip]


def state_kernel(
    modes,
    k_ref,
    v_ref,
    rim_ref,
    same_ref,
    other_ref,
    taps_ref,
    y_ref,
    s_ref,
    d_ref,
    par_ref,
    p_scr,
    y_scr,
):
    join_parameters(same_ref, other_ref, par_ref)
    rows = k_ref.shape[0]
    for block in range(SUBLANES):
        lanes = block_lanes(block)
        mixes = [
            short_mix(
                ref[:, lanes].astype(jnp.float32),
                rim_rows(rim_ref, feature, lanes),
                tap_rows(taps_ref, feature, lanes),
            )
            for feature, ref in ((1, k_ref), (2, v_ref))
        ]
        product = (mixes[0] * mixes[1]).astype(jnp.bfloat16).astype(jnp.float32)
        p_scr[pl.ds(block, rows, SUBLANES), :] = product
    decay = [jnp.exp(-par_ref[pl.ds(mode, SUBLANES, 2 * modes), :]) for mode in range(modes)]
    residue = [par_ref[pl.ds(modes + mode, SUBLANES, 2 * modes), :] for mode in range(modes)]

    def body(position, states):
        here = pl.ds(pl.multiple_of(position * SUBLANES, SUBLANES), SUBLANES)
        product = p_scr[here, :]
        states = tuple(state * rate + product for state, rate in zip(states, decay))
        terms = [state * weight for state, weight in zip(states, residue)]
        while len(terms) > 1:
            terms = [left + right for left, right in zip(terms[::2], terms[1::2])]
        y_scr[here, :] = terms[0]
        return states

    zero = jnp.zeros((SUBLANES, LANES), jnp.float32)
    states = lax.fori_loop(0, rows, body, (zero,) * modes, unroll=4)
    for mode in range(modes):
        s_ref[pl.ds(mode, SUBLANES, modes), :] = states[mode]
    for block in range(SUBLANES):
        rate = par_ref[2 * block * modes : (2 * block + 1) * modes, :]
        d_ref[block * modes : (block + 1) * modes, :] = jnp.exp(-rate * rows)
    for block in range(SUBLANES):
        y_ref[:, block_lanes(block)] = y_scr[pl.ds(block, rows, SUBLANES), :]


def output_kernel(
    modes,
    q_ref,
    y_ref,
    rim_ref,
    same_ref,
    other_par_ref,
    decay_ref,
    enter_ref,
    enter_first_ref,
    other_ref,
    taps_ref,
    out_ref,
    par_ref,
):
    join_parameters(same_ref, other_par_ref, par_ref)
    second = lax.axis_index("ctx") % 2 == 1
    rows = q_ref.shape[0]
    step = lax.broadcasted_iota(jnp.int32, (SUBLANES, LANES), 0).astype(jnp.float32) + 1.0

    def body(block, nothing):
        lanes = pl.ds(pl.multiple_of(block * LANES, LANES), LANES)
        rate = par_ref[pl.ds(pl.multiple_of(2 * block * modes, SUBLANES), modes), :]
        residue = par_ref[pl.ds(pl.multiple_of((2 * block + 1) * modes, SUBLANES), modes), :]
        here = pl.ds(pl.multiple_of(block * modes, SUBLANES), modes)
        after_first = decay_ref[here, :] * enter_ref[here, :] + other_ref[here, :]
        entering = jnp.where(second, after_first, enter_first_ref[here, :])
        weighted = residue * entering
        eight = jnp.exp(-rate * SUBLANES)
        terms = [
            weighted[mode : mode + 1] * jnp.exp(-rate[mode : mode + 1] * step)
            for mode in range(modes)
        ]
        eights = [jnp.broadcast_to(eight[mode : mode + 1], terms[0].shape) for mode in range(modes)]
        added = []
        for start in range(0, rows, SUBLANES):
            sums = list(terms)
            while len(sums) > 1:
                sums = [left + right for left, right in zip(sums[::2], sums[1::2])]
            added.append(sums[0])
            if start + SUBLANES < rows:
                terms = [term * decay for term, decay in zip(terms, eights)]
        smoothed = y_ref[:, lanes] + jnp.concatenate(added, 0)
        smoothed = smoothed.astype(jnp.bfloat16).astype(jnp.float32)
        mix = short_mix(
            q_ref[:, lanes].astype(jnp.float32),
            rim_rows(rim_ref, 0, lanes),
            tap_rows(taps_ref, 0, lanes),
        )
        out_ref[:, lanes] = (mix * smoothed).astype(out_ref.dtype)
        return nothing

    lax.fori_loop(0, SUBLANES, body, 0)


def convolution(hyena_q, hyena_k, hyena_v, short_filter, residue, decay_rate):
    rows, channels = hyena_q.shape
    devices = lax.axis_size("ctx")
    modes = residue.shape[1]
    own_blocks = residue.shape[0] // LANES
    blocks = channels // LANES
    groups = blocks // SUBLANES
    width = SUBLANES * LANES
    end = rows // 16 - 1
    par_rows = 2 * own_blocks * modes
    feature_spec = pl.BlockSpec((rows, width), lambda group: (0, group))
    rim_spec = pl.BlockSpec((8, width), lambda group: (0, group))
    chips = SUBLANES // (2 * own_blocks)
    par_spec = pl.BlockSpec((chips, par_rows, LANES), lambda group: (group, 0, 0))
    par_scratch = pltpu.VMEM((2 * SUBLANES * modes, LANES), jnp.float32)
    taps_spec = pl.BlockSpec((TAPS, TAPS, width), lambda group: (0, 0, group))
    positions = pltpu.VMEM((rows * SUBLANES, LANES), jnp.float32)

    def first_part(token):
        own_par, rim = pl.pallas_call(
            conv_pack_kernel,
            grid=(1,),
            in_specs=[pl.BlockSpec((modes, residue.shape[0]), lambda step: (0, 0))] * 2
            + [pl.BlockSpec((16, channels), lambda step: (end, 0))] * 3,
            out_specs=[
                pl.BlockSpec((devices // 2, par_rows, LANES), lambda step: (0, 0, 0)),
                pl.BlockSpec((8, channels), lambda step: (0, 0)),
            ],
            out_shape=[
                jax.ShapeDtypeStruct((devices // 2, par_rows, LANES), jnp.float32),
                jax.ShapeDtypeStruct((8, channels), jnp.float32),
            ],
            compiler_params=params(),
            cost_estimate=cost(1),
            name="conv_pack",
        )(decay_rate.T, residue.T, hyena_q, hyena_k, hyena_v)
        rim = lax.ppermute(rim, "ctx", [(index, index + 1) for index in range(devices - 1)])
        own_par = after(own_par, rim, token)
        same = lax.all_to_all(
            own_par,
            "ctx",
            split_axis=0,
            concat_axis=0,
            axis_index_groups=[list(range(core, devices, 2)) for core in range(2)],
            tiled=True,
        )
        par = (same, lax.ppermute(same, "ctx", [(index, index ^ 1) for index in range(devices)]))
        state_spec = pl.BlockSpec((SUBLANES * modes, LANES), lambda group: (group, 0))
        local_result, state, decay = pl.pallas_call(
            functools.partial(state_kernel, modes),
            grid=(groups,),
            in_specs=[feature_spec, feature_spec, rim_spec, par_spec, par_spec, taps_spec],
            out_specs=[feature_spec, state_spec, state_spec],
            out_shape=[
                jax.ShapeDtypeStruct((rows, channels), jnp.float32),
                jax.ShapeDtypeStruct((blocks * modes, LANES), jnp.float32),
                jax.ShapeDtypeStruct((blocks * modes, LANES), jnp.float32),
            ],
            scratch_shapes=[par_scratch, positions, positions],
            compiler_params=params(),
            cost_estimate=cost(9),
            name="conv_state",
        )(hyena_k, hyena_v, rim, *par, short_filter)
        return local_result, rim, par, decay, *entering_state(state, decay)

    def entering_state(state, decay):
        swap = [(index, index ^ 1) for index in range(devices)]
        other = lax.ppermute(state, "ctx", swap)
        total = state + decay * other
        entering = None
        reach = 1
        while 2 * reach < devices:
            moves = [(index, index + 2 * reach) for index in range(1, devices - 2 * reach, 2)]
            arrived = lax.ppermute(total, "ctx", moves)
            if reach == 1:
                entering = arrived
            else:
                entering = entering + decay ** (2 * (reach - 1)) * arrived
            if 4 * reach < devices:
                total = total + decay ** (2 * reach) * arrived
            reach *= 2
        return entering, lax.ppermute(entering, "ctx", swap), other

    def last_part(local_result, rim, par, decay, entering, entering_first, other):
        state_spec = pl.BlockSpec((SUBLANES * modes, LANES), lambda group: (group, 0))
        return pl.pallas_call(
            functools.partial(output_kernel, modes),
            grid=(groups,),
            in_specs=[feature_spec, feature_spec, rim_spec, par_spec, par_spec]
            + [state_spec] * 4
            + [taps_spec],
            out_specs=feature_spec,
            out_shape=jax.ShapeDtypeStruct((rows, channels), jnp.bfloat16),
            scratch_shapes=[par_scratch],
            compiler_params=params(),
            cost_estimate=cost(6),
            name="conv_output",
        )(
            hyena_q,
            local_result,
            rim,
            *par,
            decay,
            entering,
            entering_first,
            other,
            short_filter,
        )

    return first_part, last_part


def among(me, members):
    return functools.reduce(jnp.logical_or, [me == member for member in members])


def plan_moves(devices):
    quads = devices // 4
    transfers = [[(devices - 1, devices - 3)]]
    for distance in range(1, quads):
        if distance > len(transfers):
            transfers.append([])
        for quad in range(distance, quads):
            target = 4 * (quad - distance) + 2
            transfers[distance - 1] += [(4 * quad, target), (4 * quad + 2, target + 1)]
    return transfers


def soft(query, keys, values, mask=None):
    scores = lax.dot_general(
        query, keys, (((1,), (1,)), ((), ())), preferred_element_type=jnp.float32
    )
    if mask is not None:
        scores = jnp.where(mask, scores, NEGATIVE)
    top = jnp.max(scores, axis=1, keepdims=True) * EXP_SCALE
    expo = jnp.exp2(scores * EXP_SCALE - top).astype(jnp.bfloat16)
    mixed = jnp.dot(expo, values, preferred_element_type=jnp.float32)
    total = mixed[:, HEAD_DIM:]
    return mixed[:, :HEAD_DIM] / total, top + jnp.log2(total)


def pack_kernel(gathers, askers, asked, widths, starts, q_ref, qs_ref, k_ref, v_ref, *rest):
    count = len(widths)
    key_outs, query_outs = rest[:count], rest[count : count + asked]
    stages, in_sems, out_sems = rest[count + asked : -2], rest[-2], rest[-1]
    me = lax.axis_index("ctx")
    odd = me % 2

    def run(pairs):
        loads = [
            pltpu.make_async_copy(source, stage, in_sems.at[index])
            for index, ((source, _), stage) in enumerate(zip(pairs, stages))
        ]
        stores = [
            pltpu.make_async_copy(stage, target, out_sems.at[index])
            for index, ((_, target), stage) in enumerate(zip(pairs, stages))
        ]
        for load in loads:
            load.start()
        for load, store in zip(loads, stores):
            load.wait()
            store.start()
        for store in stores:
            store.wait()

    def cut(ref, chunk):
        return ref.at[:, pl.ds(starts[chunk], widths[chunk])]

    if gathers:

        @pl.when(among(me, gathers))
        def _():
            run(
                [
                    (cut(ref, chunk), key_outs[chunk].at[which])
                    for chunk in range(count)
                    for which, ref in enumerate((k_ref, v_ref))
                ]
            )

    @pl.when(among(me, askers))
    def _():
        run(
            [
                (cut(ref, chunk), query_outs[chunk].at[half])
                for chunk in range(asked)
                for ref, half in ((q_ref, odd), (qs_ref, 1 - odd))
            ]
        )


def as_rows(columns):
    lanes = lax.broadcasted_iota(jnp.int32, columns[0].shape, 1)
    sums = jnp.zeros_like(columns[0])
    for index, column in enumerate(columns):
        sums = jnp.where(lanes == index, column, sums)
    return jnp.transpose(sums)[:SUBLANES]


def as_columns(part):
    fill = jnp.zeros((LANES - part.shape[0], part.shape[1]), jnp.float32)
    return jnp.transpose(jnp.concatenate([part, fill], 0))


def partial_kernel(transfers, upper, natural, asking, onto, *refs):
    count = len(transfers)
    out_ref = refs[-1]
    if asking:
        next_refs = refs[7 + count : 9 + count]
        refs = refs[: 7 + count] + refs[9 + count :]
    q_ref, k_ref, v_ref, kp_ref, vp_ref, g_ref, gp_ref = refs[:7]
    ask_refs = refs[7 : 7 + count]
    own_ref, lse_ref = refs[7 + count + onto : 9 + count + onto]
    answer_refs = refs[9 + count + onto : -1]
    me = lax.axis_index("ctx")
    rows = q_ref.shape[0]
    heads = q_ref.shape[1] // HEAD_DIM
    half_rows = heads * rows + TAIL

    def key_value(head, with_quad):
        cut = block_lanes(head)
        keys = [kp_ref[:, cut], k_ref[:, cut]]
        values = [vp_ref[:, cut], v_ref[:, cut]]
        if with_quad:
            keys = [g_ref[0, :, cut], gp_ref[0, :, cut]] + keys
            values = [g_ref[1, :, cut], gp_ref[1, :, cut]] + values
        values = jnp.concatenate(values, 0)
        return jnp.concatenate(keys, 0), jnp.concatenate([values, jnp.ones_like(values)], 1)

    def run(with_quad):
        key_count = rows * (4 if with_quad else 2)
        row = lax.broadcasted_iota(jnp.int32, (rows, key_count), 0)
        column = lax.broadcasted_iota(jnp.int32, (rows, key_count), 1)
        column = column - (key_count - 2 * rows)
        partner_limit = jnp.where(me % 2 == 1, rows, 0)
        mask = (column < partner_limit) | ((column >= rows) & (column - rows <= row))
        sums = []
        for head in range(heads):
            keys, values = key_value(head, with_quad)
            mixed, lse = soft(q_ref[:, block_lanes(head)], keys, values, mask)
            own_ref[:, block_lanes(head)] = mixed
            out_ref[:, block_lanes(head)] = mixed.astype(out_ref.dtype)
            sums.append(lse)
        lse_ref[...] = as_rows(sums)

        def answer(index):
            sums = [[], []]
            for head in range(heads):
                keys, values = key_value(head, with_quad)
                if natural:
                    query = ask_refs[index][:, :, block_lanes(head)].reshape(2 * rows, HEAD_DIM)
                else:
                    halves = [half * half_rows + head * rows for half in range(2)]
                    query = jnp.concatenate(
                        [ask_refs[index][start : start + rows, :] for start in halves], 0
                    )
                mixed, lse = soft(query, keys, values)
                for half in range(2):
                    cut = slice(half * rows, (half + 1) * rows)
                    start = half * half_rows + head * rows
                    answer_refs[index][start : start + rows, :] = mixed[cut].astype(jnp.bfloat16)
                    sums[half].append(lse[cut])
            for half in range(2):
                start = half * half_rows + heads * rows
                lse = as_rows(sums[half])
                first = lse.astype(jnp.bfloat16).astype(jnp.float32)
                second = (lse - first).astype(jnp.bfloat16).astype(jnp.float32)
                third = lse - first - second
                tail = jnp.concatenate([first, second, third, jnp.zeros_like(lse)], 0)
                answer_refs[index][start : start + TAIL, :] = tail.astype(jnp.bfloat16)

        for index, pairs in enumerate(transfers):
            asked = [target for _, target in pairs if (target in upper) == with_quad]
            if asked:
                pl.when(among(me, asked))(functools.partial(answer, index))

    if upper:
        pl.when(among(me, upper))(functools.partial(run, True))
        pl.when(jnp.logical_not(among(me, upper)))(functools.partial(run, False))
    else:
        run(False)

    if asking:
        for index, pairs in enumerate(transfers):

            @pl.when(among(me, [source for source, _ in pairs]))
            def _():
                for ref, half in zip(next_refs, (me % 2, 1 - me % 2)):
                    for head in range(heads):
                        start = pl.multiple_of(half * half_rows + head * rows, TAIL)
                        answer_refs[index][pl.ds(start, rows), :] = ref[:, block_lanes(head)]


def merge_kernel(transfers, steps, start, own_hbm, lse_hbm, *refs):
    count = 2 * len(transfers)
    others_hbm, out_hbm = refs[:count], refs[count + 1]
    own_ref, lse_ref, *other_refs = refs[count + 2 : 2 * count + 4]
    out_ref, sems = refs[-2:]
    me = lax.axis_index("ctx")
    odd = me % 2
    rows, width = own_ref.shape
    heads = HEADS_PER_STEP
    half_rows = heads * rows + TAIL
    returned = []
    for pairs in transfers:
        members = [source for source, _ in pairs]
        returned += [members, [member ^ 1 for member in members]]

    @pl.when(among(me, sorted(set(sum(returned, [])))))
    def _():
        loads = [(own_hbm, own_ref), (lse_hbm, lse_ref)]
        for hbm, ref in zip(others_hbm, other_refs):
            for step in range(steps):
                half = pl.ds(pl.multiple_of((2 * step + odd) * half_rows, TAIL), half_rows)
                loads.append((hbm.at[half, :], ref.at[step]))
        copies = [
            pltpu.make_async_copy(source, target, sems.at[index])
            for index, (source, target) in enumerate(loads)
        ]
        for copy in copies:
            copy.start()
        for copy in copies:
            copy.wait()
        valid = [among(me, members) for members in returned]
        for step in range(steps):
            logs = [lse_ref[step * SUBLANES : (step + 1) * SUBLANES, :]]
            for index, ref in enumerate(other_refs):
                tail = ref[step, heads * rows :, :].astype(jnp.float32)
                parts = [tail[part * SUBLANES : (part + 1) * SUBLANES] for part in range(3)]
                logs.append(jnp.where(valid[index], parts[0] + parts[1] + parts[2], NEGATIVE))
            top = functools.reduce(jnp.maximum, logs)
            weights = [jnp.exp2(part - top) for part in logs]
            total = functools.reduce(jnp.add, weights)
            shares = [as_columns(weight / total) for weight in weights]
            for head in range(heads):
                cut = block_lanes(step * heads + head)
                mixed = [own_ref[:, cut]]
                for index, ref in enumerate(other_refs):
                    part = ref[step, head * rows : (head + 1) * rows, :].astype(jnp.float32)
                    mixed.append(jnp.where(valid[index], part, 0.0))
                terms = [part * share[:, head : head + 1] for part, share in zip(mixed, shares)]
                out_ref[:, cut] = functools.reduce(jnp.add, terms).astype(out_ref.dtype)
        store = pltpu.make_async_copy(
            out_ref, out_hbm.at[:, pl.ds(start, width)], sems.at[len(copies)]
        )
        store.start()
        store.wait()


def after(array, *others):
    return lax.optimization_barrier((array, *others))[0]


def attend(query, key, value, conv):
    rows, columns = query.shape
    devices = lax.axis_size("ctx")
    quads = devices // 4
    transfers = plan_moves(devices)
    step_width = HEADS_PER_STEP * HEAD_DIM
    chunks = len(CHUNK_STEPS)
    first_steps = [sum(CHUNK_STEPS[:chunk]) for chunk in range(chunks)]
    widths = [steps * step_width for steps in CHUNK_STEPS]
    starts = [step * step_width for step in first_steps]
    upper = [4 * quad + 2 + core for quad in range(quads - 1) for core in range(2)]
    gathers = [(who - 2, who) for who in upper]
    askers = sorted({source for pairs in transfers for source, _ in pairs})
    swap = [(index, index ^ 1) for index in range(devices)]

    query_swapped = lax.ppermute(query, "ctx", swap)
    key_swapped = lax.ppermute(key, "ctx", swap)
    value_swapped = lax.ppermute(value, "ctx", swap)

    both_ways = chunks > LAG and all(
        not {source for source, _ in pairs} & {target for _, target in pairs}
        for pairs in transfers
    )
    asked = LAG if both_ways else chunks

    def pack():
        hbm = pl.BlockSpec(memory_space=pl.ANY)
        shapes = [jax.ShapeDtypeStruct((2, rows, width), jnp.bfloat16) for width in widths]
        outs = pl.pallas_call(
            functools.partial(
                pack_kernel,
                [source for source, _ in gathers],
                askers,
                asked,
                widths,
                starts,
            ),
            in_specs=[hbm] * 4,
            out_specs=[hbm] * (chunks + asked),
            out_shape=shapes + shapes[:asked],
            scratch_shapes=[
                pltpu.VMEM((rows, width), jnp.bfloat16) for width in widths for _ in range(2)
            ]
            + [pltpu.SemaphoreType.DMA((2 * chunks,))] * 2,
            compiler_params=params(),
            cost_estimate=cost(1),
            name="att_pack",
        )(query, query_swapped, key, value)
        return outs[:chunks], outs[chunks:]

    key_packs, query_packs = pack()
    conv_first, conv_last = conv
    local_result, *conv_shared = conv_first(query_packs[0])
    asks, quad_kv, all_answers = {}, [], []

    def send(chunk):
        key_pack = key_packs[chunk]
        if chunk >= LAG:
            earlier = all_answers[chunk - LAG - 1] if chunk > LAG else asks[0]
            key_pack = after(key_pack, quad_kv[chunk - LAG][0], earlier[0])
        quad_kv.append([lax.ppermute(key_pack, "ctx", gathers)])
        if chunk < asked:
            query_pack = query_packs[chunk]
            if chunk >= LAG:
                query_pack = after(query_pack, *asks[chunk - LAG], all_answers[chunk - LAG][0])
            asks[chunk] = [lax.ppermute(query_pack, "ctx", pairs) for pairs in transfers]

    half_rows = HEADS_PER_STEP * rows + TAIL
    hbm = pl.BlockSpec(memory_space=pl.ANY)
    for chunk in range(min(LAG, chunks)):
        send(chunk)
    result = None
    returned = []
    for chunk in range(chunks):
        if chunk == 0:
            quad_kv[0] = [after(quad_kv[0][0], local_result)]
            asks[0] = [after(asked, local_result) for asked in asks[0]]
        quad_kv[chunk].append(lax.ppermute(quad_kv[chunk][0], "ctx", swap))
        steps, first = CHUNK_STEPS[chunk], first_steps[chunk]
        whole_spec = pl.BlockSpec((rows, step_width), lambda step, first=first: (0, first + step))
        chunk_spec = pl.BlockSpec((rows, step_width), lambda step: (0, step))
        pair_spec = pl.BlockSpec((2, rows, step_width), lambda step: (0, 0, step))
        lse_spec = pl.BlockSpec((SUBLANES, LANES), lambda step: (step, 0))
        answer_spec = pl.BlockSpec((2 * half_rows, LANES), lambda step: (step, 0))
        answer_shape = jax.ShapeDtypeStruct((2 * half_rows * steps, LANES), jnp.bfloat16)
        asking = both_ways and chunk + LAG < chunks
        natural = chunk < asked
        operands = [query, key, value, key_swapped, value_swapped, *quad_kv[chunk], *asks[chunk]]
        specs = [whole_spec] * 5 + [pair_spec] * 2
        specs += [pair_spec if natural else answer_spec] * len(transfers)
        if asking:
            later = first_steps[chunk + LAG]
            operands += [query, query_swapped]
            specs += [
                pl.BlockSpec((rows, step_width), lambda step, later=later: (0, later + step))
            ] * 2
        aliases = {}
        if result is not None:
            aliases = {len(operands): 2 + len(transfers)}
            operands.append(result)
            specs.append(hbm)
        own, lse, *answers, result = pl.pallas_call(
            functools.partial(partial_kernel, transfers, upper, natural, asking, len(aliases)),
            grid=(steps,),
            in_specs=specs,
            out_specs=[chunk_spec, lse_spec] + [answer_spec] * len(transfers) + [whole_spec],
            out_shape=[
                jax.ShapeDtypeStruct((rows, widths[chunk]), jnp.float32),
                jax.ShapeDtypeStruct((SUBLANES * steps, LANES), jnp.float32),
            ]
            + [answer_shape] * len(transfers)
            + [jax.ShapeDtypeStruct((rows, columns), jnp.bfloat16)],
            input_output_aliases=aliases,
            compiler_params=params(),
            cost_estimate=cost(4),
            name="att_partial",
        )(*operands)
        all_answers.append(answers)
        parts = [own, lse]
        arrivals = []
        for answer, pairs in zip(answers, transfers):
            moves = [(target, source) for source, target in pairs]
            if asking:
                moves += pairs
            if chunk == chunks - 1:
                live = (answer, conv_shared, [part[2] for part in returned], result)
                answer, conv_shared, early, result = lax.optimization_barrier(live)
                returned = [part[:2] + [back] for part, back in zip(returned, early)]
            arrivals.append(lax.ppermute(answer, "ctx", moves))
        if asking:
            asks[chunk + LAG] = arrivals
        returned.append([own, lse, arrivals])
        if chunk + LAG < chunks:
            send(chunk + LAG)
    hyena_out = conv_last(local_result, *conv_shared)
    for chunk, (own, lse, arrivals) in enumerate(returned):
        if chunk == chunks - 1:
            live = (arrivals, hyena_out, result)
            arrivals, hyena_out, result = lax.optimization_barrier(live)
        parts = [own, lse]
        for arrival in arrivals:
            parts += [arrival, lax.ppermute(arrival, "ctx", swap)]
        steps = CHUNK_STEPS[chunk]
        count = 2 * len(transfers)
        result = pl.pallas_call(
            functools.partial(merge_kernel, transfers, steps, starts[chunk]),
            in_specs=[hbm] * (len(parts) + 1),
            out_specs=hbm,
            out_shape=jax.ShapeDtypeStruct((rows, columns), jnp.bfloat16),
            input_output_aliases={len(parts): 0},
            scratch_shapes=[
                pltpu.VMEM((rows, widths[chunk]), jnp.float32),
                pltpu.VMEM((SUBLANES * steps, LANES), jnp.float32),
            ]
            + [pltpu.VMEM((steps, half_rows, LANES), jnp.bfloat16)] * count
            + [
                pltpu.VMEM((rows, widths[chunk]), jnp.bfloat16),
                pltpu.SemaphoreType.DMA((3 + count * steps,)),
            ],
            compiler_params=params(),
            cost_estimate=cost(2),
            name="att_merge",
        )(*parts, result)
    return hyena_out, result


def local(
    hyena_q, hyena_k, hyena_v, short_filter, residue, decay_rate, att_query, att_key, att_value
):
    conv = convolution(hyena_q, hyena_k, hyena_v, short_filter, residue, decay_rate)
    return attend(att_query, att_key, att_value, conv)


def solution(mesh):
    rows = P(("dp", "ctx"), None)
    shared = P("ctx", None)
    return jax.shard_map(
        local,
        mesh=mesh,
        in_specs=(rows, rows, rows, P(), shared, shared, rows, rows, rows),
        out_specs=(rows, rows),
        check_vma=False,
    )
```

```python
import functools
import math

import jax
import jax.numpy as jnp
from jax import lax
from jax.experimental import pallas as pl
from jax.experimental.pallas import tpu as pltpu
from jax.sharding import PartitionSpec as P

HEAD_DIM = 128
LANES = 128
SUBLANES = 8
TAIL = 4 * SUBLANES
TAPS = 3
HEADS_PER_STEP = 4
CHUNK_STEPS = (2, 2, 2, 2)
LAG = 2
NEGATIVE = -1e30
EXP_SCALE = HEAD_DIM**-0.5 * math.log2(math.e)
VMEM_LIMIT = 255 * 1024 * 256


def params(**kwargs):
    return pltpu.CompilerParams(vmem_limit_bytes=VMEM_LIMIT, **kwargs)


def cost(microseconds):
    return pl.CostEstimate(
        flops=microseconds * 10**8, bytes_accessed=2**16, transcendentals=0
    )


def block_lanes(block):
    return slice(block * LANES, (block + 1) * LANES)


def conv_pack_kernel(rate_ref, residue_ref, q_ref, k_ref, v_ref, par_ref, rim_ref):
    modes = rate_ref.shape[0]
    for block in range(rate_ref.shape[1] // LANES):
        for which, ref in enumerate((rate_ref, residue_ref)):
            start = (2 * block + which) * modes
            for device in range(par_ref.shape[0]):
                par_ref[device, start : start + modes, :] = ref[:, block_lanes(block)]
    for feature, ref in enumerate((q_ref, k_ref, v_ref)):
        last = ref[...].astype(jnp.float32)[ref.shape[0] - 2 :]
        rim_ref[2 * feature : 2 * feature + 2, :] = last
    rim_ref[2 * TAPS :, :] = jnp.zeros((2, rim_ref.shape[1]), jnp.float32)


def rim_rows(rim_ref, feature, lanes):
    return [rim_ref[pl.ds(2 * feature + row, 1), lanes] for row in range(2)]


def short_mix(feature, rim, taps):
    two_before, one_before = rim
    row = lax.broadcasted_iota(jnp.int32, feature.shape, 0)
    one = jnp.where(row == 0, one_before, pltpu.roll(feature, 1, 0))
    two = jnp.where(row == 0, two_before, jnp.where(row == 1, one_before, pltpu.roll(feature, 2, 0)))
    return taps[0] * feature + taps[1] * one + taps[2] * two


def tap_rows(taps_ref, feature, lanes):
    return [taps_ref[feature, pl.ds(tap, 1), lanes] for tap in range(TAPS)]


def join_parameters(same_ref, other_ref, par_ref):
    odd = lax.axis_index("ctx") % 2
    chips, rows, _ = same_ref.shape
    for chip in range(chips):
        for ref, core in ((same_ref, odd), (other_ref, 1 - odd)):
            start = pl.multiple_of((2 * chip + core) * rows, SUBLANES)
            par_ref[pl.ds(start, rows), :] = ref[chip]


def state_kernel(
    modes,
    k_ref,
    v_ref,
    rim_ref,
    same_ref,
    other_ref,
    taps_ref,
    y_ref,
    s_ref,
    d_ref,
    par_ref,
    p_scr,
    y_scr,
):
    join_parameters(same_ref, other_ref, par_ref)
    rows = k_ref.shape[0]
    for block in range(SUBLANES):
        lanes = block_lanes(block)
        mixes = [
            short_mix(
                ref[:, lanes].astype(jnp.float32),
                rim_rows(rim_ref, feature, lanes),
                tap_rows(taps_ref, feature, lanes),
            )
            for feature, ref in ((1, k_ref), (2, v_ref))
        ]
        product = (mixes[0] * mixes[1]).astype(jnp.bfloat16).astype(jnp.float32)
        p_scr[pl.ds(block, rows, SUBLANES), :] = product
    decay = [jnp.exp(-par_ref[pl.ds(mode, SUBLANES, 2 * modes), :]) for mode in range(modes)]
    residue = [par_ref[pl.ds(modes + mode, SUBLANES, 2 * modes), :] for mode in range(modes)]

    def body(position, states):
        here = pl.ds(pl.multiple_of(position * SUBLANES, SUBLANES), SUBLANES)
        product = p_scr[here, :]
        states = tuple(state * rate + product for state, rate in zip(states, decay))
        terms = [state * weight for state, weight in zip(states, residue)]
        while len(terms) > 1:
            terms = [left + right for left, right in zip(terms[::2], terms[1::2])]
        y_scr[here, :] = terms[0]
        return states

    zero = jnp.zeros((SUBLANES, LANES), jnp.float32)
    states = lax.fori_loop(0, rows, body, (zero,) * modes, unroll=4)
    for mode in range(modes):
        s_ref[pl.ds(mode, SUBLANES, modes), :] = states[mode]
    for block in range(SUBLANES):
        rate = par_ref[2 * block * modes : (2 * block + 1) * modes, :]
        d_ref[block * modes : (block + 1) * modes, :] = jnp.exp(-rate * rows)
    for block in range(SUBLANES):
        y_ref[:, block_lanes(block)] = y_scr[pl.ds(block, rows, SUBLANES), :]


def output_kernel(
    modes,
    q_ref,
    y_ref,
    rim_ref,
    same_ref,
    other_par_ref,
    decay_ref,
    enter_ref,
    enter_first_ref,
    other_ref,
    taps_ref,
    out_ref,
    par_ref,
):
    join_parameters(same_ref, other_par_ref, par_ref)
    second = lax.axis_index("ctx") % 2 == 1
    rows = q_ref.shape[0]
    step = lax.broadcasted_iota(jnp.int32, (SUBLANES, LANES), 0).astype(jnp.float32) + 1.0

    def body(block, nothing):
        lanes = pl.ds(pl.multiple_of(block * LANES, LANES), LANES)
        rate = par_ref[pl.ds(pl.multiple_of(2 * block * modes, SUBLANES), modes), :]
        residue = par_ref[pl.ds(pl.multiple_of((2 * block + 1) * modes, SUBLANES), modes), :]
        here = pl.ds(pl.multiple_of(block * modes, SUBLANES), modes)
        after_first = decay_ref[here, :] * enter_ref[here, :] + other_ref[here, :]
        entering = jnp.where(second, after_first, enter_first_ref[here, :])
        weighted = residue * entering
        eight = jnp.exp(-rate * SUBLANES)
        terms = [
            weighted[mode : mode + 1] * jnp.exp(-rate[mode : mode + 1] * step)
            for mode in range(modes)
        ]
        eights = [jnp.broadcast_to(eight[mode : mode + 1], terms[0].shape) for mode in range(modes)]
        added = []
        for start in range(0, rows, SUBLANES):
            sums = list(terms)
            while len(sums) > 1:
                sums = [left + right for left, right in zip(sums[::2], sums[1::2])]
            added.append(sums[0])
            if start + SUBLANES < rows:
                terms = [term * decay for term, decay in zip(terms, eights)]
        smoothed = y_ref[:, lanes] + jnp.concatenate(added, 0)
        smoothed = smoothed.astype(jnp.bfloat16).astype(jnp.float32)
        mix = short_mix(
            q_ref[:, lanes].astype(jnp.float32),
            rim_rows(rim_ref, 0, lanes),
            tap_rows(taps_ref, 0, lanes),
        )
        out_ref[:, lanes] = (mix * smoothed).astype(out_ref.dtype)
        return nothing

    lax.fori_loop(0, SUBLANES, body, 0)


def convolution(hyena_q, hyena_k, hyena_v, short_filter, residue, decay_rate):
    rows, channels = hyena_q.shape
    devices = lax.axis_size("ctx")
    modes = residue.shape[1]
    own_blocks = residue.shape[0] // LANES
    blocks = channels // LANES
    groups = blocks // SUBLANES
    width = SUBLANES * LANES
    end = rows // 16 - 1
    par_rows = 2 * own_blocks * modes
    feature_spec = pl.BlockSpec((rows, width), lambda group: (0, group))
    rim_spec = pl.BlockSpec((8, width), lambda group: (0, group))
    chips = SUBLANES // (2 * own_blocks)
    par_spec = pl.BlockSpec((chips, par_rows, LANES), lambda group: (group, 0, 0))
    par_scratch = pltpu.VMEM((2 * SUBLANES * modes, LANES), jnp.float32)
    taps_spec = pl.BlockSpec((TAPS, TAPS, width), lambda group: (0, 0, group))
    positions = pltpu.VMEM((rows * SUBLANES, LANES), jnp.float32)

    def first_part(token):
        own_par, rim = pl.pallas_call(
            conv_pack_kernel,
            grid=(1,),
            in_specs=[pl.BlockSpec((modes, residue.shape[0]), lambda step: (0, 0))] * 2
            + [pl.BlockSpec((16, channels), lambda step: (end, 0))] * 3,
            out_specs=[
                pl.BlockSpec((devices // 2, par_rows, LANES), lambda step: (0, 0, 0)),
                pl.BlockSpec((8, channels), lambda step: (0, 0)),
            ],
            out_shape=[
                jax.ShapeDtypeStruct((devices // 2, par_rows, LANES), jnp.float32),
                jax.ShapeDtypeStruct((8, channels), jnp.float32),
            ],
            compiler_params=params(),
            cost_estimate=cost(1),
            name="conv_pack",
        )(decay_rate.T, residue.T, hyena_q, hyena_k, hyena_v)
        rim = lax.ppermute(rim, "ctx", [(index, index + 1) for index in range(devices - 1)])
        own_par = after(own_par, rim, token)
        same = lax.all_to_all(
            own_par,
            "ctx",
            split_axis=0,
            concat_axis=0,
            axis_index_groups=[list(range(core, devices, 2)) for core in range(2)],
            tiled=True,
        )
        par = (same, lax.ppermute(same, "ctx", [(index, index ^ 1) for index in range(devices)]))
        state_spec = pl.BlockSpec((SUBLANES * modes, LANES), lambda group: (group, 0))
        local_result, state, decay = pl.pallas_call(
            functools.partial(state_kernel, modes),
            grid=(groups,),
            in_specs=[feature_spec, feature_spec, rim_spec, par_spec, par_spec, taps_spec],
            out_specs=[feature_spec, state_spec, state_spec],
            out_shape=[
                jax.ShapeDtypeStruct((rows, channels), jnp.float32),
                jax.ShapeDtypeStruct((blocks * modes, LANES), jnp.float32),
                jax.ShapeDtypeStruct((blocks * modes, LANES), jnp.float32),
            ],
            scratch_shapes=[par_scratch, positions, positions],
            compiler_params=params(),
            cost_estimate=cost(9),
            name="conv_state",
        )(hyena_k, hyena_v, rim, *par, short_filter)
        return local_result, rim, par, decay, *entering_state(state, decay)

    def entering_state(state, decay):
        swap = [(index, index ^ 1) for index in range(devices)]
        other = lax.ppermute(state, "ctx", swap)
        total = state + decay * other
        entering = None
        reach = 1
        while 2 * reach < devices:
            moves = [(index, index + 2 * reach) for index in range(1, devices - 2 * reach, 2)]
            arrived = lax.ppermute(total, "ctx", moves)
            if reach == 1:
                entering = arrived
            else:
                entering = entering + decay ** (2 * (reach - 1)) * arrived
            if 4 * reach < devices:
                total = total + decay ** (2 * reach) * arrived
            reach *= 2
        return entering, lax.ppermute(entering, "ctx", swap), other

    def last_part(local_result, rim, par, decay, entering, entering_first, other):
        state_spec = pl.BlockSpec((SUBLANES * modes, LANES), lambda group: (group, 0))
        return pl.pallas_call(
            functools.partial(output_kernel, modes),
            grid=(groups,),
            in_specs=[feature_spec, feature_spec, rim_spec, par_spec, par_spec]
            + [state_spec] * 4
            + [taps_spec],
            out_specs=feature_spec,
            out_shape=jax.ShapeDtypeStruct((rows, channels), jnp.bfloat16),
            scratch_shapes=[par_scratch],
            compiler_params=params(),
            cost_estimate=cost(6),
            name="conv_output",
        )(
            hyena_q,
            local_result,
            rim,
            *par,
            decay,
            entering,
            entering_first,
            other,
            short_filter,
        )

    return first_part, last_part


def among(me, members):
    return functools.reduce(jnp.logical_or, [me == member for member in members])


def plan_moves(devices):
    quads = devices // 4
    transfers = [[(devices - 1, devices - 3)]]
    for distance in range(1, quads):
        if distance > len(transfers):
            transfers.append([])
        for quad in range(distance, quads):
            target = 4 * (quad - distance) + 2
            transfers[distance - 1] += [(4 * quad, target), (4 * quad + 2, target + 1)]
    return transfers


def soft(query, keys, values, mask=None):
    scores = lax.dot_general(
        query, keys, (((1,), (1,)), ((), ())), preferred_element_type=jnp.float32
    )
    if mask is not None:
        scores = jnp.where(mask, scores, NEGATIVE)
    top = jnp.max(scores, axis=1, keepdims=True) * EXP_SCALE
    expo = jnp.exp2(scores * EXP_SCALE - top).astype(jnp.bfloat16)
    mixed = jnp.dot(expo, values, preferred_element_type=jnp.float32)
    total = mixed[:, HEAD_DIM:]
    return mixed[:, :HEAD_DIM] / total, top + jnp.log2(total)


def pack_kernel(gathers, askers, asked, widths, starts, q_ref, qs_ref, k_ref, v_ref, *rest):
    count = len(widths)
    key_outs, query_outs = rest[:count], rest[count : count + asked]
    stages, in_sems, out_sems = rest[count + asked : -2], rest[-2], rest[-1]
    me = lax.axis_index("ctx")
    odd = me % 2

    def run(pairs):
        loads = [
            pltpu.make_async_copy(source, stage, in_sems.at[index])
            for index, ((source, _), stage) in enumerate(zip(pairs, stages))
        ]
        stores = [
            pltpu.make_async_copy(stage, target, out_sems.at[index])
            for index, ((_, target), stage) in enumerate(zip(pairs, stages))
        ]
        for load in loads:
            load.start()
        for load, store in zip(loads, stores):
            load.wait()
            store.start()
        for store in stores:
            store.wait()

    def cut(ref, chunk):
        return ref.at[:, pl.ds(starts[chunk], widths[chunk])]

    if gathers:

        @pl.when(among(me, gathers))
        def _():
            run(
                [
                    (cut(ref, chunk), key_outs[chunk].at[which])
                    for chunk in range(count)
                    for which, ref in enumerate((k_ref, v_ref))
                ]
            )

    @pl.when(among(me, askers))
    def _():
        run(
            [
                (cut(ref, chunk), query_outs[chunk].at[half])
                for chunk in range(asked)
                for ref, half in ((q_ref, odd), (qs_ref, 1 - odd))
            ]
        )


def as_rows(columns):
    lanes = lax.broadcasted_iota(jnp.int32, columns[0].shape, 1)
    sums = jnp.zeros_like(columns[0])
    for index, column in enumerate(columns):
        sums = jnp.where(lanes == index, column, sums)
    return jnp.transpose(sums)[:SUBLANES]


def as_columns(part):
    fill = jnp.zeros((LANES - part.shape[0], part.shape[1]), jnp.float32)
    return jnp.transpose(jnp.concatenate([part, fill], 0))


def partial_kernel(transfers, upper, natural, asking, onto, *refs):
    count = len(transfers)
    out_ref = refs[-1]
    if asking:
        next_refs = refs[7 + count : 9 + count]
        refs = refs[: 7 + count] + refs[9 + count :]
    q_ref, k_ref, v_ref, kp_ref, vp_ref, g_ref, gp_ref = refs[:7]
    ask_refs = refs[7 : 7 + count]
    own_ref, lse_ref = refs[7 + count + onto : 9 + count + onto]
    answer_refs = refs[9 + count + onto : -1]
    me = lax.axis_index("ctx")
    rows = q_ref.shape[0]
    heads = q_ref.shape[1] // HEAD_DIM
    half_rows = heads * rows + TAIL

    def key_value(head, with_quad):
        cut = block_lanes(head)
        keys = [kp_ref[:, cut], k_ref[:, cut]]
        values = [vp_ref[:, cut], v_ref[:, cut]]
        if with_quad:
            keys = [g_ref[0, :, cut], gp_ref[0, :, cut]] + keys
            values = [g_ref[1, :, cut], gp_ref[1, :, cut]] + values
        values = jnp.concatenate(values, 0)
        return jnp.concatenate(keys, 0), jnp.concatenate([values, jnp.ones_like(values)], 1)

    def run(with_quad):
        key_count = rows * (4 if with_quad else 2)
        row = lax.broadcasted_iota(jnp.int32, (rows, key_count), 0)
        column = lax.broadcasted_iota(jnp.int32, (rows, key_count), 1)
        column = column - (key_count - 2 * rows)
        partner_limit = jnp.where(me % 2 == 1, rows, 0)
        mask = (column < partner_limit) | ((column >= rows) & (column - rows <= row))
        sums = []
        for head in range(heads):
            keys, values = key_value(head, with_quad)
            mixed, lse = soft(q_ref[:, block_lanes(head)], keys, values, mask)
            own_ref[:, block_lanes(head)] = mixed
            out_ref[:, block_lanes(head)] = mixed.astype(out_ref.dtype)
            sums.append(lse)
        lse_ref[...] = as_rows(sums)

        def answer(index):
            sums = [[], []]
            for head in range(heads):
                keys, values = key_value(head, with_quad)
                if natural:
                    query = ask_refs[index][:, :, block_lanes(head)].reshape(2 * rows, HEAD_DIM)
                else:
                    halves = [half * half_rows + head * rows for half in range(2)]
                    query = jnp.concatenate(
                        [ask_refs[index][start : start + rows, :] for start in halves], 0
                    )
                mixed, lse = soft(query, keys, values)
                for half in range(2):
                    cut = slice(half * rows, (half + 1) * rows)
                    start = half * half_rows + head * rows
                    answer_refs[index][start : start + rows, :] = mixed[cut].astype(jnp.bfloat16)
                    sums[half].append(lse[cut])
            for half in range(2):
                start = half * half_rows + heads * rows
                lse = as_rows(sums[half])
                first = lse.astype(jnp.bfloat16).astype(jnp.float32)
                second = (lse - first).astype(jnp.bfloat16).astype(jnp.float32)
                third = lse - first - second
                tail = jnp.concatenate([first, second, third, jnp.zeros_like(lse)], 0)
                answer_refs[index][start : start + TAIL, :] = tail.astype(jnp.bfloat16)

        for index, pairs in enumerate(transfers):
            asked = [target for _, target in pairs if (target in upper) == with_quad]
            if asked:
                pl.when(among(me, asked))(functools.partial(answer, index))

    if upper:
        pl.when(among(me, upper))(functools.partial(run, True))
        pl.when(jnp.logical_not(among(me, upper)))(functools.partial(run, False))
    else:
        run(False)

    if asking:
        for index, pairs in enumerate(transfers):

            @pl.when(among(me, [source for source, _ in pairs]))
            def _():
                for ref, half in zip(next_refs, (me % 2, 1 - me % 2)):
                    for head in range(heads):
                        start = pl.multiple_of(half * half_rows + head * rows, TAIL)
                        answer_refs[index][pl.ds(start, rows), :] = ref[:, block_lanes(head)]


def merge_kernel(transfers, steps, start, own_hbm, lse_hbm, *refs):
    count = 2 * len(transfers)
    others_hbm, out_hbm = refs[:count], refs[count + 1]
    own_ref, lse_ref, *other_refs = refs[count + 2 : 2 * count + 4]
    out_ref, sems = refs[-2:]
    me = lax.axis_index("ctx")
    odd = me % 2
    rows, width = own_ref.shape
    heads = HEADS_PER_STEP
    half_rows = heads * rows + TAIL
    returned = []
    for pairs in transfers:
        members = [source for source, _ in pairs]
        returned += [members, [member ^ 1 for member in members]]

    @pl.when(among(me, sorted(set(sum(returned, [])))))
    def _():
        loads = [(own_hbm, own_ref), (lse_hbm, lse_ref)]
        for hbm, ref in zip(others_hbm, other_refs):
            for step in range(steps):
                half = pl.ds(pl.multiple_of((2 * step + odd) * half_rows, TAIL), half_rows)
                loads.append((hbm.at[half, :], ref.at[step]))
        copies = [
            pltpu.make_async_copy(source, target, sems.at[index])
            for index, (source, target) in enumerate(loads)
        ]
        for copy in copies:
            copy.start()
        for copy in copies:
            copy.wait()
        valid = [among(me, members) for members in returned]
        for step in range(steps):
            logs = [lse_ref[step * SUBLANES : (step + 1) * SUBLANES, :]]
            for index, ref in enumerate(other_refs):
                tail = ref[step, heads * rows :, :].astype(jnp.float32)
                parts = [tail[part * SUBLANES : (part + 1) * SUBLANES] for part in range(3)]
                logs.append(jnp.where(valid[index], parts[0] + parts[1] + parts[2], NEGATIVE))
            top = functools.reduce(jnp.maximum, logs)
            weights = [jnp.exp2(part - top) for part in logs]
            total = functools.reduce(jnp.add, weights)
            shares = [as_columns(weight / total) for weight in weights]
            for head in range(heads):
                cut = block_lanes(step * heads + head)
                mixed = [own_ref[:, cut]]
                for index, ref in enumerate(other_refs):
                    part = ref[step, head * rows : (head + 1) * rows, :].astype(jnp.float32)
                    mixed.append(jnp.where(valid[index], part, 0.0))
                terms = [part * share[:, head : head + 1] for part, share in zip(mixed, shares)]
                out_ref[:, cut] = functools.reduce(jnp.add, terms).astype(out_ref.dtype)
        store = pltpu.make_async_copy(
            out_ref, out_hbm.at[:, pl.ds(start, width)], sems.at[len(copies)]
        )
        store.start()
        store.wait()


def after(array, *others):
    return lax.optimization_barrier((array, *others))[0]


def attend(query, key, value, conv):
    rows, columns = query.shape
    devices = lax.axis_size("ctx")
    quads = devices // 4
    transfers = plan_moves(devices)
    step_width = HEADS_PER_STEP * HEAD_DIM
    chunks = len(CHUNK_STEPS)
    first_steps = [sum(CHUNK_STEPS[:chunk]) for chunk in range(chunks)]
    widths = [steps * step_width for steps in CHUNK_STEPS]
    starts = [step * step_width for step in first_steps]
    upper = [4 * quad + 2 + core for quad in range(quads - 1) for core in range(2)]
    gathers = [(who - 2, who) for who in upper]
    askers = sorted({source for pairs in transfers for source, _ in pairs})
    swap = [(index, index ^ 1) for index in range(devices)]

    query_swapped = lax.ppermute(query, "ctx", swap)
    key_swapped = lax.ppermute(key, "ctx", swap)
    value_swapped = lax.ppermute(value, "ctx", swap)

    both_ways = chunks > LAG and all(
        not {source for source, _ in pairs} & {target for _, target in pairs}
        for pairs in transfers
    )
    asked = LAG if both_ways else chunks

    def pack():
        hbm = pl.BlockSpec(memory_space=pl.ANY)
        shapes = [jax.ShapeDtypeStruct((2, rows, width), jnp.bfloat16) for width in widths]
        outs = pl.pallas_call(
            functools.partial(
                pack_kernel,
                [source for source, _ in gathers],
                askers,
                asked,
                widths,
                starts,
            ),
            in_specs=[hbm] * 4,
            out_specs=[hbm] * (chunks + asked),
            out_shape=shapes + shapes[:asked],
            scratch_shapes=[
                pltpu.VMEM((rows, width), jnp.bfloat16) for width in widths for _ in range(2)
            ]
            + [pltpu.SemaphoreType.DMA((2 * chunks,))] * 2,
            compiler_params=params(),
            cost_estimate=cost(1),
            name="att_pack",
        )(query, query_swapped, key, value)
        return outs[:chunks], outs[chunks:]

    key_packs, query_packs = pack()
    conv_first, conv_last = conv
    local_result, *conv_shared = conv_first(query_packs[0])
    asks, quad_kv, all_answers = {}, [], []

    def send(chunk):
        key_pack = key_packs[chunk]
        if chunk >= LAG:
            earlier = all_answers[chunk - LAG - 1] if chunk > LAG else asks[0]
            key_pack = after(key_pack, quad_kv[chunk - LAG][0], earlier[0])
        quad_kv.append([lax.ppermute(key_pack, "ctx", gathers)])
        if chunk < asked:
            query_pack = query_packs[chunk]
            if chunk >= LAG:
                query_pack = after(query_pack, *asks[chunk - LAG], all_answers[chunk - LAG][0])
            asks[chunk] = [lax.ppermute(query_pack, "ctx", pairs) for pairs in transfers]

    half_rows = HEADS_PER_STEP * rows + TAIL
    hbm = pl.BlockSpec(memory_space=pl.ANY)
    for chunk in range(min(LAG, chunks)):
        send(chunk)
    result = None
    returned = []
    for chunk in range(chunks):
        if chunk == 0:
            quad_kv[0] = [after(quad_kv[0][0], local_result)]
            asks[0] = [after(asked, local_result) for asked in asks[0]]
        elif chunk == 1:
            quad_kv[1] = [after(quad_kv[1][0], all_answers[0][0])]
        quad_kv[chunk].append(lax.ppermute(quad_kv[chunk][0], "ctx", swap))
        steps, first = CHUNK_STEPS[chunk], first_steps[chunk]
        whole_spec = pl.BlockSpec((rows, step_width), lambda step, first=first: (0, first + step))
        chunk_spec = pl.BlockSpec((rows, step_width), lambda step: (0, step))
        pair_spec = pl.BlockSpec((2, rows, step_width), lambda step: (0, 0, step))
        lse_spec = pl.BlockSpec((SUBLANES, LANES), lambda step: (step, 0))
        answer_spec = pl.BlockSpec((2 * half_rows, LANES), lambda step: (step, 0))
        answer_shape = jax.ShapeDtypeStruct((2 * half_rows * steps, LANES), jnp.bfloat16)
        asking = both_ways and chunk + LAG < chunks
        natural = chunk < asked
        operands = [query, key, value, key_swapped, value_swapped, *quad_kv[chunk], *asks[chunk]]
        specs = [whole_spec] * 5 + [pair_spec] * 2
        specs += [pair_spec if natural else answer_spec] * len(transfers)
        if asking:
            later = first_steps[chunk + LAG]
            operands += [query, query_swapped]
            specs += [
                pl.BlockSpec((rows, step_width), lambda step, later=later: (0, later + step))
            ] * 2
        aliases = {}
        if result is not None:
            aliases = {len(operands): 2 + len(transfers)}
            operands.append(result)
            specs.append(hbm)
        own, lse, *answers, result = pl.pallas_call(
            functools.partial(partial_kernel, transfers, upper, natural, asking, len(aliases)),
            grid=(steps,),
            in_specs=specs,
            out_specs=[chunk_spec, lse_spec] + [answer_spec] * len(transfers) + [whole_spec],
            out_shape=[
                jax.ShapeDtypeStruct((rows, widths[chunk]), jnp.float32),
                jax.ShapeDtypeStruct((SUBLANES * steps, LANES), jnp.float32),
            ]
            + [answer_shape] * len(transfers)
            + [jax.ShapeDtypeStruct((rows, columns), jnp.bfloat16)],
            input_output_aliases=aliases,
            compiler_params=params(),
            cost_estimate=cost(4),
            name="att_partial",
        )(*operands)
        all_answers.append(answers)
        parts = [own, lse]
        arrivals = []
        for answer, pairs in zip(answers, transfers):
            moves = [(target, source) for source, target in pairs]
            if asking:
                moves += pairs
            if chunk == chunks - 1:
                live = (answer, conv_shared, [part[2] for part in returned], result)
                answer, conv_shared, early, result = lax.optimization_barrier(live)
                returned = [part[:2] + [back] for part, back in zip(returned, early)]
            arrivals.append(lax.ppermute(answer, "ctx", moves))
        if asking:
            asks[chunk + LAG] = arrivals
        returned.append([own, lse, arrivals])
        if chunk + LAG < chunks:
            send(chunk + LAG)
    hyena_out = conv_last(local_result, *conv_shared)
    for chunk, (own, lse, arrivals) in enumerate(returned):
        if chunk == chunks - 1:
            live = (arrivals, hyena_out, result)
            arrivals, hyena_out, result = lax.optimization_barrier(live)
        parts = [own, lse]
        for arrival in arrivals:
            parts += [arrival, lax.ppermute(arrival, "ctx", swap)]
        steps = CHUNK_STEPS[chunk]
        count = 2 * len(transfers)
        result = pl.pallas_call(
            functools.partial(merge_kernel, transfers, steps, starts[chunk]),
            in_specs=[hbm] * (len(parts) + 1),
            out_specs=hbm,
            out_shape=jax.ShapeDtypeStruct((rows, columns), jnp.bfloat16),
            input_output_aliases={len(parts): 0},
            scratch_shapes=[
                pltpu.VMEM((rows, widths[chunk]), jnp.float32),
                pltpu.VMEM((SUBLANES * steps, LANES), jnp.float32),
            ]
            + [pltpu.VMEM((steps, half_rows, LANES), jnp.bfloat16)] * count
            + [
                pltpu.VMEM((rows, widths[chunk]), jnp.bfloat16),
                pltpu.SemaphoreType.DMA((3 + count * steps,)),
            ],
            compiler_params=params(),
            cost_estimate=cost(2),
            name="att_merge",
        )(*parts, result)
    return hyena_out, result


def local(
    hyena_q, hyena_k, hyena_v, short_filter, residue, decay_rate, att_query, att_key, att_value
):
    conv = convolution(hyena_q, hyena_k, hyena_v, short_filter, residue, decay_rate)
    return attend(att_query, att_key, att_value, conv)


def solution(mesh):
    rows = P(("dp", "ctx"), None)
    shared = P("ctx", None)
    return jax.shard_map(
        local,
        mesh=mesh,
        in_specs=(rows, rows, rows, P(), shared, shared, rows, rows, rows),
        out_specs=(rows, rows),
        check_vma=False,
    )
```

```python
import functools
import math

import jax
import jax.numpy as jnp
from jax import lax
from jax.experimental import pallas as pl
from jax.experimental.pallas import tpu as pltpu
from jax.sharding import PartitionSpec as P

HEAD_DIM = 128
LANES = 128
SUBLANES = 8
TAIL = 4 * SUBLANES
TAPS = 3
HEADS_PER_STEP = 4
CHUNK_STEPS = (2, 2, 2, 2)
LAG = 2
NEGATIVE = -1e30
EXP_SCALE = HEAD_DIM**-0.5 * math.log2(math.e)
VMEM_LIMIT = 255 * 1024 * 256


def params(**kwargs):
    return pltpu.CompilerParams(vmem_limit_bytes=VMEM_LIMIT, **kwargs)


def cost(microseconds):
    return pl.CostEstimate(
        flops=microseconds * 10**7, bytes_accessed=2**16, transcendentals=0
    )


def block_lanes(block):
    return slice(block * LANES, (block + 1) * LANES)


def conv_pack_kernel(rate_ref, residue_ref, q_ref, k_ref, v_ref, par_ref, rim_ref):
    modes = rate_ref.shape[0]
    for block in range(rate_ref.shape[1] // LANES):
        for which, ref in enumerate((rate_ref, residue_ref)):
            start = (2 * block + which) * modes
            for device in range(par_ref.shape[0]):
                par_ref[device, start : start + modes, :] = ref[:, block_lanes(block)]
    for feature, ref in enumerate((q_ref, k_ref, v_ref)):
        last = ref[...].astype(jnp.float32)[ref.shape[0] - 2 :]
        rim_ref[2 * feature : 2 * feature + 2, :] = last
    rim_ref[2 * TAPS :, :] = jnp.zeros((2, rim_ref.shape[1]), jnp.float32)


def rim_rows(rim_ref, feature, lanes):
    return [rim_ref[pl.ds(2 * feature + row, 1), lanes] for row in range(2)]


def short_mix(feature, rim, taps):
    two_before, one_before = rim
    row = lax.broadcasted_iota(jnp.int32, feature.shape, 0)
    one = jnp.where(row == 0, one_before, pltpu.roll(feature, 1, 0))
    two = jnp.where(row == 0, two_before, jnp.where(row == 1, one_before, pltpu.roll(feature, 2, 0)))
    return taps[0] * feature + taps[1] * one + taps[2] * two


def tap_rows(taps_ref, feature, lanes):
    return [taps_ref[feature, pl.ds(tap, 1), lanes] for tap in range(TAPS)]


def join_parameters(same_ref, other_ref, par_ref):
    odd = lax.axis_index("ctx") % 2
    chips, rows, _ = same_ref.shape
    for chip in range(chips):
        for ref, core in ((same_ref, odd), (other_ref, 1 - odd)):
            start = pl.multiple_of((2 * chip + core) * rows, SUBLANES)
            par_ref[pl.ds(start, rows), :] = ref[chip]


def state_kernel(
    modes,
    k_ref,
    v_ref,
    rim_ref,
    same_ref,
    other_ref,
    taps_ref,
    y_ref,
    s_ref,
    d_ref,
    par_ref,
    p_scr,
    y_scr,
):
    join_parameters(same_ref, other_ref, par_ref)
    rows = k_ref.shape[0]
    for block in range(SUBLANES):
        lanes = block_lanes(block)
        mixes = [
            short_mix(
                ref[:, lanes].astype(jnp.float32),
                rim_rows(rim_ref, feature, lanes),
                tap_rows(taps_ref, feature, lanes),
            )
            for feature, ref in ((1, k_ref), (2, v_ref))
        ]
        product = (mixes[0] * mixes[1]).astype(jnp.bfloat16).astype(jnp.float32)
        p_scr[pl.ds(block, rows, SUBLANES), :] = product
    decay = [jnp.exp(-par_ref[pl.ds(mode, SUBLANES, 2 * modes), :]) for mode in range(modes)]
    residue = [par_ref[pl.ds(modes + mode, SUBLANES, 2 * modes), :] for mode in range(modes)]

    def body(position, states):
        here = pl.ds(pl.multiple_of(position * SUBLANES, SUBLANES), SUBLANES)
        product = p_scr[here, :]
        states = tuple(state * rate + product for state, rate in zip(states, decay))
        terms = [state * weight for state, weight in zip(states, residue)]
        while len(terms) > 1:
            terms = [left + right for left, right in zip(terms[::2], terms[1::2])]
        y_scr[here, :] = terms[0]
        return states

    zero = jnp.zeros((SUBLANES, LANES), jnp.float32)
    states = lax.fori_loop(0, rows, body, (zero,) * modes, unroll=4)
    for mode in range(modes):
        s_ref[pl.ds(mode, SUBLANES, modes), :] = states[mode]
    for block in range(SUBLANES):
        rate = par_ref[2 * block * modes : (2 * block + 1) * modes, :]
        d_ref[block * modes : (block + 1) * modes, :] = jnp.exp(-rate * rows)
    for block in range(SUBLANES):
        y_ref[:, block_lanes(block)] = y_scr[pl.ds(block, rows, SUBLANES), :]


def output_kernel(
    modes,
    q_ref,
    y_ref,
    rim_ref,
    same_ref,
    other_par_ref,
    decay_ref,
    enter_ref,
    enter_first_ref,
    other_ref,
    taps_ref,
    out_ref,
    par_ref,
):
    join_parameters(same_ref, other_par_ref, par_ref)
    second = lax.axis_index("ctx") % 2 == 1
    rows = q_ref.shape[0]
    step = lax.broadcasted_iota(jnp.int32, (SUBLANES, LANES), 0).astype(jnp.float32) + 1.0

    def body(block, nothing):
        lanes = pl.ds(pl.multiple_of(block * LANES, LANES), LANES)
        rate = par_ref[pl.ds(pl.multiple_of(2 * block * modes, SUBLANES), modes), :]
        residue = par_ref[pl.ds(pl.multiple_of((2 * block + 1) * modes, SUBLANES), modes), :]
        here = pl.ds(pl.multiple_of(block * modes, SUBLANES), modes)
        after_first = decay_ref[here, :] * enter_ref[here, :] + other_ref[here, :]
        entering = jnp.where(second, after_first, enter_first_ref[here, :])
        weighted = residue * entering
        eight = jnp.exp(-rate * SUBLANES)
        terms = [
            weighted[mode : mode + 1] * jnp.exp(-rate[mode : mode + 1] * step)
            for mode in range(modes)
        ]
        eights = [jnp.broadcast_to(eight[mode : mode + 1], terms[0].shape) for mode in range(modes)]
        added = []
        for start in range(0, rows, SUBLANES):
            sums = list(terms)
            while len(sums) > 1:
                sums = [left + right for left, right in zip(sums[::2], sums[1::2])]
            added.append(sums[0])
            if start + SUBLANES < rows:
                terms = [term * decay for term, decay in zip(terms, eights)]
        smoothed = y_ref[:, lanes] + jnp.concatenate(added, 0)
        smoothed = smoothed.astype(jnp.bfloat16).astype(jnp.float32)
        mix = short_mix(
            q_ref[:, lanes].astype(jnp.float32),
            rim_rows(rim_ref, 0, lanes),
            tap_rows(taps_ref, 0, lanes),
        )
        out_ref[:, lanes] = (mix * smoothed).astype(out_ref.dtype)
        return nothing

    lax.fori_loop(0, SUBLANES, body, 0)


def convolution(hyena_q, hyena_k, hyena_v, short_filter, residue, decay_rate):
    rows, channels = hyena_q.shape
    devices = lax.axis_size("ctx")
    modes = residue.shape[1]
    own_blocks = residue.shape[0] // LANES
    blocks = channels // LANES
    groups = blocks // SUBLANES
    width = SUBLANES * LANES
    end = rows // 16 - 1
    par_rows = 2 * own_blocks * modes
    feature_spec = pl.BlockSpec((rows, width), lambda group: (0, group))
    rim_spec = pl.BlockSpec((8, width), lambda group: (0, group))
    chips = SUBLANES // (2 * own_blocks)
    par_spec = pl.BlockSpec((chips, par_rows, LANES), lambda group: (group, 0, 0))
    par_scratch = pltpu.VMEM((2 * SUBLANES * modes, LANES), jnp.float32)
    taps_spec = pl.BlockSpec((TAPS, TAPS, width), lambda group: (0, 0, group))
    positions = pltpu.VMEM((rows * SUBLANES, LANES), jnp.float32)

    def first_part(token):
        own_par, rim = pl.pallas_call(
            conv_pack_kernel,
            grid=(1,),
            in_specs=[pl.BlockSpec((modes, residue.shape[0]), lambda step: (0, 0))] * 2
            + [pl.BlockSpec((16, channels), lambda step: (end, 0))] * 3,
            out_specs=[
                pl.BlockSpec((devices // 2, par_rows, LANES), lambda step: (0, 0, 0)),
                pl.BlockSpec((8, channels), lambda step: (0, 0)),
            ],
            out_shape=[
                jax.ShapeDtypeStruct((devices // 2, par_rows, LANES), jnp.float32),
                jax.ShapeDtypeStruct((8, channels), jnp.float32),
            ],
            compiler_params=params(),
            cost_estimate=cost(1),
            name="conv_pack",
        )(decay_rate.T, residue.T, hyena_q, hyena_k, hyena_v)
        rim = lax.ppermute(rim, "ctx", [(index, index + 1) for index in range(devices - 1)])
        own_par = after(own_par, rim, token)
        same = lax.all_to_all(
            own_par,
            "ctx",
            split_axis=0,
            concat_axis=0,
            axis_index_groups=[list(range(core, devices, 2)) for core in range(2)],
            tiled=True,
        )
        par = (same, lax.ppermute(same, "ctx", [(index, index ^ 1) for index in range(devices)]))
        state_spec = pl.BlockSpec((SUBLANES * modes, LANES), lambda group: (group, 0))
        local_result, state, decay = pl.pallas_call(
            functools.partial(state_kernel, modes),
            grid=(groups,),
            in_specs=[feature_spec, feature_spec, rim_spec, par_spec, par_spec, taps_spec],
            out_specs=[feature_spec, state_spec, state_spec],
            out_shape=[
                jax.ShapeDtypeStruct((rows, channels), jnp.float32),
                jax.ShapeDtypeStruct((blocks * modes, LANES), jnp.float32),
                jax.ShapeDtypeStruct((blocks * modes, LANES), jnp.float32),
            ],
            scratch_shapes=[par_scratch, positions, positions],
            compiler_params=params(),
            cost_estimate=cost(9),
            name="conv_state",
        )(hyena_k, hyena_v, rim, *par, short_filter)
        return local_result, rim, par, decay, *entering_state(state, decay)

    def entering_state(state, decay):
        swap = [(index, index ^ 1) for index in range(devices)]
        other = lax.ppermute(state, "ctx", swap)
        total = state + decay * other
        entering = None
        reach = 1
        while 2 * reach < devices:
            moves = [(index, index + 2 * reach) for index in range(1, devices - 2 * reach, 2)]
            arrived = lax.ppermute(total, "ctx", moves)
            if reach == 1:
                entering = arrived
            else:
                entering = entering + decay ** (2 * (reach - 1)) * arrived
            if 4 * reach < devices:
                total = total + decay ** (2 * reach) * arrived
            reach *= 2
        return entering, lax.ppermute(entering, "ctx", swap), other

    def last_part(local_result, rim, par, decay, entering, entering_first, other):
        state_spec = pl.BlockSpec((SUBLANES * modes, LANES), lambda group: (group, 0))
        return pl.pallas_call(
            functools.partial(output_kernel, modes),
            grid=(groups,),
            in_specs=[feature_spec, feature_spec, rim_spec, par_spec, par_spec]
            + [state_spec] * 4
            + [taps_spec],
            out_specs=feature_spec,
            out_shape=jax.ShapeDtypeStruct((rows, channels), jnp.bfloat16),
            scratch_shapes=[par_scratch],
            compiler_params=params(),
            cost_estimate=cost(6),
            name="conv_output",
        )(
            hyena_q,
            local_result,
            rim,
            *par,
            decay,
            entering,
            entering_first,
            other,
            short_filter,
        )

    return first_part, last_part


def among(me, members):
    return functools.reduce(jnp.logical_or, [me == member for member in members])


def plan_moves(devices):
    quads = devices // 4
    transfers = [[(devices - 1, devices - 3)]]
    for distance in range(1, quads):
        if distance > len(transfers):
            transfers.append([])
        for quad in range(distance, quads):
            target = 4 * (quad - distance) + 2
            transfers[distance - 1] += [(4 * quad, target), (4 * quad + 2, target + 1)]
    return transfers


def soft(query, keys, values, mask=None):
    scores = lax.dot_general(
        query, keys, (((1,), (1,)), ((), ())), preferred_element_type=jnp.float32
    )
    if mask is not None:
        scores = jnp.where(mask, scores, NEGATIVE)
    top = jnp.max(scores, axis=1, keepdims=True) * EXP_SCALE
    expo = jnp.exp2(scores * EXP_SCALE - top).astype(jnp.bfloat16)
    mixed = jnp.dot(expo, values, preferred_element_type=jnp.float32)
    total = mixed[:, HEAD_DIM:]
    return mixed[:, :HEAD_DIM] / total, top + jnp.log2(total)


def pack_kernel(gathers, askers, asked, widths, starts, q_ref, qs_ref, k_ref, v_ref, *rest):
    count = len(widths)
    key_outs, query_outs = rest[:count], rest[count : count + asked]
    stages, in_sems, out_sems = rest[count + asked : -2], rest[-2], rest[-1]
    me = lax.axis_index("ctx")
    odd = me % 2

    def run(pairs):
        loads = [
            pltpu.make_async_copy(source, stage, in_sems.at[index])
            for index, ((source, _), stage) in enumerate(zip(pairs, stages))
        ]
        stores = [
            pltpu.make_async_copy(stage, target, out_sems.at[index])
            for index, ((_, target), stage) in enumerate(zip(pairs, stages))
        ]
        for load in loads:
            load.start()
        for load, store in zip(loads, stores):
            load.wait()
            store.start()
        for store in stores:
            store.wait()

    def cut(ref, chunk):
        return ref.at[:, pl.ds(starts[chunk], widths[chunk])]

    if gathers:

        @pl.when(among(me, gathers))
        def _():
            run(
                [
                    (cut(ref, chunk), key_outs[chunk].at[which])
                    for chunk in range(count)
                    for which, ref in enumerate((k_ref, v_ref))
                ]
            )

    @pl.when(among(me, askers))
    def _():
        run(
            [
                (cut(ref, chunk), query_outs[chunk].at[half])
                for chunk in range(asked)
                for ref, half in ((q_ref, odd), (qs_ref, 1 - odd))
            ]
        )


def as_rows(columns):
    lanes = lax.broadcasted_iota(jnp.int32, columns[0].shape, 1)
    sums = jnp.zeros_like(columns[0])
    for index, column in enumerate(columns):
        sums = jnp.where(lanes == index, column, sums)
    return jnp.transpose(sums)[:SUBLANES]


def as_columns(part):
    fill = jnp.zeros((LANES - part.shape[0], part.shape[1]), jnp.float32)
    return jnp.transpose(jnp.concatenate([part, fill], 0))


def partial_kernel(transfers, upper, natural, asking, onto, *refs):
    count = len(transfers)
    out_ref = refs[-1]
    if asking:
        next_refs = refs[7 + count : 9 + count]
        refs = refs[: 7 + count] + refs[9 + count :]
    q_ref, k_ref, v_ref, kp_ref, vp_ref, g_ref, gp_ref = refs[:7]
    ask_refs = refs[7 : 7 + count]
    own_ref, lse_ref = refs[7 + count + onto : 9 + count + onto]
    answer_refs = refs[9 + count + onto : -1]
    me = lax.axis_index("ctx")
    rows = q_ref.shape[0]
    heads = q_ref.shape[1] // HEAD_DIM
    half_rows = heads * rows + TAIL

    def key_value(head, with_quad):
        cut = block_lanes(head)
        keys = [kp_ref[:, cut], k_ref[:, cut]]
        values = [vp_ref[:, cut], v_ref[:, cut]]
        if with_quad:
            keys = [g_ref[0, :, cut], gp_ref[0, :, cut]] + keys
            values = [g_ref[1, :, cut], gp_ref[1, :, cut]] + values
        values = jnp.concatenate(values, 0)
        return jnp.concatenate(keys, 0), jnp.concatenate([values, jnp.ones_like(values)], 1)

    def run(with_quad):
        key_count = rows * (4 if with_quad else 2)
        row = lax.broadcasted_iota(jnp.int32, (rows, key_count), 0)
        column = lax.broadcasted_iota(jnp.int32, (rows, key_count), 1)
        column = column - (key_count - 2 * rows)
        partner_limit = jnp.where(me % 2 == 1, rows, 0)
        mask = (column < partner_limit) | ((column >= rows) & (column - rows <= row))
        sums = []
        for head in range(heads):
            keys, values = key_value(head, with_quad)
            mixed, lse = soft(q_ref[:, block_lanes(head)], keys, values, mask)
            own_ref[:, block_lanes(head)] = mixed
            out_ref[:, block_lanes(head)] = mixed.astype(out_ref.dtype)
            sums.append(lse)
        lse_ref[...] = as_rows(sums)

        def answer(index):
            sums = [[], []]
            for head in range(heads):
                keys, values = key_value(head, with_quad)
                if natural:
                    query = ask_refs[index][:, :, block_lanes(head)].reshape(2 * rows, HEAD_DIM)
                else:
                    halves = [half * half_rows + head * rows for half in range(2)]
                    query = jnp.concatenate(
                        [ask_refs[index][start : start + rows, :] for start in halves], 0
                    )
                mixed, lse = soft(query, keys, values)
                for half in range(2):
                    cut = slice(half * rows, (half + 1) * rows)
                    start = half * half_rows + head * rows
                    answer_refs[index][start : start + rows, :] = mixed[cut].astype(jnp.bfloat16)
                    sums[half].append(lse[cut])
            for half in range(2):
                start = half * half_rows + heads * rows
                lse = as_rows(sums[half])
                first = lse.astype(jnp.bfloat16).astype(jnp.float32)
                second = (lse - first).astype(jnp.bfloat16).astype(jnp.float32)
                third = lse - first - second
                tail = jnp.concatenate([first, second, third, jnp.zeros_like(lse)], 0)
                answer_refs[index][start : start + TAIL, :] = tail.astype(jnp.bfloat16)

        for index, pairs in enumerate(transfers):
            asked = [target for _, target in pairs if (target in upper) == with_quad]
            if asked:
                pl.when(among(me, asked))(functools.partial(answer, index))

    if upper:
        pl.when(among(me, upper))(functools.partial(run, True))
        pl.when(jnp.logical_not(among(me, upper)))(functools.partial(run, False))
    else:
        run(False)

    if asking:
        for index, pairs in enumerate(transfers):

            @pl.when(among(me, [source for source, _ in pairs]))
            def _():
                for ref, half in zip(next_refs, (me % 2, 1 - me % 2)):
                    for head in range(heads):
                        start = pl.multiple_of(half * half_rows + head * rows, TAIL)
                        answer_refs[index][pl.ds(start, rows), :] = ref[:, block_lanes(head)]


def merge_kernel(transfers, steps, start, own_hbm, lse_hbm, *refs):
    count = 2 * len(transfers)
    others_hbm, out_hbm = refs[:count], refs[count + 1]
    own_ref, lse_ref, *other_refs = refs[count + 2 : 2 * count + 4]
    out_ref, sems = refs[-2:]
    me = lax.axis_index("ctx")
    odd = me % 2
    rows, width = own_ref.shape
    heads = HEADS_PER_STEP
    half_rows = heads * rows + TAIL
    returned = []
    for pairs in transfers:
        members = [source for source, _ in pairs]
        returned += [members, [member ^ 1 for member in members]]

    @pl.when(among(me, sorted(set(sum(returned, [])))))
    def _():
        loads = [(own_hbm, own_ref), (lse_hbm, lse_ref)]
        for hbm, ref in zip(others_hbm, other_refs):
            for step in range(steps):
                half = pl.ds(pl.multiple_of((2 * step + odd) * half_rows, TAIL), half_rows)
                loads.append((hbm.at[half, :], ref.at[step]))
        copies = [
            pltpu.make_async_copy(source, target, sems.at[index])
            for index, (source, target) in enumerate(loads)
        ]
        for copy in copies:
            copy.start()
        for copy in copies:
            copy.wait()
        valid = [among(me, members) for members in returned]
        for step in range(steps):
            logs = [lse_ref[step * SUBLANES : (step + 1) * SUBLANES, :]]
            for index, ref in enumerate(other_refs):
                tail = ref[step, heads * rows :, :].astype(jnp.float32)
                parts = [tail[part * SUBLANES : (part + 1) * SUBLANES] for part in range(3)]
                logs.append(jnp.where(valid[index], parts[0] + parts[1] + parts[2], NEGATIVE))
            top = functools.reduce(jnp.maximum, logs)
            weights = [jnp.exp2(part - top) for part in logs]
            total = functools.reduce(jnp.add, weights)
            shares = [as_columns(weight / total) for weight in weights]
            for head in range(heads):
                cut = block_lanes(step * heads + head)
                mixed = [own_ref[:, cut]]
                for index, ref in enumerate(other_refs):
                    part = ref[step, head * rows : (head + 1) * rows, :].astype(jnp.float32)
                    mixed.append(jnp.where(valid[index], part, 0.0))
                terms = [part * share[:, head : head + 1] for part, share in zip(mixed, shares)]
                out_ref[:, cut] = functools.reduce(jnp.add, terms).astype(out_ref.dtype)
        store = pltpu.make_async_copy(
            out_ref, out_hbm.at[:, pl.ds(start, width)], sems.at[len(copies)]
        )
        store.start()
        store.wait()


def after(array, *others):
    return lax.optimization_barrier((array, *others))[0]


def attend(query, key, value, conv):
    rows, columns = query.shape
    devices = lax.axis_size("ctx")
    quads = devices // 4
    transfers = plan_moves(devices)
    step_width = HEADS_PER_STEP * HEAD_DIM
    chunks = len(CHUNK_STEPS)
    first_steps = [sum(CHUNK_STEPS[:chunk]) for chunk in range(chunks)]
    widths = [steps * step_width for steps in CHUNK_STEPS]
    starts = [step * step_width for step in first_steps]
    upper = [4 * quad + 2 + core for quad in range(quads - 1) for core in range(2)]
    gathers = [(who - 2, who) for who in upper]
    askers = sorted({source for pairs in transfers for source, _ in pairs})
    swap = [(index, index ^ 1) for index in range(devices)]

    query_swapped = lax.ppermute(query, "ctx", swap)
    key_swapped = lax.ppermute(key, "ctx", swap)
    value_swapped = lax.ppermute(value, "ctx", swap)

    both_ways = chunks > LAG and all(
        not {source for source, _ in pairs} & {target for _, target in pairs}
        for pairs in transfers
    )
    asked = LAG if both_ways else chunks

    def pack():
        hbm = pl.BlockSpec(memory_space=pl.ANY)
        shapes = [jax.ShapeDtypeStruct((2, rows, width), jnp.bfloat16) for width in widths]
        outs = pl.pallas_call(
            functools.partial(
                pack_kernel,
                [source for source, _ in gathers],
                askers,
                asked,
                widths,
                starts,
            ),
            in_specs=[hbm] * 4,
            out_specs=[hbm] * (chunks + asked),
            out_shape=shapes + shapes[:asked],
            scratch_shapes=[
                pltpu.VMEM((rows, width), jnp.bfloat16) for width in widths for _ in range(2)
            ]
            + [pltpu.SemaphoreType.DMA((2 * chunks,))] * 2,
            compiler_params=params(),
            cost_estimate=cost(1),
            name="att_pack",
        )(query, query_swapped, key, value)
        return outs[:chunks], outs[chunks:]

    key_packs, query_packs = pack()
    conv_first, conv_last = conv
    local_result, *conv_shared = conv_first(query_packs[0])
    asks, quad_kv, all_answers = {}, [], []

    def send(chunk):
        key_pack = key_packs[chunk]
        if chunk >= LAG:
            key_pack = after(key_pack, quad_kv[chunk - LAG][0], *all_answers[chunk - LAG][:1])
        quad_kv.append([lax.ppermute(key_pack, "ctx", gathers)])
        if chunk < asked:
            query_pack = query_packs[chunk]
            if chunk >= LAG:
                query_pack = after(query_pack, *asks[chunk - LAG], all_answers[chunk - LAG][0])
            asks[chunk] = [lax.ppermute(query_pack, "ctx", pairs) for pairs in transfers]

    half_rows = HEADS_PER_STEP * rows + TAIL
    hbm = pl.BlockSpec(memory_space=pl.ANY)
    for chunk in range(min(LAG, chunks)):
        send(chunk)
    result = None
    returned = []
    for chunk in range(chunks):
        if chunk == 0:
            quad_kv[0] = [after(quad_kv[0][0], local_result)]
            asks[0] = [after(asked, local_result) for asked in asks[0]]
        elif chunk == chunks - 1:
            quad_kv[chunk] = [after(quad_kv[chunk][0], asks[3][0])]
        quad_kv[chunk].append(lax.ppermute(quad_kv[chunk][0], "ctx", swap))
        steps, first = CHUNK_STEPS[chunk], first_steps[chunk]
        whole_spec = pl.BlockSpec((rows, step_width), lambda step, first=first: (0, first + step))
        chunk_spec = pl.BlockSpec((rows, step_width), lambda step: (0, step))
        pair_spec = pl.BlockSpec((2, rows, step_width), lambda step: (0, 0, step))
        lse_spec = pl.BlockSpec((SUBLANES, LANES), lambda step: (step, 0))
        answer_spec = pl.BlockSpec((2 * half_rows, LANES), lambda step: (step, 0))
        answer_shape = jax.ShapeDtypeStruct((2 * half_rows * steps, LANES), jnp.bfloat16)
        asking = both_ways and chunk + LAG < chunks
        natural = chunk < asked
        operands = [query, key, value, key_swapped, value_swapped, *quad_kv[chunk], *asks[chunk]]
        specs = [whole_spec] * 5 + [pair_spec] * 2
        specs += [pair_spec if natural else answer_spec] * len(transfers)
        if asking:
            later = first_steps[chunk + LAG]
            operands += [query, query_swapped]
            specs += [
                pl.BlockSpec((rows, step_width), lambda step, later=later: (0, later + step))
            ] * 2
        aliases = {}
        if result is not None:
            aliases = {len(operands): 2 + len(transfers)}
            operands.append(result)
            specs.append(hbm)
        own, lse, *answers, result = pl.pallas_call(
            functools.partial(partial_kernel, transfers, upper, natural, asking, len(aliases)),
            grid=(steps,),
            in_specs=specs,
            out_specs=[chunk_spec, lse_spec] + [answer_spec] * len(transfers) + [whole_spec],
            out_shape=[
                jax.ShapeDtypeStruct((rows, widths[chunk]), jnp.float32),
                jax.ShapeDtypeStruct((SUBLANES * steps, LANES), jnp.float32),
            ]
            + [answer_shape] * len(transfers)
            + [jax.ShapeDtypeStruct((rows, columns), jnp.bfloat16)],
            input_output_aliases=aliases,
            compiler_params=params(),
            cost_estimate=cost(4),
            name="att_partial",
        )(*operands)
        all_answers.append(answers)
        parts = [own, lse]
        arrivals = []
        for answer, pairs in zip(answers, transfers):
            moves = [(target, source) for source, target in pairs]
            if asking:
                moves += pairs
            if chunk == chunks - 1:
                live = (answer, conv_shared, [part[2] for part in returned], result)
                answer, conv_shared, early, result = lax.optimization_barrier(live)
                returned = [part[:2] + [back] for part, back in zip(returned, early)]
            arrivals.append(lax.ppermute(answer, "ctx", moves))
        if asking:
            asks[chunk + LAG] = arrivals
        returned.append([own, lse, arrivals])
        if chunk + LAG < chunks:
            send(chunk + LAG)
    hyena_out = conv_last(local_result, *conv_shared)
    for chunk, (own, lse, arrivals) in enumerate(returned):
        if chunk == chunks - 1:
            live = (arrivals, hyena_out, result)
            arrivals, hyena_out, result = lax.optimization_barrier(live)
        parts = [own, lse]
        for arrival in arrivals:
            parts += [arrival, lax.ppermute(arrival, "ctx", swap)]
        steps = CHUNK_STEPS[chunk]
        count = 2 * len(transfers)
        result = pl.pallas_call(
            functools.partial(merge_kernel, transfers, steps, starts[chunk]),
            in_specs=[hbm] * (len(parts) + 1),
            out_specs=hbm,
            out_shape=jax.ShapeDtypeStruct((rows, columns), jnp.bfloat16),
            input_output_aliases={len(parts): 0},
            scratch_shapes=[
                pltpu.VMEM((rows, widths[chunk]), jnp.float32),
                pltpu.VMEM((SUBLANES * steps, LANES), jnp.float32),
            ]
            + [pltpu.VMEM((steps, half_rows, LANES), jnp.bfloat16)] * count
            + [
                pltpu.VMEM((rows, widths[chunk]), jnp.bfloat16),
                pltpu.SemaphoreType.DMA((3 + count * steps,)),
            ],
            compiler_params=params(),
            cost_estimate=cost(2),
            name="att_merge",
        )(*parts, result)
    return hyena_out, result


def local(
    hyena_q, hyena_k, hyena_v, short_filter, residue, decay_rate, att_query, att_key, att_value
):
    conv = convolution(hyena_q, hyena_k, hyena_v, short_filter, residue, decay_rate)
    return attend(att_query, att_key, att_value, conv)


def solution(mesh):
    rows = P(("dp", "ctx"), None)
    shared = P("ctx", None)
    return jax.shard_map(
        local,
        mesh=mesh,
        in_specs=(rows, rows, rows, P(), shared, shared, rows, rows, rows),
        out_specs=(rows, rows),
        check_vma=False,
    )
```
